32 devices in a mesh: dp: 2 (over x), fsdp: 16 (over z, y, core).
Axes of the slice: x: 2, y: 2, z: 4, core: 2. Of those that a mesh axis runs over, the one named last changes fastest.
Arguments:
- tokens: bfloat16 [32768, 768], P(('dp', 'fsdp')), may hold values from -6 to 6
- encoded: bfloat16 [32768, 768], P(('dp', 'fsdp')), may hold values from -6 to 6
- cotangent: bfloat16 [32768, 768], P(('dp', 'fsdp')), may hold values from -6 to 6
- bucket: int32 [32], P(('dp', 'fsdp')), may hold values from 0 to 1, as said below
- target_len: int32 [32, 4], P(('dp', 'fsdp')), may hold values from 0 to 1024, as said below
- source_len: int32 [32, 4], P(('dp', 'fsdp')), may hold values from 0 to 1024, as said below
- self_in: bfloat16 [768, 2304], P('fsdp'), may hold values from -0.21875 to 0.21875
- self_bias: bfloat16 [3, 768], P(None, 'fsdp'), may hold values from -1 to 1
- self_out: bfloat16 [768, 768], P('fsdp'), may hold values from -1.25 to 1.25
- cross_q: bfloat16 [768, 768], P('fsdp'), may hold values from -0.21875 to 0.21875
- cross_kv: bfloat16 [768, 1536], P('fsdp'), may hold values from -0.21875 to 0.21875
- cross_bias: bfloat16 [3, 768], P(None, 'fsdp'), may hold values from -1 to 1
- cross_out: bfloat16 [768, 768], P('fsdp'), may hold values from -1.25 to 1.25
- ffn_in: bfloat16 [768, 3072], P('fsdp'), may hold values from -0.21875 to 0.21875
- ffn_in_bias: bfloat16 [3072], P('fsdp'), may hold values from -1 to 1
- ffn_out: bfloat16 [3072, 768], P('fsdp'), may hold values from -0.109375 to 0.109375
- ffn_out_bias: bfloat16 [768], P('fsdp'), may hold values from -1 to 1
- norm_gain: bfloat16 [3, 768], P(None, 'fsdp'), may hold values from 0.5 to 1.5
- norm_shift: bfloat16 [3, 768], P(None, 'fsdp'), may hold values from -1 to 1
Outputs:
- output: bfloat16 [32768, 768], P(('dp', 'fsdp'))
- tokens_grad: bfloat16 [32768, 768], P(('dp', 'fsdp'))
- encoded_grad: bfloat16 [32768, 768], P(('dp', 'fsdp'))
- self_in_grad: float32 [768, 2304], P('fsdp')
- self_bias_grad: float32 [3, 768], P(None, 'fsdp')
- self_out_grad: float32 [768, 768], P('fsdp')
- cross_q_grad: float32 [768, 768], P('fsdp')
- cross_kv_grad: float32 [768, 1536], P('fsdp')
- cross_bias_grad: float32 [3, 768], P(None, 'fsdp')
- cross_out_grad: float32 [768, 768], P('fsdp')
- ffn_in_grad: float32 [768, 3072], P('fsdp')
- ffn_in_bias_grad: float32 [3072], P('fsdp')
- ffn_out_grad: float32 [3072, 768], P('fsdp')
- ffn_out_bias_grad: float32 [768], P('fsdp')
- norm_gain_grad: float32 [3, 768], P(None, 'fsdp')
- norm_shift_grad: float32 [3, 768], P(None, 'fsdp')
The draws below stay inside these ranges and needn't reach their ends.
Inputs may be any that keep to these rules, and one draw needn't show every extreme that they name: bucket[s] = 1: slot s holds one sequence of up to 1024 tokens; 0: 4 sequences of up to 256 tokens each. Both buckets occur in every draw. `target_len`: for a slot of bucket 1 the first entry is its sequence's length, 1 to 1024, and the others are 0; for bucket 0 every entry is a length of 1 to 256. Some slot's sequence has 1024 tokens and some short sequence has 256. `source_len`: laid out as target_len, for the encoder rows of each sequence; some slot's sequence has 1024 and some short sequence has 256.
All inputs are finite; a program needn't handle non-finite values.
Results may differ from the reference program's by a relative error of at most 0.024.
Values may be sent and summed in bfloat16 or wider, within the bound.
A program may use at most 448 MiB of HBM per device.

```python
import jax
import jax.numpy as jnp
from jax import lax

D = 768
H = 12
FF = 3072
HD = 64
LONG = 1024
SEGS = 4
SHORT = 256
SLOT_ALL = 32
TOKENS = 32768


def slot_kinds(key):
    rolled = jax.random.randint(jax.random.fold_in(key, 101), (SLOT_ALL,), 0, 5)
    chosen = jax.random.randint(jax.random.fold_in(key, 102), (), 0, SLOT_ALL)
    places = jnp.arange(SLOT_ALL)
    bucket_ids = jnp.where(rolled < 2, 1, 0)
    bucket_ids = jnp.where(places == chosen, 1, bucket_ids)
    bucket_ids = jnp.where(places == (chosen + 1) % SLOT_ALL, 0, bucket_ids)
    return (bucket_ids.astype(jnp.int32), chosen)


def length_table(key, bucket_ids, chosen):
    short_part = jax.random.randint(jax.random.fold_in(key, 1), (SLOT_ALL, SEGS), 1, SHORT + 1)
    long_part = jax.random.randint(jax.random.fold_in(key, 2), (SLOT_ALL,), 1, LONG + 1)
    segment_pick = jax.random.randint(jax.random.fold_in(key, 3), (), 0, SEGS)
    places = jnp.arange(SLOT_ALL)
    columns = jnp.arange(SEGS)
    long_part = jnp.where(places == chosen, LONG, long_part)
    short_hit = (places[:, None] == (chosen + 1) % SLOT_ALL) & (columns[None, :] == segment_pick)
    short_part = jnp.where(short_hit, SHORT, short_part)
    long_rows = jnp.where(columns[None, :] == 0, long_part[:, None], 0)
    return jnp.where(bucket_ids[:, None] == 1, long_rows, short_part).astype(jnp.int32)


def draw_bucket(key, part):
    bucket_ids, chosen = slot_kinds(key)
    return bucket_ids


def draw_target_len(key, part):
    bucket_ids, chosen = slot_kinds(key)
    key = jax.random.fold_in(key, 7)
    return length_table(key, bucket_ids, chosen)


def draw_source_len(key, part):
    bucket_ids, chosen = slot_kinds(key)
    key = jax.random.fold_in(key, 9)
    return length_table(key, bucket_ids, chosen)


def block_levels(rng, dims, split, low, largest):
    factor_of, own = 1.0, jax.random.fold_in(rng, 6)
    for dim, parts in split:
        heights = jnp.exp(jax.random.uniform(jax.random.fold_in(own, dim), (parts,), jnp.float32, low / len(split), largest / len(split)))
        factor_of = factor_of * jnp.repeat(heights, dims[dim] // parts).reshape([-1 if axis == dim else 1 for axis in range(len(dims))])
    return factor_of


def centred(rng, extent, width, most, split=(), kind=jnp.bfloat16):
    values = width * jax.random.normal(rng, extent, jnp.float32)
    if split:
        values = values * block_levels(rng, extent, split, -0.22, 0.18)
    return jnp.clip(values, -most, most).astype(kind)


def setup_inputs(seed: int = 0) -> dict:
    splits = jax.random.split(jax.random.key(seed), 20)
    tokens = centred(splits[0], (TOKENS, D), 1.0, 6.0, ((0, 32),))
    encoded = centred(splits[1], (TOKENS, D), 1.0, 6.0, ((0, 32),))
    cotangent = centred(splits[2], (TOKENS, D), 1.0, 6.0, ((0, 32),))
    bucket = draw_bucket(jax.random.fold_in(splits[19], 71), 0)
    target_len = draw_target_len(jax.random.fold_in(splits[19], 71), 0)
    source_len = draw_source_len(jax.random.fold_in(splits[19], 71), 0)
    self_in = centred(splits[6], (D, 3 * D), D ** -0.5, 0.21875, ((0, 16),))
    self_bias = centred(splits[7], (3, D), 0.2, 1.0, ((1, 16),))
    self_out = centred(splits[8], (D, D), (D // 32) ** -0.5, 1.25, ((0, 16),))
    cross_q = centred(splits[9], (D, D), D ** -0.5, 0.21875, ((0, 16),))
    cross_kv = centred(splits[10], (D, 2 * D), D ** -0.5, 0.21875, ((0, 16),))
    cross_bias = centred(splits[11], (3, D), 0.2, 1.0, ((1, 16),))
    cross_out = centred(splits[12], (D, D), (D // 32) ** -0.5, 1.25, ((0, 16),))
    ffn_in = centred(splits[13], (D, FF), D ** -0.5, 0.21875, ((0, 16),))
    ffn_in_bias = centred(splits[14], (FF,), 0.2, 1.0, ((0, 16),))
    ffn_out = centred(splits[15], (FF, D), FF ** -0.5, 0.109375, ((0, 16),))
    ffn_out_bias = centred(splits[16], (D,), 0.2, 1.0, ((0, 16),))
    norm_gain = jnp.clip(1.0 + 0.1 * jax.random.normal(splits[17], (3, D), jnp.float32), 0.5, 1.5).astype(jnp.bfloat16)
    norm_shift = centred(splits[18], (3, D), 0.2, 1.0, ((1, 16),))
    return {"tokens": tokens, "encoded": encoded, "cotangent": cotangent, "bucket": bucket, "target_len": target_len, "source_len": source_len, "self_in": self_in, "self_bias": self_bias, "self_out": self_out, "cross_q": cross_q, "cross_kv": cross_kv, "cross_bias": cross_bias, "cross_out": cross_out, "ffn_in": ffn_in, "ffn_in_bias": ffn_in_bias, "ffn_out": ffn_out, "ffn_out_bias": ffn_out_bias, "norm_gain": norm_gain, "norm_shift": norm_shift}


EPS = 1e-05
NEG = -1e+30

@jax.custom_vjp
def low(v):
    return lax.optimization_barrier(v.astype(jnp.bfloat16)).astype(jnp.float32)

@jax.custom_vjp
def low_back(v):
    return v

def low_keep(v):
    return (low(v), None)

def low_pass(kept, grad):
    return (grad,)

def back_keep(v):
    return (v, None)

def back_low(kept, grad):
    return (low(grad),)
low.defvjp(low_keep, low_pass)
low_back.defvjp(back_keep, back_low)

def rounded(value):
    return low_back(low(value))

def matmul(left_mat, right_mat):
    return jnp.dot(left_mat, right_mat, preferred_element_type=jnp.float32, precision=lax.Precision.HIGHEST)

def layer_norm(residual, gains, shifts):
    row_mean = lax.optimization_barrier(jnp.mean(residual, axis=-1, keepdims=True))
    centered = residual - row_mean
    variance = lax.optimization_barrier(jnp.mean(centered * centered, axis=-1, keepdims=True))
    return centered * lax.rsqrt(variance + EPS) * gains + shifts

def attention(query, keys, values, allowed):
    heads_q = query.reshape(LONG, H, HD)
    heads_k = keys.reshape(LONG, H, HD)
    heads_v = values.reshape(LONG, H, HD)
    scores = low_back(jnp.einsum('qhd,khd->hqk', heads_q, heads_k, precision=lax.Precision.HIGHEST))
    scores = jnp.where(allowed[None], scores, NEG)
    row_max = lax.optimization_barrier(jnp.max(scores, axis=-1, keepdims=True))
    expo = jnp.exp(scores - row_max)
    probs = low(expo / lax.optimization_barrier(jnp.sum(expo, axis=-1, keepdims=True)))
    mixed = jnp.einsum('hqk,khd->qhd', probs, heads_v, precision=lax.Precision.HIGHEST)
    return rounded(mixed.reshape(LONG, D))

def slot_layer(params, slot_tokens, slot_encoded, kind, target_row, source_row):
    self_in, self_bias, self_out, cross_q, cross_kv, cross_bias, cross_out, ffn_in, ffn_in_bias, ffn_out, ffn_out_bias, norm_gain, norm_shift = params
    scaling = HD ** (-0.5)
    places = jnp.arange(LONG, dtype=jnp.int32)
    segment = jnp.where(kind == 1, 0, places // SHORT).astype(jnp.int32)
    offset = jnp.where(kind == 1, places, places % SHORT)
    target_live = offset < target_row[segment]
    source_live = offset < source_row[segment]
    same_segment = segment[:, None] == segment[None, :]
    self_allowed = same_segment & (places[None, :] <= places[:, None]) & target_live[None, :]
    cross_allowed = same_segment & source_live[None, :]
    mixed = matmul(slot_tokens, self_in)
    query = rounded((mixed[:, :D] + self_bias[0]) * scaling)
    keys = rounded(mixed[:, D:2 * D])
    values = rounded(mixed[:, 2 * D:] + self_bias[1])
    self_att = attention(query, keys, values, self_allowed)
    branch1 = low_back(matmul(self_att, self_out) + self_bias[2])
    hidden1 = low(layer_norm(slot_tokens + branch1, norm_gain[0], norm_shift[0]))
    pairs = matmul(slot_encoded, cross_kv)
    cross_query = rounded((matmul(hidden1, cross_q) + cross_bias[0]) * scaling)
    cross_keys = rounded(pairs[:, :D])
    cross_values = rounded(pairs[:, D:] + cross_bias[1])
    cross_att = attention(cross_query, cross_keys, cross_values, cross_allowed)
    branch2 = low_back(matmul(cross_att, cross_out) + cross_bias[2])
    hidden2 = low(layer_norm(hidden1 + branch2, norm_gain[1], norm_shift[1]))
    pre_act = low_back(matmul(hidden2, ffn_in) + ffn_in_bias)
    activ = low(jax.nn.gelu(pre_act, approximate=False))
    branch3 = low_back(matmul(activ, ffn_out) + ffn_out_bias)
    return layer_norm(hidden2 + branch3, norm_gain[2], norm_shift[2])

def forward(params, tokens, encoded, bucket, target_len, source_len):
    layer = jax.checkpoint(slot_layer)

    def visit(carry, member):
        slot_tokens, slot_encoded, kind, target_row, source_row = member
        return (carry, layer(params, slot_tokens, slot_encoded, kind, target_row, source_row))
    token_slots = tokens.reshape(SLOT_ALL, LONG, D)
    encoded_slots = encoded.reshape(SLOT_ALL, LONG, D)
    start = jnp.zeros((), jnp.float32)
    _, outputs = lax.scan(visit, start, (token_slots, encoded_slots, bucket, target_len, source_len))
    return outputs.reshape(SLOT_ALL * LONG, D)

def reference(tokens, encoded, cotangent, bucket, target_len, source_len, self_in, self_bias, self_out, cross_q, cross_kv, cross_bias, cross_out, ffn_in, ffn_in_bias, ffn_out, ffn_out_bias, norm_gain, norm_shift):
    params = tuple((member.astype(jnp.float32) for member in (self_in, self_bias, self_out, cross_q, cross_kv, cross_bias, cross_out, ffn_in, ffn_in_bias, ffn_out, ffn_out_bias, norm_gain, norm_shift)))

    def whole_layer(tokens32, encoded32, params32):
        return forward(params32, tokens32, encoded32, bucket, target_len, source_len)
    output, pullback = jax.vjp(whole_layer, tokens.astype(jnp.float32), encoded.astype(jnp.float32), params)
    tokens_grad, encoded_grad, param_grads = pullback(cotangent.astype(jnp.float32))
    return (output.astype(jnp.bfloat16), tokens_grad.astype(jnp.bfloat16), encoded_grad.astype(jnp.bfloat16), param_grads[0], param_grads[1], param_grads[2], param_grads[3], param_grads[4], param_grads[5], param_grads[6], param_grads[7], param_grads[8], param_grads[9], param_grads[10], param_grads[11], param_grads[12])
```

```python
from functools import partial

import jax
import jax.numpy as jnp
from jax import lax
from jax.experimental import pallas as pl
from jax.experimental.pallas import tpu as pltpu
from jax.sharding import PartitionSpec as P

D = 768
H = 12
HD = 64
FF = 3072
LONG = 1024
SEGS = 4
SHORT = 256
PAIRS = H // 2
WIDE = 2 * HD

EPS = 1e-05
NEG = -1e30
SCALE = HD ** (-0.5)
F32 = jnp.float32
BF16 = jnp.bfloat16
MESH_ID = pl.DeviceIdType.MESH
VMEM_LIMIT = 56 << 20

SELF_B, CROSS_B, GAIN, SHIFT, OUT_B, IN_B = 0, 3, 6, 9, 12, 13
VEC_ROWS = 17
PACK = 2048


def mm(left, right, left_dim=1, right_dim=0):
    return lax.dot_general(
        left, right, (((left_dim,), (right_dim,)), ((), ())), preferred_element_type=F32
    )


def params(**kwargs):
    return pltpu.CompilerParams(vmem_limit_bytes=VMEM_LIMIT, **kwargs)


def cost(flops, nbytes, trans=0):
    return pl.CostEstimate(flops=int(flops), bytes_accessed=int(nbytes), transcendentals=int(trans))


def any_spec():
    return pl.BlockSpec(memory_space=pl.ANY)


def whole(shape):
    return pl.BlockSpec(shape, lambda *_: (0,) * len(shape))


def normed(resid):
    centered = resid - jnp.mean(resid, axis=-1, keepdims=True)
    inv = lax.rsqrt(jnp.mean(centered * centered, axis=-1, keepdims=True) + EPS)
    return centered * inv, inv


def norm_back(xhat, inv, gain, grad):
    scaled = grad * gain
    first = jnp.mean(scaled, axis=-1, keepdims=True)
    second = jnp.mean(scaled * xhat, axis=-1, keepdims=True)
    return (scaled - first - xhat * second) * inv


def col_sum(values):
    return jnp.sum(values, axis=0, keepdims=True)


def my_place():
    dp, index = lax.axis_index("dp"), lax.axis_index("fsdp")
    return dp, index // 4, (index // 2) % 2, index % 2


def place(dp, z, y, core):
    return {"dp": dp, "fsdp": (z * 2 + y) * 2 + core}


def neighbours():
    x, z, y, c = my_place()
    return [place(x, (z + k) % 4, y, c) for k in (1, 2, 3)] + [
        place(1 - x, z, y, c),
        place(x, z, 1 - y, c),
        place(x, z, y, 1 - c),
    ]


def greet():
    barrier = pltpu.get_barrier_semaphore()
    others = neighbours()
    for other in others:
        pl.semaphore_signal(barrier, inc=1, device_id=other, device_id_type=MESH_ID)
    pl.semaphore_wait(barrier, len(others))


def remote(src, dst, sems, index, device):
    return pltpu.make_async_remote_copy(
        src_ref=src,
        dst_ref=dst,
        send_sem=sems.at[0, index],
        recv_sem=sems.at[1, index],
        device_id=device,
        device_id_type=MESH_ID,
    )


GATHER_COPIES = 11


def gather_copies(shard, full, sems, local_sem):
    x, z, y, c = my_place()
    half = shard.shape[1] // 2
    mine = pl.ds(pl.multiple_of(x * half, 128), half)
    other = pl.ds(pl.multiple_of((1 - x) * half, 128), half)
    to_x, to_y, to_c = place(1 - x, z, y, c), place(x, z, 1 - y, c), place(x, z, y, 1 - c)

    def same(index, where, device):
        ref = full.at[where]
        return remote(ref, ref, sems, index, device)

    own = (slice(None), y, c, slice(None), mine)
    from_x = (slice(None), y, c, slice(None), other)
    from_y = (slice(None), 1 - y, c, slice(None), mine)
    diagonal = (slice(None), 1 - y, c, slice(None), other)
    copies = [
        remote(shard.at[:, mine], full.at[z, y, c, :, mine], sems, k - 1, place(x, (z + k) % 4, y, c))
        for k in (1, 2, 3)
    ]
    copies += [same(3, own, to_x), same(4, own, to_y)]
    copies += [
        same(5, (pl.ds(0, 2), 1 - y, c, slice(None), mine), to_x),
        same(6, (pl.ds(2, 2), y, c, slice(None), other), to_y),
    ]
    copies += [same(7, own, to_c), same(8, from_x, to_c), same(9, from_y, to_c), same(10, diagonal, to_c)]
    local = pltpu.make_async_copy(shard.at[:, mine], full.at[z, y, c, :, mine], local_sem)
    return copies, local


def gather_steps(shard, full, sems, local_sem):
    copies, local = gather_copies(shard, full, sems, local_sem)

    def first():
        local.start()
        for copy in copies[:3]:
            copy.start()

    def second():
        local.wait()
        for copy in copies[:3]:
            copy.wait_recv()
        for index in (3, 4, 7):
            copies[index].start()

    def third():
        copies[3].wait_recv()
        copies[4].wait_recv()
        for index in (5, 6, 8, 9):
            copies[index].start()

    def fourth():
        copies[5].wait_recv()
        copies[6].wait_recv()
        copies[10].start()

    def last():
        for index in (7, 8, 9, 10):
            copies[index].wait_recv()
        for copy in copies:
            copy.wait_send()

    return [first, second, third, fourth, last]


SMALL_COPIES = 5


def small_gather_steps(shard, full, sems, local_sem):
    x, z, y, c = my_place()
    local = pltpu.make_async_copy(shard, full.at[z, y, c], local_sem)
    copies = [
        remote(shard, full.at[z, y, c], sems, k - 1, place(x, (z + k) % 4, y, c)) for k in (1, 2, 3)
    ]
    copies.append(remote(full.at[:, y, c], full.at[:, y, c], sems, 3, place(x, z, 1 - y, c)))
    copies.append(remote(full.at[:, :, c], full.at[:, :, c], sems, 4, place(x, z, y, 1 - c)))

    def first():
        local.start()
        for copy in copies[:3]:
            copy.start()

    def second():
        local.wait()
        for copy in copies[:3]:
            copy.wait_recv()
        copies[3].start()

    def third():
        copies[3].wait_recv()
        copies[4].start()

    def last():
        copies[4].wait_recv()
        for copy in copies:
            copy.wait_send()

    return [first, second, third, last]


def gather_kernel(count, small, *refs):
    total = count + small
    shards, fulls = refs[:total], refs[total : 2 * total]
    sems = refs[2 * total :]
    greet()
    plans = [
        gather_steps(shards[i], fulls[i], sems[2 * i], sems[2 * i + 1].at[0]) for i in range(count)
    ]
    if small:
        plans.append(
            small_gather_steps(shards[count], fulls[count], sems[2 * count], sems[2 * count + 1].at[0])
        )
    for step in range(5):
        for plan in plans:
            if step < len(plan):
                plan[step]()


def gather_scratch(count, small):
    scratch = []
    for _ in range(count):
        scratch += [pltpu.SemaphoreType.DMA((2, GATHER_COPIES)), pltpu.SemaphoreType.DMA((1,))]
    if small:
        scratch += [pltpu.SemaphoreType.DMA((2, SMALL_COPIES)), pltpu.SemaphoreType.DMA((1,))]
    return scratch


def gather_shape(shard):
    return jax.ShapeDtypeStruct((4, 2, 2) + shard.shape, shard.dtype)


def gather_call(shards, small, collective_id, name):
    count = len(shards)
    arrays = list(shards) + ([small] if small is not None else [])
    has_small = int(small is not None)
    return pl.pallas_call(
        partial(gather_kernel, count, has_small),
        out_shape=[gather_shape(a) for a in arrays],
        in_specs=[any_spec()] * len(arrays),
        out_specs=[any_spec()] * len(arrays),
        scratch_shapes=gather_scratch(count, has_small),
        compiler_params=params(collective_id=collective_id, has_side_effects=True),
        name=name,
    )(*arrays)


SCATTER_COPIES = 10


def scatter_scratch(rows, cols):
    half = cols // 2
    return [
        pltpu.VMEM((4, 2, 2, rows, half), BF16),
        pltpu.VMEM((4, 2, 2, rows, half), BF16),
        pltpu.VMEM((2, 2, rows, half), BF16),
        pltpu.VMEM((2, rows, half), BF16),
        pltpu.VMEM((2, 2, rows, half), BF16),
        pltpu.VMEM((2, rows, half), BF16),
        pltpu.VMEM((4, rows, half), BF16),
        pltpu.VMEM((3, rows, half), BF16),
        pltpu.VMEM((rows, half), BF16),
        pltpu.VMEM((rows, half), BF16),
        pltpu.SemaphoreType.DMA((2, SCATTER_COPIES)),
        pltpu.SemaphoreType.DMA((2,)),
    ]


SCATTER_REFS = 12


def add_into(dst, left, right):
    dst[...] = (left[...].astype(F32) + right[...].astype(F32)).astype(BF16)


def scatter_steps(grads, share, bufs):
    own, peer, x_one, x_two, y_one, y_two, quarter, z_in, half_mine, half_other, sems, local = bufs
    x, z, y, c = my_place()
    half = own.shape[-1]
    to_x, to_y, to_c = place(1 - x, z, y, c), place(x, z, 1 - y, c), place(x, z, y, 1 - c)
    cols = [pl.ds(h * half, half) for h in range(2)]
    loads = [
        pltpu.make_async_copy(grads.at[:, :, c, :, cols[h]], own.at[:, :, h], local.at[h])
        for h in range(2)
    ]
    swaps = [
        remote(grads.at[:, :, 1 - c, :, cols[h]], peer.at[:, :, h], sems, h, to_c) for h in range(2)
    ]
    x_first = remote(own.at[pl.ds(0, 2), :, 1 - x], x_one, sems, 2, to_x)
    y_first = remote(own.at[pl.ds(2, 2), 1 - y], y_one, sems, 3, to_y)
    x_second = remote(own.at[pl.ds(2, 2), y, 1 - x], x_two, sems, 4, to_x)
    y_second = remote(own.at[pl.ds(0, 2), 1 - y, x], y_two, sems, 5, to_y)
    z_sends = [
        remote(quarter.at[(z + k) % 4], z_in.at[k - 1], sems, 5 + k, place(x, (z + k) % 4, y, c))
        for k in (1, 2, 3)
    ]
    last_swap = remote(half_mine, half_other, sems, 9, to_x)

    def start():
        for copy in loads + swaps:
            copy.start()

    def sum_cores():
        for copy in loads:
            copy.wait()
        for copy in swaps:
            copy.wait_recv()

        @pl.loop(0, 16)
        def _(i):
            place_of = (i // 4, (i // 2) % 2, i % 2)
            add_into(own.at[place_of], own.at[place_of], peer.at[place_of])

        x_first.start()
        y_first.start()

    def sum_first():
        x_first.wait_recv()
        y_first.wait_recv()

        @pl.loop(0, 2)
        def _(i):
            add_into(own.at[i, 1 - y, x], own.at[i, 1 - y, x], x_one.at[i, 1 - y])
            add_into(own.at[2 + i, y, 1 - x], own.at[2 + i, y, 1 - x], y_one.at[i, 1 - x])

        x_second.start()
        y_second.start()

        @pl.loop(0, 2)
        def _(i):
            add_into(own.at[i, y, x], own.at[i, y, x], x_one.at[i, y])
            add_into(own.at[2 + i, y, x], own.at[2 + i, y, x], y_one.at[i, x])

    def sum_second():
        x_second.wait_recv()
        y_second.wait_recv()

        @pl.loop(0, 2)
        def _(i):
            add_into(quarter.at[i], own.at[i, y, x], y_two.at[i])
            add_into(quarter.at[2 + i], own.at[2 + i, y, x], x_two.at[i])

        for copy in z_sends:
            copy.start()

    def sum_z():
        for copy in z_sends:
            copy.wait_recv()
        total = quarter[z].astype(F32)
        for k in range(3):
            total = total + z_in[k].astype(F32)
        half_mine[...] = total.astype(BF16)
        last_swap.start()

    def finish():
        last_swap.wait_recv()
        share[:, pl.ds(pl.multiple_of(x * half, 128), half)] = half_mine[...].astype(F32)
        share[:, pl.ds(pl.multiple_of((1 - x) * half, 128), half)] = half_other[...].astype(F32)
        for copy in swaps + [x_first, y_first, x_second, y_second] + z_sends + [last_swap]:
            copy.wait_send()

    return [start, sum_cores, sum_first, sum_second, sum_z, finish]


SMALL_SCATTER = 6


def small_scatter_scratch():
    return [
        pltpu.VMEM((4, 2, 2, 16, 128), F32),
        pltpu.VMEM((4, 2, 16, 128), F32),
        pltpu.VMEM((4, 2, 16, 128), F32),
        pltpu.VMEM((4, 16, 128), F32),
        pltpu.VMEM((4, 16, 128), F32),
        pltpu.VMEM((3, 16, 128), F32),
        pltpu.VMEM((16, 128), F32),
        pltpu.VMEM((16, 128), F32),
        pltpu.SemaphoreType.DMA((2, SMALL_SCATTER)),
    ]


SMALL_REFS = 9


def small_scatter_steps(grads, share, bufs):
    held, pair, peer, line, from_y, z_in, mine, other, sems = bufs
    x, z, y, c = my_place()
    swap = remote(held.at[:, :, 1 - c], peer, sems, 0, place(x, z, y, 1 - c))
    to_y = remote(pair.at[:, 1 - y], from_y, sems, 1, place(x, z, 1 - y, c))
    z_sends = [
        remote(line.at[(z + k) % 4], z_in.at[k - 1], sems, 1 + k, place(x, (z + k) % 4, y, c))
        for k in (1, 2, 3)
    ]
    to_x = remote(mine, other, sems, 5, place(1 - x, z, y, c))

    def start():
        held[...] = grads[...]
        swap.start()

    def sum_cores():
        swap.wait_recv()
        pair[...] = held[:, :, c] + peer[...]
        to_y.start()

    def sum_y():
        to_y.wait_recv()
        line[...] = pair[:, y] + from_y[...]
        for copy in z_sends:
            copy.start()

    def sum_z():
        for copy in z_sends:
            copy.wait_recv()
        mine[...] = line[z] + z_in[0] + z_in[1] + z_in[2]
        to_x.start()

    def finish():
        to_x.wait_recv()
        share[...] = mine[...] + other[...]
        for copy in [swap, to_y, to_x] + z_sends:
            copy.wait_send()

    return [start, sum_cores, sum_y, sum_z, finish]


def scatter_kernel(count, small, *refs):
    total = count + small
    grads, shares = refs[:total], refs[total : 2 * total]
    scratch = refs[2 * total :]
    greet()
    plans = [
        scatter_steps(grads[i], shares[i], scratch[i * SCATTER_REFS : (i + 1) * SCATTER_REFS])
        for i in range(count)
    ]
    if small:
        plans.append(
            small_scatter_steps(grads[count], shares[count], scratch[count * SCATTER_REFS :])
        )
    for step in range(6):
        for plan in plans:
            if step < len(plan):
                plan[step]()


def scatter_call(grads, small, collective_id, name):
    count = len(grads)
    scratch, shapes = [], []
    for grad in grads:
        rows, cols = grad.shape[-2:]
        scratch += scatter_scratch(rows, cols)
        shapes.append(jax.ShapeDtypeStruct((rows, cols), F32))
    arrays = list(grads)
    in_specs = [any_spec()] * count
    if small is not None:
        arrays.append(small)
        scratch += small_scatter_scratch()
        shapes.append(jax.ShapeDtypeStruct((16, 128), F32))
        in_specs.append(pl.BlockSpec(memory_space=pltpu.VMEM))
    return pl.pallas_call(
        partial(scatter_kernel, count, int(small is not None)),
        out_shape=shapes,
        in_specs=in_specs,
        out_specs=[pl.BlockSpec(memory_space=pltpu.VMEM)] * len(shapes),
        scratch_shapes=scratch,
        compiler_params=params(collective_id=collective_id, has_side_effects=True),
        name=name,
    )(*arrays)


def mask_lanes(kind, target_row, source_row):
    places = jnp.arange(LONG, dtype=jnp.int32)
    segment = jnp.where(kind == 1, 0, places // SHORT)
    offset = jnp.where(kind == 1, places, places % SHORT)
    lane = jnp.arange(WIDE, dtype=jnp.int32) % HD
    inside = segment[:, None] == lane[None, :]
    row_side = jnp.where(inside | (lane == SEGS)[None, :], 1.0, 0.0).astype(BF16)
    picker = segment[:, None] == jnp.arange(SEGS, dtype=jnp.int32)[None, :]

    def key_side(lengths):
        live = offset < jnp.sum(jnp.where(picker, lengths[None, :], 0), axis=1)
        blocked = ((lane < SEGS)[None, :] & ~inside) | ((lane == SEGS)[None, :] & ~live[:, None])
        ones = ((lane > SEGS) & (lane < SEGS + 4))[None, :]
        return jnp.where(blocked, NEG, jnp.where(ones, 1.0, 0.0)).astype(BF16)

    return row_side, key_side(target_row), key_side(source_row)


def lower(block, row_dim):
    rows = lax.broadcasted_iota(jnp.int32, (block, block), row_dim)
    cols = lax.broadcasted_iota(jnp.int32, (block, block), 1 - row_dim)
    return cols <= rows


def attend(causal, block, q_ref, k_ref, v_ref, row_ref, key_ref, att_ref, lse_ref):
    lane = lax.broadcasted_iota(jnp.int32, (1, WIDE), 1)
    results = []
    for head in range(2):
        inside = lane // HD == head
        spare = HD * (1 - head)
        keys = jnp.where(inside, k_ref[...], key_ref[...])
        vals = jnp.where(inside, v_ref[...], jnp.where(lane == spare, 1.0, 0.0).astype(BF16))
        parts = []
        for index in range(LONG // block):
            part = pl.ds(index * block, block)
            rows = jnp.where(inside, q_ref[part, :], row_ref[part, :])
            reach = (index + 1) * block if causal else LONG
            scores = mm(rows, keys[:reach], 1, 1)
            if causal:
                edge = jnp.where(lower(block, 0), scores[:, reach - block :], NEG)
                scores = (
                    edge
                    if reach == block
                    else jnp.concatenate([scores[:, : reach - block], edge], axis=1)
                )
            top = jnp.max(scores, axis=1, keepdims=True)
            weights = jnp.exp(scores - top).astype(BF16)
            mixed = mm(weights, vals[:reach])
            total = mixed[:, spare : spare + 1]
            parts.append((mixed / total, top + jnp.log(total)))
        results.append(parts)
    for index in range(LONG // block):
        part = pl.ds(index * block, block)
        (first, lse_first), (second, lse_second) = results[0][index], results[1][index]
        att_ref[part, :] = jnp.where(lane < HD, first, second).astype(BF16)
        lse_ref[0, part, :] = jnp.where(lane == 0, lse_first, lse_second)[:, :8]


def pair_spec(offset):
    return pl.BlockSpec((LONG, WIDE), lambda i: (0, offset + i))


def lse_spec():
    return pl.BlockSpec((1, LONG, 8), lambda i: (i, 0, 0))


def attention_forward(query, keys, values, row_side, key_side, causal, name):
    return pl.pallas_call(
        partial(attend, causal, 512),
        grid=(PAIRS,),
        in_specs=[pair_spec(query[1]), pair_spec(keys[1]), pair_spec(values[1])]
        + [whole((LONG, WIDE))] * 2,
        out_specs=[pair_spec(0), lse_spec()],
        out_shape=[
            jax.ShapeDtypeStruct((LONG, D), BF16),
            jax.ShapeDtypeStruct((PAIRS, LONG, 8), F32),
        ],
        compiler_params=params(),
        cost_estimate=cost(4 * LONG * LONG * D, 8 * LONG * D, H * LONG * LONG),
        name=name,
    )(query[0], keys[0], values[0], row_side, key_side)


def three_parts(value):
    high = value.astype(BF16)
    rest = value - high.astype(F32)
    middle = rest.astype(BF16)
    return high, middle, (rest - middle.astype(F32)).astype(BF16)


def attend_back(
    causal, block, q_ref, k_ref, v_ref, att_ref, grad_ref, lse_ref, row_ref, key_ref, dq_ref, dk_ref, dv_ref
):
    lane = lax.broadcasted_iota(jnp.int32, (1, WIDE), 1)
    blocks = LONG // block
    product = att_ref[...].astype(F32) * grad_ref[...].astype(F32)
    results = []
    for head in range(2):
        inside = lane // HD == head
        spare = HD * (1 - head)
        lse_parts = three_parts(-lse_ref[0, :, head : head + 1])
        delta_parts = three_parts(
            -jnp.sum(jnp.where(inside, product, 0.0), axis=1, keepdims=True)
        )
        row_extra, grad_extra = row_ref[...], jnp.zeros((LONG, WIDE), BF16)
        for i in range(3):
            here = lane == spare + SEGS + 1 + i
            row_extra = jnp.where(here, lse_parts[i], row_extra)
            grad_extra = jnp.where(here, delta_parts[i], grad_extra)
        rows = jnp.where(inside, q_ref[...], row_extra)
        grads = jnp.where(inside, grad_ref[...], grad_extra)
        keys = jnp.where(inside, k_ref[...], key_ref[...])
        ones = (lane > spare + SEGS) & (lane < spare + SEGS + 4)
        vals = jnp.where(inside, v_ref[...], jnp.where(ones, 1.0, 0.0).astype(BF16))
        dq, dk, dv = [None] * blocks, [], []
        for index in range(blocks):
            first = index * block if causal else 0
            key_part, val_part = keys[index * block :][:block], vals[index * block :][:block]
            scores = mm(key_part, rows[first:], 1, 1)
            if causal:
                edge = jnp.where(lower(block, 1), scores[:, :block], NEG)
                scores = (
                    edge
                    if first + block == LONG
                    else jnp.concatenate([edge, scores[:, block:]], axis=1)
                )
            probs = jnp.exp(scores)
            centered = mm(val_part, grads[first:], 1, 1)
            dscores = (probs * centered).astype(BF16)
            dv.append(mm(probs.astype(BF16), grads[first:]))
            dk.append(mm(dscores, rows[first:]))
            terms = mm(dscores, key_part, 0, 0)
            for q_index in range(first // block, blocks):
                term = terms[q_index * block - first :][:block]
                dq[q_index] = term if dq[q_index] is None else dq[q_index] + term
        results.append((dq, dk, dv))
    for index in range(blocks):
        part = pl.ds(index * block, block)
        for ref, member, factor in ((dq_ref, 0, SCALE), (dk_ref, 1, 1.0), (dv_ref, 2, 1.0)):
            both = jnp.where(lane < HD, results[0][member][index], results[1][member][index])
            ref[part, :] = (both * factor).astype(BF16)


def attention_backward(query, keys, values, att, grad, lse, row_side, key_side, causal, name):
    shape = jax.ShapeDtypeStruct((LONG, D), BF16)
    return pl.pallas_call(
        partial(attend_back, causal, 256 if causal else 512),
        grid=(PAIRS,),
        in_specs=[pair_spec(query[1]), pair_spec(keys[1]), pair_spec(values[1]), pair_spec(0), pair_spec(0)]
        + [lse_spec()]
        + [whole((LONG, WIDE))] * 2,
        out_specs=[pair_spec(0)] * 3,
        out_shape=[shape] * 3,
        compiler_params=params(),
        cost_estimate=cost(10 * LONG * LONG * D, 16 * LONG * D, H * LONG * LONG),
        name=name,
    )(query[0], keys[0], values[0], att, grad, lse, row_side, key_side)


def rows_spec(block, width):
    return pl.BlockSpec((block, width), lambda i: (i, 0))


def project_in(tokens_ref, weight_ref, vec_ref, out_ref):
    mixed = mm(tokens_ref[...], weight_ref[...])
    out_ref[:, :D] = ((mixed[:, :D] + vec_ref[SELF_B : SELF_B + 1]) * SCALE).astype(BF16)
    out_ref[:, D : 2 * D] = mixed[:, D : 2 * D].astype(BF16)
    out_ref[:, 2 * D :] = (mixed[:, 2 * D :] + vec_ref[SELF_B + 1 : SELF_B + 2]).astype(BF16)


def between(
    tokens_ref, att_ref, encoded_ref, out_w, q_w, kv_w, vec_ref, resid_ref, hidden_ref, query_ref, pairs_ref
):
    pairs = mm(encoded_ref[...], kv_w[...])
    pairs_ref[:, :D] = pairs[:, :D].astype(BF16)
    pairs_ref[:, D:] = (pairs[:, D:] + vec_ref[CROSS_B + 1 : CROSS_B + 2]).astype(BF16)
    resid = tokens_ref[...].astype(F32) + mm(att_ref[...], out_w[...]) + vec_ref[SELF_B + 2 : SELF_B + 3]
    resid_ref[...] = resid
    xhat, _ = normed(resid)
    hidden = (xhat * vec_ref[GAIN : GAIN + 1] + vec_ref[SHIFT : SHIFT + 1]).astype(BF16)
    hidden_ref[...] = hidden
    query_ref[...] = ((mm(hidden, q_w[...]) + vec_ref[CROSS_B : CROSS_B + 1]) * SCALE).astype(BF16)


INV_SQRT2 = 0.7071067811865476
INV_SQRT_2PI = 0.3989422804014327


def middle(
    hidden1_ref,
    att_ref,
    cot_ref,
    cross_out,
    ffn_in,
    ffn_out,
    vec_ref,
    bias_ref,
    out_ref,
    activ_ref,
    branch3_ref,
    dpre_ref,
    hidden2_ref,
    dresid2_ref,
    branch2_ref,
    datt_ref,
    sums_ref,
    bias_sum_ref,
):
    def vec(row):
        return vec_ref[row : row + 1]

    resid2 = hidden1_ref[...].astype(F32) + mm(att_ref[...], cross_out[...]) + vec(CROSS_B + 2)
    xhat2, inv2 = normed(resid2)
    hidden2 = (xhat2 * vec(GAIN + 1) + vec(SHIFT + 1)).astype(BF16)
    hidden2_ref[...] = hidden2
    pre = mm(hidden2, ffn_in[...]) + bias_ref[...]
    phi = 0.5 + 0.5 * lax.erf(pre * INV_SQRT2)
    activ = (pre * phi).astype(BF16)
    slope = phi + pre * (INV_SQRT_2PI * jnp.exp(-0.5 * pre * pre))
    activ_ref[...] = activ
    resid3 = hidden2.astype(F32) + mm(activ, ffn_out[...]) + vec(OUT_B)
    xhat3, inv3 = normed(resid3)
    out_ref[...] = (xhat3 * vec(GAIN + 2) + vec(SHIFT + 2)).astype(BF16)
    cot = cot_ref[...].astype(F32)
    dresid3 = norm_back(xhat3, inv3, vec(GAIN + 2), cot)
    branch3 = dresid3.astype(BF16)
    branch3_ref[...] = branch3
    dpre = (mm(branch3, ffn_out[...], 1, 1) * slope).astype(BF16)
    dpre_ref[...] = dpre
    dhidden2 = dresid3 + mm(dpre, ffn_in[...], 1, 1)
    dresid2 = norm_back(xhat2, inv2, vec(GAIN + 1), dhidden2)
    dresid2_ref[...] = dresid2
    branch2 = dresid2.astype(BF16)
    branch2_ref[...] = branch2
    datt_ref[...] = mm(branch2, cross_out[...], 1, 1).astype(BF16)

    sums = jnp.concatenate(
        [
            col_sum(dhidden2 * xhat2),
            col_sum(cot * xhat3),
            col_sum(dhidden2),
            col_sum(cot),
            col_sum(branch2.astype(F32)),
            col_sum(branch3.astype(F32)),
            jnp.zeros((2, D), F32),
        ],
        axis=0,
    )
    bias_sum = col_sum(dpre.astype(F32))
    fresh = pl.program_id(0) == 0
    sums_ref[...] = jnp.where(fresh, sums, sums_ref[...] + sums)
    bias_sum_ref[...] = jnp.where(fresh, bias_sum, bias_sum_ref[...] + bias_sum)


def after_cross(
    dq_ref,
    dk_ref,
    dv_ref,
    dresid2_ref,
    resid1_ref,
    q_w,
    kv_w,
    out_w,
    vec_ref,
    encoded_grad_ref,
    dresid1_ref,
    branch1_ref,
    datt_ref,
    sums_ref,
):
    dq, dk, dv = dq_ref[...], dk_ref[...], dv_ref[...]
    encoded_grad_ref[...] = (mm(dk, kv_w[:, :D], 1, 1) + mm(dv, kv_w[:, D:], 1, 1)).astype(BF16)
    dhidden1 = dresid2_ref[...] + mm(dq, q_w[...], 1, 1)
    xhat, inv = normed(resid1_ref[...])
    dresid1 = norm_back(xhat, inv, vec_ref[GAIN : GAIN + 1], dhidden1)
    dresid1_ref[...] = dresid1
    branch1 = dresid1.astype(BF16)
    branch1_ref[...] = branch1
    datt_ref[...] = mm(branch1, out_w[...], 1, 1).astype(BF16)
    sums = jnp.concatenate(
        [
            col_sum(dhidden1 * xhat),
            col_sum(dhidden1),
            col_sum(branch1.astype(F32)),
            col_sum(dq.astype(F32)),
            col_sum(dv.astype(F32)),
            jnp.zeros((3, D), F32),
        ],
        axis=0,
    )
    sums_ref[...] = jnp.where(pl.program_id(0) == 0, sums, sums_ref[...] + sums)


def tokens_back(dq_ref, dk_ref, dv_ref, dresid1_ref, weight_ref, out_ref):
    total = dresid1_ref[...] + mm(dq_ref[...], weight_ref[:, :D], 1, 1)
    total = total + mm(dk_ref[...], weight_ref[:, D : 2 * D], 1, 1)
    out_ref[...] = (total + mm(dv_ref[...], weight_ref[:, 2 * D :], 1, 1)).astype(BF16)


def row_call(kernel, block, ins, weights, outs, sums, name, flops):
    in_specs = [rows_spec(block, a.shape[1]) for a in ins]
    for _, shape, index in weights:
        in_specs.append(pl.BlockSpec(shape, lambda i, index=index: index))
    out_specs = [rows_spec(block, width) for width, _ in outs] + [whole(s) for s in sums]
    out_shape = [jax.ShapeDtypeStruct((LONG, width), dtype) for width, dtype in outs]
    out_shape += [jax.ShapeDtypeStruct(s, F32) for s in sums]
    return pl.pallas_call(
        kernel,
        grid=(LONG // block,),
        in_specs=in_specs,
        out_specs=out_specs,
        out_shape=out_shape,
        compiler_params=params(),
        cost_estimate=cost(flops, flops / 500),
        name=name,
    )(*ins, *[w[0] for w in weights])


def ffn_grads(activ_ref, branch3_ref, hidden2_ref, dpre_ref, out_grad_ref, in_grad_ref):
    out_grad_ref[...] = mm(activ_ref[...], branch3_ref[...], 0, 0).astype(BF16)
    in_grad_ref[...] = mm(hidden2_ref[...], dpre_ref[...], 0, 0).astype(BF16)


def ffn_grads_call(activ, branch3, hidden2, dpre):
    tile = 512
    return pl.pallas_call(
        ffn_grads,
        grid=(FF // tile,),
        in_specs=[
            pl.BlockSpec((LONG, tile), lambda i: (0, i)),
            whole((LONG, D)),
            whole((LONG, D)),
            pl.BlockSpec((LONG, tile), lambda i: (0, i)),
        ],
        out_specs=[
            pl.BlockSpec((tile, D), lambda i: (i, 0)),
            pl.BlockSpec((D, tile), lambda i: (0, i)),
        ],
        out_shape=[jax.ShapeDtypeStruct((FF, D), BF16), jax.ShapeDtypeStruct((D, FF), BF16)],
        compiler_params=params(),
        cost_estimate=cost(4 * LONG * D * FF, 8 * LONG * FF),
        name="ffn_grads",
    )(activ, branch3, hidden2, dpre)


def pair_grads(count, *refs):
    out_ref = refs[2 * count]
    for index in range(count):

        @pl.when(pl.program_id(0) == index)
        def _(index=index):
            out_ref[...] = mm(refs[index][...], refs[count + index][...], 0, 0).astype(BF16)


def pair_grads_call(lefts, rights, name):
    count = len(lefts)
    return pl.pallas_call(
        partial(pair_grads, count),
        grid=(count,),
        in_specs=[whole((LONG, D))] * (2 * count),
        out_specs=pl.BlockSpec((D, D), lambda i: (0, i)),
        out_shape=jax.ShapeDtypeStruct((D, D * count), BF16),
        compiler_params=params(),
        cost_estimate=cost(2 * LONG * D * D * count, 4 * LONG * D * count),
        name=name,
    )(*lefts, *rights)


def body(
    tokens,
    encoded,
    cotangent,
    bucket,
    target_len,
    source_len,
    self_in,
    self_bias,
    self_out,
    cross_q,
    cross_kv,
    cross_bias,
    cross_out,
    ffn_in,
    ffn_in_bias,
    ffn_out,
    ffn_out_bias,
    norm_gain,
    norm_shift,
):
    rows = self_in.shape[0]
    owners = D // rows
    direct = owners == 16
    row_side, target_side, source_side = mask_lanes(bucket[0], target_len[0], source_len[0])

    small = jnp.concatenate(
        [
            self_bias.reshape(-1),
            cross_bias.reshape(-1),
            norm_gain.reshape(-1),
            norm_shift.reshape(-1),
            ffn_out_bias,
            ffn_in_bias,
        ]
    )
    mixed_w = jnp.concatenate([self_out, cross_q, cross_kv, cross_out], axis=1)
    if direct:
        small = jnp.pad(small, (0, PACK - small.shape[0])).reshape(16, 128)
        self_w, small_all = gather_call([self_in], small, 0, "gather_self")
        (mixed_w,) = gather_call([mixed_w], None, 1, "gather_cross")
        ffn_in_w, ffn_out_w = gather_call([ffn_in, ffn_out], None, 2, "gather_ffn")
        small_all = small_all.reshape(16, PACK)
    else:
        everyone = partial(lax.all_gather, axis_name="fsdp", axis=0, tiled=True)
        self_w, mixed_w, ffn_in_w, ffn_out_w = map(everyone, (self_in, mixed_w, ffn_in, ffn_out))
        small_all = lax.all_gather(small, "fsdp", axis=0, tiled=False)
    self_w, mixed_w = self_w.reshape(D, 3 * D), mixed_w.reshape(D, 5 * D)
    ffn_in_w, ffn_out_w = ffn_in_w.reshape(D, FF), ffn_out_w.reshape(FF, D)
    small_all = small_all.astype(F32)
    vec = small_all[:, : IN_B * rows].reshape(owners, IN_B, rows).transpose(1, 0, 2).reshape(IN_B, D)
    vec = jnp.pad(vec, ((0, 3), (0, 0)))
    bias = small_all[:, IN_B * rows : VEC_ROWS * rows].reshape(1, FF)
    vec_weight = (vec, (16, D), (0, 0))
    square = (D, D)

    (mixed,) = row_call(
        project_in,
        512,
        [tokens],
        [(self_w, (D, 3 * D), (0, 0)), vec_weight],
        [(3 * D, BF16)],
        [],
        "project_in",
        6 * LONG * D * D,
    )
    self_att, self_lse = attention_forward(
        (mixed, 0), (mixed, PAIRS), (mixed, 2 * PAIRS), row_side, target_side, True, "self_forward"
    )
    resid1, hidden1, query, pairs = row_call(
        between,
        512,
        [tokens, self_att, encoded],
        [(mixed_w, square, (0, 0)), (mixed_w, square, (0, 1)), (mixed_w, (D, 2 * D), (0, 1)), vec_weight],
        [(D, F32), (D, BF16), (D, BF16), (2 * D, BF16)],
        [],
        "between",
        8 * LONG * D * D,
    )
    cross_att, cross_lse = attention_forward(
        (query, 0), (pairs, 0), (pairs, PAIRS), row_side, source_side, False, "cross_forward"
    )
    (output, activ, branch3, dpre, hidden2, dresid2, branch2, d_cross_att, sums_mid, bias_sum) = row_call(
        middle,
        256,
        [hidden1, cross_att, cotangent],
        [
            (mixed_w, square, (0, 4)),
            (ffn_in_w, (D, FF), (0, 0)),
            (ffn_out_w, (FF, D), (0, 0)),
            vec_weight,
            (bias, (1, FF), (0, 0)),
        ],
        [(D, BF16), (FF, BF16), (D, BF16), (FF, BF16), (D, BF16), (D, F32), (D, BF16), (D, BF16)],
        [(8, D), (1, FF)],
        "middle",
        36 * LONG * D * D,
    )
    ffn_out_grad, ffn_in_grad = ffn_grads_call(activ, branch3, hidden2, dpre)
    dcq, dck, dcv = attention_backward(
        (query, 0),
        (pairs, 0),
        (pairs, PAIRS),
        cross_att,
        d_cross_att,
        cross_lse,
        row_side,
        source_side,
        False,
        "cross_backward",
    )
    encoded_grad, dresid1, branch1, d_self_att, sums_cross = row_call(
        after_cross,
        512,
        [dcq, dck, dcv, dresid2, resid1],
        [(mixed_w, square, (0, 1)), (mixed_w, (D, 2 * D), (0, 1)), (mixed_w, square, (0, 0)), vec_weight],
        [(D, BF16), (D, F32), (D, BF16), (D, BF16)],
        [(8, D)],
        "after_cross",
        8 * LONG * D * D,
    )
    mixed_grad = pair_grads_call(
        [self_att, hidden1, encoded, encoded, cross_att],
        [branch1, dcq, dck, dcv, branch2],
        "cross_grads",
    )
    dq, dk, dv = attention_backward(
        (mixed, 0),
        (mixed, PAIRS),
        (mixed, 2 * PAIRS),
        self_att,
        d_self_att,
        self_lse,
        row_side,
        target_side,
        True,
        "self_backward",
    )
    self_grad = pair_grads_call([tokens] * 3, [dq, dk, dv], "self_grads")
    (tokens_grad,) = row_call(
        tokens_back,
        512,
        [dq, dk, dv, dresid1],
        [(self_w, (D, 3 * D), (0, 0))],
        [(D, BF16)],
        [],
        "tokens_back",
        6 * LONG * D * D,
    )

    dq_sum = jnp.sum(dq.astype(F32), axis=0, keepdims=True)
    dv_sum = jnp.sum(dv.astype(F32), axis=0, keepdims=True)
    small_rows = jnp.concatenate(
        [
            dq_sum,
            dv_sum,
            sums_cross[2:5],
            sums_mid[4:5],
            sums_cross[0:1],
            sums_mid[0:2],
            sums_cross[1:2],
            sums_mid[2:4],
            sums_mid[5:6],
        ],
        axis=0,
    )
    packed = small_rows.reshape(IN_B, owners, rows).transpose(1, 0, 2).reshape(owners, IN_B * rows)
    packed = jnp.concatenate([packed, bias_sum.reshape(owners, 4 * rows)], axis=1)
    grads = [self_grad, mixed_grad, ffn_in_grad, ffn_out_grad]
    if direct:
        packed = jnp.pad(packed, ((0, 0), (0, PACK - packed.shape[1]))).reshape(4, 2, 2, 16, 128)

        def cut(grad):
            return grad.reshape(4, 2, 2, grad.shape[0] // 16, grad.shape[1])

        ffn_in_share, ffn_out_share = scatter_call(
            [cut(ffn_in_grad), cut(ffn_out_grad)], None, 3, "scatter_ffn"
        )
        (mixed_share,) = scatter_call([cut(mixed_grad)], None, 4, "scatter_cross")
        self_share, packed_share = scatter_call([cut(self_grad)], packed, 5, "scatter_self")
        packed_share = packed_share.reshape(-1)
    else:

        def share_of(grad):
            share = lax.psum_scatter(grad.astype(F32), "fsdp", scatter_dimension=0, tiled=True)
            return lax.psum(share, "dp")

        self_share, mixed_share, ffn_in_share, ffn_out_share = map(share_of, grads)
        packed_share = share_of(packed).reshape(-1)

    def rows_of(first, count):
        return packed_share[first * rows : (first + count) * rows]

    return (
        output,
        tokens_grad,
        encoded_grad,
        self_share,
        rows_of(SELF_B, 3).reshape(3, rows),
        mixed_share[:, :D],
        mixed_share[:, D : 2 * D],
        mixed_share[:, 2 * D : 4 * D],
        rows_of(CROSS_B, 3).reshape(3, rows),
        mixed_share[:, 4 * D :],
        ffn_in_share,
        rows_of(IN_B, 4),
        ffn_out_share,
        rows_of(OUT_B, 1),
        rows_of(GAIN, 3).reshape(3, rows),
        rows_of(SHIFT, 3).reshape(3, rows),
    )


def solution(mesh):
    both = P(("dp", "fsdp"), None)
    rows, cols, flat = P("fsdp", None), P(None, "fsdp"), P("fsdp")
    return jax.shard_map(
        body,
        mesh=mesh,
        in_specs=(both, both, both, P(("dp", "fsdp")), both, both)
        + (rows, cols, rows, rows, rows, cols, rows, rows, flat, rows, flat, cols, cols),
        out_specs=(both, both, both)
        + (rows, cols, rows, rows, rows, cols, rows, rows, flat, rows, flat, cols, cols),
        check_vma=False,
    )
```

```python
from functools import partial

import jax
import jax.numpy as jnp
from jax import lax
from jax.experimental import pallas as pl
from jax.experimental.pallas import tpu as pltpu
from jax.sharding import PartitionSpec as P

D = 768
H = 12
HD = 64
FF = 3072
LONG = 1024
SEGS = 4
SHORT = 256
PAIRS = H // 2
WIDE = 2 * HD

EPS = 1e-05
NEG = -1e30
SCALE = HD ** (-0.5)
F32 = jnp.float32
BF16 = jnp.bfloat16
MESH_ID = pl.DeviceIdType.MESH
VMEM_LIMIT = 60 << 20

SELF_B, CROSS_B, GAIN, SHIFT, OUT_B, IN_B = 0, 3, 6, 9, 12, 13
VEC_ROWS = 17
PACK = 2048


def mm(left, right, left_dim=1, right_dim=0):
    return lax.dot_general(
        left, right, (((left_dim,), (right_dim,)), ((), ())), preferred_element_type=F32
    )


def params(**kwargs):
    return pltpu.CompilerParams(vmem_limit_bytes=VMEM_LIMIT, **kwargs)


def cost(flops, nbytes, trans=0):
    return pl.CostEstimate(flops=int(flops), bytes_accessed=int(nbytes), transcendentals=int(trans))


def any_spec():
    return pl.BlockSpec(memory_space=pl.ANY)


def whole(shape):
    return pl.BlockSpec(shape, lambda *_: (0,) * len(shape))


def normed(resid):
    centered = resid - jnp.mean(resid, axis=-1, keepdims=True)
    inv = lax.rsqrt(jnp.mean(centered * centered, axis=-1, keepdims=True) + EPS)
    return centered * inv, inv


def norm_back(xhat, inv, gain, grad):
    scaled = grad * gain
    first = jnp.mean(scaled, axis=-1, keepdims=True)
    second = jnp.mean(scaled * xhat, axis=-1, keepdims=True)
    return (scaled - first - xhat * second) * inv


def col_sum(values):
    return jnp.sum(values, axis=0, keepdims=True)


def my_place():
    dp, index = lax.axis_index("dp"), lax.axis_index("fsdp")
    return dp, index // 4, (index // 2) % 2, index % 2


def place(dp, z, y, core):
    return {"dp": dp, "fsdp": (z * 2 + y) * 2 + core}


def neighbours():
    x, z, y, c = my_place()
    return [place(x, (z + k) % 4, y, c) for k in (1, 2, 3)] + [
        place(1 - x, z, y, c),
        place(x, z, 1 - y, c),
        place(x, z, y, 1 - c),
    ]


def greet():
    barrier = pltpu.get_barrier_semaphore()
    others = neighbours()
    for other in others:
        pl.semaphore_signal(barrier, inc=1, device_id=other, device_id_type=MESH_ID)
    pl.semaphore_wait(barrier, len(others))


def remote(src, dst, sems, index, device):
    return pltpu.make_async_remote_copy(
        src_ref=src,
        dst_ref=dst,
        send_sem=sems.at[0, index],
        recv_sem=sems.at[1, index],
        device_id=device,
        device_id_type=MESH_ID,
    )


GATHER_COPIES = 11


def gather_copies(shard, full, sems, local_sem):
    x, z, y, c = my_place()
    half = shard.shape[-1] // 2
    mine = pl.ds(pl.multiple_of(x * half, 128), half)
    other = pl.ds(pl.multiple_of((1 - x) * half, 128), half)
    to_x, to_y, to_c = place(1 - x, z, y, c), place(x, z, 1 - y, c), place(x, z, y, 1 - c)

    def same(index, where, device):
        ref = full.at[where]
        return remote(ref, ref, sems, index, device)

    own = (slice(None), y, c, slice(None), mine)
    from_x = (slice(None), y, c, slice(None), other)
    from_y = (slice(None), 1 - y, c, slice(None), mine)
    diagonal = (slice(None), 1 - y, c, slice(None), other)
    copies = [
        remote(shard.at[:, mine], full.at[z, y, c, :, mine], sems, k - 1, place(x, (z + k) % 4, y, c))
        for k in (1, 2, 3)
    ]
    copies += [same(3, own, to_x), same(4, own, to_y)]
    copies += [
        same(5, (pl.ds(0, 2), 1 - y, c, slice(None), mine), to_x),
        same(6, (pl.ds(2, 2), y, c, slice(None), other), to_y),
    ]
    copies += [same(7, own, to_c), same(8, from_x, to_c), same(9, from_y, to_c), same(10, diagonal, to_c)]
    local = pltpu.make_async_copy(shard.at[:, mine], full.at[z, y, c, :, mine], local_sem)
    return copies, local


def gather_steps(shard, full, sems, local_sem):
    copies, local = gather_copies(shard, full, sems, local_sem)

    def first():
        local.start()
        for copy in copies[:3]:
            copy.start()

    def second():
        local.wait()
        for copy in copies[:3]:
            copy.wait_recv()
        for index in (3, 4, 7):
            copies[index].start()

    def third():
        copies[3].wait_recv()
        copies[4].wait_recv()
        for index in (5, 6, 8, 9):
            copies[index].start()

    def fourth():
        copies[5].wait_recv()
        copies[6].wait_recv()
        copies[10].start()

    def arrive():
        for index in (7, 8, 9, 10):
            copies[index].wait_recv()

    def last():
        for copy in copies:
            copy.wait_send()

    return [first, second, third, fourth, arrive, last]


SMALL_COPIES = 5


def small_gather_steps(shard, full, sems, local_sem):
    x, z, y, c = my_place()
    local = pltpu.make_async_copy(shard, full.at[z, y, c], local_sem)
    copies = [
        remote(shard, full.at[z, y, c], sems, k - 1, place(x, (z + k) % 4, y, c)) for k in (1, 2, 3)
    ]
    copies.append(remote(full.at[:, y, c], full.at[:, y, c], sems, 3, place(x, z, 1 - y, c)))
    copies.append(remote(full.at[:, :, c], full.at[:, :, c], sems, 4, place(x, z, y, 1 - c)))

    def first():
        local.start()
        for copy in copies[:3]:
            copy.start()

    def second():
        local.wait()
        for copy in copies[:3]:
            copy.wait_recv()
        copies[3].start()

    def third():
        copies[3].wait_recv()
        copies[4].start()

    def fourth():
        copies[4].wait_recv()

    def last():
        for copy in copies:
            copy.wait_send()

    return [first, second, third, fourth, last]


def gather_shape(rows, cols):
    return (4, 2, 2, rows, cols)


SCATTER_COPIES = 10


def scatter_scratch(rows, cols):
    half = cols // 2
    return [
        pltpu.VMEM((4, 2, 2, rows, half), BF16),
        pltpu.VMEM((4, 2, 2, rows, half), BF16),
        pltpu.VMEM((2, 2, rows, half), BF16),
        pltpu.VMEM((2, rows, half), BF16),
        pltpu.VMEM((2, 2, rows, half), BF16),
        pltpu.VMEM((2, rows, half), BF16),
        pltpu.VMEM((4, rows, half), BF16),
        pltpu.VMEM((3, rows, half), BF16),
        pltpu.VMEM((rows, half), BF16),
        pltpu.VMEM((rows, half), BF16),
        pltpu.SemaphoreType.DMA((2, SCATTER_COPIES)),
        pltpu.SemaphoreType.DMA((2,)),
    ]


SCATTER_REFS = 12


def add_into(dst, left, right):
    dst[...] = (left[...].astype(F32) + right[...].astype(F32)).astype(BF16)


def scatter_steps(grads, share, bufs):
    own, peer, x_one, x_two, y_one, y_two, quarter, z_in, half_mine, half_other, sems, local = bufs
    x, z, y, c = my_place()
    half = own.shape[-1]
    to_x, to_y, to_c = place(1 - x, z, y, c), place(x, z, 1 - y, c), place(x, z, y, 1 - c)
    cols = [pl.ds(h * half, half) for h in range(2)]
    loads = [
        pltpu.make_async_copy(grads.at[:, :, c, :, cols[h]], own.at[:, :, h], local.at[h])
        for h in range(2)
    ]
    swaps = [
        remote(grads.at[:, :, 1 - c, :, cols[h]], peer.at[:, :, h], sems, h, to_c) for h in range(2)
    ]
    x_first = remote(own.at[pl.ds(0, 2), :, 1 - x], x_one, sems, 2, to_x)
    y_first = remote(own.at[pl.ds(2, 2), 1 - y], y_one, sems, 3, to_y)
    x_second = remote(own.at[pl.ds(2, 2), y, 1 - x], x_two, sems, 4, to_x)
    y_second = remote(own.at[pl.ds(0, 2), 1 - y, x], y_two, sems, 5, to_y)
    z_sends = [
        remote(quarter.at[(z + k) % 4], z_in.at[k - 1], sems, 5 + k, place(x, (z + k) % 4, y, c))
        for k in (1, 2, 3)
    ]
    last_swap = remote(half_mine, half_other, sems, 9, to_x)

    def start():
        for copy in loads + swaps:
            copy.start()

    def sum_cores():
        for copy in loads:
            copy.wait()
        for copy in swaps:
            copy.wait_recv()

        @pl.loop(0, 16)
        def _(i):
            place_of = (i // 4, (i // 2) % 2, i % 2)
            add_into(own.at[place_of], own.at[place_of], peer.at[place_of])

        x_first.start()
        y_first.start()

    def sum_first():
        x_first.wait_recv()
        y_first.wait_recv()

        @pl.loop(0, 2)
        def _(i):
            add_into(own.at[i, 1 - y, x], own.at[i, 1 - y, x], x_one.at[i, 1 - y])
            add_into(own.at[2 + i, y, 1 - x], own.at[2 + i, y, 1 - x], y_one.at[i, 1 - x])

        x_second.start()
        y_second.start()

        @pl.loop(0, 2)
        def _(i):
            add_into(own.at[i, y, x], own.at[i, y, x], x_one.at[i, y])
            add_into(own.at[2 + i, y, x], own.at[2 + i, y, x], y_one.at[i, x])

    def sum_second():
        x_second.wait_recv()
        y_second.wait_recv()

        @pl.loop(0, 2)
        def _(i):
            add_into(quarter.at[i], own.at[i, y, x], y_two.at[i])
            add_into(quarter.at[2 + i], own.at[2 + i, y, x], x_two.at[i])

        for copy in z_sends:
            copy.start()

    def sum_z():
        for copy in z_sends:
            copy.wait_recv()
        total = quarter[z].astype(F32)
        for k in range(3):
            total = total + z_in[k].astype(F32)
        half_mine[...] = total.astype(BF16)
        last_swap.start()

    def finish():
        last_swap.wait_recv()
        share[:, pl.ds(pl.multiple_of(x * half, 128), half)] = half_mine[...].astype(F32)
        share[:, pl.ds(pl.multiple_of((1 - x) * half, 128), half)] = half_other[...].astype(F32)
        for copy in swaps + [x_first, y_first, x_second, y_second] + z_sends + [last_swap]:
            copy.wait_send()

    return [start, sum_cores, sum_first, sum_second, sum_z, finish]


SMALL_SCATTER = 6


def small_scatter_scratch():
    return [
        pltpu.VMEM((4, 2, 2, 16, 128), F32),
        pltpu.VMEM((4, 2, 16, 128), F32),
        pltpu.VMEM((4, 2, 16, 128), F32),
        pltpu.VMEM((4, 16, 128), F32),
        pltpu.VMEM((4, 16, 128), F32),
        pltpu.VMEM((3, 16, 128), F32),
        pltpu.VMEM((16, 128), F32),
        pltpu.VMEM((16, 128), F32),
        pltpu.SemaphoreType.DMA((2, SMALL_SCATTER)),
    ]


SMALL_REFS = 9


def small_scatter_steps(grads, share, bufs):
    held, pair, peer, line, from_y, z_in, mine, other, sems = bufs
    x, z, y, c = my_place()
    swap = remote(held.at[:, :, 1 - c], peer, sems, 0, place(x, z, y, 1 - c))
    to_y = remote(pair.at[:, 1 - y], from_y, sems, 1, place(x, z, 1 - y, c))
    z_sends = [
        remote(line.at[(z + k) % 4], z_in.at[k - 1], sems, 1 + k, place(x, (z + k) % 4, y, c))
        for k in (1, 2, 3)
    ]
    to_x = remote(mine, other, sems, 5, place(1 - x, z, y, c))

    def start():
        held[...] = grads[...]
        swap.start()

    def sum_cores():
        swap.wait_recv()
        pair[...] = held[:, :, c] + peer[...]
        to_y.start()

    def sum_y():
        to_y.wait_recv()
        line[...] = pair[:, y] + from_y[...]
        for copy in z_sends:
            copy.start()

    def sum_z():
        for copy in z_sends:
            copy.wait_recv()
        mine[...] = line[z] + z_in[0] + z_in[1] + z_in[2]
        to_x.start()

    def finish():
        to_x.wait_recv()
        share[...] = mine[...] + other[...]
        for copy in [swap, to_y, to_x] + z_sends:
            copy.wait_send()

    return [start, sum_cores, sum_y, sum_z, finish]


def scatter_kernel(count, small, *refs):
    total = count + small
    grads, shares = refs[:total], refs[total : 2 * total]
    scratch = refs[2 * total :]
    greet()
    plans = [
        scatter_steps(grads[i], shares[i], scratch[i * SCATTER_REFS : (i + 1) * SCATTER_REFS])
        for i in range(count)
    ]
    if small:
        plans.append(
            small_scatter_steps(grads[count], shares[count], scratch[count * SCATTER_REFS :])
        )
    for step in range(6):
        for plan in plans:
            if step < len(plan):
                plan[step]()


def scatter_call(grads, small, collective_id, name):
    count = len(grads)
    scratch, shapes = [], []
    for grad in grads:
        rows, cols = grad.shape[-2:]
        scratch += scatter_scratch(rows, cols)
        shapes.append(jax.ShapeDtypeStruct((rows, cols), F32))
    arrays = list(grads)
    in_specs = [any_spec()] * count
    if small is not None:
        arrays.append(small)
        scratch += small_scatter_scratch()
        shapes.append(jax.ShapeDtypeStruct((16, 128), F32))
        in_specs.append(pl.BlockSpec(memory_space=pltpu.VMEM))
    return pl.pallas_call(
        partial(scatter_kernel, count, int(small is not None)),
        out_shape=shapes,
        in_specs=in_specs,
        out_specs=[pl.BlockSpec(memory_space=pltpu.VMEM)] * len(shapes),
        scratch_shapes=scratch,
        compiler_params=params(collective_id=collective_id, has_side_effects=True),
        name=name,
    )(*arrays)


def mask_lanes(kind, target_row, source_row):
    places = jnp.arange(LONG, dtype=jnp.int32)
    segment = jnp.where(kind == 1, 0, places // SHORT)
    offset = jnp.where(kind == 1, places, places % SHORT)
    lane = jnp.arange(WIDE, dtype=jnp.int32) % HD
    inside = segment[:, None] == lane[None, :]
    row_side = jnp.where(inside | (lane == SEGS)[None, :], 1.0, 0.0).astype(BF16)
    picker = segment[:, None] == jnp.arange(SEGS, dtype=jnp.int32)[None, :]

    def key_side(lengths):
        live = offset < jnp.sum(jnp.where(picker, lengths[None, :], 0), axis=1)
        blocked = ((lane < SEGS)[None, :] & ~inside) | ((lane == SEGS)[None, :] & ~live[:, None])
        ones = ((lane > SEGS) & (lane < SEGS + 4))[None, :]
        return jnp.where(blocked, NEG, jnp.where(ones, 1.0, 0.0)).astype(BF16)

    return row_side, key_side(target_row), key_side(source_row)


def lower(block, row_dim):
    rows = lax.broadcasted_iota(jnp.int32, (block, block), row_dim)
    cols = lax.broadcasted_iota(jnp.int32, (block, block), 1 - row_dim)
    return cols <= rows


def attend(causal, block, q_ref, k_ref, v_ref, row_ref, key_ref, att_ref, lse_ref):
    lane = lax.broadcasted_iota(jnp.int32, (1, WIDE), 1)
    results = []
    for head in range(2):
        inside = lane // HD == head
        spare = HD * (1 - head)
        keys = jnp.where(inside, k_ref[...], key_ref[...])
        vals = jnp.where(inside, v_ref[...], jnp.where(lane == spare, 1.0, 0.0).astype(BF16))
        parts = []
        for index in range(LONG // block):
            part = pl.ds(index * block, block)
            rows = jnp.where(inside, q_ref[part, :], row_ref[part, :])
            reach = (index + 1) * block if causal else LONG
            scores = mm(rows, keys[:reach], 1, 1)
            if causal:
                edge = jnp.where(lower(block, 0), scores[:, reach - block :], NEG)
                scores = (
                    edge
                    if reach == block
                    else jnp.concatenate([scores[:, : reach - block], edge], axis=1)
                )
            top = jnp.max(scores, axis=1, keepdims=True)
            weights = jnp.exp(scores - top).astype(BF16)
            mixed = mm(weights, vals[:reach])
            total = mixed[:, spare : spare + 1]
            parts.append((mixed / total, top + jnp.log(total)))
        results.append(parts)
    for index in range(LONG // block):
        part = pl.ds(index * block, block)
        (first, lse_first), (second, lse_second) = results[0][index], results[1][index]
        att_ref[part, :] = jnp.where(lane < HD, first, second).astype(BF16)
        lse_ref[0, part, :] = jnp.where(lane == 0, lse_first, lse_second)[:, :8]


def pair_spec(offset):
    return pl.BlockSpec((LONG, WIDE), lambda i: (0, offset + i))


def lse_spec():
    return pl.BlockSpec((1, LONG, 8), lambda i: (i, 0, 0))


def attention_forward(query, keys, values, row_side, key_side, causal, name):
    return pl.pallas_call(
        partial(attend, causal, 512),
        grid=(PAIRS,),
        in_specs=[pair_spec(query[1]), pair_spec(keys[1]), pair_spec(values[1])]
        + [whole((LONG, WIDE))] * 2,
        out_specs=[pair_spec(0), lse_spec()],
        out_shape=[
            jax.ShapeDtypeStruct((LONG, D), BF16),
            jax.ShapeDtypeStruct((PAIRS, LONG, 8), F32),
        ],
        compiler_params=params(),
        cost_estimate=cost(4 * LONG * LONG * D, 8 * LONG * D, H * LONG * LONG),
        name=name,
    )(query[0], keys[0], values[0], row_side, key_side)


def three_parts(value):
    high = value.astype(BF16)
    rest = value - high.astype(F32)
    middle = rest.astype(BF16)
    return high, middle, (rest - middle.astype(F32)).astype(BF16)


def attend_back(
    causal, block, q_ref, k_ref, v_ref, att_ref, grad_ref, lse_ref, row_ref, key_ref, dq_ref, dk_ref, dv_ref
):
    lane = lax.broadcasted_iota(jnp.int32, (1, WIDE), 1)
    blocks = LONG // block
    product = att_ref[...].astype(F32) * grad_ref[...].astype(F32)
    results = []
    for head in range(2):
        inside = lane // HD == head
        spare = HD * (1 - head)
        lse_parts = three_parts(-lse_ref[0, :, head : head + 1])
        delta_parts = three_parts(
            -jnp.sum(jnp.where(inside, product, 0.0), axis=1, keepdims=True)
        )
        row_extra, grad_extra = row_ref[...], jnp.zeros((LONG, WIDE), BF16)
        for i in range(3):
            here = lane == spare + SEGS + 1 + i
            row_extra = jnp.where(here, lse_parts[i], row_extra)
            grad_extra = jnp.where(here, delta_parts[i], grad_extra)
        rows = jnp.where(inside, q_ref[...], row_extra)
        grads = jnp.where(inside, grad_ref[...], grad_extra)
        keys = jnp.where(inside, k_ref[...], key_ref[...])
        ones = (lane > spare + SEGS) & (lane < spare + SEGS + 4)
        vals = jnp.where(inside, v_ref[...], jnp.where(ones, 1.0, 0.0).astype(BF16))
        dq, dk, dv = [None] * blocks, [], []
        for index in range(blocks):
            first = index * block if causal else 0
            key_part, val_part = keys[index * block :][:block], vals[index * block :][:block]
            scores = mm(key_part, rows[first:], 1, 1)
            if causal:
                edge = jnp.where(lower(block, 1), scores[:, :block], NEG)
                scores = (
                    edge
                    if first + block == LONG
                    else jnp.concatenate([edge, scores[:, block:]], axis=1)
                )
            probs = jnp.exp(scores)
            centered = mm(val_part, grads[first:], 1, 1)
            dscores = (probs * centered).astype(BF16)
            dv.append(mm(probs.astype(BF16), grads[first:]))
            dk.append(mm(dscores, rows[first:]))
            terms = mm(dscores, key_part, 0, 0)
            for q_index in range(first // block, blocks):
                term = terms[q_index * block - first :][:block]
                dq[q_index] = term if dq[q_index] is None else dq[q_index] + term
        results.append((dq, dk, dv))
    for index in range(blocks):
        part = pl.ds(index * block, block)
        for ref, member, factor in ((dq_ref, 0, SCALE), (dk_ref, 1, 1.0), (dv_ref, 2, 1.0)):
            both = jnp.where(lane < HD, results[0][member][index], results[1][member][index])
            ref[part, :] = (both * factor).astype(BF16)


def attention_backward(query, keys, values, att, grad, lse, row_side, key_side, causal, name):
    shape = jax.ShapeDtypeStruct((LONG, D), BF16)
    return pl.pallas_call(
        partial(attend_back, causal, 256 if causal else 512),
        grid=(PAIRS,),
        in_specs=[pair_spec(query[1]), pair_spec(keys[1]), pair_spec(values[1]), pair_spec(0), pair_spec(0)]
        + [lse_spec()]
        + [whole((LONG, WIDE))] * 2,
        out_specs=[pair_spec(0)] * 3,
        out_shape=[shape] * 3,
        compiler_params=params(),
        cost_estimate=cost(10 * LONG * LONG * D, 16 * LONG * D, H * LONG * LONG),
        name=name,
    )(query[0], keys[0], values[0], att, grad, lse, row_side, key_side)


def rows_spec(block, width):
    return pl.BlockSpec((block, width), lambda i: (i, 0))


def project_in(tokens_ref, q_w, k_w, v_w, vec_ref, out_ref):
    left = tokens_ref[...]
    out_ref[:, :D] = ((mm(left, q_w[...]) + vec_ref[SELF_B : SELF_B + 1]) * SCALE).astype(BF16)
    out_ref[:, D : 2 * D] = mm(left, k_w[...]).astype(BF16)
    out_ref[:, 2 * D :] = (mm(left, v_w[...]) + vec_ref[SELF_B + 1 : SELF_B + 2]).astype(BF16)


def between(
    tokens_ref, att_ref, encoded_ref, out_w, q_w, kv_w, vec_ref, resid_ref, hidden_ref, query_ref, pairs_ref
):
    pairs = mm(encoded_ref[...], kv_w[...])
    pairs_ref[:, :D] = pairs[:, :D].astype(BF16)
    pairs_ref[:, D:] = (pairs[:, D:] + vec_ref[CROSS_B + 1 : CROSS_B + 2]).astype(BF16)
    resid = tokens_ref[...].astype(F32) + mm(att_ref[...], out_w[...]) + vec_ref[SELF_B + 2 : SELF_B + 3]
    resid_ref[...] = resid
    xhat, _ = normed(resid)
    hidden = (xhat * vec_ref[GAIN : GAIN + 1] + vec_ref[SHIFT : SHIFT + 1]).astype(BF16)
    hidden_ref[...] = hidden
    query_ref[...] = ((mm(hidden, q_w[...]) + vec_ref[CROSS_B : CROSS_B + 1]) * SCALE).astype(BF16)


INV_SQRT2 = 0.7071067811865476
INV_SQRT_2PI = 0.3989422804014327


def middle(
    hidden1_ref,
    att_ref,
    cot_ref,
    cross_out,
    ffn_in,
    ffn_out,
    vec_ref,
    bias_ref,
    out_ref,
    activ_ref,
    branch3_ref,
    dpre_ref,
    hidden2_ref,
    dresid2_ref,
    branch2_ref,
    datt_ref,
    sums_ref,
    bias_sum_ref,
):
    def vec(row):
        return vec_ref[row : row + 1]

    resid2 = hidden1_ref[...].astype(F32) + mm(att_ref[...], cross_out[...]) + vec(CROSS_B + 2)
    xhat2, inv2 = normed(resid2)
    hidden2 = (xhat2 * vec(GAIN + 1) + vec(SHIFT + 1)).astype(BF16)
    hidden2_ref[...] = hidden2
    pre = mm(hidden2, ffn_in[...]) + bias_ref[...]
    phi = 0.5 + 0.5 * lax.erf(pre * INV_SQRT2)
    activ = (pre * phi).astype(BF16)
    slope = phi + pre * (INV_SQRT_2PI * jnp.exp(-0.5 * pre * pre))
    activ_ref[...] = activ
    resid3 = hidden2.astype(F32) + mm(activ, ffn_out[...]) + vec(OUT_B)
    xhat3, inv3 = normed(resid3)
    out_ref[...] = (xhat3 * vec(GAIN + 2) + vec(SHIFT + 2)).astype(BF16)
    cot = cot_ref[...].astype(F32)
    dresid3 = norm_back(xhat3, inv3, vec(GAIN + 2), cot)
    branch3 = dresid3.astype(BF16)
    branch3_ref[...] = branch3
    dpre = (mm(branch3, ffn_out[...], 1, 1) * slope).astype(BF16)
    dpre_ref[...] = dpre
    dhidden2 = dresid3 + mm(dpre, ffn_in[...], 1, 1)
    dresid2 = norm_back(xhat2, inv2, vec(GAIN + 1), dhidden2)
    dresid2_ref[...] = dresid2
    branch2 = dresid2.astype(BF16)
    branch2_ref[...] = branch2
    datt_ref[...] = mm(branch2, cross_out[...], 1, 1).astype(BF16)

    sums = jnp.concatenate(
        [
            col_sum(dhidden2 * xhat2),
            col_sum(cot * xhat3),
            col_sum(dhidden2),
            col_sum(cot),
            col_sum(branch2.astype(F32)),
            col_sum(branch3.astype(F32)),
            jnp.zeros((2, D), F32),
        ],
        axis=0,
    )
    bias_sum = col_sum(dpre.astype(F32))
    fresh = pl.program_id(0) == 0
    sums_ref[...] = jnp.where(fresh, sums, sums_ref[...] + sums)
    bias_sum_ref[...] = jnp.where(fresh, bias_sum, bias_sum_ref[...] + bias_sum)


def after_cross(
    dq_ref,
    dk_ref,
    dv_ref,
    dresid2_ref,
    resid1_ref,
    q_w,
    kv_w,
    out_w,
    vec_ref,
    encoded_grad_ref,
    dresid1_ref,
    branch1_ref,
    datt_ref,
    sums_ref,
):
    dq, dk, dv = dq_ref[...], dk_ref[...], dv_ref[...]
    encoded_grad_ref[...] = (mm(dk, kv_w[:, :D], 1, 1) + mm(dv, kv_w[:, D:], 1, 1)).astype(BF16)
    dhidden1 = dresid2_ref[...] + mm(dq, q_w[...], 1, 1)
    xhat, inv = normed(resid1_ref[...])
    dresid1 = norm_back(xhat, inv, vec_ref[GAIN : GAIN + 1], dhidden1)
    dresid1_ref[...] = dresid1
    branch1 = dresid1.astype(BF16)
    branch1_ref[...] = branch1
    datt_ref[...] = mm(branch1, out_w[...], 1, 1).astype(BF16)
    sums = jnp.concatenate(
        [
            col_sum(dhidden1 * xhat),
            col_sum(dhidden1),
            col_sum(branch1.astype(F32)),
            col_sum(dq.astype(F32)),
            col_sum(dv.astype(F32)),
            jnp.zeros((3, D), F32),
        ],
        axis=0,
    )
    sums_ref[...] = jnp.where(pl.program_id(0) == 0, sums, sums_ref[...] + sums)


def tokens_back(dq_ref, dk_ref, dv_ref, dresid1_ref, q_w, k_w, v_w, out_ref):
    total = dresid1_ref[...] + mm(dq_ref[...], q_w[...], 1, 1)
    total = total + mm(dk_ref[...], k_w[...], 1, 1)
    out_ref[...] = (total + mm(dv_ref[...], v_w[...], 1, 1)).astype(BF16)


def row_call(kernel, block, ins, weights, outs, sums, name, flops):
    in_specs = [rows_spec(block, a.shape[1]) for a in ins]
    for _, shape, index in weights:
        in_specs.append(pl.BlockSpec(shape, lambda i, index=index: index))
    out_specs = [rows_spec(block, width) for width, _ in outs] + [whole(s) for s in sums]
    out_shape = [jax.ShapeDtypeStruct((LONG, width), dtype) for width, dtype in outs]
    out_shape += [jax.ShapeDtypeStruct(s, F32) for s in sums]
    return pl.pallas_call(
        kernel,
        grid=(LONG // block,),
        in_specs=in_specs,
        out_specs=out_specs,
        out_shape=out_shape,
        compiler_params=params(),
        cost_estimate=cost(flops, flops / 500),
        name=name,
    )(*ins, *[w[0] for w in weights])


def write_masks(kind, target_row, source_row, row_ref, target_ref, source_ref):
    places = lax.broadcasted_iota(jnp.int32, (LONG, 1), 0)
    long = kind == 1
    segment = jnp.where(long, 0, lax.shift_right_logical(places, 8))
    offset = jnp.where(long, places, places & (SHORT - 1))
    lane = lax.broadcasted_iota(jnp.int32, (1, WIDE), 1) & (HD - 1)
    inside = segment == lane
    row_ref[...] = jnp.where(inside | (lane == SEGS), 1.0, 0.0).astype(BF16)
    ones = (lane > SEGS) & (lane < SEGS + 4)
    for ref, lengths in ((target_ref, target_row), (source_ref, source_row)):
        length = jnp.zeros((LONG, 1), jnp.int32)
        for index in range(SEGS):
            length = jnp.where(segment == index, lengths[index], length)
        dead = offset >= length
        blocked = ((lane < SEGS) & ~inside) | ((lane == SEGS) & dead)
        ref[...] = jnp.where(blocked, NEG, jnp.where(ones, 1.0, 0.0)).astype(BF16)


FORWARD_CHUNKS = 9
FORWARD_LOCAL = 32


def forward_kernel(*refs):
    (
        kind_ref, target_len, source_len,
        self_b, cross_b, gain, shift, out_b, in_b,
        tokens_hbm, encoded_hbm, self_in, self_out, cross_q, cross_kv, cross_out, ffn_in, ffn_out,
        w_q_out, w_k_out, w_v_out, w_o_out, w_cq_out, w_ckv_out, w_co_full, w_fi_full, w_fo_full,
        mixed_out, self_att_out, self_lse_out, resid_out, hidden_out, query_out, pairs_out,
        cross_att_out, cross_lse_out, row_out, target_out, source_out, vec_ref, bias_ref,
        w_q, w_k, w_v, w_o, w_cq, w_ckv,
        tokens, encoded, mixed, self_att, self_lse, resid, hidden, query, pairs,
        cross_att, cross_lse, row_side, target_side, source_side,
        pack, pack16, small_full,
        sems, small_sems, chunk_local, local,
    ) = refs
    used = [0]

    def move(src, dst):
        copy = pltpu.make_async_copy(src, dst, local.at[used[0]])
        used[0] += 1
        copy.start()
        return copy

    load_tokens, load_encoded = move(tokens_hbm, tokens), move(encoded_hbm, encoded)
    rows = self_b.shape[1]
    pack[...] = jnp.zeros_like(pack)
    for start, ref in ((SELF_B, self_b), (CROSS_B, cross_b), (GAIN, gain), (SHIFT, shift), (OUT_B, out_b)):
        pack[start : start + ref.shape[0], :rows] = ref[...].astype(F32)
    pack[IN_B : IN_B + 1, : 4 * rows] = in_b[...].astype(F32)
    pack16[...] = pack[...].astype(BF16)

    greet()
    chunks = [
        (self_in.at[:, pl.ds(0, D)], w_q),
        (self_in.at[:, pl.ds(D, D)], w_k),
        (self_in.at[:, pl.ds(2 * D, D)], w_v),
        (self_out, w_o),
        (cross_q, w_cq),
        (cross_kv, w_ckv),
        (cross_out, w_co_full),
        (ffn_in, w_fi_full),
        (ffn_out, w_fo_full),
    ]
    plans = [
        gather_steps(shard, full, sems.at[:, pl.ds(i * GATHER_COPIES, GATHER_COPIES)], chunk_local.at[i])
        for i, (shard, full) in enumerate(chunks)
    ]
    small_plan = small_gather_steps(pack16, small_full, small_sems, chunk_local.at[FORWARD_CHUNKS])
    first_group, second_group, third_group, fourth_group = (0, 1, 2), (3, 4, 5), (6, 7), (8,)

    def step(group, number):
        for index in group:
            plans[index][number]()

    small_plan[0]()
    step(first_group, 0)
    write_masks(
        kind_ref[0],
        [target_len[0, i] for i in range(SEGS)],
        [source_len[0, i] for i in range(SEGS)],
        row_side,
        target_side,
        source_side,
    )
    saves = [move(row_side, row_out), move(target_side, target_out), move(source_side, source_out)]
    small_plan[1]()
    step(first_group, 1)
    step(second_group, 0)
    small_plan[2]()
    step(first_group, 2)
    small_plan[3]()
    for z in range(4):
        for y in range(2):
            for c in range(2):
                owner = (z * 2 + y) * 2 + c
                tile = small_full[z, y, c].astype(F32)
                vec_ref[:, owner * rows : (owner + 1) * rows] = tile[:, :rows]
                bias_ref[:, owner * 4 * rows : (owner + 1) * 4 * rows] = tile[IN_B : IN_B + 1, : 4 * rows]
    step(first_group, 3)
    step(second_group, 1)
    step(third_group, 0)
    step(first_group, 4)
    saves += [move(w_q, w_q_out), move(w_k, w_k_out), move(w_v, w_v_out)]
    load_tokens.wait()

    def vec(row):
        return vec_ref[row : row + 1, :]

    def square(ref):
        return ref[...].reshape(D, ref.shape[-1])

    block = 512

    @pl.loop(0, LONG // block)
    def _(i):
        part = pl.ds(pl.multiple_of(i * block, block), block)
        left = tokens[part, :]
        mixed[part, :D] = ((mm(left, square(w_q)) + vec(SELF_B)) * SCALE).astype(BF16)
        mixed[part, D : 2 * D] = mm(left, square(w_k)).astype(BF16)
        mixed[part, 2 * D :] = (mm(left, square(w_v)) + vec(SELF_B + 1)).astype(BF16)

    saves.append(move(mixed, mixed_out))

    def ticks(index, table):
        for at, work in table.items():

            @pl.when(index == at)
            def _(work=work):
                for group, number in work:
                    step(group, number)

    @pl.loop(0, PAIRS)
    def _(pair):
        def cols(offset):
            return pl.ds(pl.multiple_of(offset + pair * WIDE, WIDE), WIDE)

        attend(
            True,
            512,
            mixed.at[:, cols(0)],
            mixed.at[:, cols(D)],
            mixed.at[:, cols(2 * D)],
            row_side,
            target_side,
            self_att.at[:, cols(0)],
            self_lse.at[pl.ds(pair, 1)],
        )
        ticks(
            pair,
            {
                1: [(second_group, 2), (third_group, 1), (fourth_group, 0)],
                3: [(second_group, 3)],
            },
        )

    saves += [move(self_att, self_att_out), move(self_lse, self_lse_out)]
    load_encoded.wait()
    step(second_group, 4)
    saves += [move(w_o, w_o_out), move(w_cq, w_cq_out), move(w_ckv, w_ckv_out)]

    @pl.loop(0, LONG // block)
    def _(i):
        part = pl.ds(pl.multiple_of(i * block, block), block)
        both = mm(encoded[part, :], square(w_ckv))
        pairs[part, :D] = both[:, :D].astype(BF16)
        pairs[part, D:] = (both[:, D:] + vec(CROSS_B + 1)).astype(BF16)
        total = tokens[part, :].astype(F32) + mm(self_att[part, :], square(w_o)) + vec(SELF_B + 2)
        resid[part, :] = total
        xhat, _ = normed(total)
        normal = (xhat * vec(GAIN) + vec(SHIFT)).astype(BF16)
        hidden[part, :] = normal
        query[part, :] = ((mm(normal, square(w_cq)) + vec(CROSS_B)) * SCALE).astype(BF16)

    saves += [move(resid, resid_out), move(hidden, hidden_out), move(query, query_out), move(pairs, pairs_out)]
    step(third_group, 2)
    step(fourth_group, 1)

    @pl.loop(0, PAIRS)
    def _(pair):
        def cols(offset):
            return pl.ds(pl.multiple_of(offset + pair * WIDE, WIDE), WIDE)

        attend(
            False,
            512,
            query.at[:, cols(0)],
            pairs.at[:, cols(0)],
            pairs.at[:, cols(D)],
            row_side,
            source_side,
            cross_att.at[:, cols(0)],
            cross_lse.at[pl.ds(pair, 1)],
        )
        ticks(pair, {2: [(third_group, 3)], 4: [(fourth_group, 2)]})

    saves += [move(cross_att, cross_att_out), move(cross_lse, cross_lse_out)]
    step(fourth_group, 3)
    step(third_group, 4)
    step(fourth_group, 4)
    for plan in plans + [small_plan]:
        plan[-1]()
    for copy in saves:
        copy.wait()


def forward_call(ints, smalls, arrays):
    rows = smalls[0].shape[1]
    square = gather_shape(rows, D)
    lse = (PAIRS, LONG, 8)
    wide = (LONG, WIDE)

    def bf(*shape):
        return jax.ShapeDtypeStruct(shape, BF16)

    def f32(*shape):
        return jax.ShapeDtypeStruct(shape, F32)

    held = [bf(*square)] * 5 + [bf(*gather_shape(rows, 2 * D))]
    saved = [
        bf(LONG, 3 * D), bf(LONG, D), f32(*lse), f32(LONG, D), bf(LONG, D), bf(LONG, D), bf(LONG, 2 * D),
        bf(LONG, D), f32(*lse), bf(*wide), bf(*wide), bf(*wide),
    ]
    outs = held + [bf(*square), bf(*gather_shape(rows, FF)), bf(*gather_shape(4 * rows, D))]
    outs += saved + [f32(16, D), f32(1, FF)]
    in_vmem = pl.BlockSpec(memory_space=pltpu.VMEM)
    scratch = [pltpu.VMEM(s.shape, s.dtype) for s in held + [bf(LONG, D), bf(LONG, D)] + saved]
    scratch += [
        pltpu.VMEM((16, 256), F32),
        pltpu.VMEM((16, 256), BF16),
        pltpu.VMEM((4, 2, 2, 16, 256), BF16),
        pltpu.SemaphoreType.DMA((2, FORWARD_CHUNKS * GATHER_COPIES)),
        pltpu.SemaphoreType.DMA((2, SMALL_COPIES)),
        pltpu.SemaphoreType.DMA((FORWARD_CHUNKS + 1,)),
        pltpu.SemaphoreType.DMA((FORWARD_LOCAL,)),
    ]
    return pl.pallas_call(
        forward_kernel,
        out_shape=outs,
        in_specs=[pl.BlockSpec(memory_space=pltpu.SMEM)] * len(ints)
        + [in_vmem] * len(smalls)
        + [any_spec()] * len(arrays),
        out_specs=[any_spec()] * (len(outs) - 2) + [in_vmem] * 2,
        scratch_shapes=scratch,
        compiler_params=params(collective_id=0, has_side_effects=True),
        cost_estimate=cost(14 * LONG * D * D + 8 * LONG * LONG * D, 60 << 20),
        name="gather_forward",
    )(*ints, *smalls, *arrays)


def ffn_grads(activ_ref, branch3_ref, hidden2_ref, dpre_ref, out_grad_ref, in_grad_ref):
    out_grad_ref[...] = mm(activ_ref[...], branch3_ref[...], 0, 0).astype(BF16)
    in_grad_ref[...] = mm(hidden2_ref[...], dpre_ref[...], 0, 0).astype(BF16)


def ffn_grads_call(activ, branch3, hidden2, dpre):
    tile = 512
    return pl.pallas_call(
        ffn_grads,
        grid=(FF // tile,),
        in_specs=[
            pl.BlockSpec((LONG, tile), lambda i: (0, i)),
            whole((LONG, D)),
            whole((LONG, D)),
            pl.BlockSpec((LONG, tile), lambda i: (0, i)),
        ],
        out_specs=[
            pl.BlockSpec((tile, D), lambda i: (i, 0)),
            pl.BlockSpec((D, tile), lambda i: (0, i)),
        ],
        out_shape=[jax.ShapeDtypeStruct((FF, D), BF16), jax.ShapeDtypeStruct((D, FF), BF16)],
        compiler_params=params(),
        cost_estimate=cost(4 * LONG * D * FF, 8 * LONG * FF),
        name="ffn_grads",
    )(activ, branch3, hidden2, dpre)


def pair_grads(count, *refs):
    out_ref = refs[2 * count]
    for index in range(count):

        @pl.when(pl.program_id(0) == index)
        def _(index=index):
            out_ref[...] = mm(refs[index][...], refs[count + index][...], 0, 0).astype(BF16)


def pair_grads_call(lefts, rights, name):
    count = len(lefts)
    return pl.pallas_call(
        partial(pair_grads, count),
        grid=(count,),
        in_specs=[whole((LONG, D))] * (2 * count),
        out_specs=pl.BlockSpec((D, D), lambda i: (0, i)),
        out_shape=jax.ShapeDtypeStruct((D, D * count), BF16),
        compiler_params=params(),
        cost_estimate=cost(2 * LONG * D * D * count, 4 * LONG * D * count),
        name=name,
    )(*lefts, *rights)


def body(
    tokens,
    encoded,
    cotangent,
    bucket,
    target_len,
    source_len,
    self_in,
    self_bias,
    self_out,
    cross_q,
    cross_kv,
    cross_bias,
    cross_out,
    ffn_in,
    ffn_in_bias,
    ffn_out,
    ffn_out_bias,
    norm_gain,
    norm_shift,
):
    rows = self_in.shape[0]
    owners = D // rows
    direct = owners == 16
    square = (D, D)
    if direct:
        smalls = [self_bias, cross_bias, norm_gain, norm_shift]
        smalls += [ffn_out_bias.reshape(1, rows), ffn_in_bias.reshape(1, 4 * rows)]
        arrays = [tokens, encoded, self_in, self_out, cross_q, cross_kv, cross_out, ffn_in, ffn_out]
        results = forward_call([bucket, target_len, source_len], smalls, arrays)
        weights = [w.reshape(16 * w.shape[3], w.shape[4]) for w in results[:9]]
        (mixed, self_att, self_lse, resid1, hidden1, query, pairs, cross_att, cross_lse) = results[9:18]
        row_side, target_side, source_side, vec, bias = results[18:]
    else:
        everyone = partial(lax.all_gather, axis_name="fsdp", axis=0, tiled=True)
        self_w = everyone(self_in)
        weights = [self_w[:, i * D : (i + 1) * D] for i in range(3)]
        weights += [everyone(w) for w in (self_out, cross_q, cross_kv, cross_out, ffn_in, ffn_out)]
        small = [self_bias, cross_bias, norm_gain, norm_shift, ffn_out_bias, ffn_in_bias]
        small_all = everyone(jnp.concatenate([w.reshape(1, -1) for w in small], axis=1)).astype(F32)
        vec = small_all[:, : IN_B * rows].reshape(owners, IN_B, rows).transpose(1, 0, 2).reshape(IN_B, D)
        vec = jnp.pad(vec, ((0, 3), (0, 0)))
        bias = small_all[:, IN_B * rows : VEC_ROWS * rows].reshape(1, FF)
        row_side, target_side, source_side = mask_lanes(bucket[0], target_len[0], source_len[0])
        (mixed,) = row_call(
            project_in,
            512,
            [tokens],
            [(w, square, (0, 0)) for w in weights[:3]] + [(vec, (16, D), (0, 0))],
            [(3 * D, BF16)],
            [],
            "project_in",
            6 * LONG * D * D,
        )
        self_att, self_lse = attention_forward(
            (mixed, 0), (mixed, PAIRS), (mixed, 2 * PAIRS), row_side, target_side, True, "self_forward"
        )
        resid1, hidden1, query, pairs = row_call(
            between,
            512,
            [tokens, self_att, encoded],
            [(weights[3], square, (0, 0)), (weights[4], square, (0, 0)), (weights[5], (D, 2 * D), (0, 0))]
            + [(vec, (16, D), (0, 0))],
            [(D, F32), (D, BF16), (D, BF16), (2 * D, BF16)],
            [],
            "between",
            8 * LONG * D * D,
        )
        cross_att, cross_lse = attention_forward(
            (query, 0), (pairs, 0), (pairs, PAIRS), row_side, source_side, False, "cross_forward"
        )
    w_q, w_k, w_v, w_o, w_cq, w_ckv, w_co, w_fi, w_fo = weights
    vec_weight = (vec, (16, D), (0, 0))
    (output, activ, branch3, dpre, hidden2, dresid2, branch2, d_cross_att, sums_mid, bias_sum) = row_call(
        middle,
        256,
        [hidden1, cross_att, cotangent],
        [
            (w_co, square, (0, 0)),
            (w_fi, (D, FF), (0, 0)),
            (w_fo, (FF, D), (0, 0)),
            vec_weight,
            (bias, (1, FF), (0, 0)),
        ],
        [(D, BF16), (FF, BF16), (D, BF16), (FF, BF16), (D, BF16), (D, F32), (D, BF16), (D, BF16)],
        [(8, D), (1, FF)],
        "middle",
        36 * LONG * D * D,
    )
    ffn_out_grad, ffn_in_grad = ffn_grads_call(activ, branch3, hidden2, dpre)
    dcq, dck, dcv = attention_backward(
        (query, 0),
        (pairs, 0),
        (pairs, PAIRS),
        cross_att,
        d_cross_att,
        cross_lse,
        row_side,
        source_side,
        False,
        "cross_backward",
    )
    encoded_grad, dresid1, branch1, d_self_att, sums_cross = row_call(
        after_cross,
        512,
        [dcq, dck, dcv, dresid2, resid1],
        [(w_cq, square, (0, 0)), (w_ckv, (D, 2 * D), (0, 0)), (w_o, square, (0, 0)), vec_weight],
        [(D, BF16), (D, F32), (D, BF16), (D, BF16)],
        [(8, D)],
        "after_cross",
        8 * LONG * D * D,
    )
    mixed_grad = pair_grads_call(
        [self_att, hidden1, encoded, encoded, cross_att],
        [branch1, dcq, dck, dcv, branch2],
        "cross_grads",
    )
    dq, dk, dv = attention_backward(
        (mixed, 0),
        (mixed, PAIRS),
        (mixed, 2 * PAIRS),
        self_att,
        d_self_att,
        self_lse,
        row_side,
        target_side,
        True,
        "self_backward",
    )
    self_grad = pair_grads_call([tokens] * 3, [dq, dk, dv], "self_grads")
    (tokens_grad,) = row_call(
        tokens_back,
        512,
        [dq, dk, dv, dresid1],
        [(w, square, (0, 0)) for w in weights[:3]],
        [(D, BF16)],
        [],
        "tokens_back",
        6 * LONG * D * D,
    )

    dq_sum = jnp.sum(dq.astype(F32), axis=0, keepdims=True)
    dv_sum = jnp.sum(dv.astype(F32), axis=0, keepdims=True)
    small_rows = jnp.concatenate(
        [
            dq_sum,
            dv_sum,
            sums_cross[2:5],
            sums_mid[4:5],
            sums_cross[0:1],
            sums_mid[0:2],
            sums_cross[1:2],
            sums_mid[2:4],
            sums_mid[5:6],
        ],
        axis=0,
    )
    packed = small_rows.reshape(IN_B, owners, rows).transpose(1, 0, 2).reshape(owners, IN_B * rows)
    packed = jnp.concatenate([packed, bias_sum.reshape(owners, 4 * rows)], axis=1)
    grads = [self_grad, mixed_grad, ffn_in_grad, ffn_out_grad]
    if direct:
        packed = jnp.pad(packed, ((0, 0), (0, PACK - packed.shape[1]))).reshape(4, 2, 2, 16, 128)

        def cut(grad):
            return grad.reshape(4, 2, 2, grad.shape[0] // 16, grad.shape[1])

        ffn_in_share, ffn_out_share = scatter_call(
            [cut(ffn_in_grad), cut(ffn_out_grad)], None, 3, "scatter_ffn"
        )
        (mixed_share,) = scatter_call([cut(mixed_grad)], None, 4, "scatter_cross")
        self_share, packed_share = scatter_call([cut(self_grad)], packed, 5, "scatter_self")
        packed_share = packed_share.reshape(-1)
    else:

        def share_of(grad):
            share = lax.psum_scatter(grad.astype(F32), "fsdp", scatter_dimension=0, tiled=True)
            return lax.psum(share, "dp")

        self_share, mixed_share, ffn_in_share, ffn_out_share = map(share_of, grads)
        packed_share = share_of(packed).reshape(-1)

    def rows_of(first, count):
        return packed_share[first * rows : (first + count) * rows]

    return (
        output,
        tokens_grad,
        encoded_grad,
        self_share,
        rows_of(SELF_B, 3).reshape(3, rows),
        mixed_share[:, :D],
        mixed_share[:, D : 2 * D],
        mixed_share[:, 2 * D : 4 * D],
        rows_of(CROSS_B, 3).reshape(3, rows),
        mixed_share[:, 4 * D :],
        ffn_in_share,
        rows_of(IN_B, 4),
        ffn_out_share,
        rows_of(OUT_B, 1),
        rows_of(GAIN, 3).reshape(3, rows),
        rows_of(SHIFT, 3).reshape(3, rows),
    )


def solution(mesh):
    both = P(("dp", "fsdp"), None)
    rows, cols, flat = P("fsdp", None), P(None, "fsdp"), P("fsdp")
    return jax.shard_map(
        body,
        mesh=mesh,
        in_specs=(both, both, both, P(("dp", "fsdp")), both, both)
        + (rows, cols, rows, rows, rows, cols, rows, rows, flat, rows, flat, cols, cols),
        out_specs=(both, both, both)
        + (rows, cols, rows, rows, rows, cols, rows, rows, flat, rows, flat, cols, cols),
        check_vma=False,
    )
```

```python
from functools import partial

import jax
import jax.numpy as jnp
from jax import lax
from jax.experimental import pallas as pl
from jax.experimental.pallas import tpu as pltpu
from jax.sharding import PartitionSpec as P

D = 768
H = 12
HD = 64
FF = 3072
LONG = 1024
SEGS = 4
SHORT = 256
PAIRS = H // 2
WIDE = 2 * HD

EPS = 1e-05
NEG = -1e30
SCALE = HD ** (-0.5)
F32 = jnp.float32
BF16 = jnp.bfloat16
MESH_ID = pl.DeviceIdType.MESH
VMEM_LIMIT = 60 << 20

SELF_B, CROSS_B, GAIN, SHIFT, OUT_B, IN_B = 0, 3, 6, 9, 12, 13
VEC_ROWS = 17
PACK = 2048


def mm(left, right, left_dim=1, right_dim=0):
    return lax.dot_general(
        left, right, (((left_dim,), (right_dim,)), ((), ())), preferred_element_type=F32
    )


def params(**kwargs):
    return pltpu.CompilerParams(vmem_limit_bytes=VMEM_LIMIT, **kwargs)


def cost(flops, nbytes, trans=0):
    return pl.CostEstimate(flops=int(flops), bytes_accessed=int(nbytes), transcendentals=int(trans))


def any_spec():
    return pl.BlockSpec(memory_space=pl.ANY)


def whole(shape):
    return pl.BlockSpec(shape, lambda *_: (0,) * len(shape))


def normed(resid):
    centered = resid - jnp.mean(resid, axis=-1, keepdims=True)
    inv = lax.rsqrt(jnp.mean(centered * centered, axis=-1, keepdims=True) + EPS)
    return centered * inv, inv


def norm_back(xhat, inv, gain, grad):
    scaled = grad * gain
    first = jnp.mean(scaled, axis=-1, keepdims=True)
    second = jnp.mean(scaled * xhat, axis=-1, keepdims=True)
    return (scaled - first - xhat * second) * inv


def col_sum(values):
    return jnp.sum(values, axis=0, keepdims=True)


def my_place():
    dp, index = lax.axis_index("dp"), lax.axis_index("fsdp")
    return dp, index // 4, (index // 2) % 2, index % 2


def place(dp, z, y, core):
    return {"dp": dp, "fsdp": (z * 2 + y) * 2 + core}


def neighbours():
    x, z, y, c = my_place()
    return [place(x, (z + k) % 4, y, c) for k in (1, 2, 3)] + [
        place(1 - x, z, y, c),
        place(x, z, 1 - y, c),
        place(x, z, y, 1 - c),
    ]


def greet():
    barrier = pltpu.get_barrier_semaphore()
    others = neighbours()
    for other in others:
        pl.semaphore_signal(barrier, inc=1, device_id=other, device_id_type=MESH_ID)
    pl.semaphore_wait(barrier, len(others))


def remote(src, dst, sems, index, device):
    return pltpu.make_async_remote_copy(
        src_ref=src,
        dst_ref=dst,
        send_sem=sems.at[0, index],
        recv_sem=sems.at[1, index],
        device_id=device,
        device_id_type=MESH_ID,
    )


GATHER_COPIES = 11


def gather_copies(shard, full, sems, local_sem):
    x, z, y, c = my_place()
    half = shard.shape[-1] // 2
    mine = pl.ds(pl.multiple_of(x * half, 128), half)
    other = pl.ds(pl.multiple_of((1 - x) * half, 128), half)
    to_x, to_y, to_c = place(1 - x, z, y, c), place(x, z, 1 - y, c), place(x, z, y, 1 - c)

    def same(index, where, device):
        ref = full.at[where]
        return remote(ref, ref, sems, index, device)

    own = (slice(None), y, c, slice(None), mine)
    from_x = (slice(None), y, c, slice(None), other)
    from_y = (slice(None), 1 - y, c, slice(None), mine)
    diagonal = (slice(None), 1 - y, c, slice(None), other)
    copies = [
        remote(shard.at[:, mine], full.at[z, y, c, :, mine], sems, k - 1, place(x, (z + k) % 4, y, c))
        for k in (1, 2, 3)
    ]
    copies += [same(3, own, to_x), same(4, own, to_y)]
    copies += [
        same(5, (pl.ds(0, 2), 1 - y, c, slice(None), mine), to_x),
        same(6, (pl.ds(2, 2), y, c, slice(None), other), to_y),
    ]
    copies += [same(7, own, to_c), same(8, from_x, to_c), same(9, from_y, to_c), same(10, diagonal, to_c)]
    local = pltpu.make_async_copy(shard.at[:, mine], full.at[z, y, c, :, mine], local_sem)
    return copies, local


def gather_steps(shard, full, sems, local_sem):
    copies, local = gather_copies(shard, full, sems, local_sem)

    def first():
        local.start()
        for copy in copies[:3]:
            copy.start()

    def second():
        local.wait()
        for copy in copies[:3]:
            copy.wait_recv()
        for index in (3, 4, 7):
            copies[index].start()

    def third():
        copies[3].wait_recv()
        copies[4].wait_recv()
        for index in (5, 6, 8, 9):
            copies[index].start()

    def fourth():
        copies[5].wait_recv()
        copies[6].wait_recv()
        copies[10].start()

    def arrive():
        for index in (7, 8, 9, 10):
            copies[index].wait_recv()

    def last():
        for copy in copies:
            copy.wait_send()

    return [first, second, third, fourth, arrive, last]


SMALL_COPIES = 5


def small_gather_steps(shard, full, sems, local_sem):
    x, z, y, c = my_place()
    local = pltpu.make_async_copy(shard, full.at[z, y, c], local_sem)
    copies = [
        remote(shard, full.at[z, y, c], sems, k - 1, place(x, (z + k) % 4, y, c)) for k in (1, 2, 3)
    ]
    copies.append(remote(full.at[:, y, c], full.at[:, y, c], sems, 3, place(x, z, 1 - y, c)))
    copies.append(remote(full.at[:, :, c], full.at[:, :, c], sems, 4, place(x, z, y, 1 - c)))

    def first():
        local.start()
        for copy in copies[:3]:
            copy.start()

    def second():
        local.wait()
        for copy in copies[:3]:
            copy.wait_recv()
        copies[3].start()

    def third():
        copies[3].wait_recv()
        copies[4].start()

    def fourth():
        copies[4].wait_recv()

    def last():
        for copy in copies:
            copy.wait_send()

    return [first, second, third, fourth, last]


def gather_shape(rows, cols):
    return (4, 2, 2, rows, cols)


SCATTER_COPIES = 9
SCATTER_REFS = 10


def scatter_scratch(rows, cols):
    half = cols // 2
    return [
        pltpu.VMEM((4, 2, 2, rows, cols), BF16),
        pltpu.VMEM((4, 2, rows, cols), BF16),
        pltpu.VMEM((2, 2, rows, half), BF16),
        pltpu.VMEM((2, rows, half), BF16),
        pltpu.VMEM((2, rows, cols), BF16),
        pltpu.VMEM((2, rows, half), BF16),
        pltpu.VMEM((4, rows, half), BF16),
        pltpu.VMEM((3, rows, half), BF16),
        pltpu.VMEM((2, rows, half), BF16),
        pltpu.SemaphoreType.DMA((2, SCATTER_COPIES)),
    ]


def add_into(dst, where, left, right):
    dst[where] = (left.astype(F32) + right.astype(F32)).astype(BF16)


def scatter_steps(write, bufs):
    grads, peer, x_one, x_two, y_one, y_two, quarter, z_in, halves, sems = bufs
    x, z, y, c = my_place()
    half = grads.shape[-1] // 2
    to_x, to_y, to_c = place(1 - x, z, y, c), place(x, z, 1 - y, c), place(x, z, y, 1 - c)
    mine = pl.ds(pl.multiple_of(x * half, 128), half)
    other = pl.ds(pl.multiple_of((1 - x) * half, 128), half)
    every = slice(None)
    low, high = pl.ds(0, 2), pl.ds(2, 2)
    swap = remote(grads.at[:, :, 1 - c], peer, sems, 0, to_c)
    x_first = remote(grads.at[low, :, c, :, other], x_one, sems, 1, to_x)
    y_first = remote(grads.at[high, 1 - y, c], y_one, sems, 2, to_y)
    x_second = remote(grads.at[high, y, c, :, other], x_two, sems, 3, to_x)
    y_second = remote(grads.at[low, 1 - y, c, :, mine], y_two, sems, 4, to_y)
    z_sends = [
        remote(quarter.at[(z + k) % 4], z_in.at[k - 1], sems, 4 + k, place(x, (z + k) % 4, y, c))
        for k in (1, 2, 3)
    ]
    last_swap = remote(halves.at[0], halves.at[1], sems, 8, to_x)

    def start():
        swap.start()

    def sum_cores():
        swap.wait_recv()

        @pl.loop(0, 8)
        def _(i):
            where = (i // 2, i % 2, c)
            add_into(grads, where, grads[where], peer[i // 2, i % 2])

        x_first.start()
        y_first.start()

    def sum_first():
        x_first.wait_recv()
        y_first.wait_recv()

        @pl.loop(0, 2)
        def _(i):
            where = (i, 1 - y, c, every, mine)
            add_into(grads, where, grads[where], x_one[i, 1 - y])
            where = (2 + i, y, c, every, other)
            add_into(grads, where, grads[where], y_one[i, :, other])

        x_second.start()
        y_second.start()

        @pl.loop(0, 2)
        def _(i):
            add_into(quarter, i, grads[i, y, c, :, mine], x_one[i, y])
            add_into(quarter, 2 + i, grads[2 + i, y, c, :, mine], y_one[i, :, mine])

    def sum_second():
        x_second.wait_recv()
        y_second.wait_recv()

        @pl.loop(0, 2)
        def _(i):
            add_into(quarter, i, quarter[i], y_two[i])
            add_into(quarter, 2 + i, quarter[2 + i], x_two[i])

        for copy in z_sends:
            copy.start()

    def sum_z():
        for copy in z_sends:
            copy.wait_recv()
        total = quarter[z].astype(F32)
        for k in range(3):
            total = total + z_in[k].astype(F32)
        halves[0] = total.astype(BF16)
        last_swap.start()

    def finish():
        last_swap.wait_recv()
        write(x, halves[0].astype(F32))
        write(1 - x, halves[1].astype(F32))
        for copy in [swap, x_first, y_first, x_second, y_second] + z_sends + [last_swap]:
            copy.wait_send()

    return [start, sum_cores, sum_first, sum_second, sum_z, finish]


def write_half(share, first=0):
    def write(half_index, value):
        width = value.shape[1]
        share[:, pl.ds(pl.multiple_of(first + half_index * width, 128), width)] = value

    return write


SMALL_SCATTER = 6
SMALL_REFS = 9
SMALL_TILE = (16, 256)


def small_scatter_scratch():
    return [
        pltpu.VMEM((4, 2, 2) + SMALL_TILE, F32),
        pltpu.VMEM((4, 2) + SMALL_TILE, F32),
        pltpu.VMEM((4, 2) + SMALL_TILE, F32),
        pltpu.VMEM((4,) + SMALL_TILE, F32),
        pltpu.VMEM((4,) + SMALL_TILE, F32),
        pltpu.VMEM((3,) + SMALL_TILE, F32),
        pltpu.VMEM(SMALL_TILE, F32),
        pltpu.VMEM(SMALL_TILE, F32),
        pltpu.SemaphoreType.DMA((2, SMALL_SCATTER)),
    ]


def small_scatter_steps(write, bufs):
    held, pair, peer, line, from_y, z_in, mine, other, sems = bufs
    x, z, y, c = my_place()
    swap = remote(held.at[:, :, 1 - c], peer, sems, 0, place(x, z, y, 1 - c))
    to_y = remote(pair.at[:, 1 - y], from_y, sems, 1, place(x, z, 1 - y, c))
    z_sends = [
        remote(line.at[(z + k) % 4], z_in.at[k - 1], sems, 1 + k, place(x, (z + k) % 4, y, c))
        for k in (1, 2, 3)
    ]
    to_x = remote(mine, other, sems, 5, place(1 - x, z, y, c))

    def start():
        swap.start()

    def sum_cores():
        swap.wait_recv()
        pair[...] = held[:, :, c] + peer[...]
        to_y.start()

    def sum_y():
        to_y.wait_recv()
        line[...] = pair[:, y] + from_y[...]
        for copy in z_sends:
            copy.start()

    def sum_z():
        for copy in z_sends:
            copy.wait_recv()
        mine[...] = line[z] + z_in[0] + z_in[1] + z_in[2]
        to_x.start()

    def finish():
        to_x.wait_recv()
        write(mine[...] + other[...])
        for copy in [swap, to_y, to_x] + z_sends:
            copy.wait_send()

    return [start, sum_cores, sum_y, sum_z, finish]


def mask_lanes(kind, target_row, source_row):
    places = jnp.arange(LONG, dtype=jnp.int32)
    segment = jnp.where(kind == 1, 0, places // SHORT)
    offset = jnp.where(kind == 1, places, places % SHORT)
    lane = jnp.arange(WIDE, dtype=jnp.int32) % HD
    inside = segment[:, None] == lane[None, :]
    row_side = jnp.where(inside | (lane == SEGS)[None, :], 1.0, 0.0).astype(BF16)
    picker = segment[:, None] == jnp.arange(SEGS, dtype=jnp.int32)[None, :]

    def key_side(lengths):
        live = offset < jnp.sum(jnp.where(picker, lengths[None, :], 0), axis=1)
        blocked = ((lane < SEGS)[None, :] & ~inside) | ((lane == SEGS)[None, :] & ~live[:, None])
        ones = ((lane > SEGS) & (lane < SEGS + 4))[None, :]
        return jnp.where(blocked, NEG, jnp.where(ones, 1.0, 0.0)).astype(BF16)

    return row_side, key_side(target_row), key_side(source_row)


def lower(block, row_dim):
    rows = lax.broadcasted_iota(jnp.int32, (block, block), row_dim)
    cols = lax.broadcasted_iota(jnp.int32, (block, block), 1 - row_dim)
    return cols <= rows


def attend(causal, block, q_ref, k_ref, v_ref, row_ref, key_ref, att_ref, lse_ref):
    lane = lax.broadcasted_iota(jnp.int32, (1, WIDE), 1)
    results = []
    for head in range(2):
        inside = lane // HD == head
        spare = HD * (1 - head)
        keys = jnp.where(inside, k_ref[...], key_ref[...])
        vals = jnp.where(inside, v_ref[...], jnp.where(lane == spare, 1.0, 0.0).astype(BF16))
        parts = []
        for index in range(LONG // block):
            part = pl.ds(index * block, block)
            rows = jnp.where(inside, q_ref[part, :], row_ref[part, :])
            reach = (index + 1) * block if causal else LONG
            scores = mm(rows, keys[:reach], 1, 1)
            if causal:
                edge = jnp.where(lower(block, 0), scores[:, reach - block :], NEG)
                scores = (
                    edge
                    if reach == block
                    else jnp.concatenate([scores[:, : reach - block], edge], axis=1)
                )
            top = jnp.max(scores, axis=1, keepdims=True)
            weights = jnp.exp(scores - top).astype(BF16)
            mixed = mm(weights, vals[:reach])
            total = mixed[:, spare : spare + 1]
            parts.append((mixed / total, top + jnp.log(total)))
        results.append(parts)
    for index in range(LONG // block):
        part = pl.ds(index * block, block)
        (first, lse_first), (second, lse_second) = results[0][index], results[1][index]
        att_ref[part, :] = jnp.where(lane < HD, first, second).astype(BF16)
        lse_ref[0, part, :] = jnp.where(lane == 0, lse_first, lse_second)[:, :8]


def pair_spec(offset):
    return pl.BlockSpec((LONG, WIDE), lambda i: (0, offset + i))


def lse_spec():
    return pl.BlockSpec((1, LONG, 8), lambda i: (i, 0, 0))


def attention_forward(query, keys, values, row_side, key_side, causal, name):
    return pl.pallas_call(
        partial(attend, causal, 512),
        grid=(PAIRS,),
        in_specs=[pair_spec(query[1]), pair_spec(keys[1]), pair_spec(values[1])]
        + [whole((LONG, WIDE))] * 2,
        out_specs=[pair_spec(0), lse_spec()],
        out_shape=[
            jax.ShapeDtypeStruct((LONG, D), BF16),
            jax.ShapeDtypeStruct((PAIRS, LONG, 8), F32),
        ],
        compiler_params=params(),
        cost_estimate=cost(4 * LONG * LONG * D, 8 * LONG * D, H * LONG * LONG),
        name=name,
    )(query[0], keys[0], values[0], row_side, key_side)


def three_parts(value):
    high = value.astype(BF16)
    rest = value - high.astype(F32)
    middle = rest.astype(BF16)
    return high, middle, (rest - middle.astype(F32)).astype(BF16)


def attend_back(
    causal, block, q_ref, k_ref, v_ref, att_ref, grad_ref, lse_ref, row_ref, key_ref, dq_ref, dk_ref, dv_ref
):
    lane = lax.broadcasted_iota(jnp.int32, (1, WIDE), 1)
    blocks = LONG // block
    product = att_ref[...].astype(F32) * grad_ref[...].astype(F32)
    results = []
    for head in range(2):
        inside = lane // HD == head
        spare = HD * (1 - head)
        lse_parts = three_parts(-lse_ref[0, :, head : head + 1])
        delta_parts = three_parts(
            -jnp.sum(jnp.where(inside, product, 0.0), axis=1, keepdims=True)
        )
        row_extra, grad_extra = row_ref[...], jnp.zeros((LONG, WIDE), BF16)
        for i in range(3):
            here = lane == spare + SEGS + 1 + i
            row_extra = jnp.where(here, lse_parts[i], row_extra)
            grad_extra = jnp.where(here, delta_parts[i], grad_extra)
        rows = jnp.where(inside, q_ref[...], row_extra)
        grads = jnp.where(inside, grad_ref[...], grad_extra)
        keys = jnp.where(inside, k_ref[...], key_ref[...])
        ones = (lane > spare + SEGS) & (lane < spare + SEGS + 4)
        vals = jnp.where(inside, v_ref[...], jnp.where(ones, 1.0, 0.0).astype(BF16))
        dq, dk, dv = [None] * blocks, [], []
        for index in range(blocks):
            first = index * block if causal else 0
            key_part, val_part = keys[index * block :][:block], vals[index * block :][:block]
            scores = mm(key_part, rows[first:], 1, 1)
            if causal:
                edge = jnp.where(lower(block, 1), scores[:, :block], NEG)
                scores = (
                    edge
                    if first + block == LONG
                    else jnp.concatenate([edge, scores[:, block:]], axis=1)
                )
            probs = jnp.exp(scores)
            centered = mm(val_part, grads[first:], 1, 1)
            dscores = (probs * centered).astype(BF16)
            dv.append(mm(probs.astype(BF16), grads[first:]))
            dk.append(mm(dscores, rows[first:]))
            terms = mm(dscores, key_part, 0, 0)
            for q_index in range(first // block, blocks):
                term = terms[q_index * block - first :][:block]
                dq[q_index] = term if dq[q_index] is None else dq[q_index] + term
        results.append((dq, dk, dv))
    for index in range(blocks):
        part = pl.ds(index * block, block)
        for ref, member, factor in ((dq_ref, 0, SCALE), (dk_ref, 1, 1.0), (dv_ref, 2, 1.0)):
            both = jnp.where(lane < HD, results[0][member][index], results[1][member][index])
            ref[part, :] = (both * factor).astype(BF16)


def attention_backward(query, keys, values, att, grad, lse, row_side, key_side, causal, name):
    shape = jax.ShapeDtypeStruct((LONG, D), BF16)
    return pl.pallas_call(
        partial(attend_back, causal, 256 if causal else 512),
        grid=(PAIRS,),
        in_specs=[pair_spec(query[1]), pair_spec(keys[1]), pair_spec(values[1]), pair_spec(0), pair_spec(0)]
        + [lse_spec()]
        + [whole((LONG, WIDE))] * 2,
        out_specs=[pair_spec(0)] * 3,
        out_shape=[shape] * 3,
        compiler_params=params(),
        cost_estimate=cost(10 * LONG * LONG * D, 16 * LONG * D, H * LONG * LONG),
        name=name,
    )(query[0], keys[0], values[0], att, grad, lse, row_side, key_side)


def rows_spec(block, width):
    return pl.BlockSpec((block, width), lambda i: (i, 0))


def project_in(tokens_ref, q_w, k_w, v_w, vec_ref, out_ref):
    left = tokens_ref[...]
    out_ref[:, :D] = ((mm(left, q_w[...]) + vec_ref[SELF_B : SELF_B + 1]) * SCALE).astype(BF16)
    out_ref[:, D : 2 * D] = mm(left, k_w[...]).astype(BF16)
    out_ref[:, 2 * D :] = (mm(left, v_w[...]) + vec_ref[SELF_B + 1 : SELF_B + 2]).astype(BF16)


def between(
    tokens_ref, att_ref, encoded_ref, out_w, q_w, kv_w, vec_ref, resid_ref, hidden_ref, query_ref, pairs_ref
):
    pairs = mm(encoded_ref[...], kv_w[...])
    pairs_ref[:, :D] = pairs[:, :D].astype(BF16)
    pairs_ref[:, D:] = (pairs[:, D:] + vec_ref[CROSS_B + 1 : CROSS_B + 2]).astype(BF16)
    resid = tokens_ref[...].astype(F32) + mm(att_ref[...], out_w[...]) + vec_ref[SELF_B + 2 : SELF_B + 3]
    resid_ref[...] = resid
    xhat, _ = normed(resid)
    hidden = (xhat * vec_ref[GAIN : GAIN + 1] + vec_ref[SHIFT : SHIFT + 1]).astype(BF16)
    hidden_ref[...] = hidden
    query_ref[...] = ((mm(hidden, q_w[...]) + vec_ref[CROSS_B : CROSS_B + 1]) * SCALE).astype(BF16)


INV_SQRT2 = 0.7071067811865476
INV_SQRT_2PI = 0.3989422804014327


def middle(
    hidden1_ref,
    att_ref,
    cot_ref,
    cross_out,
    ffn_in,
    ffn_out,
    vec_ref,
    bias_ref,
    out_ref,
    activ_ref,
    branch3_ref,
    dpre_ref,
    hidden2_ref,
    dresid2_ref,
    branch2_ref,
    datt_ref,
    sums_ref,
    bias_sum_ref,
):
    def vec(row):
        return vec_ref[row : row + 1]

    resid2 = hidden1_ref[...].astype(F32) + mm(att_ref[...], cross_out[...]) + vec(CROSS_B + 2)
    xhat2, inv2 = normed(resid2)
    hidden2 = (xhat2 * vec(GAIN + 1) + vec(SHIFT + 1)).astype(BF16)
    hidden2_ref[...] = hidden2
    pre = mm(hidden2, ffn_in[...]) + bias_ref[...]
    phi = 0.5 + 0.5 * lax.erf(pre * INV_SQRT2)
    activ = (pre * phi).astype(BF16)
    slope = phi + pre * (INV_SQRT_2PI * jnp.exp(-0.5 * pre * pre))
    activ_ref[...] = activ
    resid3 = hidden2.astype(F32) + mm(activ, ffn_out[...]) + vec(OUT_B)
    xhat3, inv3 = normed(resid3)
    out_ref[...] = (xhat3 * vec(GAIN + 2) + vec(SHIFT + 2)).astype(BF16)
    cot = cot_ref[...].astype(F32)
    dresid3 = norm_back(xhat3, inv3, vec(GAIN + 2), cot)
    branch3 = dresid3.astype(BF16)
    branch3_ref[...] = branch3
    dpre = (mm(branch3, ffn_out[...], 1, 1) * slope).astype(BF16)
    dpre_ref[...] = dpre
    dhidden2 = dresid3 + mm(dpre, ffn_in[...], 1, 1)
    dresid2 = norm_back(xhat2, inv2, vec(GAIN + 1), dhidden2)
    dresid2_ref[...] = dresid2
    branch2 = dresid2.astype(BF16)
    branch2_ref[...] = branch2
    datt_ref[...] = mm(branch2, cross_out[...], 1, 1).astype(BF16)

    sums = jnp.concatenate(
        [
            col_sum(dhidden2 * xhat2),
            col_sum(cot * xhat3),
            col_sum(dhidden2),
            col_sum(cot),
            col_sum(branch2.astype(F32)),
            col_sum(branch3.astype(F32)),
            jnp.zeros((2, D), F32),
        ],
        axis=0,
    )
    bias_sum = col_sum(dpre.astype(F32))
    fresh = pl.program_id(0) == 0
    sums_ref[...] = jnp.where(fresh, sums, sums_ref[...] + sums)
    bias_sum_ref[...] = jnp.where(fresh, bias_sum, bias_sum_ref[...] + bias_sum)


def after_cross(
    dq_ref,
    dk_ref,
    dv_ref,
    dresid2_ref,
    resid1_ref,
    q_w,
    kv_w,
    out_w,
    vec_ref,
    encoded_grad_ref,
    dresid1_ref,
    branch1_ref,
    datt_ref,
    sums_ref,
):
    dq, dk, dv = dq_ref[...], dk_ref[...], dv_ref[...]
    encoded_grad_ref[...] = (mm(dk, kv_w[:, :D], 1, 1) + mm(dv, kv_w[:, D:], 1, 1)).astype(BF16)
    dhidden1 = dresid2_ref[...] + mm(dq, q_w[...], 1, 1)
    xhat, inv = normed(resid1_ref[...])
    dresid1 = norm_back(xhat, inv, vec_ref[GAIN : GAIN + 1], dhidden1)
    dresid1_ref[...] = dresid1
    branch1 = dresid1.astype(BF16)
    branch1_ref[...] = branch1
    datt_ref[...] = mm(branch1, out_w[...], 1, 1).astype(BF16)
    sums = jnp.concatenate(
        [
            col_sum(dhidden1 * xhat),
            col_sum(dhidden1),
            col_sum(branch1.astype(F32)),
            col_sum(dq.astype(F32)),
            col_sum(dv.astype(F32)),
            jnp.zeros((3, D), F32),
        ],
        axis=0,
    )
    sums_ref[...] = jnp.where(pl.program_id(0) == 0, sums, sums_ref[...] + sums)


def tokens_back(dq_ref, dk_ref, dv_ref, dresid1_ref, q_w, k_w, v_w, out_ref):
    total = dresid1_ref[...] + mm(dq_ref[...], q_w[...], 1, 1)
    total = total + mm(dk_ref[...], k_w[...], 1, 1)
    out_ref[...] = (total + mm(dv_ref[...], v_w[...], 1, 1)).astype(BF16)


def row_call(kernel, block, ins, weights, outs, sums, name, flops):
    in_specs = [rows_spec(block, a.shape[1]) for a in ins]
    for _, shape, index in weights:
        in_specs.append(pl.BlockSpec(shape, lambda i, index=index: index))
    out_specs = [rows_spec(block, width) for width, _ in outs] + [whole(s) for s in sums]
    out_shape = [jax.ShapeDtypeStruct((LONG, width), dtype) for width, dtype in outs]
    out_shape += [jax.ShapeDtypeStruct(s, F32) for s in sums]
    return pl.pallas_call(
        kernel,
        grid=(LONG // block,),
        in_specs=in_specs,
        out_specs=out_specs,
        out_shape=out_shape,
        compiler_params=params(),
        cost_estimate=cost(flops, flops / 500),
        name=name,
    )(*ins, *[w[0] for w in weights])


def write_masks(kind, target_row, source_row, row_ref, target_ref, source_ref):
    places = lax.broadcasted_iota(jnp.int32, (LONG, 1), 0)
    long = kind == 1
    segment = jnp.where(long, 0, lax.shift_right_logical(places, 8))
    offset = jnp.where(long, places, places & (SHORT - 1))
    lane = lax.broadcasted_iota(jnp.int32, (1, WIDE), 1) & (HD - 1)
    inside = segment == lane
    row_ref[...] = jnp.where(inside | (lane == SEGS), 1.0, 0.0).astype(BF16)
    ones = (lane > SEGS) & (lane < SEGS + 4)
    for ref, lengths in ((target_ref, target_row), (source_ref, source_row)):
        length = jnp.zeros((LONG, 1), jnp.int32)
        for index in range(SEGS):
            length = jnp.where(segment == index, lengths[index], length)
        dead = offset >= length
        blocked = ((lane < SEGS) & ~inside) | ((lane == SEGS) & dead)
        ref[...] = jnp.where(blocked, NEG, jnp.where(ones, 1.0, 0.0)).astype(BF16)


FORWARD_CHUNKS = 9
FORWARD_LOCAL = 32


def forward_kernel(*refs):
    (
        kind_ref, target_len, source_len,
        self_b, cross_b, gain, shift, out_b, in_b,
        tokens_hbm, encoded_hbm, self_in, self_out, cross_q, cross_kv, cross_out, ffn_in, ffn_out,
        w_q_out, w_k_out, w_v_out, w_o_out, w_cq_out, w_ckv_out, w_co_full, w_fi_full, w_fo_full,
        mixed_out, self_att_out, self_lse_out, resid_out, hidden_out, query_out, pairs_out,
        cross_att_out, cross_lse_out, row_out, target_out, source_out, vec_ref, bias_ref,
        w_q, w_k, w_v, w_o, w_cq, w_ckv,
        tokens, encoded, mixed, self_att, self_lse, resid, hidden, query, pairs,
        cross_att, cross_lse, row_side, target_side, source_side,
        pack, pack16, small_full,
        sems, small_sems, chunk_local, local,
    ) = refs
    used = [0]

    def move(src, dst):
        copy = pltpu.make_async_copy(src, dst, local.at[used[0]])
        used[0] += 1
        copy.start()
        return copy

    load_tokens, load_encoded = move(tokens_hbm, tokens), move(encoded_hbm, encoded)
    rows = self_b.shape[1]
    pack[...] = jnp.zeros_like(pack)
    for start, ref in ((SELF_B, self_b), (CROSS_B, cross_b), (GAIN, gain), (SHIFT, shift), (OUT_B, out_b)):
        pack[start : start + ref.shape[0], :rows] = ref[...].astype(F32)
    pack[IN_B : IN_B + 1, : 4 * rows] = in_b[...].astype(F32)
    pack16[...] = pack[...].astype(BF16)

    greet()
    chunks = [
        (self_in.at[:, pl.ds(0, D)], w_q),
        (self_in.at[:, pl.ds(D, D)], w_k),
        (self_in.at[:, pl.ds(2 * D, D)], w_v),
        (self_out, w_o),
        (cross_q, w_cq),
        (cross_kv, w_ckv),
        (cross_out, w_co_full),
        (ffn_in, w_fi_full),
        (ffn_out, w_fo_full),
    ]
    plans = [
        gather_steps(shard, full, sems.at[:, pl.ds(i * GATHER_COPIES, GATHER_COPIES)], chunk_local.at[i])
        for i, (shard, full) in enumerate(chunks)
    ]
    small_plan = small_gather_steps(pack16, small_full, small_sems, chunk_local.at[FORWARD_CHUNKS])
    first_group, second_group, third_group, fourth_group = (0, 1, 2), (3, 4, 5), (6, 7), (8,)

    def step(group, number):
        for index in group:
            plans[index][number]()

    small_plan[0]()
    step(first_group, 0)
    write_masks(
        kind_ref[0],
        [target_len[0, i] for i in range(SEGS)],
        [source_len[0, i] for i in range(SEGS)],
        row_side,
        target_side,
        source_side,
    )
    saves = [move(row_side, row_out), move(target_side, target_out), move(source_side, source_out)]
    small_plan[1]()
    step(first_group, 1)
    step(second_group, 0)
    small_plan[2]()
    step(first_group, 2)
    small_plan[3]()
    for z in range(4):
        for y in range(2):
            for c in range(2):
                owner = (z * 2 + y) * 2 + c
                tile = small_full[z, y, c].astype(F32)
                vec_ref[:, owner * rows : (owner + 1) * rows] = tile[:, :rows]
                bias_ref[:, owner * 4 * rows : (owner + 1) * 4 * rows] = tile[IN_B : IN_B + 1, : 4 * rows]
    step(first_group, 3)
    step(second_group, 1)
    step(third_group, 0)
    step(first_group, 4)
    saves += [move(w_q, w_q_out), move(w_k, w_k_out), move(w_v, w_v_out)]
    load_tokens.wait()

    def vec(row):
        return vec_ref[row : row + 1, :]

    def square(ref):
        return ref[...].reshape(D, ref.shape[-1])

    block = 512

    @pl.loop(0, LONG // block)
    def _(i):
        part = pl.ds(pl.multiple_of(i * block, block), block)
        left = tokens[part, :]
        mixed[part, :D] = ((mm(left, square(w_q)) + vec(SELF_B)) * SCALE).astype(BF16)
        mixed[part, D : 2 * D] = mm(left, square(w_k)).astype(BF16)
        mixed[part, 2 * D :] = (mm(left, square(w_v)) + vec(SELF_B + 1)).astype(BF16)

    saves.append(move(mixed, mixed_out))

    def ticks(index, table):
        for at, work in table.items():

            @pl.when(index == at)
            def _(work=work):
                for group, number in work:
                    step(group, number)

    @pl.loop(0, PAIRS)
    def _(pair):
        def cols(offset):
            return pl.ds(pl.multiple_of(offset + pair * WIDE, WIDE), WIDE)

        attend(
            True,
            512,
            mixed.at[:, cols(0)],
            mixed.at[:, cols(D)],
            mixed.at[:, cols(2 * D)],
            row_side,
            target_side,
            self_att.at[:, cols(0)],
            self_lse.at[pl.ds(pair, 1)],
        )
        ticks(
            pair,
            {
                1: [(second_group, 2), (third_group, 1), (fourth_group, 0)],
                3: [(second_group, 3)],
            },
        )

    saves += [move(self_att, self_att_out), move(self_lse, self_lse_out)]
    load_encoded.wait()
    step(second_group, 4)
    saves += [move(w_o, w_o_out), move(w_cq, w_cq_out), move(w_ckv, w_ckv_out)]

    @pl.loop(0, LONG // block)
    def _(i):
        part = pl.ds(pl.multiple_of(i * block, block), block)
        both = mm(encoded[part, :], square(w_ckv))
        pairs[part, :D] = both[:, :D].astype(BF16)
        pairs[part, D:] = (both[:, D:] + vec(CROSS_B + 1)).astype(BF16)
        total = tokens[part, :].astype(F32) + mm(self_att[part, :], square(w_o)) + vec(SELF_B + 2)
        resid[part, :] = total
        xhat, _ = normed(total)
        normal = (xhat * vec(GAIN) + vec(SHIFT)).astype(BF16)
        hidden[part, :] = normal
        query[part, :] = ((mm(normal, square(w_cq)) + vec(CROSS_B)) * SCALE).astype(BF16)

    saves += [move(resid, resid_out), move(hidden, hidden_out), move(query, query_out), move(pairs, pairs_out)]
    step(third_group, 2)
    step(fourth_group, 1)

    @pl.loop(0, PAIRS)
    def _(pair):
        def cols(offset):
            return pl.ds(pl.multiple_of(offset + pair * WIDE, WIDE), WIDE)

        attend(
            False,
            512,
            query.at[:, cols(0)],
            pairs.at[:, cols(0)],
            pairs.at[:, cols(D)],
            row_side,
            source_side,
            cross_att.at[:, cols(0)],
            cross_lse.at[pl.ds(pair, 1)],
        )
        ticks(pair, {2: [(third_group, 3)], 4: [(fourth_group, 2)]})

    saves += [move(cross_att, cross_att_out), move(cross_lse, cross_lse_out)]
    step(fourth_group, 3)
    step(third_group, 4)
    step(fourth_group, 4)
    for plan in plans + [small_plan]:
        plan[-1]()
    for copy in saves:
        copy.wait()


def forward_call(ints, smalls, arrays):
    rows = smalls[0].shape[1]
    square = gather_shape(rows, D)
    lse = (PAIRS, LONG, 8)
    wide = (LONG, WIDE)

    def bf(*shape):
        return jax.ShapeDtypeStruct(shape, BF16)

    def f32(*shape):
        return jax.ShapeDtypeStruct(shape, F32)

    held = [bf(*square)] * 5 + [bf(*gather_shape(rows, 2 * D))]
    saved = [
        bf(LONG, 3 * D), bf(LONG, D), f32(*lse), f32(LONG, D), bf(LONG, D), bf(LONG, D), bf(LONG, 2 * D),
        bf(LONG, D), f32(*lse), bf(*wide), bf(*wide), bf(*wide),
    ]
    outs = held + [bf(*square), bf(*gather_shape(rows, FF)), bf(*gather_shape(4 * rows, D))]
    outs += saved + [f32(16, D), f32(1, FF)]
    in_vmem = pl.BlockSpec(memory_space=pltpu.VMEM)
    scratch = [pltpu.VMEM(s.shape, s.dtype) for s in held + [bf(LONG, D), bf(LONG, D)] + saved]
    scratch += [
        pltpu.VMEM((16, 256), F32),
        pltpu.VMEM((16, 256), BF16),
        pltpu.VMEM((4, 2, 2, 16, 256), BF16),
        pltpu.SemaphoreType.DMA((2, FORWARD_CHUNKS * GATHER_COPIES)),
        pltpu.SemaphoreType.DMA((2, SMALL_COPIES)),
        pltpu.SemaphoreType.DMA((FORWARD_CHUNKS + 1,)),
        pltpu.SemaphoreType.DMA((FORWARD_LOCAL,)),
    ]
    return pl.pallas_call(
        forward_kernel,
        out_shape=outs,
        in_specs=[pl.BlockSpec(memory_space=pltpu.SMEM)] * len(ints)
        + [in_vmem] * len(smalls)
        + [any_spec()] * len(arrays),
        out_specs=[any_spec()] * (len(outs) - 2) + [in_vmem] * 2,
        scratch_shapes=scratch,
        compiler_params=params(collective_id=0, has_side_effects=True),
        cost_estimate=cost(14 * LONG * D * D + 8 * LONG * LONG * D, 60 << 20),
        name="gather_forward",
    )(*ints, *smalls, *arrays)


def ffn_grads(activ_ref, branch3_ref, hidden2_ref, dpre_ref, out_grad_ref, in_grad_ref):
    out_grad_ref[...] = mm(activ_ref[...], branch3_ref[...], 0, 0).astype(BF16)
    in_grad_ref[...] = mm(hidden2_ref[...], dpre_ref[...], 0, 0).astype(BF16)


def ffn_grads_call(activ, branch3, hidden2, dpre):
    tile = 512
    return pl.pallas_call(
        ffn_grads,
        grid=(FF // tile,),
        in_specs=[
            pl.BlockSpec((LONG, tile), lambda i: (0, i)),
            whole((LONG, D)),
            whole((LONG, D)),
            pl.BlockSpec((LONG, tile), lambda i: (0, i)),
        ],
        out_specs=[
            pl.BlockSpec((tile, D), lambda i: (i, 0)),
            pl.BlockSpec((D, tile), lambda i: (0, i)),
        ],
        out_shape=[jax.ShapeDtypeStruct((FF, D), BF16), jax.ShapeDtypeStruct((D, FF), BF16)],
        compiler_params=params(),
        cost_estimate=cost(4 * LONG * D * FF, 8 * LONG * FF),
        name="ffn_grads",
    )(activ, branch3, hidden2, dpre)


def pair_grads(count, *refs):
    out_ref = refs[2 * count]
    for index in range(count):

        @pl.when(pl.program_id(0) == index)
        def _(index=index):
            out_ref[...] = mm(refs[index][...], refs[count + index][...], 0, 0).astype(BF16)


def pair_grads_call(lefts, rights, name):
    count = len(lefts)
    return pl.pallas_call(
        partial(pair_grads, count),
        grid=(count,),
        in_specs=[whole((LONG, D))] * (2 * count),
        out_specs=pl.BlockSpec((D, D), lambda i: (0, i)),
        out_shape=jax.ShapeDtypeStruct((D, D * count), BF16),
        compiler_params=params(),
        cost_estimate=cost(2 * LONG * D * D * count, 4 * LONG * D * count),
        name=name,
    )(*lefts, *rights)


def pair_fetcher(sources, lse, slots, lse_slots, sems):
    def copies(pair, slot):
        out = []
        for index, (ref, first) in enumerate(sources):
            cols = pl.ds(pl.multiple_of(first + pair * WIDE, WIDE), WIDE)
            out.append(
                pltpu.make_async_copy(ref.at[:, cols], slots.at[slot, index], sems.at[slot, index])
            )
        count = len(sources)
        out.append(pltpu.make_async_copy(lse.at[pair], lse_slots.at[slot, 0], sems.at[slot, count]))
        return out

    return copies


def pair_scratch():
    return [
        pltpu.VMEM((2, 5, LONG, WIDE), BF16),
        pltpu.VMEM((2, 1, LONG, 8), F32),
        pltpu.SemaphoreType.DMA((2, 6)),
    ]


def back_pairs(causal, fetch, slots, lse_slots, row_side, key_side, dq, dk, dv, after):
    block = 256

    @pl.loop(0, PAIRS)
    def _(pair):
        slot = pair % 2

        @pl.when(pair < PAIRS - 1)
        def _():
            for copy in fetch(pair + 1, 1 - slot):
                copy.start()

        for copy in fetch(pair, slot):
            copy.wait()

        def target(member):
            ref, first = member
            return ref.at[:, pl.ds(pl.multiple_of(first + pair * WIDE, WIDE), WIDE)]

        attend_back(
            causal,
            block,
            *[slots.at[slot, i] for i in range(5)],
            lse_slots.at[slot],
            row_side,
            key_side,
            target(dq),
            target(dk),
            target(dv),
        )
        for at, work in after.items():

            @pl.when(pair == at)
            def _(work=work):
                for member in work:
                    member()


FIRST_LOCAL = 24


def back_first_kernel(*refs):
    (
        row_side, source_side, vec_ref,
        activ_hbm, branch3_hbm, hidden2_hbm, dpre_hbm,
        query_hbm, pairs_hbm, cross_att_hbm, datt_hbm, lse_hbm,
        dresid2_hbm, resid1_hbm, w_cq_hbm, w_o_hbm, w_ckv_hbm,
        dcq_out, dck_out, dcv_out, branch1_out, self_datt_out, dresid1_out, encoded_grad_out,
        ffn_in_share, ffn_out_share, sums_ref,
        activ, dpre, branch3, hidden2, dresid, resid, w_cq, w_o, w_ckv,
        slots, lse_slots, pair_sems,
        local, *scatter_bufs,
    ) = refs
    used = [0]

    def move(src, dst):
        copy = pltpu.make_async_copy(src, dst, local.at[used[0]])
        used[0] += 1
        copy.start()
        return copy

    quarters = [pl.ds(i * D, D) for i in range(FF // D)]
    load_branch3 = move(branch3_hbm, branch3)
    load_activ = [move(activ_hbm.at[:, q], activ.at[:, q]) for q in quarters]
    load_hidden2 = move(hidden2_hbm, hidden2)
    load_dpre = [move(dpre_hbm.at[:, q], dpre.at[:, q]) for q in quarters]
    greet()
    fetch = pair_fetcher(
        [(query_hbm, 0), (pairs_hbm, 0), (pairs_hbm, D), (cross_att_hbm, 0), (datt_hbm, 0)],
        lse_hbm,
        slots,
        lse_slots,
        pair_sems,
    )
    for copy in fetch(0, 0):
        copy.start()
    later = [
        move(dresid2_hbm, dresid),
        move(resid1_hbm, resid),
        move(w_cq_hbm, w_cq),
        move(w_o_hbm, w_o),
        move(w_ckv_hbm, w_ckv),
    ]
    out_bufs, in_bufs = scatter_bufs[:SCATTER_REFS], scatter_bufs[SCATTER_REFS:]
    out_plan = scatter_steps(write_half(ffn_out_share), out_bufs)
    in_plan = scatter_steps(write_half(ffn_in_share), in_bufs)
    out_rows = out_bufs[0].shape[3]
    tile = 2 * out_rows
    load_branch3.wait()
    for q in range(FF // D):
        load_activ[q].wait()
        for part in range(D // tile):
            index = q * (D // tile) + part
            left = activ[:, index * tile : (index + 1) * tile]
            grad = mm(left, branch3[...], 0, 0).astype(BF16)
            out_bufs[0][index // 2, index % 2] = grad.reshape(2, out_rows, D)
    out_plan[0]()
    load_hidden2.wait()
    in_rows = in_bufs[0].shape[3]
    for q in range(FF // D):
        load_dpre[q].wait()
        grad = mm(hidden2[...], dpre[:, quarters[q]], 0, 0).astype(BF16)
        in_bufs[0][:, :, :, :, quarters[q]] = grad.reshape(4, 2, 2, in_rows, D)
    out_plan[1]()
    in_plan[0]()
    back_pairs(
        False,
        fetch,
        slots,
        lse_slots,
        row_side,
        source_side,
        (activ, 0),
        (activ, D),
        (activ, 2 * D),
        {
            0: [in_plan[1]],
            1: [out_plan[2]],
            3: [out_plan[3], in_plan[2]],
            5: [in_plan[3], out_plan[4]],
        },
    )
    dcq, dck, dcv, branch1 = (activ.at[:, q] for q in quarters)
    self_datt, encoded_grad = dpre.at[:, quarters[0]], dpre.at[:, quarters[1]]
    saves = [move(dcq, dcq_out), move(dck, dck_out), move(dcv, dcv_out)]
    for copy in later:
        copy.wait()

    def square(ref):
        return ref[...].reshape(D, ref.shape[-1])

    block = 512
    sums_ref[...] = jnp.zeros_like(sums_ref)

    @pl.loop(0, LONG // block)
    def _(i):
        part = pl.ds(pl.multiple_of(i * block, block), block)
        left = dcq[part, :]
        dhidden = dresid[part, :] + mm(left, square(w_cq), 1, 1)
        xhat, inv = normed(resid[part, :])
        dresid1 = norm_back(xhat, inv, vec_ref[GAIN : GAIN + 1], dhidden)
        dresid[part, :] = dresid1
        low = dresid1.astype(BF16)
        branch1[part, :] = low
        self_datt[part, :] = mm(low, square(w_o), 1, 1).astype(BF16)
        sums_ref[0:1] += col_sum(dhidden * xhat)
        sums_ref[1:2] += col_sum(dhidden)
        sums_ref[2:3] += col_sum(low.astype(F32))
        sums_ref[3:4] += col_sum(left.astype(F32))
        sums_ref[4:5] += col_sum(dcv[part, :].astype(F32))

    saves += [move(branch1, branch1_out), move(self_datt, self_datt_out), move(dresid, dresid1_out)]
    out_plan[5]()
    in_plan[4]()

    @pl.loop(0, LONG // block)
    def _(i):
        part = pl.ds(pl.multiple_of(i * block, block), block)
        weight = square(w_ckv)
        total = mm(dck[part, :], weight[:, :D], 1, 1) + mm(dcv[part, :], weight[:, D:], 1, 1)
        encoded_grad[part, :] = total.astype(BF16)

    saves.append(move(encoded_grad, encoded_grad_out))
    in_plan[5]()
    for copy in saves:
        copy.wait()


def back_first_call(vmem_arrays, hbm_arrays, rows):
    in_vmem = pl.BlockSpec(memory_space=pltpu.VMEM)
    square = gather_shape(rows, D)

    def bf(*shape):
        return jax.ShapeDtypeStruct(shape, BF16)

    def f32(*shape):
        return jax.ShapeDtypeStruct(shape, F32)

    outs = [bf(LONG, D)] * 5 + [f32(LONG, D), bf(LONG, D)]
    outs += [f32(rows, FF), f32(4 * rows, D), f32(8, D)]
    held = [bf(LONG, FF)] * 2 + [bf(LONG, D)] * 2 + [f32(LONG, D)] * 2
    held += [bf(*square)] * 2 + [bf(*gather_shape(rows, 2 * D))]
    scratch = [pltpu.VMEM(h.shape, h.dtype) for h in held] + pair_scratch()
    scratch += [pltpu.SemaphoreType.DMA((FIRST_LOCAL,))]
    scratch += scatter_scratch(4 * rows, D) + scatter_scratch(rows, FF)
    return pl.pallas_call(
        back_first_kernel,
        out_shape=outs,
        in_specs=[in_vmem] * len(vmem_arrays) + [any_spec()] * len(hbm_arrays),
        out_specs=[any_spec()] * 7 + [in_vmem] * 3,
        scratch_shapes=scratch,
        compiler_params=params(collective_id=1, has_side_effects=True),
        cost_estimate=cost(26 * LONG * D * D + 10 * LONG * LONG * D, 60 << 20),
        name="backward_cross_scatter_ffn",
    )(*vmem_arrays, *hbm_arrays)


SECOND_LOCAL = 24
CROSS_PARTS = 5
SELF_PARTS = 3


def back_second_kernel(*refs):
    (
        row_side, target_side, sums_mid, bias_sum, sums_cross,
        self_att_hbm, cross_att_hbm, hidden1_hbm, encoded_hbm,
        branch1_hbm, branch2_hbm, dcq_hbm, dck_hbm, dcv_hbm,
        mixed_hbm, datt_hbm, lse_hbm, tokens_hbm, dresid1_hbm, w_q_hbm, w_k_hbm, w_v_hbm,
        tokens_grad_out,
        self_in_share, self_out_share, cross_q_share, cross_kv_share, cross_out_share,
        self_b_out, cross_b_out, gain_out, shift_out, out_b_out, in_b_out,
        lefts, rights, tokens, dresid, w_q, w_k, w_v, vec_sums,
        slots, lse_slots, pair_sems,
        local, *scatter_bufs,
    ) = refs
    used = [0]

    def move(src, dst):
        copy = pltpu.make_async_copy(src, dst, local.at[used[0]])
        used[0] += 1
        copy.start()
        return copy

    left_sources = (self_att_hbm, cross_att_hbm, hidden1_hbm, encoded_hbm)
    right_sources = (branch1_hbm, branch2_hbm, dcq_hbm, dck_hbm, dcv_hbm)
    load_left, load_right = [], []
    for index, source in enumerate(right_sources):
        if index < len(left_sources):
            load_left.append(move(left_sources[index], lefts.at[index]))
        load_right.append(move(source, rights.at[index]))
    greet()
    fetch = pair_fetcher(
        [(mixed_hbm, 0), (mixed_hbm, D), (mixed_hbm, 2 * D), (self_att_hbm, 0), (datt_hbm, 0)],
        lse_hbm,
        slots,
        lse_slots,
        pair_sems,
    )
    for copy in fetch(0, 0):
        copy.start()
    load_tokens = move(tokens_hbm, tokens)
    later = [
        move(dresid1_hbm, dresid),
        move(w_q_hbm, w_q),
        move(w_k_hbm, w_k),
        move(w_v_hbm, w_v),
    ]

    def bufs(index):
        return scatter_bufs[index * SCATTER_REFS : (index + 1) * SCATTER_REFS]

    writers = [
        write_half(self_out_share),
        write_half(cross_out_share),
        write_half(cross_q_share),
        write_half(cross_kv_share),
        write_half(cross_kv_share, D),
    ]
    cross_plans = [scatter_steps(writers[i], bufs(i)) for i in range(CROSS_PARTS)]

    def write_self(part):
        def write(half_index, value):
            for index in range(3):
                at = half_index * 3 + index
                first = (at // 2) * D + part * 256 + (at % 2) * 128
                cols = pl.ds(pl.multiple_of(first, 128), 128)
                self_in_share[:, cols] = value[:, index * 128 : (index + 1) * 128]

        return write

    self_plans = [scatter_steps(write_self(i), bufs(CROSS_PARTS + i)) for i in range(SELF_PARTS)]
    small_bufs = scatter_bufs[(CROSS_PARTS + SELF_PARTS) * SCATTER_REFS :]

    def write_small(total):
        rows = self_b_out.shape[1]
        for start, ref in (
            (SELF_B, self_b_out),
            (CROSS_B, cross_b_out),
            (GAIN, gain_out),
            (SHIFT, shift_out),
            (OUT_B, out_b_out),
        ):
            ref[...] = total[start : start + ref.shape[0], :rows]
        in_b_out[...] = total[IN_B : IN_B + 1, : 4 * rows]

    small_plan = small_scatter_steps(write_small, small_bufs)
    rows = bufs(0)[0].shape[3]
    for index in range(CROSS_PARTS):
        if index < len(load_left):
            load_left[index].wait()
        load_right[index].wait()
        left = lefts[min(index, len(left_sources) - 1)]
        grad = mm(left, rights[index], 0, 0).astype(BF16)
        bufs(index)[0][...] = grad.reshape(4, 2, 2, rows, D)
        cross_plans[index][0]()
        if index:
            cross_plans[index - 1][1]()
    load_tokens.wait()
    vec_sums[...] = jnp.zeros_like(vec_sums)
    dq, dk, dv = rights.at[2], rights.at[3], rights.at[4]

    def self_part(part):
        def work():
            cols = pl.ds(part * 256, 256)
            target = bufs(CROSS_PARTS + part)[0]
            left = tokens[...]
            ones = jnp.ones((8, LONG), BF16)
            for index, ref in enumerate((dq, dk, dv)):
                right = ref[:, cols]
                grad = mm(left, right, 0, 0).astype(BF16)
                target[:, :, :, :, index * 256 : (index + 1) * 256] = grad.reshape(4, 2, 2, rows, 256)
                if index != 1:
                    row = SELF_B + index // 2
                    vec_sums[row : row + 1, cols] = mm(ones, right)[0:1]
            self_plans[part][0]()

        return work

    def both(members, number):
        return [cross_plans[i][number] for i in members]

    back_pairs(
        True,
        fetch,
        slots,
        lse_slots,
        row_side,
        target_side,
        (dq, 0),
        (dk, 0),
        (dv, 0),
        {
            0: both((4,), 1) + both((0, 1), 2),
            1: [self_part(0)] + both((2, 3), 2) + both((0, 1), 3),
            2: [self_plans[0][1]] + both((4,), 2) + both((2, 3), 3) + both((0, 1), 4),
            3: [self_part(1), self_plans[0][2]] + both((4,), 3) + both((2, 3), 4) + both((0, 1), 5),
            4: [self_plans[1][1], self_plans[0][3]] + both((4,), 4) + both((2, 3), 5),
            5: [self_part(2), self_plans[1][2], self_plans[0][4]] + both((4,), 5),
        },
    )

    vec_sums[SELF_B + 2 : CROSS_B + 2] = sums_cross[2:5]
    vec_sums[CROSS_B + 2 : CROSS_B + 3] = sums_mid[4:5]
    vec_sums[GAIN : GAIN + 1] = sums_cross[0:1]
    vec_sums[GAIN + 1 : GAIN + 3] = sums_mid[0:2]
    vec_sums[SHIFT : SHIFT + 1] = sums_cross[1:2]
    vec_sums[SHIFT + 1 : SHIFT + 3] = sums_mid[2:4]
    vec_sums[OUT_B : OUT_B + 1] = sums_mid[5:6]
    held = small_bufs[0]
    held[...] = jnp.zeros_like(held)
    for owner in range(16):
        tile = held.at[owner // 4, (owner // 2) % 2, owner % 2]
        tile[:, :rows] = vec_sums[:, owner * rows : (owner + 1) * rows]
        tile[IN_B : IN_B + 1, : 4 * rows] = bias_sum[:, owner * 4 * rows : (owner + 1) * 4 * rows]
    small_plan[0]()
    for copy in later:
        copy.wait()

    def square(ref):
        return ref[...].reshape(D, D)

    block = 256

    def rows_back(index):
        part = pl.ds(index * block, block)
        total = dresid[part, :] + mm(dq[part, :], square(w_q), 1, 1)
        total = total + mm(dk[part, :], square(w_k), 1, 1)
        tokens[part, :] = (total + mm(dv[part, :], square(w_v), 1, 1)).astype(BF16)

    rows_back(0)
    self_plans[2][1]()
    small_plan[1]()
    self_plans[1][3]()
    self_plans[0][5]()
    rows_back(1)
    small_plan[2]()
    rows_back(2)
    self_plans[2][2]()
    self_plans[1][4]()
    small_plan[3]()
    rows_back(3)
    save = move(tokens, tokens_grad_out)
    self_plans[2][3]()
    self_plans[1][5]()
    small_plan[4]()
    self_plans[2][4]()
    self_plans[2][5]()
    save.wait()


def back_second_call(vmem_arrays, hbm_arrays, rows):
    in_vmem = pl.BlockSpec(memory_space=pltpu.VMEM)
    square = gather_shape(rows, D)

    def bf(*shape):
        return jax.ShapeDtypeStruct(shape, BF16)

    def f32(*shape):
        return jax.ShapeDtypeStruct(shape, F32)

    outs = [bf(LONG, D), f32(rows, 3 * D), f32(rows, D), f32(rows, D), f32(rows, 2 * D), f32(rows, D)]
    outs += [f32(3, rows)] * 4 + [f32(1, rows), f32(1, 4 * rows)]
    held = [bf(4, LONG, D), bf(5, LONG, D), bf(LONG, D), f32(LONG, D)] + [bf(*square)] * 3 + [f32(16, D)]
    scratch = [pltpu.VMEM(h.shape, h.dtype) for h in held] + pair_scratch()
    scratch += [pltpu.SemaphoreType.DMA((SECOND_LOCAL,))]
    for _ in range(CROSS_PARTS + SELF_PARTS):
        scratch += scatter_scratch(rows, D)
    scratch += small_scatter_scratch()
    return pl.pallas_call(
        back_second_kernel,
        out_shape=outs,
        in_specs=[in_vmem] * len(vmem_arrays) + [any_spec()] * len(hbm_arrays),
        out_specs=[any_spec()] + [in_vmem] * (len(outs) - 1),
        scratch_shapes=scratch,
        compiler_params=params(collective_id=2, has_side_effects=True),
        cost_estimate=cost(22 * LONG * D * D + 10 * LONG * LONG * D, 60 << 20),
        name="backward_self_scatter_rest",
    )(*vmem_arrays, *hbm_arrays)


def body(
    tokens,
    encoded,
    cotangent,
    bucket,
    target_len,
    source_len,
    self_in,
    self_bias,
    self_out,
    cross_q,
    cross_kv,
    cross_bias,
    cross_out,
    ffn_in,
    ffn_in_bias,
    ffn_out,
    ffn_out_bias,
    norm_gain,
    norm_shift,
):
    rows = self_in.shape[0]
    owners = D // rows
    direct = owners == 16
    square = (D, D)
    if direct:
        smalls = [self_bias, cross_bias, norm_gain, norm_shift]
        smalls += [ffn_out_bias.reshape(1, rows), ffn_in_bias.reshape(1, 4 * rows)]
        arrays = [tokens, encoded, self_in, self_out, cross_q, cross_kv, cross_out, ffn_in, ffn_out]
        results = forward_call([bucket, target_len, source_len], smalls, arrays)
        weights = [w.reshape(16 * w.shape[3], w.shape[4]) for w in results[:9]]
        (mixed, self_att, self_lse, resid1, hidden1, query, pairs, cross_att, cross_lse) = results[9:18]
        row_side, target_side, source_side, vec, bias = results[18:]
    else:
        everyone = partial(lax.all_gather, axis_name="fsdp", axis=0, tiled=True)
        self_w = everyone(self_in)
        weights = [self_w[:, i * D : (i + 1) * D] for i in range(3)]
        weights += [everyone(w) for w in (self_out, cross_q, cross_kv, cross_out, ffn_in, ffn_out)]
        small = [self_bias, cross_bias, norm_gain, norm_shift, ffn_out_bias, ffn_in_bias]
        small_all = everyone(jnp.concatenate([w.reshape(1, -1) for w in small], axis=1)).astype(F32)
        vec = small_all[:, : IN_B * rows].reshape(owners, IN_B, rows).transpose(1, 0, 2).reshape(IN_B, D)
        vec = jnp.pad(vec, ((0, 3), (0, 0)))
        bias = small_all[:, IN_B * rows : VEC_ROWS * rows].reshape(1, FF)
        row_side, target_side, source_side = mask_lanes(bucket[0], target_len[0], source_len[0])
        (mixed,) = row_call(
            project_in,
            512,
            [tokens],
            [(w, square, (0, 0)) for w in weights[:3]] + [(vec, (16, D), (0, 0))],
            [(3 * D, BF16)],
            [],
            "project_in",
            6 * LONG * D * D,
        )
        self_att, self_lse = attention_forward(
            (mixed, 0), (mixed, PAIRS), (mixed, 2 * PAIRS), row_side, target_side, True, "self_forward"
        )
        resid1, hidden1, query, pairs = row_call(
            between,
            512,
            [tokens, self_att, encoded],
            [(weights[3], square, (0, 0)), (weights[4], square, (0, 0)), (weights[5], (D, 2 * D), (0, 0))]
            + [(vec, (16, D), (0, 0))],
            [(D, F32), (D, BF16), (D, BF16), (2 * D, BF16)],
            [],
            "between",
            8 * LONG * D * D,
        )
        cross_att, cross_lse = attention_forward(
            (query, 0), (pairs, 0), (pairs, PAIRS), row_side, source_side, False, "cross_forward"
        )
    w_q, w_k, w_v, w_o, w_cq, w_ckv, w_co, w_fi, w_fo = weights
    vec_weight = (vec, (16, D), (0, 0))
    (output, activ, branch3, dpre, hidden2, dresid2, branch2, d_cross_att, sums_mid, bias_sum) = row_call(
        middle,
        256,
        [hidden1, cross_att, cotangent],
        [
            (w_co, square, (0, 0)),
            (w_fi, (D, FF), (0, 0)),
            (w_fo, (FF, D), (0, 0)),
            vec_weight,
            (bias, (1, FF), (0, 0)),
        ],
        [(D, BF16), (FF, BF16), (D, BF16), (FF, BF16), (D, BF16), (D, F32), (D, BF16), (D, BF16)],
        [(8, D), (1, FF)],
        "middle",
        36 * LONG * D * D,
    )
    if direct:
        pieces = results[:6]
        first = back_first_call(
            [row_side, source_side, vec],
            [activ, branch3, hidden2, dpre, query, pairs, cross_att, d_cross_att, cross_lse]
            + [dresid2, resid1, pieces[4], pieces[3], pieces[5]],
            rows,
        )
        dcq, dck, dcv, branch1, d_self_att, dresid1, encoded_grad, ffn_in_share, ffn_out_share, sums_cross = first
        second = back_second_call(
            [row_side, target_side, sums_mid, bias_sum, sums_cross],
            [self_att, cross_att, hidden1, encoded, branch1, branch2, dcq, dck, dcv]
            + [mixed, d_self_att, self_lse, tokens, dresid1, pieces[0], pieces[1], pieces[2]],
            rows,
        )
        tokens_grad, self_in_share, self_out_share, cross_q_share, cross_kv_share, cross_out_share = second[:6]
        self_b_share, cross_b_share, gain_share, shift_share, out_b_share, in_b_share = second[6:]
        return (
            output,
            tokens_grad,
            encoded_grad,
            self_in_share,
            self_b_share,
            self_out_share,
            cross_q_share,
            cross_kv_share,
            cross_b_share,
            cross_out_share,
            ffn_in_share,
            in_b_share.reshape(-1),
            ffn_out_share,
            out_b_share.reshape(-1),
            gain_share,
            shift_share,
        )

    ffn_out_grad, ffn_in_grad = ffn_grads_call(activ, branch3, hidden2, dpre)
    dcq, dck, dcv = attention_backward(
        (query, 0),
        (pairs, 0),
        (pairs, PAIRS),
        cross_att,
        d_cross_att,
        cross_lse,
        row_side,
        source_side,
        False,
        "cross_backward",
    )
    encoded_grad, dresid1, branch1, d_self_att, sums_cross = row_call(
        after_cross,
        512,
        [dcq, dck, dcv, dresid2, resid1],
        [(w_cq, square, (0, 0)), (w_ckv, (D, 2 * D), (0, 0)), (w_o, square, (0, 0)), vec_weight],
        [(D, BF16), (D, F32), (D, BF16), (D, BF16)],
        [(8, D)],
        "after_cross",
        8 * LONG * D * D,
    )
    cross_grad = pair_grads_call(
        [self_att, hidden1, encoded, encoded, cross_att],
        [branch1, dcq, dck, dcv, branch2],
        "cross_grads",
    )
    dq, dk, dv = attention_backward(
        (mixed, 0),
        (mixed, PAIRS),
        (mixed, 2 * PAIRS),
        self_att,
        d_self_att,
        self_lse,
        row_side,
        target_side,
        True,
        "self_backward",
    )
    self_grad = pair_grads_call([tokens] * 3, [dq, dk, dv], "self_grads")
    (tokens_grad,) = row_call(
        tokens_back,
        512,
        [dq, dk, dv, dresid1],
        [(w, square, (0, 0)) for w in weights[:3]],
        [(D, BF16)],
        [],
        "tokens_back",
        6 * LONG * D * D,
    )

    def share_of(grad):
        share = lax.psum_scatter(grad.astype(F32), "fsdp", scatter_dimension=0, tiled=True)
        return lax.psum(share, "dp")

    dq_sum = jnp.sum(dq.astype(F32), axis=0, keepdims=True)
    dv_sum = jnp.sum(dv.astype(F32), axis=0, keepdims=True)
    small_rows = jnp.concatenate(
        [
            dq_sum,
            dv_sum,
            sums_cross[2:5],
            sums_mid[4:5],
            sums_cross[0:1],
            sums_mid[0:2],
            sums_cross[1:2],
            sums_mid[2:4],
            sums_mid[5:6],
        ],
        axis=0,
    )
    packed = small_rows.reshape(IN_B, owners, rows).transpose(1, 0, 2).reshape(owners, IN_B * rows)
    packed = jnp.concatenate([packed, bias_sum.reshape(owners, 4 * rows)], axis=1)
    packed_share = share_of(packed).reshape(-1)
    self_share, cross_share, ffn_in_share, ffn_out_share = map(
        share_of, (self_grad, cross_grad, ffn_in_grad, ffn_out_grad)
    )

    def rows_of(first, count):
        return packed_share[first * rows : (first + count) * rows]

    return (
        output,
        tokens_grad,
        encoded_grad,
        self_share,
        rows_of(SELF_B, 3).reshape(3, rows),
        cross_share[:, :D],
        cross_share[:, D : 2 * D],
        cross_share[:, 2 * D : 4 * D],
        rows_of(CROSS_B, 3).reshape(3, rows),
        cross_share[:, 4 * D :],
        ffn_in_share,
        rows_of(IN_B, 4),
        ffn_out_share,
        rows_of(OUT_B, 1),
        rows_of(GAIN, 3).reshape(3, rows),
        rows_of(SHIFT, 3).reshape(3, rows),
    )


def solution(mesh):
    both = P(("dp", "fsdp"), None)
    rows, cols, flat = P("fsdp", None), P(None, "fsdp"), P("fsdp")
    return jax.shard_map(
        body,
        mesh=mesh,
        in_specs=(both, both, both, P(("dp", "fsdp")), both, both)
        + (rows, cols, rows, rows, rows, cols, rows, rows, flat, rows, flat, cols, cols),
        out_specs=(both, both, both)
        + (rows, cols, rows, rows, rows, cols, rows, rows, flat, rows, flat, cols, cols),
        check_vma=False,
    )
```

```python
from functools import partial

import jax
import jax.numpy as jnp
from jax import lax
from jax.experimental import pallas as pl
from jax.experimental.pallas import tpu as pltpu
from jax.sharding import PartitionSpec as P

D = 768
H = 12
HD = 64
FF = 3072
LONG = 1024
SEGS = 4
SHORT = 256
PAIRS = H // 2
WIDE = 2 * HD

EPS = 1e-05
NEG = -1e30
SCALE = HD ** (-0.5)
F32 = jnp.float32
BF16 = jnp.bfloat16
MESH_ID = pl.DeviceIdType.MESH
VMEM_LIMIT = 60 << 20

SELF_B, CROSS_B, GAIN, SHIFT, OUT_B, IN_B = 0, 3, 6, 9, 12, 13
VEC_ROWS = 17
PACK = 2048


def mm(left, right, left_dim=1, right_dim=0):
    return lax.dot_general(
        left, right, (((left_dim,), (right_dim,)), ((), ())), preferred_element_type=F32
    )


def params(**kwargs):
    return pltpu.CompilerParams(vmem_limit_bytes=VMEM_LIMIT, **kwargs)


def cost(flops, nbytes, trans=0):
    return pl.CostEstimate(flops=int(flops), bytes_accessed=int(nbytes), transcendentals=int(trans))


def any_spec():
    return pl.BlockSpec(memory_space=pl.ANY)


def whole(shape):
    return pl.BlockSpec(shape, lambda *_: (0,) * len(shape))


def normed(resid):
    centered = resid - jnp.mean(resid, axis=-1, keepdims=True)
    inv = lax.rsqrt(jnp.mean(centered * centered, axis=-1, keepdims=True) + EPS)
    return centered * inv, inv


def norm_back(xhat, inv, gain, grad):
    scaled = grad * gain
    first = jnp.mean(scaled, axis=-1, keepdims=True)
    second = jnp.mean(scaled * xhat, axis=-1, keepdims=True)
    return (scaled - first - xhat * second) * inv


def col_sum(values):
    return jnp.sum(values, axis=0, keepdims=True)


def my_place():
    dp, index = lax.axis_index("dp"), lax.axis_index("fsdp")
    return dp, index // 4, (index // 2) % 2, index % 2


def place(dp, z, y, core):
    return {"dp": dp, "fsdp": (z * 2 + y) * 2 + core}


def neighbours():
    x, z, y, c = my_place()
    return [place(x, (z + k) % 4, y, c) for k in (1, 2, 3)] + [
        place(1 - x, z, y, c),
        place(x, z, 1 - y, c),
        place(x, z, y, 1 - c),
    ]


def greet():
    barrier = pltpu.get_barrier_semaphore()
    others = neighbours()
    for other in others:
        pl.semaphore_signal(barrier, inc=1, device_id=other, device_id_type=MESH_ID)
    pl.semaphore_wait(barrier, len(others))


def remote(src, dst, sems, index, device):
    return pltpu.make_async_remote_copy(
        src_ref=src,
        dst_ref=dst,
        send_sem=sems.at[0, index],
        recv_sem=sems.at[1, index],
        device_id=device,
        device_id_type=MESH_ID,
    )


GATHER_COPIES = 11


def gather_copies(shard, full, sems, local_sem):
    x, z, y, c = my_place()
    half = shard.shape[-1] // 2
    mine = pl.ds(pl.multiple_of(x * half, 128), half)
    other = pl.ds(pl.multiple_of((1 - x) * half, 128), half)
    to_x, to_y, to_c = place(1 - x, z, y, c), place(x, z, 1 - y, c), place(x, z, y, 1 - c)

    def same(index, where, device):
        ref = full.at[where]
        return remote(ref, ref, sems, index, device)

    own = (slice(None), y, c, slice(None), mine)
    from_x = (slice(None), y, c, slice(None), other)
    from_y = (slice(None), 1 - y, c, slice(None), mine)
    diagonal = (slice(None), 1 - y, c, slice(None), other)
    copies = [
        remote(shard.at[:, mine], full.at[z, y, c, :, mine], sems, k - 1, place(x, (z + k) % 4, y, c))
        for k in (1, 2, 3)
    ]
    copies += [same(3, own, to_x), same(4, own, to_y)]
    copies += [
        same(5, (pl.ds(0, 2), 1 - y, c, slice(None), mine), to_x),
        same(6, (pl.ds(2, 2), y, c, slice(None), other), to_y),
    ]
    copies += [same(7, own, to_c), same(8, from_x, to_c), same(9, from_y, to_c), same(10, diagonal, to_c)]
    local = pltpu.make_async_copy(shard.at[:, mine], full.at[z, y, c, :, mine], local_sem)
    return copies, local


def gather_steps(shard, full, sems, local_sem):
    copies, local = gather_copies(shard, full, sems, local_sem)

    def first():
        local.start()
        for copy in copies[:3]:
            copy.start()

    def second():
        local.wait()
        for copy in copies[:3]:
            copy.wait_recv()
        for index in (3, 4, 7):
            copies[index].start()

    def third():
        copies[3].wait_recv()
        copies[4].wait_recv()
        for index in (5, 6, 8, 9):
            copies[index].start()

    def fourth():
        copies[5].wait_recv()
        copies[6].wait_recv()
        copies[10].start()

    def arrive():
        for index in (7, 8, 9, 10):
            copies[index].wait_recv()

    def last():
        for copy in copies:
            copy.wait_send()

    return [first, second, third, fourth, arrive, last]


COLUMN_COPIES = 3


def column_steps(shard, column, sems, local_sem):
    x, z, y, c = my_place()
    local = pltpu.make_async_copy(shard, column.at[z], local_sem)
    copies = [remote(shard, column.at[z], sems, k - 1, place(x, (z + k) % 4, y, c)) for k in (1, 2, 3)]

    def first():
        local.start()
        for copy in copies:
            copy.start()

    def last():
        local.wait()
        for copy in copies:
            copy.wait()

    return [first, last]


SPREAD_COPIES = 11


def spread_steps(column, full, sems, local_sem):
    x, z, y, c = my_place()
    half = full.shape[-1] // 2
    mine = pl.ds(pl.multiple_of(x * half, 128), half)
    other = pl.ds(pl.multiple_of((1 - x) * half, 128), half)
    to_x, to_y, to_c = place(1 - x, z, y, c), place(x, z, 1 - y, c), place(x, z, y, 1 - c)
    every = slice(None)
    local = pltpu.make_async_copy(column, full.at[:, y, c], local_sem)

    def same(index, where, device):
        ref = full.at[where]
        return remote(ref, ref, sems, index, device)

    over_y = [same(i, (i, y, c, every, mine), to_y) for i in range(4)]
    over_x = [same(4 + i, (i, 1 - y, c, every, mine), to_x) for i in range(4)]
    cores = [
        same(8, (every, y, c), to_c),
        same(9, (every, 1 - y, c, every, mine), to_c),
        same(10, (every, 1 - y, c, every, other), to_c),
    ]

    def load():
        local.start()

    def start():
        local.wait()
        for copy in over_y:
            copy.start()
        cores[0].start()

    def forward(index):
        def step():
            over_y[index].wait_recv()
            over_x[index].start()

        return step

    def pass_y():
        cores[1].start()

    def pass_x():
        for copy in over_x:
            copy.wait_recv()
        cores[2].start()

    def arrive():
        for copy in cores:
            copy.wait_recv()

    def last():
        for copy in over_y + over_x + cores:
            copy.wait_send()

    return [load, start] + [forward(i) for i in range(4)] + [pass_y, pass_x, arrive, last]


SMALL_COPIES = 5


def small_gather_steps(shard, full, sems, local_sem):
    x, z, y, c = my_place()
    local = pltpu.make_async_copy(shard, full.at[z, y, c], local_sem)
    copies = [
        remote(shard, full.at[z, y, c], sems, k - 1, place(x, (z + k) % 4, y, c)) for k in (1, 2, 3)
    ]
    copies.append(remote(full.at[:, y, c], full.at[:, y, c], sems, 3, place(x, z, 1 - y, c)))
    copies.append(remote(full.at[:, :, c], full.at[:, :, c], sems, 4, place(x, z, y, 1 - c)))

    def first():
        local.start()
        for copy in copies[:3]:
            copy.start()

    def second():
        local.wait()
        for copy in copies[:3]:
            copy.wait_recv()
        copies[3].start()

    def third():
        copies[3].wait_recv()
        copies[4].start()

    def fourth():
        copies[4].wait_recv()

    def last():
        for copy in copies:
            copy.wait_send()

    return [first, second, third, fourth, last]


def gather_shape(rows, cols):
    return (4, 2, 2, rows, cols)


SCATTER_COPIES = 9
SCATTER_REFS = 10


def scatter_scratch(rows, cols):
    half = cols // 2
    return [
        pltpu.VMEM((4, 2, 2, rows, cols), BF16),
        pltpu.VMEM((4, 2, rows, cols), BF16),
        pltpu.VMEM((2, 2, rows, half), BF16),
        pltpu.VMEM((2, rows, half), BF16),
        pltpu.VMEM((2, rows, cols), BF16),
        pltpu.VMEM((2, rows, half), BF16),
        pltpu.VMEM((4, rows, half), BF16),
        pltpu.VMEM((3, rows, half), BF16),
        pltpu.VMEM((2, rows, half), BF16),
        pltpu.SemaphoreType.DMA((2, SCATTER_COPIES)),
    ]


def add_into(dst, where, left, right):
    dst[where] = (left.astype(F32) + right.astype(F32)).astype(BF16)


def scatter_steps(share, bufs):
    grads, peer, x_one, x_two, y_one, y_two, quarter, z_in, halves, sems = bufs
    x, z, y, c = my_place()
    half = grads.shape[-1] // 2
    to_x, to_y, to_c = place(1 - x, z, y, c), place(x, z, 1 - y, c), place(x, z, y, 1 - c)
    mine = pl.ds(pl.multiple_of(x * half, 128), half)
    other = pl.ds(pl.multiple_of((1 - x) * half, 128), half)
    every = slice(None)
    low, high = pl.ds(0, 2), pl.ds(2, 2)
    swap = remote(grads.at[:, :, 1 - c], peer, sems, 0, to_c)
    x_first = remote(grads.at[low, :, c, :, other], x_one, sems, 1, to_x)
    y_first = remote(grads.at[high, 1 - y, c], y_one, sems, 2, to_y)
    x_second = remote(grads.at[high, y, c, :, other], x_two, sems, 3, to_x)
    y_second = remote(grads.at[low, 1 - y, c, :, mine], y_two, sems, 4, to_y)
    def start():
        swap.start()

    def sum_cores():
        swap.wait_recv()

        @pl.loop(0, 8)
        def _(i):
            where = (i // 2, i % 2, c)
            add_into(grads, where, grads[where], peer[i // 2, i % 2])

        x_first.start()
        y_first.start()

    def sum_first():
        x_first.wait_recv()
        y_first.wait_recv()

        @pl.loop(0, 2)
        def _(i):
            where = (i, 1 - y, c, every, mine)
            add_into(grads, where, grads[where], x_one[i, 1 - y])
            where = (2 + i, y, c, every, other)
            add_into(grads, where, grads[where], y_one[i, :, other])

        x_second.start()
        y_second.start()

        @pl.loop(0, 2)
        def _(i):
            add_into(quarter, i, grads[i, y, c, :, mine], x_one[i, y])
            add_into(quarter, 2 + i, grads[2 + i, y, c, :, mine], y_one[i, :, mine])

    def sum_second():
        x_second.wait_recv()
        y_second.wait_recv()

        @pl.loop(0, 2)
        def _(i):
            add_into(quarter, i, quarter[i], y_two[i])
            add_into(quarter, 2 + i, quarter[2 + i], x_two[i])

    def sent():
        for copy in (swap, x_first, y_first, x_second, y_second):
            copy.wait_send()

    tail = scatter_tail(share, quarter, z_in, halves, sems)
    last = tail[-1]

    def finish():
        sent()
        last()

    return [start, sum_cores, sum_first, sum_second] + tail[:-1] + [finish, sent]


def scatter_tail(share, quarter, z_in, halves, sems):
    x, z, y, c = my_place()
    z_sends = [
        remote(quarter.at[(z + k) % 4], z_in.at[k - 1], sems, 4 + k, place(x, (z + k) % 4, y, c))
        for k in (1, 2, 3)
    ]

    def send_z():
        for copy in z_sends:
            copy.start()

    def sum_z():
        for copy in z_sends:
            copy.wait_recv()
        total = quarter[z].astype(F32)
        for k in range(3):
            total = total + z_in[k].astype(F32)
        halves[0] = total.astype(BF16)
        for copy in z_sends:
            copy.wait_send()

    return [send_z, sum_z] + scatter_last(share, halves, sems)


def scatter_last(share, halves, sems):
    x, z, y, c = my_place()
    last_swap = remote(halves.at[0], halves.at[1], sems, 8, place(1 - x, z, y, c))

    def swap_x():
        last_swap.start()

    def finish():
        last_swap.wait()
        share[x] = halves[0]
        share[1 - x] = halves[1]

    return [swap_x, finish]


SMALL_SCATTER = 6
SMALL_REFS = 9
SMALL_TILE = (16, 256)


def small_scatter_scratch():
    return [
        pltpu.VMEM((4, 2, 2) + SMALL_TILE, F32),
        pltpu.VMEM((4, 2) + SMALL_TILE, F32),
        pltpu.VMEM((4, 2) + SMALL_TILE, F32),
        pltpu.VMEM((4,) + SMALL_TILE, F32),
        pltpu.VMEM((4,) + SMALL_TILE, F32),
        pltpu.VMEM((3,) + SMALL_TILE, F32),
        pltpu.VMEM(SMALL_TILE, F32),
        pltpu.VMEM(SMALL_TILE, F32),
        pltpu.SemaphoreType.DMA((2, SMALL_SCATTER)),
    ]


def small_scatter_steps(share, bufs):
    held, pair, peer, line, from_y, z_in, mine, other, sems = bufs
    x, z, y, c = my_place()
    swap = remote(held.at[:, :, 1 - c], peer, sems, 0, place(x, z, y, 1 - c))
    to_y = remote(pair.at[:, 1 - y], from_y, sems, 1, place(x, z, 1 - y, c))
    z_sends = [
        remote(line.at[(z + k) % 4], z_in.at[k - 1], sems, 1 + k, place(x, (z + k) % 4, y, c))
        for k in (1, 2, 3)
    ]
    to_x = remote(mine, other, sems, 5, place(1 - x, z, y, c))

    def start():
        swap.start()

    def sum_cores():
        swap.wait_recv()
        pair[...] = held[:, :, c] + peer[...]
        to_y.start()

    def sum_y():
        to_y.wait_recv()
        line[...] = pair[:, y] + from_y[...]
        for copy in z_sends:
            copy.start()

    def sum_z():
        for copy in z_sends:
            copy.wait_recv()
        mine[...] = line[z] + z_in[0] + z_in[1] + z_in[2]
        to_x.start()

    def finish():
        to_x.wait_recv()
        share[...] = mine[...] + other[...]
        for copy in [swap, to_y, to_x] + z_sends:
            copy.wait_send()

    return [start, sum_cores, sum_y, sum_z, finish]


def mask_lanes(kind, target_row, source_row):
    places = jnp.arange(LONG, dtype=jnp.int32)
    segment = jnp.where(kind == 1, 0, places // SHORT)
    offset = jnp.where(kind == 1, places, places % SHORT)
    lane = jnp.arange(WIDE, dtype=jnp.int32) % HD
    inside = segment[:, None] == lane[None, :]
    row_side = jnp.where(inside | (lane == SEGS)[None, :], 1.0, 0.0).astype(BF16)
    picker = segment[:, None] == jnp.arange(SEGS, dtype=jnp.int32)[None, :]

    def key_side(lengths):
        live = offset < jnp.sum(jnp.where(picker, lengths[None, :], 0), axis=1)
        blocked = ((lane < SEGS)[None, :] & ~inside) | ((lane == SEGS)[None, :] & ~live[:, None])
        ones = ((lane > SEGS) & (lane < SEGS + 4))[None, :]
        return jnp.where(blocked, NEG, jnp.where(ones, 1.0, 0.0)).astype(BF16)

    return row_side, key_side(target_row), key_side(source_row)


def lower(block, row_dim):
    rows = lax.broadcasted_iota(jnp.int32, (block, block), row_dim)
    cols = lax.broadcasted_iota(jnp.int32, (block, block), 1 - row_dim)
    return cols <= rows


def attend(causal, q_ref, k_ref, v_ref, row_ref, key_ref, att_ref, lse_ref):
    block, cuts = (512, 1) if causal else (LONG, 4)
    lane = lax.broadcasted_iota(jnp.int32, (1, WIDE), 1)
    feature = lax.broadcasted_iota(jnp.int32, (WIDE, 1), 0)
    vals_across = v_ref[...].T
    keys = [jnp.where(lane // HD == head, k_ref[...], key_ref[...]) for head in range(2)]
    vals = [jnp.where(feature // HD == head, vals_across, jnp.ones((), BF16)) for head in range(2)]
    items = [(head, index) for index in range(LONG // block) for head in range(2)]

    def reach_of(index):
        return (index + 1) * block if causal else LONG

    def score(item):
        head, index = item
        part, reach = pl.ds(index * block, block), reach_of(index)
        rows = jnp.where(lane // HD == head, q_ref[part, :], row_ref[part, :])
        scores = mm(keys[head][:reach], rows, 1, 1)
        if causal:
            edge = jnp.where(lower(block, 1), scores[reach - block :], NEG)
            scores = (
                edge
                if reach == block
                else jnp.concatenate([scores[: reach - block], edge], axis=0)
            )
        return scores, jnp.max(scores, axis=0, keepdims=True)

    def mix(item, scores, top):
        head, index = item
        step = reach_of(index) // cuts
        mixed = None
        for cut in range(cuts):
            part = slice(cut * step, (cut + 1) * step)
            term = mm(vals[head][:, part], jnp.exp(scores[part] - top).astype(BF16))
            mixed = term if mixed is None else mixed + term
        spare = HD * (1 - head)
        total = mixed[spare : spare + 1]
        return mixed[head * HD : (head + 1) * HD] / total, top + jnp.log(total)

    results = {}
    ready = score(items[0])
    for number, item in enumerate(items):
        upcoming = score(items[number + 1]) if number + 1 < len(items) else None
        results[item] = mix(item, *ready)
        ready = upcoming
    for index in range(LONG // block):
        part = pl.ds(index * block, block)
        (first, lse_first), (second, lse_second) = results[0, index], results[1, index]
        att_ref[part, :] = jnp.concatenate([first, second], axis=0).T.astype(BF16)
        lse_ref[0, 0:1, part] = lse_first
        lse_ref[0, 1:2, part] = lse_second


def pair_spec(offset):
    return pl.BlockSpec((LONG, WIDE), lambda i: (0, offset + i))


def lse_spec():
    return pl.BlockSpec((1, 8, LONG), lambda i: (i, 0, 0))


def attention_forward(query, keys, values, row_side, key_side, causal, name):
    return pl.pallas_call(
        partial(attend, causal),
        grid=(PAIRS,),
        in_specs=[pair_spec(query[1]), pair_spec(keys[1]), pair_spec(values[1])]
        + [whole((LONG, WIDE))] * 2,
        out_specs=[pair_spec(0), lse_spec()],
        out_shape=[
            jax.ShapeDtypeStruct((LONG, D), BF16),
            jax.ShapeDtypeStruct((PAIRS, 8, LONG), F32),
        ],
        compiler_params=params(),
        cost_estimate=cost(4 * LONG * LONG * D, 8 * LONG * D, H * LONG * LONG),
        name=name,
    )(query[0], keys[0], values[0], row_side, key_side)


def three_parts(value):
    high = value.astype(BF16)
    rest = value - high.astype(F32)
    middle = rest.astype(BF16)
    return high, middle, (rest - middle.astype(F32)).astype(BF16)


def attend_back(
    causal, q_ref, k_ref, v_ref, att_ref, grad_ref, lse_ref, row_ref, key_ref, dq_ref, dk_ref, dv_ref
):
    block = 256 if causal else 512
    blocks = LONG // block
    lane = lax.broadcasted_iota(jnp.int32, (1, WIDE), 1)
    product = att_ref[...].astype(F32) * grad_ref[...].astype(F32)
    q_across, grad_across = q_ref[...].T, grad_ref[...].T
    lse_down = lse_ref[0].T
    results = []
    for head in range(2):
        inside = lane // HD == head
        spare = HD * (1 - head)
        lse_parts = three_parts(-lse_down[:, head : head + 1])
        delta_parts = three_parts(
            -jnp.sum(jnp.where(inside, product, 0.0), axis=1, keepdims=True)
        )
        row_extra, grad_extra = row_ref[...], jnp.zeros((LONG, WIDE), BF16)
        for i in range(3):
            here = lane == spare + SEGS + 1 + i
            row_extra = jnp.where(here, lse_parts[i], row_extra)
            grad_extra = jnp.where(here, delta_parts[i], grad_extra)
        rows = jnp.where(inside, q_ref[...], row_extra)
        grads = jnp.where(inside, grad_ref[...], grad_extra)
        keys = jnp.where(inside, k_ref[...], key_ref[...])
        ones = (lane > spare + SEGS) & (lane < spare + SEGS + 4)
        vals = jnp.where(inside, v_ref[...], jnp.where(ones, 1.0, 0.0).astype(BF16))
        dq, dk, dv = [], [None] * blocks, [None] * blocks
        for index in range(blocks):
            part = slice(index * block, (index + 1) * block)
            reach = (index + 1) * block if causal else LONG
            scores = mm(rows[part], keys[:reach], 1, 1)
            if causal:
                edge = jnp.where(lower(block, 0), scores[:, reach - block :], NEG)
                scores = (
                    edge
                    if reach == block
                    else jnp.concatenate([scores[:, : reach - block], edge], axis=1)
                )
            probs = jnp.exp(scores)
            dscores = (probs * mm(grads[part], vals[:reach], 1, 1)).astype(BF16)
            dq.append(mm(dscores, keys[:reach]))
            dv_terms = mm(grad_across[:, part], probs.astype(BF16))
            dk_terms = mm(q_across[:, part], dscores)
            for other in range(reach // block):
                cols = slice(other * block, (other + 1) * block)
                for sums, terms in ((dk, dk_terms), (dv, dv_terms)):
                    term = terms[:, cols]
                    sums[other] = term if sums[other] is None else sums[other] + term
        results.append((dq, dk, dv))
    for index in range(blocks):
        part = pl.ds(index * block, block)
        both = jnp.where(lane < HD, results[0][0][index], results[1][0][index])
        dq_ref[part, :] = (both * SCALE).astype(BF16)
        for ref, member in ((dk_ref, 1), (dv_ref, 2)):
            both = [results[0][member][index][:HD], results[1][member][index][HD:]]
            ref[part, :] = jnp.concatenate(both, axis=0).T.astype(BF16)


def attention_backward(query, keys, values, att, grad, lse, row_side, key_side, causal, name):
    shape = jax.ShapeDtypeStruct((LONG, D), BF16)
    return pl.pallas_call(
        partial(attend_back, causal),
        grid=(PAIRS,),
        in_specs=[pair_spec(query[1]), pair_spec(keys[1]), pair_spec(values[1]), pair_spec(0), pair_spec(0)]
        + [lse_spec()]
        + [whole((LONG, WIDE))] * 2,
        out_specs=[pair_spec(0)] * 3,
        out_shape=[shape] * 3,
        compiler_params=params(),
        cost_estimate=cost(10 * LONG * LONG * D, 16 * LONG * D, H * LONG * LONG),
        name=name,
    )(query[0], keys[0], values[0], att, grad, lse, row_side, key_side)


def rows_spec(block, width):
    return pl.BlockSpec((block, width), lambda i: (i, 0))


def project_in(tokens_ref, q_w, k_w, v_w, vec_ref, out_ref):
    left = tokens_ref[...]
    out_ref[:, :D] = ((mm(left, q_w[...]) + vec_ref[SELF_B : SELF_B + 1]) * SCALE).astype(BF16)
    out_ref[:, D : 2 * D] = mm(left, k_w[...]).astype(BF16)
    out_ref[:, 2 * D :] = (mm(left, v_w[...]) + vec_ref[SELF_B + 1 : SELF_B + 2]).astype(BF16)


def between(
    tokens_ref, att_ref, encoded_ref, out_w, q_w, kv_w, vec_ref, resid_ref, hidden_ref, query_ref, pairs_ref
):
    pairs = mm(encoded_ref[...], kv_w[...])
    pairs_ref[:, :D] = pairs[:, :D].astype(BF16)
    pairs_ref[:, D:] = (pairs[:, D:] + vec_ref[CROSS_B + 1 : CROSS_B + 2]).astype(BF16)
    resid = tokens_ref[...].astype(F32) + mm(att_ref[...], out_w[...]) + vec_ref[SELF_B + 2 : SELF_B + 3]
    resid_ref[...] = resid
    xhat, _ = normed(resid)
    hidden = (xhat * vec_ref[GAIN : GAIN + 1] + vec_ref[SHIFT : SHIFT + 1]).astype(BF16)
    hidden_ref[...] = hidden
    query_ref[...] = ((mm(hidden, q_w[...]) + vec_ref[CROSS_B : CROSS_B + 1]) * SCALE).astype(BF16)


INV_SQRT2 = 0.7071067811865476
INV_SQRT_2PI = 0.3989422804014327


def middle(
    hidden1_ref,
    att_ref,
    cot_ref,
    cross_out,
    ffn_in,
    ffn_out,
    vec_ref,
    bias_ref,
    out_ref,
    activ_ref,
    branch3_ref,
    dpre_ref,
    hidden2_ref,
    dresid2_ref,
    branch2_ref,
    datt_ref,
    sums_ref,
    bias_sum_ref,
):
    def vec(row):
        return vec_ref[row : row + 1]

    resid2 = hidden1_ref[...].astype(F32) + mm(att_ref[...], cross_out[...]) + vec(CROSS_B + 2)
    xhat2, inv2 = normed(resid2)
    hidden2 = (xhat2 * vec(GAIN + 1) + vec(SHIFT + 1)).astype(BF16)
    hidden2_ref[...] = hidden2
    pre = mm(hidden2, ffn_in[...]) + bias_ref[...]
    phi = 0.5 + 0.5 * lax.erf(pre * INV_SQRT2)
    activ = (pre * phi).astype(BF16)
    slope = phi + pre * (INV_SQRT_2PI * jnp.exp(-0.5 * pre * pre))
    activ_ref[...] = activ
    resid3 = hidden2.astype(F32) + mm(activ, ffn_out[...]) + vec(OUT_B)
    xhat3, inv3 = normed(resid3)
    out_ref[...] = (xhat3 * vec(GAIN + 2) + vec(SHIFT + 2)).astype(BF16)
    cot = cot_ref[...].astype(F32)
    dresid3 = norm_back(xhat3, inv3, vec(GAIN + 2), cot)
    branch3 = dresid3.astype(BF16)
    branch3_ref[...] = branch3
    dpre = (mm(branch3, ffn_out[...], 1, 1) * slope).astype(BF16)
    dpre_ref[...] = dpre
    dhidden2 = dresid3 + mm(dpre, ffn_in[...], 1, 1)
    dresid2 = norm_back(xhat2, inv2, vec(GAIN + 1), dhidden2)
    dresid2_ref[...] = dresid2
    branch2 = dresid2.astype(BF16)
    branch2_ref[...] = branch2
    datt_ref[...] = mm(branch2, cross_out[...], 1, 1).astype(BF16)

    sums = jnp.concatenate(
        [
            col_sum(dhidden2 * xhat2),
            col_sum(cot * xhat3),
            col_sum(dhidden2),
            col_sum(cot),
            col_sum(branch2.astype(F32)),
            col_sum(branch3.astype(F32)),
            jnp.zeros((2, D), F32),
        ],
        axis=0,
    )
    bias_sum = col_sum(dpre.astype(F32))
    fresh = pl.program_id(0) == 0
    sums_ref[...] = jnp.where(fresh, sums, sums_ref[...] + sums)
    bias_sum_ref[...] = jnp.where(fresh, bias_sum, bias_sum_ref[...] + bias_sum)


def after_cross(
    dq_ref,
    dk_ref,
    dv_ref,
    dresid2_ref,
    resid1_ref,
    q_w,
    kv_w,
    out_w,
    vec_ref,
    encoded_grad_ref,
    dresid1_ref,
    branch1_ref,
    datt_ref,
    sums_ref,
):
    dq, dk, dv = dq_ref[...], dk_ref[...], dv_ref[...]
    encoded_grad_ref[...] = (mm(dk, kv_w[:, :D], 1, 1) + mm(dv, kv_w[:, D:], 1, 1)).astype(BF16)
    dhidden1 = dresid2_ref[...] + mm(dq, q_w[...], 1, 1)
    xhat, inv = normed(resid1_ref[...])
    dresid1 = norm_back(xhat, inv, vec_ref[GAIN : GAIN + 1], dhidden1)
    dresid1_ref[...] = dresid1
    branch1 = dresid1.astype(BF16)
    branch1_ref[...] = branch1
    datt_ref[...] = mm(branch1, out_w[...], 1, 1).astype(BF16)
    sums = jnp.concatenate(
        [
            col_sum(dhidden1 * xhat),
            col_sum(dhidden1),
            col_sum(branch1.astype(F32)),
            col_sum(dq.astype(F32)),
            col_sum(dv.astype(F32)),
            jnp.zeros((3, D), F32),
        ],
        axis=0,
    )
    sums_ref[...] = jnp.where(pl.program_id(0) == 0, sums, sums_ref[...] + sums)


def tokens_back(dq_ref, dk_ref, dv_ref, dresid1_ref, q_w, k_w, v_w, out_ref):
    total = dresid1_ref[...] + mm(dq_ref[...], q_w[...], 1, 1)
    total = total + mm(dk_ref[...], k_w[...], 1, 1)
    out_ref[...] = (total + mm(dv_ref[...], v_w[...], 1, 1)).astype(BF16)


def row_call(kernel, block, ins, weights, outs, sums, name, flops):
    in_specs = [rows_spec(block, a.shape[1]) for a in ins]
    for _, shape, index in weights:
        in_specs.append(pl.BlockSpec(shape, lambda i, index=index: index))
    out_specs = [rows_spec(block, width) for width, _ in outs] + [whole(s) for s in sums]
    out_shape = [jax.ShapeDtypeStruct((LONG, width), dtype) for width, dtype in outs]
    out_shape += [jax.ShapeDtypeStruct(s, F32) for s in sums]
    return pl.pallas_call(
        kernel,
        grid=(LONG // block,),
        in_specs=in_specs,
        out_specs=out_specs,
        out_shape=out_shape,
        compiler_params=params(),
        cost_estimate=cost(flops, flops / 500),
        name=name,
    )(*ins, *[w[0] for w in weights])


def write_masks(kind, target_row, source_row, row_ref, target_ref, source_ref):
    places = lax.broadcasted_iota(jnp.int32, (LONG, 1), 0)
    long = kind == 1
    segment = jnp.where(long, 0, lax.shift_right_logical(places, 8))
    offset = jnp.where(long, places, places & (SHORT - 1))
    lane = lax.broadcasted_iota(jnp.int32, (1, WIDE), 1) & (HD - 1)
    inside = segment == lane
    row_ref[...] = jnp.where(inside | (lane == SEGS), 1.0, 0.0).astype(BF16)
    ones = (lane > SEGS) & (lane < SEGS + 4)
    for ref, lengths in ((target_ref, target_row), (source_ref, source_row)):
        length = jnp.zeros((LONG, 1), jnp.int32)
        for index in range(SEGS):
            length = jnp.where(segment == index, lengths[index], length)
        dead = offset >= length
        blocked = ((lane < SEGS) & ~inside) | ((lane == SEGS) & dead)
        ref[...] = jnp.where(blocked, NEG, jnp.where(ones, 1.0, 0.0)).astype(BF16)


FORWARD_CHUNKS = 8
FORWARD_LOCAL = 32


def forward_kernel(*refs):
    (
        kind_ref, target_len, source_len,
        self_b, cross_b, gain, shift, out_b, in_b,
        tokens_hbm, encoded_hbm, self_in, self_out, cross_q, cross_kv, cross_out, ffn_in, ffn_out,
        w_q_out, w_k_out, w_v_out, w_o_out, w_cq_out, w_ckv_out, w_co_full, w_fi_full, fo_column,
        mixed_out, self_att_out, self_lse_out, resid_out, hidden_out, query_out, pairs_out,
        cross_att_out, cross_lse_out, row_out, target_out, source_out, vec_ref, bias_ref,
        w_q, w_k, w_v, w_o, w_cq, w_ckv,
        tokens, encoded, mixed, self_att, self_lse, resid, hidden, query, pairs,
        cross_att, cross_lse, row_side, target_side, source_side,
        pack, pack16, small_full,
        sems, small_sems, column_sems, chunk_local, local,
    ) = refs
    used = [0]

    def move(src, dst):
        copy = pltpu.make_async_copy(src, dst, local.at[used[0]])
        used[0] += 1
        copy.start()
        return copy

    load_tokens, load_encoded = move(tokens_hbm, tokens), move(encoded_hbm, encoded)
    rows = self_b.shape[1]
    pack[...] = jnp.zeros_like(pack)
    for start, ref in ((SELF_B, self_b), (CROSS_B, cross_b), (GAIN, gain), (SHIFT, shift), (OUT_B, out_b)):
        pack[start : start + ref.shape[0], :rows] = ref[...].astype(F32)
    pack[IN_B : IN_B + 1, : 4 * rows] = in_b[...].astype(F32)
    pack16[...] = pack[...].astype(BF16)

    greet()
    chunks = [
        (self_in.at[:, pl.ds(0, D)], w_q),
        (self_in.at[:, pl.ds(D, D)], w_k),
        (self_in.at[:, pl.ds(2 * D, D)], w_v),
        (self_out, w_o),
        (cross_q, w_cq),
        (cross_kv, w_ckv),
        (cross_out, w_co_full),
        (ffn_in, w_fi_full),
    ]
    plans = [
        gather_steps(shard, full, sems.at[:, pl.ds(i * GATHER_COPIES, GATHER_COPIES)], chunk_local.at[i])
        for i, (shard, full) in enumerate(chunks)
    ]
    small_plan = small_gather_steps(pack16, small_full, small_sems, chunk_local.at[FORWARD_CHUNKS])
    column_plan = column_steps(ffn_out, fo_column, column_sems, chunk_local.at[FORWARD_CHUNKS + 1])
    first_group, second_group, third_group, fourth_group = (0, 1, 2), (3, 4), (5,), (6, 7)

    def step(group, number):
        for index in group:
            plans[index][number]()

    def vec(row):
        return vec_ref[row : row + 1, :]

    def square(ref):
        return ref[...].reshape(D, ref.shape[-1])

    block = 512

    def project(weight, column, finish):
        @pl.loop(0, LONG // block)
        def _(i):
            part = pl.ds(pl.multiple_of(i * block, block), block)
            mixed[part, column * D : (column + 1) * D] = finish(mm(tokens[part, :], square(weight))).astype(BF16)

    small_plan[0]()
    step(first_group, 0)
    write_masks(
        kind_ref[0],
        [target_len[0, i] for i in range(SEGS)],
        [source_len[0, i] for i in range(SEGS)],
        row_side,
        target_side,
        source_side,
    )
    saves = [move(row_side, row_out), move(target_side, target_out), move(source_side, source_out)]
    small_plan[1]()
    step((0, 1), 1)
    step((0,), 2)
    step((2,), 1)
    step(second_group, 0)
    step(third_group, 0)
    small_plan[2]()
    step((1,), 2)
    step((0,), 3)
    small_plan[3]()
    for z in range(4):
        for y in range(2):
            for c in range(2):
                owner = (z * 2 + y) * 2 + c
                tile = small_full[z, y, c].astype(F32)
                vec_ref[:, owner * rows : (owner + 1) * rows] = tile[:, :rows]
                bias_ref[:, owner * 4 * rows : (owner + 1) * 4 * rows] = tile[IN_B : IN_B + 1, : 4 * rows]
    step((2,), 2)
    step((1,), 3)
    step((0,), 4)
    load_tokens.wait()
    project(w_q, 0, lambda value: (value + vec(SELF_B)) * SCALE)
    step((2,), 3)
    step((1,), 4)
    step(second_group, 1)
    step(fourth_group, 0)
    project(w_k, 1, lambda value: value)
    step((2,), 4)
    project(w_v, 2, lambda value: value + vec(SELF_B + 1))
    saves += [move(w_q, w_q_out), move(w_k, w_k_out), move(w_v, w_v_out)]
    step(second_group, 2)
    step(third_group, 1)
    saves.append(move(mixed, mixed_out))

    def ticks(index, table):
        for at, work in table.items():

            @pl.when(index == at)
            def _(work=work):
                for group, number in work:
                    step(group, number)

    @pl.loop(0, PAIRS)
    def _(pair):
        def cols(offset):
            return pl.ds(pl.multiple_of(offset + pair * WIDE, WIDE), WIDE)

        attend(
            True,
            mixed.at[:, cols(0)],
            mixed.at[:, cols(D)],
            mixed.at[:, cols(2 * D)],
            row_side,
            target_side,
            self_att.at[:, cols(0)],
            self_lse.at[pl.ds(pair, 1)],
        )
        ticks(
            pair,
            {
                1: [(second_group, 3)],
                4: [(third_group, 2)],
                5: [(fourth_group, 1)],
            },
        )

    saves += [move(self_att, self_att_out), move(self_lse, self_lse_out)]
    step(second_group, 4)
    column_plan[0]()
    saves += [move(w_o, w_o_out), move(w_cq, w_cq_out)]

    @pl.loop(0, LONG // block)
    def _(i):
        part = pl.ds(pl.multiple_of(i * block, block), block)
        total = tokens[part, :].astype(F32) + mm(self_att[part, :], square(w_o)) + vec(SELF_B + 2)
        resid[part, :] = total
        xhat, _ = normed(total)
        normal = (xhat * vec(GAIN) + vec(SHIFT)).astype(BF16)
        hidden[part, :] = normal
        query[part, :] = ((mm(normal, square(w_cq)) + vec(CROSS_B)) * SCALE).astype(BF16)

    saves += [move(resid, resid_out), move(hidden, hidden_out), move(query, query_out)]
    step(third_group, 3)
    step(third_group, 4)
    saves.append(move(w_ckv, w_ckv_out))
    load_encoded.wait()

    @pl.loop(0, LONG // block)
    def _(i):
        part = pl.ds(pl.multiple_of(i * block, block), block)
        both = mm(encoded[part, :], square(w_ckv))
        pairs[part, :D] = both[:, :D].astype(BF16)
        pairs[part, D:] = (both[:, D:] + vec(CROSS_B + 1)).astype(BF16)

    saves.append(move(pairs, pairs_out))

    @pl.loop(0, PAIRS)
    def _(pair):
        def cols(offset):
            return pl.ds(pl.multiple_of(offset + pair * WIDE, WIDE), WIDE)

        attend(
            False,
            query.at[:, cols(0)],
            pairs.at[:, cols(0)],
            pairs.at[:, cols(D)],
            row_side,
            source_side,
            cross_att.at[:, cols(0)],
            cross_lse.at[pl.ds(pair, 1)],
        )
        ticks(pair, {2: [(fourth_group, 2)]})

    saves += [move(cross_att, cross_att_out), move(cross_lse, cross_lse_out)]
    step(fourth_group, 3)
    step(fourth_group, 4)
    column_plan[1]()
    for plan in plans + [small_plan]:
        plan[-1]()
    for copy in saves:
        copy.wait()


def forward_call(ints, smalls, arrays):
    rows = smalls[0].shape[1]
    square = gather_shape(rows, D)
    lse = (PAIRS, 8, LONG)
    wide = (LONG, WIDE)

    def bf(*shape):
        return jax.ShapeDtypeStruct(shape, BF16)

    def f32(*shape):
        return jax.ShapeDtypeStruct(shape, F32)

    held = [bf(*square)] * 5 + [bf(*gather_shape(rows, 2 * D))]
    saved = [
        bf(LONG, 3 * D), bf(LONG, D), f32(*lse), f32(LONG, D), bf(LONG, D), bf(LONG, D), bf(LONG, 2 * D),
        bf(LONG, D), f32(*lse), bf(*wide), bf(*wide), bf(*wide),
    ]
    outs = held + [bf(*square), bf(*gather_shape(rows, FF)), bf(4, 4 * rows, D)]
    outs += saved + [f32(16, D), f32(1, FF)]
    in_vmem = pl.BlockSpec(memory_space=pltpu.VMEM)
    scratch = [pltpu.VMEM(s.shape, s.dtype) for s in held + [bf(LONG, D), bf(LONG, D)] + saved]
    scratch += [
        pltpu.VMEM((16, 256), F32),
        pltpu.VMEM((16, 256), BF16),
        pltpu.VMEM((4, 2, 2, 16, 256), BF16),
        pltpu.SemaphoreType.DMA((2, FORWARD_CHUNKS * GATHER_COPIES)),
        pltpu.SemaphoreType.DMA((2, SMALL_COPIES)),
        pltpu.SemaphoreType.DMA((2, COLUMN_COPIES)),
        pltpu.SemaphoreType.DMA((FORWARD_CHUNKS + 2,)),
        pltpu.SemaphoreType.DMA((FORWARD_LOCAL,)),
    ]
    return pl.pallas_call(
        forward_kernel,
        out_shape=outs,
        in_specs=[pl.BlockSpec(memory_space=pltpu.SMEM)] * len(ints)
        + [in_vmem] * len(smalls)
        + [any_spec()] * len(arrays),
        out_specs=[any_spec()] * (len(outs) - 2) + [in_vmem] * 2,
        scratch_shapes=scratch,
        compiler_params=params(collective_id=0, has_side_effects=True),
        cost_estimate=cost(14 * LONG * D * D + 8 * LONG * LONG * D, 60 << 20),
        name="gather_forward",
    )(*ints, *smalls, *arrays)


FFN_LOCAL = 32


def ffn_kernel(*refs):
    (
        vec_ref, bias_ref,
        hidden1_hbm, att_hbm, cot_hbm, w_co_hbm, w_fi_hbm, fo_column,
        activ_out, branch3_out, dpre_out, hidden2_out, dresid2_out, branch2_out, datt_out, output_out,
        sums_ref, bias_sum_ref,
        hidden1, att, cot, w_co, w_fi, w_fo, activ, slope, hidden2, resid, branch3,
        sems, local,
    ) = refs
    used = [1]

    def move(src, dst):
        copy = pltpu.make_async_copy(src, dst, local.at[used[0]])
        used[0] += 1
        copy.start()
        return copy

    plan = spread_steps(fo_column, w_fo, sems, local.at[0])
    plan[0]()
    loads = [move(w_co_hbm, w_co), move(att_hbm, att), move(hidden1_hbm, hidden1)]
    load_in, load_cot = move(w_fi_hbm, w_fi), move(cot_hbm, cot)
    greet()
    plan[1]()
    for copy in loads:
        copy.wait()

    def vec(row):
        return vec_ref[row : row + 1]

    def square(ref, width=D):
        return ref[...].reshape(-1, width)

    block, width = 512, D
    parts = [pl.ds(i * block, block) for i in range(LONG // block)]
    columns = [slice(i * width, (i + 1) * width) for i in range(FF // width)]
    saves = []
    w_in, w_out = (lambda: square(w_fi, FF)), (lambda: square(w_fo))
    ticks = [[], [plan[2]], [plan[3]], [], [], [plan[4]], [plan[5]], []]

    def before(part):
        total = hidden1[part, :].astype(F32) + mm(att[part, :], square(w_co)) + vec(CROSS_B + 2)
        resid[part, :] = total
        xhat, _ = normed(total)
        low = (xhat * vec(GAIN + 1) + vec(SHIFT + 1)).astype(BF16)
        hidden2[part, :] = low
        return low

    def activate(part, column, product):
        pre = product + bias_ref[:, column]
        phi = 0.5 + 0.5 * lax.erf(pre * INV_SQRT2)
        activ[part, column] = (pre * phi).astype(BF16)
        slope[part, column] = (phi + pre * (INV_SQRT_2PI * jnp.exp(-0.5 * pre * pre))).astype(BF16)

    number = 0
    lows = [before(part) for part in parts]
    load_in.wait()
    for part, low in zip(parts, lows):
        ready = mm(low, w_in()[:, columns[0]])
        for index, column in enumerate(columns):
            upcoming = mm(low, w_in()[:, columns[index + 1]]) if index + 1 < len(columns) else None
            activate(part, column, ready)
            ready = upcoming
            for work in ticks[number]:
                work()
            number += 1
    saves += [move(hidden2, hidden2_out), move(activ, activ_out)]
    plan[6]()
    plan[7]()
    load_cot.wait()
    plan[8]()

    sums = [None] * 6
    bias_sums = [None] * len(columns)

    def accumulate(store, index, value):
        store[index] = value if store[index] is None else store[index] + value

    for part in parts:
        low2 = hidden2[part, :]
        resid3 = low2.astype(F32) + mm(activ[part, :], w_out()) + vec(OUT_B)
        xhat3, inv3 = normed(resid3)
        grad = cot[part, :].astype(F32)
        cot[part, :] = (xhat3 * vec(GAIN + 2) + vec(SHIFT + 2)).astype(BF16)
        dresid3 = norm_back(xhat3, inv3, vec(GAIN + 2), grad)
        low3 = dresid3.astype(BF16)
        branch3[part, :] = low3
        saves += [move(cot.at[part], output_out.at[part]), move(branch3.at[part], branch3_out.at[part])]
        accumulate(sums, 1, col_sum(grad * xhat3))
        accumulate(sums, 3, col_sum(grad))
        accumulate(sums, 5, col_sum(low3.astype(F32)))
        dhidden2 = dresid3
        ready = mm(low3, w_out()[columns[0]], 1, 1)
        for index, column in enumerate(columns):
            upcoming = mm(low3, w_out()[columns[index + 1]], 1, 1) if index + 1 < len(columns) else None
            dpre = (ready * slope[part, column].astype(F32)).astype(BF16)
            slope[part, column] = dpre
            accumulate(bias_sums, index, col_sum(dpre.astype(F32)))
            dhidden2 = dhidden2 + mm(dpre, w_in()[:, column], 1, 1)
            ready = upcoming
        saves.append(move(slope.at[part], dpre_out.at[part]))
        xhat2, inv2 = normed(resid[part, :])
        dresid2 = norm_back(xhat2, inv2, vec(GAIN + 1), dhidden2)
        resid[part, :] = dresid2
        branch2 = dresid2.astype(BF16)
        hidden1[part, :] = branch2
        att[part, :] = mm(branch2, square(w_co), 1, 1).astype(BF16)
        saves += [
            move(resid.at[part], dresid2_out.at[part]),
            move(hidden1.at[part], branch2_out.at[part]),
            move(att.at[part], datt_out.at[part]),
        ]
        accumulate(sums, 0, col_sum(dhidden2 * xhat2))
        accumulate(sums, 2, col_sum(dhidden2))
        accumulate(sums, 4, col_sum(branch2.astype(F32)))

    sums_ref[...] = jnp.concatenate(sums + [jnp.zeros((2, D), F32)], axis=0)
    bias_sum_ref[...] = jnp.concatenate(bias_sums, axis=1)
    plan[9]()
    for copy in saves:
        copy.wait()


def ffn_call(vmem_arrays, hbm_arrays, rows):
    in_vmem = pl.BlockSpec(memory_space=pltpu.VMEM)

    def bf(*shape):
        return jax.ShapeDtypeStruct(shape, BF16)

    def f32(*shape):
        return jax.ShapeDtypeStruct(shape, F32)

    outs = [bf(LONG, FF), bf(LONG, D), bf(LONG, FF), bf(LONG, D), f32(LONG, D)] + [bf(LONG, D)] * 3
    outs += [f32(8, D), f32(1, FF)]
    held = [bf(LONG, D)] * 3 + [bf(*gather_shape(rows, D)), bf(*gather_shape(rows, FF))]
    held += [bf(*gather_shape(4 * rows, D)), bf(LONG, FF), bf(LONG, FF), bf(LONG, D), f32(LONG, D), bf(LONG, D)]
    return pl.pallas_call(
        ffn_kernel,
        out_shape=outs,
        in_specs=[in_vmem] * len(vmem_arrays) + [any_spec()] * len(hbm_arrays),
        out_specs=[any_spec()] * 8 + [in_vmem] * 2,
        scratch_shapes=[pltpu.VMEM(h.shape, h.dtype) for h in held]
        + [pltpu.SemaphoreType.DMA((2, SPREAD_COPIES)), pltpu.SemaphoreType.DMA((FFN_LOCAL,))],
        compiler_params=params(collective_id=3, has_side_effects=True),
        cost_estimate=cost(36 * LONG * D * D, 60 << 20),
        name="ffn_forward_backward",
    )(*vmem_arrays, *hbm_arrays)


def ffn_grads(activ_ref, branch3_ref, hidden2_ref, dpre_ref, out_grad_ref, in_grad_ref):
    out_grad_ref[...] = mm(activ_ref[...], branch3_ref[...], 0, 0).astype(BF16)
    in_grad_ref[...] = mm(hidden2_ref[...], dpre_ref[...], 0, 0).astype(BF16)


def ffn_grads_call(activ, branch3, hidden2, dpre):
    tile = 512
    return pl.pallas_call(
        ffn_grads,
        grid=(FF // tile,),
        in_specs=[
            pl.BlockSpec((LONG, tile), lambda i: (0, i)),
            whole((LONG, D)),
            whole((LONG, D)),
            pl.BlockSpec((LONG, tile), lambda i: (0, i)),
        ],
        out_specs=[
            pl.BlockSpec((tile, D), lambda i: (i, 0)),
            pl.BlockSpec((D, tile), lambda i: (0, i)),
        ],
        out_shape=[jax.ShapeDtypeStruct((FF, D), BF16), jax.ShapeDtypeStruct((D, FF), BF16)],
        compiler_params=params(),
        cost_estimate=cost(4 * LONG * D * FF, 8 * LONG * FF),
        name="ffn_grads",
    )(activ, branch3, hidden2, dpre)


def pair_grads(count, *refs):
    out_ref = refs[2 * count]
    for index in range(count):

        @pl.when(pl.program_id(0) == index)
        def _(index=index):
            out_ref[...] = mm(refs[index][...], refs[count + index][...], 0, 0).astype(BF16)


def pair_grads_call(lefts, rights, name):
    count = len(lefts)
    return pl.pallas_call(
        partial(pair_grads, count),
        grid=(count,),
        in_specs=[whole((LONG, D))] * (2 * count),
        out_specs=pl.BlockSpec((D, D), lambda i: (0, i)),
        out_shape=jax.ShapeDtypeStruct((D, D * count), BF16),
        compiler_params=params(),
        cost_estimate=cost(2 * LONG * D * D * count, 4 * LONG * D * count),
        name=name,
    )(*lefts, *rights)


def pair_fetcher(sources, lse, slots, lse_slots, sems):
    def copies(pair, slot):
        out = []
        for index, (ref, first) in enumerate(sources):
            cols = pl.ds(pl.multiple_of(first + pair * WIDE, WIDE), WIDE)
            out.append(
                pltpu.make_async_copy(ref.at[:, cols], slots.at[slot, index], sems.at[slot, index])
            )
        count = len(sources)
        out.append(pltpu.make_async_copy(lse.at[pair], lse_slots.at[slot, 0], sems.at[slot, count]))
        return out

    return copies


def pair_scratch():
    return [
        pltpu.VMEM((2, 5, LONG, WIDE), BF16),
        pltpu.VMEM((2, 1, 8, LONG), F32),
        pltpu.SemaphoreType.DMA((2, 6)),
    ]


def back_pairs(causal, fetch, slots, lse_slots, row_side, key_side, dq, dk, dv, after):
    @pl.loop(0, PAIRS)
    def _(pair):
        slot = pair % 2

        @pl.when(pair < PAIRS - 1)
        def _():
            for copy in fetch(pair + 1, 1 - slot):
                copy.start()

        for copy in fetch(pair, slot):
            copy.wait()

        def target(member):
            ref, first = member
            return ref.at[:, pl.ds(pl.multiple_of(first + pair * WIDE, WIDE), WIDE)]

        attend_back(
            causal,
            *[slots.at[slot, i] for i in range(5)],
            lse_slots.at[slot],
            row_side,
            key_side,
            target(dq),
            target(dk),
            target(dv),
        )
        for at, work in after.items():

            @pl.when(pair == at)
            def _(work=work):
                for member in work:
                    member()


FIRST_LOCAL = 24


def back_first_kernel(*refs):
    (
        row_side, source_side, vec_ref,
        activ_hbm, branch3_hbm, hidden2_hbm, dpre_hbm,
        query_hbm, pairs_hbm, cross_att_hbm, datt_hbm, lse_hbm,
        dresid2_hbm, resid1_hbm, w_cq_hbm, w_o_hbm,
        dcq_out, dck_out, dcv_out, branch1_out, self_datt_out, dresid1_out,
        in_quarter_out, out_quarter_out, sums_ref,
        activ, dpre, branch3, hidden2, dresid, resid, w_cq, w_o,
        slots, lse_slots, pair_sems,
        local, *scatter_bufs,
    ) = refs
    used = [0]

    def move(src, dst):
        copy = pltpu.make_async_copy(src, dst, local.at[used[0]])
        used[0] += 1
        copy.start()
        return copy

    quarters = [pl.ds(i * D, D) for i in range(FF // D)]
    load_branch3 = move(branch3_hbm, branch3)
    load_activ = [move(activ_hbm.at[:, q], activ.at[:, q]) for q in quarters]
    load_hidden2 = move(hidden2_hbm, hidden2)
    load_dpre = [move(dpre_hbm.at[:, q], dpre.at[:, q]) for q in quarters]
    greet()
    fetch = pair_fetcher(
        [(query_hbm, 0), (pairs_hbm, 0), (pairs_hbm, D), (cross_att_hbm, 0), (datt_hbm, 0)],
        lse_hbm,
        slots,
        lse_slots,
        pair_sems,
    )
    for copy in fetch(0, 0):
        copy.start()
    later = [
        move(dresid2_hbm, dresid),
        move(resid1_hbm, resid),
        move(w_cq_hbm, w_cq),
        move(w_o_hbm, w_o),
    ]
    out_bufs, in_bufs = scatter_bufs[:SCATTER_REFS], scatter_bufs[SCATTER_REFS:]
    out_plan, in_plan = scatter_steps(None, out_bufs), scatter_steps(None, in_bufs)
    out_rows = out_bufs[0].shape[3]
    tile = 2 * out_rows
    load_branch3.wait()
    for q in range(FF // D):
        load_activ[q].wait()
        for part in range(D // tile):
            index = q * (D // tile) + part
            left = activ[:, index * tile : (index + 1) * tile]
            grad = mm(left, branch3[...], 0, 0).astype(BF16)
            out_bufs[0][index // 2, index % 2] = grad.reshape(2, out_rows, D)
    out_plan[0]()
    load_hidden2.wait()
    in_rows = in_bufs[0].shape[3]
    for q in range(FF // D):
        load_dpre[q].wait()
        grad = mm(hidden2[...], dpre[:, quarters[q]], 0, 0).astype(BF16)
        in_bufs[0][:, :, :, :, quarters[q]] = grad.reshape(4, 2, 2, in_rows, D)
    out_plan[1]()
    in_plan[0]()
    back_pairs(
        False,
        fetch,
        slots,
        lse_slots,
        row_side,
        source_side,
        (activ, 0),
        (activ, D),
        (activ, 2 * D),
        {
            0: [in_plan[1]],
            3: [out_plan[2]],
            5: [out_plan[3], in_plan[2]],
        },
    )
    dcq, dck, dcv, branch1 = (activ.at[:, q] for q in quarters)
    self_datt = dpre.at[:, quarters[0]]
    saves = [move(dcq, dcq_out), move(dck, dck_out), move(dcv, dcv_out)]
    for copy in later:
        copy.wait()

    def square(ref):
        return ref[...].reshape(D, ref.shape[-1])

    block = 512
    sums_ref[...] = jnp.zeros_like(sums_ref)

    @pl.loop(0, LONG // block)
    def _(i):
        part = pl.ds(pl.multiple_of(i * block, block), block)
        left = dcq[part, :]
        dhidden = dresid[part, :] + mm(left, square(w_cq), 1, 1)
        xhat, inv = normed(resid[part, :])
        dresid1 = norm_back(xhat, inv, vec_ref[GAIN : GAIN + 1], dhidden)
        dresid[part, :] = dresid1
        low = dresid1.astype(BF16)
        branch1[part, :] = low
        self_datt[part, :] = mm(low, square(w_o), 1, 1).astype(BF16)
        sums_ref[0:1] += col_sum(dhidden * xhat)
        sums_ref[1:2] += col_sum(dhidden)
        sums_ref[2:3] += col_sum(low.astype(F32))
        sums_ref[3:4] += col_sum(left.astype(F32))
        sums_ref[4:5] += col_sum(dcv[part, :].astype(F32))

    saves += [move(branch1, branch1_out), move(self_datt, self_datt_out), move(dresid, dresid1_out)]
    saves.append(move(out_bufs[6], out_quarter_out))
    in_plan[3]()
    saves.append(move(in_bufs[6], in_quarter_out))
    in_plan[-1]()
    out_plan[-1]()
    for copy in saves:
        copy.wait()


def back_first_call(vmem_arrays, hbm_arrays, rows):
    in_vmem = pl.BlockSpec(memory_space=pltpu.VMEM)
    square = gather_shape(rows, D)

    def bf(*shape):
        return jax.ShapeDtypeStruct(shape, BF16)

    def f32(*shape):
        return jax.ShapeDtypeStruct(shape, F32)

    outs = [bf(LONG, D)] * 5 + [f32(LONG, D)]
    outs += [bf(4, rows, FF // 2), bf(4, 4 * rows, D // 2), f32(8, D)]
    held = [bf(LONG, FF)] * 2 + [bf(LONG, D)] * 2 + [f32(LONG, D)] * 2
    held += [bf(*square)] * 2
    scratch = [pltpu.VMEM(h.shape, h.dtype) for h in held] + pair_scratch()
    scratch += [pltpu.SemaphoreType.DMA((FIRST_LOCAL,))]
    scratch += scatter_scratch(4 * rows, D) + scatter_scratch(rows, FF)
    return pl.pallas_call(
        back_first_kernel,
        out_shape=outs,
        in_specs=[in_vmem] * len(vmem_arrays) + [any_spec()] * len(hbm_arrays),
        out_specs=[any_spec()] * 8 + [in_vmem],
        scratch_shapes=scratch,
        compiler_params=params(collective_id=1, has_side_effects=True),
        cost_estimate=cost(26 * LONG * D * D + 10 * LONG * LONG * D, 60 << 20),
        name="backward_cross_scatter_ffn",
    )(*vmem_arrays, *hbm_arrays)


SECOND_LOCAL = 32
SECOND_SHARES = 10
CROSS_PARTS = 5
SELF_PARTS = 3


def back_second_kernel(*refs):
    (
        row_side, target_side, sums_mid, bias_sum, sums_cross,
        self_att_hbm, cross_att_hbm, hidden1_hbm, encoded_hbm,
        branch1_hbm, branch2_hbm, dcq_hbm, dck_hbm, dcv_hbm,
        mixed_hbm, datt_hbm, lse_hbm, tokens_hbm, dresid1_hbm, w_q_hbm, w_k_hbm, w_v_hbm, w_ckv_hbm,
        in_quarter_hbm, out_quarter_hbm,
        tokens_grad_out, encoded_grad_out, *rest,
    ) = refs
    shares, small_share, rest = rest[:SECOND_SHARES], rest[SECOND_SHARES], rest[SECOND_SHARES + 1 :]
    (
        lefts, rights, tokens, dresid, w_q, w_k, w_v, w_ckv, vec_sums,
        slots, lse_slots, pair_sems,
        in_quarter, in_z, in_halves, in_sems, out_quarter, out_z, out_halves, out_sems,
        local, *scatter_bufs,
    ) = rest
    used = [0]

    def move(src, dst):
        copy = pltpu.make_async_copy(src, dst, local.at[used[0]])
        used[0] += 1
        copy.start()
        return copy

    left_sources = (self_att_hbm, cross_att_hbm, hidden1_hbm, encoded_hbm)
    right_sources = (branch1_hbm, branch2_hbm, dcq_hbm, dck_hbm, dcv_hbm)
    load_ffn = [move(in_quarter_hbm, in_quarter), move(out_quarter_hbm, out_quarter)]
    load_left, load_right = [], []
    for index, source in enumerate(right_sources):
        if index < len(left_sources):
            load_left.append(move(left_sources[index], lefts.at[index]))
        load_right.append(move(source, rights.at[index]))
    greet()
    fetch = pair_fetcher(
        [(mixed_hbm, 0), (mixed_hbm, D), (mixed_hbm, 2 * D), (self_att_hbm, 0), (datt_hbm, 0)],
        lse_hbm,
        slots,
        lse_slots,
        pair_sems,
    )
    for copy in fetch(0, 0):
        copy.start()
    load_tokens = move(tokens_hbm, tokens)
    later = [
        move(dresid1_hbm, dresid),
        move(w_q_hbm, w_q),
        move(w_k_hbm, w_k),
        move(w_v_hbm, w_v),
        move(w_ckv_hbm, w_ckv),
    ]

    def bufs(index):
        return scatter_bufs[index * SCATTER_REFS : (index + 1) * SCATTER_REFS]

    plans = [scatter_steps(shares[i], bufs(i)) for i in range(CROSS_PARTS + SELF_PARTS)]
    cross_plans, self_plans = plans[:CROSS_PARTS], plans[CROSS_PARTS:]
    in_plan = scatter_tail(shares[CROSS_PARTS + SELF_PARTS], in_quarter, in_z, in_halves, in_sems)
    out_plan = scatter_tail(shares[CROSS_PARTS + SELF_PARTS + 1], out_quarter, out_z, out_halves, out_sems)
    small_bufs = scatter_bufs[(CROSS_PARTS + SELF_PARTS) * SCATTER_REFS :]
    small_plan = small_scatter_steps(small_share, small_bufs)
    for copy in load_ffn:
        copy.wait()
    in_plan[0]()
    out_plan[0]()
    rows = bufs(0)[0].shape[3]
    for index in range(CROSS_PARTS):
        if index < len(load_left):
            load_left[index].wait()
        load_right[index].wait()
        left = lefts[min(index, len(left_sources) - 1)]
        grad = mm(left, rights[index], 0, 0).astype(BF16)
        bufs(index)[0][...] = grad.reshape(4, 2, 2, rows, D)
        cross_plans[index][0]()
        if index:
            cross_plans[index - 1][1]()
    load_tokens.wait()
    vec_sums[...] = jnp.zeros_like(vec_sums)
    dq, dk, dv = rights.at[0], rights.at[1], rights.at[2]

    def self_part(part):
        def work():
            cols = pl.ds(part * 256, 256)
            target = bufs(CROSS_PARTS + part)[0]
            left = tokens[...]
            ones = jnp.ones((8, LONG), BF16)
            for index, ref in enumerate((dq, dk, dv)):
                right = ref[:, cols]
                grad = mm(left, right, 0, 0).astype(BF16)
                target[:, :, :, :, index * 256 : (index + 1) * 256] = grad.reshape(4, 2, 2, rows, 256)
                if index != 1:
                    row = SELF_B + index // 2
                    vec_sums[row : row + 1, cols] = mm(ones, right)[0:1]
            self_plans[part][0]()

        return work

    def both(members, number):
        return [cross_plans[i][number] for i in members]

    back_pairs(
        True,
        fetch,
        slots,
        lse_slots,
        row_side,
        target_side,
        (dq, 0),
        (dk, 0),
        (dv, 0),
        {
            0: both((4,), 1),
            1: [self_part(0)] + both((0, 1, 2, 3), 2),
            2: [self_plans[0][1]] + both((4,), 2) + both((0, 1), 3) + both((0, 1), 4),
            3: [self_part(1), self_plans[0][2], in_plan[1], out_plan[1], in_plan[2], out_plan[2]]
            + both((2, 3, 4), 3)
            + both((2, 3, 4), 4),
            4: [self_plans[1][1], self_plans[0][3], self_plans[0][4]] + both((0, 1), 5) + both((0, 1), 6),
            5: [self_part(2), self_plans[1][2]]
            + both((2, 3, 4), 5)
            + both((2, 3, 4), 6)
            + both((0, 1), 7)
            + [self_plans[0][5], self_plans[0][6], in_plan[3], out_plan[3]],
        },
    )

    vec_sums[SELF_B + 2 : CROSS_B + 2] = sums_cross[2:5]
    vec_sums[CROSS_B + 2 : CROSS_B + 3] = sums_mid[4:5]
    vec_sums[GAIN : GAIN + 1] = sums_cross[0:1]
    vec_sums[GAIN + 1 : GAIN + 3] = sums_mid[0:2]
    vec_sums[SHIFT : SHIFT + 1] = sums_cross[1:2]
    vec_sums[SHIFT + 1 : SHIFT + 3] = sums_mid[2:4]
    vec_sums[OUT_B : OUT_B + 1] = sums_mid[5:6]
    held = small_bufs[0]
    held[...] = jnp.zeros_like(held)
    for owner in range(16):
        tile = held.at[owner // 4, (owner // 2) % 2, owner % 2]
        tile[:, :rows] = vec_sums[:, owner * rows : (owner + 1) * rows]
        tile[IN_B : IN_B + 1, : 4 * rows] = bias_sum[:, owner * 4 * rows : (owner + 1) * 4 * rows]
    small_plan[0]()
    for copy in later:
        copy.wait()

    def square(ref):
        return ref[...].reshape(D, D)

    block = 256

    def rows_back(index):
        part = pl.ds(index * block, block)
        total = dresid[part, :] + mm(dq[part, :], square(w_q), 1, 1)
        total = total + mm(dk[part, :], square(w_k), 1, 1)
        tokens[part, :] = (total + mm(dv[part, :], square(w_v), 1, 1)).astype(BF16)

    encoded_grad = lefts.at[0]

    def encoded_back(index):
        part = pl.ds(index * block, block)
        weight = w_ckv[...].reshape(D, 2 * D)
        total = mm(rights[CROSS_PARTS - 2, part, :], weight[:, :D], 1, 1)
        total = total + mm(rights[CROSS_PARTS - 1, part, :], weight[:, D:], 1, 1)
        encoded_grad[part, :] = total.astype(BF16)

    rows_back(0)
    self_plans[2][1]()
    small_plan[1]()
    self_plans[1][3]()
    self_plans[1][4]()
    rows_back(1)
    for index in (2, 3, 4):
        cross_plans[index][7]()
    rows_back(2)
    small_plan[2]()
    self_plans[2][2]()
    self_plans[0][7]()
    rows_back(3)
    save = [move(tokens, tokens_grad_out)]
    small_plan[3]()
    self_plans[1][5]()
    self_plans[1][6]()
    self_plans[2][3]()
    self_plans[2][4]()
    encoded_back(0)
    encoded_back(1)
    encoded_back(2)
    small_plan[4]()
    self_plans[1][7]()
    self_plans[2][5]()
    self_plans[2][6]()
    encoded_back(3)
    save.append(move(encoded_grad, encoded_grad_out))
    self_plans[2][7]()
    for copy in save:
        copy.wait()


def back_second_call(vmem_arrays, hbm_arrays, rows):
    in_vmem = pl.BlockSpec(memory_space=pltpu.VMEM)
    square = gather_shape(rows, D)

    def bf(*shape):
        return jax.ShapeDtypeStruct(shape, BF16)

    def f32(*shape):
        return jax.ShapeDtypeStruct(shape, F32)

    outs = [bf(LONG, D)] * 2 + [bf(2, rows, D // 2)] * (CROSS_PARTS + SELF_PARTS)
    outs += [bf(2, rows, FF // 2), bf(2, 4 * rows, D // 2), f32(*SMALL_TILE)]
    held = [bf(4, LONG, D), bf(5, LONG, D), bf(LONG, D), f32(LONG, D)] + [bf(*square)] * 3
    held += [bf(*gather_shape(rows, 2 * D)), f32(16, D)]
    scratch = [pltpu.VMEM(h.shape, h.dtype) for h in held] + pair_scratch()
    scratch += [
        pltpu.VMEM((4, rows, FF // 2), BF16),
        pltpu.VMEM((3, rows, FF // 2), BF16),
        pltpu.VMEM((2, rows, FF // 2), BF16),
        pltpu.SemaphoreType.DMA((2, SCATTER_COPIES)),
        pltpu.VMEM((4, 4 * rows, D // 2), BF16),
        pltpu.VMEM((3, 4 * rows, D // 2), BF16),
        pltpu.VMEM((2, 4 * rows, D // 2), BF16),
        pltpu.SemaphoreType.DMA((2, SCATTER_COPIES)),
        pltpu.SemaphoreType.DMA((SECOND_LOCAL,)),
    ]
    for _ in range(CROSS_PARTS + SELF_PARTS):
        scratch += scatter_scratch(rows, D)
    scratch += small_scatter_scratch()
    return pl.pallas_call(
        back_second_kernel,
        out_shape=outs,
        in_specs=[in_vmem] * len(vmem_arrays) + [any_spec()] * len(hbm_arrays),
        out_specs=[any_spec()] * 2 + [in_vmem] * (len(outs) - 2),
        scratch_shapes=scratch,
        compiler_params=params(collective_id=2, has_side_effects=True),
        cost_estimate=cost(22 * LONG * D * D + 10 * LONG * LONG * D, 60 << 20),
        name="backward_self_scatter_rest",
    )(*vmem_arrays, *hbm_arrays)


BIG = 3


def hand_out_kernel(*refs):
    big_in, shares = refs[:BIG], list(refs[BIG : BIG + 11])
    big_out, outs = refs[BIG + 11 : 2 * BIG + 11], refs[2 * BIG + 11 : 2 * BIG + 24]
    held, sems = refs[2 * BIG + 24 :]
    small = shares.pop()
    loads = [pltpu.make_async_copy(ref, held.at[i], sems.at[i]) for i, ref in enumerate(big_in)]
    copies = [pltpu.make_async_copy(held.at[i], ref, sems.at[BIG + i]) for i, ref in enumerate(big_out)]
    for load in loads:
        load.start()
    for load, copy in zip(loads, copies):
        load.wait()
        copy.start()
    self_in, self_b, self_out, cross_q, cross_kv, cross_b, cross_out, ffn_in, in_b, ffn_out, out_b, gain, shift = outs
    plain = [(self_out, 0, 0), (cross_out, 1, 0), (cross_q, 2, 0), (cross_kv, 3, 0), (cross_kv, 4, D)]
    plain += [(ffn_in, 8, 0), (ffn_out, 9, 0)]
    for ref, index, first in plain:
        half = shares[index].shape[2]
        for h in range(2):
            ref[:, first + h * half : first + (h + 1) * half] = shares[index][h].astype(F32)
    for part in range(SELF_PARTS):
        for at in range(6):
            first = (at // 2) * D + part * 256 + (at % 2) * 128
            piece = shares[CROSS_PARTS + part][at // 3, :, (at % 3) * 128 : (at % 3 + 1) * 128]
            self_in[:, first : first + 128] = piece.astype(F32)
    rows = self_b.shape[1]
    for start, ref in ((SELF_B, self_b), (CROSS_B, cross_b), (GAIN, gain), (SHIFT, shift), (OUT_B, out_b)):
        ref[...] = small[start : start + ref.shape[0], :rows]
    in_b[...] = small[IN_B : IN_B + 1, : 4 * rows]
    for copy in copies:
        copy.wait()


def hand_out_call(arrays, rows):
    in_vmem = pl.BlockSpec(memory_space=pltpu.VMEM)

    def f32(*shape):
        return jax.ShapeDtypeStruct(shape, F32)

    outs = [jax.ShapeDtypeStruct((LONG, D), BF16)] * BIG
    outs += [f32(rows, 3 * D), f32(3, rows), f32(rows, D), f32(rows, D), f32(rows, 2 * D), f32(3, rows)]
    outs += [f32(rows, D), f32(rows, FF), f32(1, 4 * rows), f32(4 * rows, D), f32(1, rows), f32(3, rows), f32(3, rows)]
    return pl.pallas_call(
        hand_out_kernel,
        out_shape=outs,
        in_specs=[any_spec()] * BIG + [in_vmem] * (len(arrays) - BIG),
        out_specs=[any_spec()] * BIG + [in_vmem] * (len(outs) - BIG),
        scratch_shapes=[pltpu.VMEM((BIG, LONG, D), BF16), pltpu.SemaphoreType.DMA((2 * BIG,))],
        compiler_params=params(),
        name="hand_out",
    )(*arrays)


def body(
    tokens,
    encoded,
    cotangent,
    bucket,
    target_len,
    source_len,
    self_in,
    self_bias,
    self_out,
    cross_q,
    cross_kv,
    cross_bias,
    cross_out,
    ffn_in,
    ffn_in_bias,
    ffn_out,
    ffn_out_bias,
    norm_gain,
    norm_shift,
):
    rows = self_in.shape[0]
    owners = D // rows
    direct = owners == 16
    square = (D, D)
    if direct:
        smalls = [self_bias, cross_bias, norm_gain, norm_shift]
        smalls += [ffn_out_bias.reshape(1, rows), ffn_in_bias.reshape(1, 4 * rows)]
        arrays = [tokens, encoded, self_in, self_out, cross_q, cross_kv, cross_out, ffn_in, ffn_out]
        results = forward_call([bucket, target_len, source_len], smalls, arrays)
        pieces = results[:9]
        (mixed, self_att, self_lse, resid1, hidden1, query, pairs, cross_att, cross_lse) = results[9:18]
        row_side, target_side, source_side, vec, bias = results[18:]
        (activ, branch3, dpre, hidden2, dresid2, branch2, d_cross_att, output, sums_mid, bias_sum) = ffn_call(
            [vec, bias], [hidden1, cross_att, cotangent, pieces[6], pieces[7], pieces[8]], rows
        )
        first = back_first_call(
            [row_side, source_side, vec],
            [activ, branch3, hidden2, dpre, query, pairs, cross_att, d_cross_att, cross_lse]
            + [dresid2, resid1, pieces[4], pieces[3]],
            rows,
        )
        dcq, dck, dcv, branch1, d_self_att, dresid1, in_quarter, out_half, sums_cross = first
        second = back_second_call(
            [row_side, target_side, sums_mid, bias_sum, sums_cross],
            [self_att, cross_att, hidden1, encoded, branch1, branch2, dcq, dck, dcv]
            + [mixed, d_self_att, self_lse, tokens, dresid1, pieces[0], pieces[1], pieces[2], pieces[5]]
            + [in_quarter, out_half],
            rows,
        )
        final = list(hand_out_call([output, *second], rows))
        final[11], final[13] = final[11].reshape(-1), final[13].reshape(-1)
        return tuple(final)

    else:
        everyone = partial(lax.all_gather, axis_name="fsdp", axis=0, tiled=True)
        self_w = everyone(self_in)
        weights = [self_w[:, i * D : (i + 1) * D] for i in range(3)]
        weights += [everyone(w) for w in (self_out, cross_q, cross_kv, cross_out, ffn_in, ffn_out)]
        small = [self_bias, cross_bias, norm_gain, norm_shift, ffn_out_bias, ffn_in_bias]
        small_all = everyone(jnp.concatenate([w.reshape(1, -1) for w in small], axis=1)).astype(F32)
        vec = small_all[:, : IN_B * rows].reshape(owners, IN_B, rows).transpose(1, 0, 2).reshape(IN_B, D)
        vec = jnp.pad(vec, ((0, 3), (0, 0)))
        bias = small_all[:, IN_B * rows : VEC_ROWS * rows].reshape(1, FF)
        row_side, target_side, source_side = mask_lanes(bucket[0], target_len[0], source_len[0])
        (mixed,) = row_call(
            project_in,
            512,
            [tokens],
            [(w, square, (0, 0)) for w in weights[:3]] + [(vec, (16, D), (0, 0))],
            [(3 * D, BF16)],
            [],
            "project_in",
            6 * LONG * D * D,
        )
        self_att, self_lse = attention_forward(
            (mixed, 0), (mixed, PAIRS), (mixed, 2 * PAIRS), row_side, target_side, True, "self_forward"
        )
        resid1, hidden1, query, pairs = row_call(
            between,
            512,
            [tokens, self_att, encoded],
            [(weights[3], square, (0, 0)), (weights[4], square, (0, 0)), (weights[5], (D, 2 * D), (0, 0))]
            + [(vec, (16, D), (0, 0))],
            [(D, F32), (D, BF16), (D, BF16), (2 * D, BF16)],
            [],
            "between",
            8 * LONG * D * D,
        )
        cross_att, cross_lse = attention_forward(
            (query, 0), (pairs, 0), (pairs, PAIRS), row_side, source_side, False, "cross_forward"
        )
    w_q, w_k, w_v, w_o, w_cq, w_ckv, w_co, w_fi, w_fo = weights
    vec_weight = (vec, (16, D), (0, 0))
    (output, activ, branch3, dpre, hidden2, dresid2, branch2, d_cross_att, sums_mid, bias_sum) = row_call(
        middle,
        256,
        [hidden1, cross_att, cotangent],
        [
            (w_co, square, (0, 0)),
            (w_fi, (D, FF), (0, 0)),
            (w_fo, (FF, D), (0, 0)),
            vec_weight,
            (bias, (1, FF), (0, 0)),
        ],
        [(D, BF16), (FF, BF16), (D, BF16), (FF, BF16), (D, BF16), (D, F32), (D, BF16), (D, BF16)],
        [(8, D), (1, FF)],
        "middle",
        36 * LONG * D * D,
    )
    ffn_out_grad, ffn_in_grad = ffn_grads_call(activ, branch3, hidden2, dpre)
    dcq, dck, dcv = attention_backward(
        (query, 0),
        (pairs, 0),
        (pairs, PAIRS),
        cross_att,
        d_cross_att,
        cross_lse,
        row_side,
        source_side,
        False,
        "cross_backward",
    )
    encoded_grad, dresid1, branch1, d_self_att, sums_cross = row_call(
        after_cross,
        512,
        [dcq, dck, dcv, dresid2, resid1],
        [(w_cq, square, (0, 0)), (w_ckv, (D, 2 * D), (0, 0)), (w_o, square, (0, 0)), vec_weight],
        [(D, BF16), (D, F32), (D, BF16), (D, BF16)],
        [(8, D)],
        "after_cross",
        8 * LONG * D * D,
    )
    cross_grad = pair_grads_call(
        [self_att, hidden1, encoded, encoded, cross_att],
        [branch1, dcq, dck, dcv, branch2],
        "cross_grads",
    )
    dq, dk, dv = attention_backward(
        (mixed, 0),
        (mixed, PAIRS),
        (mixed, 2 * PAIRS),
        self_att,
        d_self_att,
        self_lse,
        row_side,
        target_side,
        True,
        "self_backward",
    )
    self_grad = pair_grads_call([tokens] * 3, [dq, dk, dv], "self_grads")
    (tokens_grad,) = row_call(
        tokens_back,
        512,
        [dq, dk, dv, dresid1],
        [(w, square, (0, 0)) for w in weights[:3]],
        [(D, BF16)],
        [],
        "tokens_back",
        6 * LONG * D * D,
    )

    def share_of(grad):
        share = lax.psum_scatter(grad.astype(F32), "fsdp", scatter_dimension=0, tiled=True)
        return lax.psum(share, "dp")

    dq_sum = jnp.sum(dq.astype(F32), axis=0, keepdims=True)
    dv_sum = jnp.sum(dv.astype(F32), axis=0, keepdims=True)
    small_rows = jnp.concatenate(
        [
            dq_sum,
            dv_sum,
            sums_cross[2:5],
            sums_mid[4:5],
            sums_cross[0:1],
            sums_mid[0:2],
            sums_cross[1:2],
            sums_mid[2:4],
            sums_mid[5:6],
        ],
        axis=0,
    )
    packed = small_rows.reshape(IN_B, owners, rows).transpose(1, 0, 2).reshape(owners, IN_B * rows)
    packed = jnp.concatenate([packed, bias_sum.reshape(owners, 4 * rows)], axis=1)
    packed_share = share_of(packed).reshape(-1)
    self_share, cross_share, ffn_in_share, ffn_out_share = map(
        share_of, (self_grad, cross_grad, ffn_in_grad, ffn_out_grad)
    )

    def rows_of(first, count):
        return packed_share[first * rows : (first + count) * rows]

    return (
        output,
        tokens_grad,
        encoded_grad,
        self_share,
        rows_of(SELF_B, 3).reshape(3, rows),
        cross_share[:, :D],
        cross_share[:, D : 2 * D],
        cross_share[:, 2 * D : 4 * D],
        rows_of(CROSS_B, 3).reshape(3, rows),
        cross_share[:, 4 * D :],
        ffn_in_share,
        rows_of(IN_B, 4),
        ffn_out_share,
        rows_of(OUT_B, 1),
        rows_of(GAIN, 3).reshape(3, rows),
        rows_of(SHIFT, 3).reshape(3, rows),
    )


def solution(mesh):
    both = P(("dp", "fsdp"), None)
    rows, cols, flat = P("fsdp", None), P(None, "fsdp"), P("fsdp")
    return jax.shard_map(
        body,
        mesh=mesh,
        in_specs=(both, both, both, P(("dp", "fsdp")), both, both)
        + (rows, cols, rows, rows, rows, cols, rows, rows, flat, rows, flat, cols, cols),
        out_specs=(both, both, both)
        + (rows, cols, rows, rows, rows, cols, rows, rows, flat, rows, flat, cols, cols),
        check_vma=False,
    )
```

```python
from functools import partial

import jax
import jax.numpy as jnp
from jax import lax
from jax.experimental import pallas as pl
from jax.experimental.pallas import tpu as pltpu
from jax.sharding import PartitionSpec as P

D = 768
H = 12
HD = 64
FF = 3072
LONG = 1024
SEGS = 4
SHORT = 256
PAIRS = H // 2
WIDE = 2 * HD

EPS = 1e-05
NEG = -1e30
SCALE = HD ** (-0.5)
F32 = jnp.float32
BF16 = jnp.bfloat16
MESH_ID = pl.DeviceIdType.MESH
VMEM_LIMIT = 60 << 20

SELF_B, CROSS_B, GAIN, SHIFT, OUT_B, IN_B = 0, 3, 6, 9, 12, 13
VEC_ROWS = 17
PACK = 2048


def mm(left, right, left_dim=1, right_dim=0):
    return lax.dot_general(
        left, right, (((left_dim,), (right_dim,)), ((), ())), preferred_element_type=F32
    )


def params(**kwargs):
    return pltpu.CompilerParams(vmem_limit_bytes=VMEM_LIMIT, **kwargs)


def cost(flops, nbytes, trans=0):
    return pl.CostEstimate(flops=int(flops), bytes_accessed=int(nbytes), transcendentals=int(trans))


def any_spec():
    return pl.BlockSpec(memory_space=pl.ANY)


def whole(shape):
    return pl.BlockSpec(shape, lambda *_: (0,) * len(shape))


def normed(resid):
    centered = resid - jnp.mean(resid, axis=-1, keepdims=True)
    inv = lax.rsqrt(jnp.mean(centered * centered, axis=-1, keepdims=True) + EPS)
    return centered * inv, inv


def norm_back(xhat, inv, gain, grad):
    scaled = grad * gain
    first = jnp.mean(scaled, axis=-1, keepdims=True)
    second = jnp.mean(scaled * xhat, axis=-1, keepdims=True)
    return (scaled - first - xhat * second) * inv


def col_sum(values):
    return jnp.sum(values, axis=0, keepdims=True)


def my_place():
    dp, index = lax.axis_index("dp"), lax.axis_index("fsdp")
    return dp, index // 4, (index // 2) % 2, index % 2


def far_first(z):
    first, second = 3 - 2 * (z % 2), 1 + (z + 1) // 2
    return (first, second, 6 - first - second)


def place(dp, z, y, core):
    return {"dp": dp, "fsdp": (z * 2 + y) * 2 + core}


def neighbours():
    x, z, y, c = my_place()
    return [place(x, (z + k) % 4, y, c) for k in (1, 2, 3)] + [
        place(1 - x, z, y, c),
        place(x, z, 1 - y, c),
        place(x, z, y, 1 - c),
    ]


def greet():
    barrier = pltpu.get_barrier_semaphore()
    others = neighbours()
    for other in others:
        pl.semaphore_signal(barrier, inc=1, device_id=other, device_id_type=MESH_ID)
    pl.semaphore_wait(barrier, len(others))


def remote(src, dst, sems, index, device):
    return pltpu.make_async_remote_copy(
        src_ref=src,
        dst_ref=dst,
        send_sem=sems.at[0, index],
        recv_sem=sems.at[1, index],
        device_id=device,
        device_id_type=MESH_ID,
    )


GATHER_COPIES = 11


def gather_copies(shard, full, sems, local_sem):
    x, z, y, c = my_place()
    half = shard.shape[-1] // 2
    mine = pl.ds(pl.multiple_of(x * half, 128), half)
    other = pl.ds(pl.multiple_of((1 - x) * half, 128), half)
    to_x, to_y, to_c = place(1 - x, z, y, c), place(x, z, 1 - y, c), place(x, z, y, 1 - c)

    def same(index, where, device):
        ref = full.at[where]
        return remote(ref, ref, sems, index, device)

    own = (slice(None), y, c, slice(None), mine)
    from_x = (slice(None), y, c, slice(None), other)
    from_y = (slice(None), 1 - y, c, slice(None), mine)
    diagonal = (slice(None), 1 - y, c, slice(None), other)
    copies = [
        remote(shard.at[:, mine], full.at[z, y, c, :, mine], sems, k - 1, place(x, (z + k) % 4, y, c))
        for k in far_first(z)
    ]
    copies += [same(3, own, to_x), same(4, own, to_y)]
    copies += [
        same(5, (pl.ds(0, 2), 1 - y, c, slice(None), mine), to_x),
        same(6, (pl.ds(2, 2), y, c, slice(None), other), to_y),
    ]
    copies += [same(7, own, to_c), same(8, from_x, to_c), same(9, from_y, to_c), same(10, diagonal, to_c)]
    local = pltpu.make_async_copy(shard.at[:, mine], full.at[z, y, c, :, mine], local_sem)
    return copies, local


def gather_steps(shard, full, sems, local_sem):
    copies, local = gather_copies(shard, full, sems, local_sem)

    def first():
        local.start()
        for copy in copies[:3]:
            copy.start()

    def second():
        local.wait()
        for copy in copies[:3]:
            copy.wait_recv()
        for index in (3, 4, 7):
            copies[index].start()

    def third():
        copies[3].wait_recv()
        copies[4].wait_recv()
        for index in (5, 6, 8, 9):
            copies[index].start()

    def fourth():
        copies[5].wait_recv()
        copies[6].wait_recv()
        copies[10].start()

    def arrive():
        for index in (7, 8, 9, 10):
            copies[index].wait_recv()

    def last():
        for copy in copies:
            copy.wait_send()

    return [first, second, third, fourth, arrive, last]


SMALL_COPIES = 5


def small_gather_steps(shard, full, sems, local_sem):
    x, z, y, c = my_place()
    local = pltpu.make_async_copy(shard, full.at[z, y, c], local_sem)
    copies = [
        remote(shard, full.at[z, y, c], sems, k - 1, place(x, (z + k) % 4, y, c)) for k in far_first(z)
    ]
    copies.append(remote(full.at[:, y, c], full.at[:, y, c], sems, 3, place(x, z, 1 - y, c)))
    copies.append(remote(full.at[:, :, c], full.at[:, :, c], sems, 4, place(x, z, y, 1 - c)))

    def first():
        local.start()
        for copy in copies[:3]:
            copy.start()

    def second():
        local.wait()
        for copy in copies[:3]:
            copy.wait_recv()
        copies[3].start()

    def third():
        copies[3].wait_recv()
        copies[4].start()

    def fourth():
        copies[4].wait_recv()

    def last():
        for copy in copies:
            copy.wait_send()

    return [first, second, third, fourth, last]


def gather_shape(rows, cols):
    return (4, 2, 2, rows, cols)


SCATTER_COPIES = 9
SCATTER_REFS = 10


def scatter_scratch(rows, cols):
    half = cols // 2
    return [
        pltpu.VMEM((4, 2, 2, rows, cols), BF16),
        pltpu.VMEM((4, 2, rows, cols), BF16),
        pltpu.VMEM((2, 2, rows, half), BF16),
        pltpu.VMEM((2, rows, half), BF16),
        pltpu.VMEM((2, rows, cols), BF16),
        pltpu.VMEM((2, rows, half), BF16),
        pltpu.VMEM((4, rows, half), BF16),
        pltpu.VMEM((3, rows, half), BF16),
        pltpu.VMEM((2, rows, half), BF16),
        pltpu.SemaphoreType.DMA((2, SCATTER_COPIES)),
    ]


def add_into(dst, where, left, right):
    dst[where] = (left.astype(F32) + right.astype(F32)).astype(BF16)


def scatter_steps(share, bufs):
    grads, peer, x_one, x_two, y_one, y_two, quarter, z_in, halves, sems = bufs
    x, z, y, c = my_place()
    half = grads.shape[-1] // 2
    to_x, to_y, to_c = place(1 - x, z, y, c), place(x, z, 1 - y, c), place(x, z, y, 1 - c)
    mine = pl.ds(pl.multiple_of(x * half, 128), half)
    other = pl.ds(pl.multiple_of((1 - x) * half, 128), half)
    every = slice(None)
    low, high = pl.ds(0, 2), pl.ds(2, 2)
    swap = remote(grads.at[:, :, 1 - c], peer, sems, 0, to_c)
    x_first = remote(grads.at[low, :, c, :, other], x_one, sems, 1, to_x)
    y_first = remote(grads.at[high, 1 - y, c], y_one, sems, 2, to_y)
    x_second = remote(grads.at[high, y, c, :, other], x_two, sems, 3, to_x)
    y_second = remote(grads.at[low, 1 - y, c, :, mine], y_two, sems, 4, to_y)
    def start():
        swap.start()

    def sum_cores():
        swap.wait_recv()

        @pl.loop(0, 8)
        def _(i):
            where = (i // 2, i % 2, c)
            add_into(grads, where, grads[where], peer[i // 2, i % 2])

        x_first.start()
        y_first.start()

    def sum_first():
        x_first.wait_recv()
        y_first.wait_recv()

        @pl.loop(0, 2)
        def _(i):
            where = (i, 1 - y, c, every, mine)
            add_into(grads, where, grads[where], x_one[i, 1 - y])
            where = (2 + i, y, c, every, other)
            add_into(grads, where, grads[where], y_one[i, :, other])

        x_second.start()
        y_second.start()

        @pl.loop(0, 2)
        def _(i):
            add_into(quarter, i, grads[i, y, c, :, mine], x_one[i, y])
            add_into(quarter, 2 + i, grads[2 + i, y, c, :, mine], y_one[i, :, mine])

    def sum_second():
        x_second.wait_recv()
        y_second.wait_recv()

        @pl.loop(0, 2)
        def _(i):
            add_into(quarter, i, quarter[i], y_two[i])
            add_into(quarter, 2 + i, quarter[2 + i], x_two[i])

    def sent():
        for copy in (swap, x_first, y_first, x_second, y_second):
            copy.wait_send()

    tail = scatter_tail(share, quarter, z_in, halves, sems)
    last = tail[-1]

    def finish():
        sent()
        last()

    return [start, sum_cores, sum_first, sum_second] + tail[:-1] + [finish, sent]


def scatter_tail(share, quarter, z_in, halves, sems):
    x, z, y, c = my_place()
    z_sends = [
        remote(quarter.at[(z + k) % 4], z_in.at[k - 1], sems, 4 + k, place(x, (z + k) % 4, y, c))
        for k in far_first(z)
    ]

    def send_z():
        for copy in z_sends:
            copy.start()

    def sum_z():
        for copy in z_sends:
            copy.wait_recv()
        total = quarter[z].astype(F32)
        for k in range(3):
            total = total + z_in[k].astype(F32)
        halves[0] = total.astype(BF16)
        for copy in z_sends:
            copy.wait_send()

    return [send_z, sum_z] + scatter_last(share, halves, sems)


def scatter_last(share, halves, sems):
    x, z, y, c = my_place()
    last_swap = remote(halves.at[0], halves.at[1], sems, 8, place(1 - x, z, y, c))

    def swap_x():
        last_swap.start()

    def finish():
        last_swap.wait()
        share[x] = halves[0]
        share[1 - x] = halves[1]

    return [swap_x, finish]


SMALL_SCATTER = 6
SMALL_REFS = 9
SMALL_TILE = (16, 256)


def small_scatter_scratch():
    return [
        pltpu.VMEM((4, 2, 2) + SMALL_TILE, F32),
        pltpu.VMEM((4, 2) + SMALL_TILE, F32),
        pltpu.VMEM((4, 2) + SMALL_TILE, F32),
        pltpu.VMEM((4,) + SMALL_TILE, F32),
        pltpu.VMEM((4,) + SMALL_TILE, F32),
        pltpu.VMEM((3,) + SMALL_TILE, F32),
        pltpu.VMEM(SMALL_TILE, F32),
        pltpu.VMEM(SMALL_TILE, F32),
        pltpu.SemaphoreType.DMA((2, SMALL_SCATTER)),
    ]


def small_scatter_steps(share, bufs):
    held, pair, peer, line, from_y, z_in, mine, other, sems = bufs
    x, z, y, c = my_place()
    swap = remote(held.at[:, :, 1 - c], peer, sems, 0, place(x, z, y, 1 - c))
    to_y = remote(pair.at[:, 1 - y], from_y, sems, 1, place(x, z, 1 - y, c))
    z_sends = [
        remote(line.at[(z + k) % 4], z_in.at[k - 1], sems, 1 + k, place(x, (z + k) % 4, y, c))
        for k in far_first(z)
    ]
    to_x = remote(mine, other, sems, 5, place(1 - x, z, y, c))

    def start():
        swap.start()

    def sum_cores():
        swap.wait_recv()
        pair[...] = held[:, :, c] + peer[...]
        to_y.start()

    def sum_y():
        to_y.wait_recv()
        line[...] = pair[:, y] + from_y[...]
        for copy in z_sends:
            copy.start()

    def sum_z():
        for copy in z_sends:
            copy.wait_recv()
        mine[...] = line[z] + z_in[0] + z_in[1] + z_in[2]
        to_x.start()

    def finish():
        to_x.wait_recv()
        share[...] = mine[...] + other[...]
        for copy in [swap, to_y, to_x] + z_sends:
            copy.wait_send()

    return [start, sum_cores, sum_y, sum_z, finish]


def mask_lanes(kind, target_row, source_row):
    places = jnp.arange(LONG, dtype=jnp.int32)
    segment = jnp.where(kind == 1, 0, places // SHORT)
    offset = jnp.where(kind == 1, places, places % SHORT)
    lane = jnp.arange(WIDE, dtype=jnp.int32) % HD
    inside = segment[:, None] == lane[None, :]
    row_side = jnp.where(inside | (lane == SEGS)[None, :], 1.0, 0.0).astype(BF16)
    picker = segment[:, None] == jnp.arange(SEGS, dtype=jnp.int32)[None, :]

    def key_side(lengths):
        live = offset < jnp.sum(jnp.where(picker, lengths[None, :], 0), axis=1)
        blocked = ((lane < SEGS)[None, :] & ~inside) | ((lane == SEGS)[None, :] & ~live[:, None])
        ones = ((lane > SEGS) & (lane < SEGS + 4))[None, :]
        return jnp.where(blocked, NEG, jnp.where(ones, 1.0, 0.0)).astype(BF16)

    return row_side, key_side(target_row), key_side(source_row)


def lower(block, row_dim):
    rows = lax.broadcasted_iota(jnp.int32, (block, block), row_dim)
    cols = lax.broadcasted_iota(jnp.int32, (block, block), 1 - row_dim)
    return cols <= rows


def attend(causal, q_ref, k_ref, v_ref, row_ref, key_ref, att_ref, lse_ref):
    block, cuts = 512, 1 if causal else 2
    lane = lax.broadcasted_iota(jnp.int32, (1, WIDE), 1)
    feature = lax.broadcasted_iota(jnp.int32, (WIDE, 1), 0)
    vals_across = v_ref[...].T
    keys = [jnp.where(lane // HD == head, k_ref[...], key_ref[...]) for head in range(2)]
    vals = [jnp.where(feature // HD == head, vals_across, jnp.ones((), BF16)) for head in range(2)]
    items = [(head, index) for index in range(LONG // block) for head in range(2)]

    def reach_of(index):
        return (index + 1) * block if causal else LONG

    def score(item):
        head, index = item
        part, reach = pl.ds(index * block, block), reach_of(index)
        rows = jnp.where(lane // HD == head, q_ref[part, :], row_ref[part, :])
        scores = mm(keys[head][:reach], rows, 1, 1)
        if causal:
            edge = jnp.where(lower(block, 1), scores[reach - block :], NEG)
            scores = (
                edge
                if reach == block
                else jnp.concatenate([scores[: reach - block], edge], axis=0)
            )
        return scores, jnp.max(scores, axis=0, keepdims=True)

    def mix(item, scores, top):
        head, index = item
        step = reach_of(index) // cuts
        mixed = None
        for cut in range(cuts):
            part = slice(cut * step, (cut + 1) * step)
            term = mm(vals[head][:, part], jnp.exp(scores[part] - top).astype(BF16))
            mixed = term if mixed is None else mixed + term
        spare = HD * (1 - head)
        total = mixed[spare : spare + 1]
        return mixed[head * HD : (head + 1) * HD] / total, top + jnp.log(total)

    results = {}
    ready = score(items[0])
    for number, item in enumerate(items):
        upcoming = score(items[number + 1]) if number + 1 < len(items) else None
        results[item] = mix(item, *ready)
        ready = upcoming
    for index in range(LONG // block):
        part = pl.ds(index * block, block)
        (first, lse_first), (second, lse_second) = results[0, index], results[1, index]
        att_ref[part, :] = jnp.concatenate([first, second], axis=0).T.astype(BF16)
        lse_ref[0, 0:1, part] = lse_first
        lse_ref[0, 1:2, part] = lse_second


def pair_spec(offset):
    return pl.BlockSpec((LONG, WIDE), lambda i: (0, offset + i))


def lse_spec():
    return pl.BlockSpec((1, 8, LONG), lambda i: (i, 0, 0))


def attention_forward(query, keys, values, row_side, key_side, causal, name):
    return pl.pallas_call(
        partial(attend, causal),
        grid=(PAIRS,),
        in_specs=[pair_spec(query[1]), pair_spec(keys[1]), pair_spec(values[1])]
        + [whole((LONG, WIDE))] * 2,
        out_specs=[pair_spec(0), lse_spec()],
        out_shape=[
            jax.ShapeDtypeStruct((LONG, D), BF16),
            jax.ShapeDtypeStruct((PAIRS, 8, LONG), F32),
        ],
        compiler_params=params(),
        cost_estimate=cost(4 * LONG * LONG * D, 8 * LONG * D, H * LONG * LONG),
        name=name,
    )(query[0], keys[0], values[0], row_side, key_side)


def three_parts(value):
    high = value.astype(BF16)
    rest = value - high.astype(F32)
    middle = rest.astype(BF16)
    return high, middle, (rest - middle.astype(F32)).astype(BF16)


def attend_back(
    causal, q_ref, k_ref, v_ref, att_ref, grad_ref, lse_ref, row_ref, key_ref, dq_ref, dk_ref, dv_ref
):
    block = 256 if causal else 512
    blocks = LONG // block
    lane = lax.broadcasted_iota(jnp.int32, (1, WIDE), 1)
    product = att_ref[...].astype(F32) * grad_ref[...].astype(F32)
    q_across, grad_across = q_ref[...].T, grad_ref[...].T
    lse_down = lse_ref[0].T
    results = []
    for head in range(2):
        inside = lane // HD == head
        spare = HD * (1 - head)
        lse_parts = three_parts(-lse_down[:, head : head + 1])
        delta_parts = three_parts(
            -jnp.sum(jnp.where(inside, product, 0.0), axis=1, keepdims=True)
        )
        row_extra, grad_extra = row_ref[...], jnp.zeros((LONG, WIDE), BF16)
        for i in range(3):
            here = lane == spare + SEGS + 1 + i
            row_extra = jnp.where(here, lse_parts[i], row_extra)
            grad_extra = jnp.where(here, delta_parts[i], grad_extra)
        rows = jnp.where(inside, q_ref[...], row_extra)
        grads = jnp.where(inside, grad_ref[...], grad_extra)
        keys = jnp.where(inside, k_ref[...], key_ref[...])
        ones = (lane > spare + SEGS) & (lane < spare + SEGS + 4)
        vals = jnp.where(inside, v_ref[...], jnp.where(ones, 1.0, 0.0).astype(BF16))
        dq, dk, dv = [], [None] * blocks, [None] * blocks
        for index in range(blocks):
            part = slice(index * block, (index + 1) * block)
            reach = (index + 1) * block if causal else LONG
            scores = mm(rows[part], keys[:reach], 1, 1)
            if causal:
                edge = jnp.where(lower(block, 0), scores[:, reach - block :], NEG)
                scores = (
                    edge
                    if reach == block
                    else jnp.concatenate([scores[:, : reach - block], edge], axis=1)
                )
            probs = jnp.exp(scores)
            dscores = (probs * mm(grads[part], vals[:reach], 1, 1)).astype(BF16)
            dq.append(mm(dscores, keys[:reach]))
            dv_terms = mm(grad_across[:, part], probs.astype(BF16))
            dk_terms = mm(q_across[:, part], dscores)
            for other in range(reach // block):
                cols = slice(other * block, (other + 1) * block)
                for sums, terms in ((dk, dk_terms), (dv, dv_terms)):
                    term = terms[:, cols]
                    sums[other] = term if sums[other] is None else sums[other] + term
        results.append((dq, dk, dv))
    for index in range(blocks):
        part = pl.ds(index * block, block)
        both = jnp.where(lane < HD, results[0][0][index], results[1][0][index])
        dq_ref[part, :] = (both * SCALE).astype(BF16)
        for ref, member in ((dk_ref, 1), (dv_ref, 2)):
            both = [results[0][member][index][:HD], results[1][member][index][HD:]]
            ref[part, :] = jnp.concatenate(both, axis=0).T.astype(BF16)


def attention_backward(query, keys, values, att, grad, lse, row_side, key_side, causal, name):
    shape = jax.ShapeDtypeStruct((LONG, D), BF16)
    return pl.pallas_call(
        partial(attend_back, causal),
        grid=(PAIRS,),
        in_specs=[pair_spec(query[1]), pair_spec(keys[1]), pair_spec(values[1]), pair_spec(0), pair_spec(0)]
        + [lse_spec()]
        + [whole((LONG, WIDE))] * 2,
        out_specs=[pair_spec(0)] * 3,
        out_shape=[shape] * 3,
        compiler_params=params(),
        cost_estimate=cost(10 * LONG * LONG * D, 16 * LONG * D, H * LONG * LONG),
        name=name,
    )(query[0], keys[0], values[0], att, grad, lse, row_side, key_side)


def rows_spec(block, width):
    return pl.BlockSpec((block, width), lambda i: (i, 0))


def project_in(tokens_ref, q_w, k_w, v_w, vec_ref, out_ref):
    left = tokens_ref[...]
    out_ref[:, :D] = ((mm(left, q_w[...]) + vec_ref[SELF_B : SELF_B + 1]) * SCALE).astype(BF16)
    out_ref[:, D : 2 * D] = mm(left, k_w[...]).astype(BF16)
    out_ref[:, 2 * D :] = (mm(left, v_w[...]) + vec_ref[SELF_B + 1 : SELF_B + 2]).astype(BF16)


def between(
    tokens_ref, att_ref, encoded_ref, out_w, q_w, kv_w, vec_ref, resid_ref, hidden_ref, query_ref, pairs_ref
):
    pairs = mm(encoded_ref[...], kv_w[...])
    pairs_ref[:, :D] = pairs[:, :D].astype(BF16)
    pairs_ref[:, D:] = (pairs[:, D:] + vec_ref[CROSS_B + 1 : CROSS_B + 2]).astype(BF16)
    resid = tokens_ref[...].astype(F32) + mm(att_ref[...], out_w[...]) + vec_ref[SELF_B + 2 : SELF_B + 3]
    resid_ref[...] = resid
    xhat, _ = normed(resid)
    hidden = (xhat * vec_ref[GAIN : GAIN + 1] + vec_ref[SHIFT : SHIFT + 1]).astype(BF16)
    hidden_ref[...] = hidden
    query_ref[...] = ((mm(hidden, q_w[...]) + vec_ref[CROSS_B : CROSS_B + 1]) * SCALE).astype(BF16)


INV_SQRT2 = 0.7071067811865476
INV_SQRT_2PI = 0.3989422804014327


def middle(
    hidden1_ref,
    att_ref,
    cot_ref,
    cross_out,
    ffn_in,
    ffn_out,
    vec_ref,
    bias_ref,
    out_ref,
    activ_ref,
    branch3_ref,
    dpre_ref,
    hidden2_ref,
    dresid2_ref,
    branch2_ref,
    datt_ref,
    sums_ref,
    bias_sum_ref,
):
    def vec(row):
        return vec_ref[row : row + 1]

    resid2 = hidden1_ref[...].astype(F32) + mm(att_ref[...], cross_out[...]) + vec(CROSS_B + 2)
    xhat2, inv2 = normed(resid2)
    hidden2 = (xhat2 * vec(GAIN + 1) + vec(SHIFT + 1)).astype(BF16)
    hidden2_ref[...] = hidden2
    pre = mm(hidden2, ffn_in[...]) + bias_ref[...]
    phi = 0.5 + 0.5 * lax.erf(pre * INV_SQRT2)
    activ = (pre * phi).astype(BF16)
    slope = phi + pre * (INV_SQRT_2PI * jnp.exp(-0.5 * pre * pre))
    activ_ref[...] = activ
    resid3 = hidden2.astype(F32) + mm(activ, ffn_out[...]) + vec(OUT_B)
    xhat3, inv3 = normed(resid3)
    out_ref[...] = (xhat3 * vec(GAIN + 2) + vec(SHIFT + 2)).astype(BF16)
    cot = cot_ref[...].astype(F32)
    dresid3 = norm_back(xhat3, inv3, vec(GAIN + 2), cot)
    branch3 = dresid3.astype(BF16)
    branch3_ref[...] = branch3
    dpre = (mm(branch3, ffn_out[...], 1, 1) * slope).astype(BF16)
    dpre_ref[...] = dpre
    dhidden2 = dresid3 + mm(dpre, ffn_in[...], 1, 1)
    dresid2 = norm_back(xhat2, inv2, vec(GAIN + 1), dhidden2)
    dresid2_ref[...] = dresid2
    branch2 = dresid2.astype(BF16)
    branch2_ref[...] = branch2
    datt_ref[...] = mm(branch2, cross_out[...], 1, 1).astype(BF16)

    sums = jnp.concatenate(
        [
            col_sum(dhidden2 * xhat2),
            col_sum(cot * xhat3),
            col_sum(dhidden2),
            col_sum(cot),
            col_sum(branch2.astype(F32)),
            col_sum(branch3.astype(F32)),
            jnp.zeros((2, D), F32),
        ],
        axis=0,
    )
    bias_sum = col_sum(dpre.astype(F32))
    fresh = pl.program_id(0) == 0
    sums_ref[...] = jnp.where(fresh, sums, sums_ref[...] + sums)
    bias_sum_ref[...] = jnp.where(fresh, bias_sum, bias_sum_ref[...] + bias_sum)


def after_cross(
    dq_ref,
    dk_ref,
    dv_ref,
    dresid2_ref,
    resid1_ref,
    q_w,
    kv_w,
    out_w,
    vec_ref,
    encoded_grad_ref,
    dresid1_ref,
    branch1_ref,
    datt_ref,
    sums_ref,
):
    dq, dk, dv = dq_ref[...], dk_ref[...], dv_ref[...]
    encoded_grad_ref[...] = (mm(dk, kv_w[:, :D], 1, 1) + mm(dv, kv_w[:, D:], 1, 1)).astype(BF16)
    dhidden1 = dresid2_ref[...] + mm(dq, q_w[...], 1, 1)
    xhat, inv = normed(resid1_ref[...])
    dresid1 = norm_back(xhat, inv, vec_ref[GAIN : GAIN + 1], dhidden1)
    dresid1_ref[...] = dresid1
    branch1 = dresid1.astype(BF16)
    branch1_ref[...] = branch1
    datt_ref[...] = mm(branch1, out_w[...], 1, 1).astype(BF16)
    sums = jnp.concatenate(
        [
            col_sum(dhidden1 * xhat),
            col_sum(dhidden1),
            col_sum(branch1.astype(F32)),
            col_sum(dq.astype(F32)),
            col_sum(dv.astype(F32)),
            jnp.zeros((3, D), F32),
        ],
        axis=0,
    )
    sums_ref[...] = jnp.where(pl.program_id(0) == 0, sums, sums_ref[...] + sums)


def tokens_back(dq_ref, dk_ref, dv_ref, dresid1_ref, q_w, k_w, v_w, out_ref):
    total = dresid1_ref[...] + mm(dq_ref[...], q_w[...], 1, 1)
    total = total + mm(dk_ref[...], k_w[...], 1, 1)
    out_ref[...] = (total + mm(dv_ref[...], v_w[...], 1, 1)).astype(BF16)


def row_call(kernel, block, ins, weights, outs, sums, name, flops):
    in_specs = [rows_spec(block, a.shape[1]) for a in ins]
    for _, shape, index in weights:
        in_specs.append(pl.BlockSpec(shape, lambda i, index=index: index))
    out_specs = [rows_spec(block, width) for width, _ in outs] + [whole(s) for s in sums]
    out_shape = [jax.ShapeDtypeStruct((LONG, width), dtype) for width, dtype in outs]
    out_shape += [jax.ShapeDtypeStruct(s, F32) for s in sums]
    return pl.pallas_call(
        kernel,
        grid=(LONG // block,),
        in_specs=in_specs,
        out_specs=out_specs,
        out_shape=out_shape,
        compiler_params=params(),
        cost_estimate=cost(flops, flops / 500),
        name=name,
    )(*ins, *[w[0] for w in weights])


def write_masks(kind, target_row, source_row, row_ref, target_ref, source_ref):
    places = lax.broadcasted_iota(jnp.int32, (LONG, 1), 0)
    long = kind == 1
    segment = jnp.where(long, 0, lax.shift_right_logical(places, 8))
    offset = jnp.where(long, places, places & (SHORT - 1))
    lane = lax.broadcasted_iota(jnp.int32, (1, WIDE), 1) & (HD - 1)
    inside = segment == lane
    row_ref[...] = jnp.where(inside | (lane == SEGS), 1.0, 0.0).astype(BF16)
    ones = (lane > SEGS) & (lane < SEGS + 4)
    for ref, lengths in ((target_ref, target_row), (source_ref, source_row)):
        length = jnp.zeros((LONG, 1), jnp.int32)
        for index in range(SEGS):
            length = jnp.where(segment == index, lengths[index], length)
        dead = offset >= length
        blocked = ((lane < SEGS) & ~inside) | ((lane == SEGS) & dead)
        ref[...] = jnp.where(blocked, NEG, jnp.where(ones, 1.0, 0.0)).astype(BF16)


FORWARD_CHUNKS = 11
FORWARD_LOCAL = 64


def forward_kernel(*refs):
    (
        kind_ref, target_len, source_len,
        self_b, cross_b, gain, shift, out_b, in_b,
        tokens_hbm, encoded_hbm, cot_hbm,
        self_in, self_out, cross_q, cross_kv, cross_out, ffn_in, ffn_out,
        w_q_out, w_k_out, w_v_out, w_o_out, w_cq_out, w_ckv_out,
        mixed_out, self_att_out, self_lse_out, resid_out, hidden_out, query_out, pairs_out,
        cross_att_out, cross_lse_out, row_out, target_out, source_out,
        activ_out, branch3_out, dpre_out, hidden2_out, dresid2_out, branch2_out, datt_out, output_out,
        vec_ref, sums_ref, bias_sum_ref,
        w_q, w_k, w_v, w_o, w_cq, w_ckv, w_co, w_fi, w_fo,
        wide, deep, tokens, self_att, resid, hidden, cross_att,
        self_lse, cross_lse, row_side, target_side, source_side,
        bias_ref, pack, pack16, small_full,
        sems, small_sems, chunk_local, local,
    ) = refs
    mixed, branch3 = wide, wide.at[:, pl.ds(0, D)]
    pairs, query, encoded = deep.at[:, pl.ds(0, 2 * D)], deep.at[:, pl.ds(2 * D, D)], deep.at[:, pl.ds(3 * D, D)]
    used = [0]

    def move(src, dst):
        copy = pltpu.make_async_copy(src, dst, local.at[used[0]])
        used[0] += 1
        copy.start()
        return copy

    load_tokens, load_encoded = move(tokens_hbm, tokens), move(encoded_hbm, encoded)
    rows = self_b.shape[1]
    pack[...] = jnp.zeros_like(pack)
    for start, ref in ((SELF_B, self_b), (CROSS_B, cross_b), (GAIN, gain), (SHIFT, shift), (OUT_B, out_b)):
        pack[start : start + ref.shape[0], :rows] = ref[...].astype(F32)
    pack[IN_B : IN_B + 1, : 4 * rows] = in_b[...].astype(F32)
    pack16[...] = pack[...].astype(BF16)

    greet()
    chunks = [
        (self_in.at[:, pl.ds(0, D)], w_q),
        (self_in.at[:, pl.ds(D, D)], w_k),
        (self_in.at[:, pl.ds(2 * D, D)], w_v),
        (self_out, w_o),
        (cross_q, w_cq),
        (cross_kv, w_ckv),
        (cross_out, w_co),
        (ffn_in.at[:, pl.ds(0, FF // 2)], w_fi.at[:, :, :, :, pl.ds(0, FF // 2)]),
        (ffn_in.at[:, pl.ds(FF // 2, FF // 2)], w_fi.at[:, :, :, :, pl.ds(FF // 2, FF // 2)]),
        (ffn_out.at[pl.ds(0, 2 * rows)], w_fo.at[:, :, :, pl.ds(0, 2 * rows)]),
        (ffn_out.at[pl.ds(2 * rows, 2 * rows)], w_fo.at[:, :, :, pl.ds(2 * rows, 2 * rows)]),
    ]
    def chunk_sems(index):
        return sems.at[:, pl.ds(index * GATHER_COPIES, GATHER_COPIES)], chunk_local.at[index]

    plans = [gather_steps(shard, full, *chunk_sems(i)) for i, (shard, full) in enumerate(chunks)]
    small_plan = small_gather_steps(pack16, small_full, small_sems, chunk_local.at[FORWARD_CHUNKS])
    first_group, second_group, third_group, fourth_group, fifth_group = (0, 1, 2), (3, 4), (5,), (6, 7), (8,)

    def step(group, number):
        for index in group:
            plans[index][number]()

    def vec(row):
        return vec_ref[row : row + 1, :]

    def square(ref):
        return ref[...].reshape(-1, ref.shape[-1])

    block = 512

    def project(weight, column, finish):
        @pl.loop(0, LONG // block)
        def _(i):
            part = pl.ds(pl.multiple_of(i * block, block), block)
            mixed[part, column * D : (column + 1) * D] = finish(mm(tokens[part, :], square(weight))).astype(BF16)

    small_plan[0]()
    step(first_group, 0)
    write_masks(
        kind_ref[0],
        [target_len[0, i] for i in range(SEGS)],
        [source_len[0, i] for i in range(SEGS)],
        row_side,
        target_side,
        source_side,
    )
    saves = [move(row_side, row_out), move(target_side, target_out), move(source_side, source_out)]
    small_plan[1]()
    step((0, 1), 1)
    step((0,), 2)
    step((2,), 1)
    step(second_group, 0)
    step(third_group, 0)
    small_plan[2]()
    step((1,), 2)
    step((0,), 3)
    small_plan[3]()
    for z in range(4):
        for y in range(2):
            for c in range(2):
                owner = (z * 2 + y) * 2 + c
                tile = small_full[z, y, c].astype(F32)
                vec_ref[:, owner * rows : (owner + 1) * rows] = tile[:, :rows]
                bias_ref[:, owner * 4 * rows : (owner + 1) * 4 * rows] = tile[IN_B : IN_B + 1, : 4 * rows]
    step((2,), 2)
    step((1,), 3)
    step((0,), 4)
    load_tokens.wait()
    project(w_q, 0, lambda value: (value + vec(SELF_B)) * SCALE)
    step((2,), 3)
    step((1,), 4)
    step(second_group, 1)
    step(fourth_group, 0)
    project(w_k, 1, lambda value: value)
    step((2,), 4)
    project(w_v, 2, lambda value: value + vec(SELF_B + 1))
    saves += [move(w_q, w_q_out), move(w_k, w_k_out), move(w_v, w_v_out)]
    save_mixed = move(mixed.at[:, pl.ds(0, 3 * D)], mixed_out)
    step(third_group, 1)
    step(fifth_group, 0)

    def ticks(index, table):
        for at, work in table.items():

            @pl.when(index == at)
            def _(work=work):
                for group, number in work:
                    step(group, number)

    @pl.loop(0, PAIRS)
    def _(pair):
        def cols(offset):
            return pl.ds(pl.multiple_of(offset + pair * WIDE, WIDE), WIDE)

        attend(
            True,
            mixed.at[:, cols(0)],
            mixed.at[:, cols(D)],
            mixed.at[:, cols(2 * D)],
            row_side,
            target_side,
            self_att.at[:, cols(0)],
            self_lse.at[pl.ds(pair, 1)],
        )
        ticks(
            pair,
            {
                3: [(second_group, 2)],
                5: [(third_group, 2), (second_group, 3), (fourth_group, 1)],
            },
        )

    save_self = move(self_att, self_att_out)
    saves.append(move(self_lse, self_lse_out))
    step((9,), 0)
    step(second_group, 4)
    saves += [move(w_o, w_o_out), move(w_cq, w_cq_out)]

    @pl.loop(0, LONG // block)
    def _(i):
        part = pl.ds(pl.multiple_of(i * block, block), block)
        total = tokens[part, :].astype(F32) + mm(self_att[part, :], square(w_o)) + vec(SELF_B + 2)
        resid[part, :] = total
        xhat, _ = normed(total)
        normal = (xhat * vec(GAIN) + vec(SHIFT)).astype(BF16)
        hidden[part, :] = normal
        query[part, :] = ((mm(normal, square(w_cq)) + vec(CROSS_B)) * SCALE).astype(BF16)

    save_later = [move(resid, resid_out), move(hidden, hidden_out), move(query, query_out)]
    step(third_group, 3)
    step(fifth_group, 1)
    step((10,), 0)
    step(third_group, 4)
    saves.append(move(w_ckv, w_ckv_out))
    load_encoded.wait()

    @pl.loop(0, LONG // block)
    def _(i):
        part = pl.ds(pl.multiple_of(i * block, block), block)
        both = mm(encoded[part, :], square(w_ckv))
        pairs[part, :D] = both[:, :D].astype(BF16)
        pairs[part, D:] = (both[:, D:] + vec(CROSS_B + 1)).astype(BF16)

    save_later.append(move(pairs, pairs_out))
    save_self.wait()
    load_cot = move(cot_hbm, self_att)

    @pl.loop(0, PAIRS)
    def _(pair):
        def cols(offset):
            return pl.ds(pl.multiple_of(offset + pair * WIDE, WIDE), WIDE)

        attend(
            False,
            query.at[:, cols(0)],
            pairs.at[:, cols(0)],
            pairs.at[:, cols(D)],
            row_side,
            source_side,
            cross_att.at[:, cols(0)],
            cross_lse.at[pl.ds(pair, 1)],
        )
        ticks(
            pair,
            {
                1: [(fourth_group, 2)],
                3: [(fifth_group, 2), ((9,), 1)],
                4: [(fourth_group, 3)],
                5: [(fifth_group, 3)],
            },
        )

    saves.append(move(cross_lse, cross_lse_out))
    save_later.append(move(cross_att, cross_att_out))
    step(fourth_group, 4)
    save_mixed.wait()
    for copy in save_later:
        copy.wait()

    width = D
    parts = [pl.ds(i * block, block) for i in range(LONG // block)]
    columns = [slice(i * width, (i + 1) * width) for i in range(FF // width)]
    w_in, w_out = (lambda: square(w_fi)), (lambda: square(w_fo))
    work = [
        [((10,), 1)], [], [((9,), 2)], [], [((9,), 3)], [((10,), 2)], [], [((10,), 3)],
    ]

    def before(part):
        total = hidden[part, :].astype(F32) + mm(cross_att[part, :], square(w_co)) + vec(CROSS_B + 2)
        resid[part, :] = total
        xhat, _ = normed(total)
        low = (xhat * vec(GAIN + 1) + vec(SHIFT + 1)).astype(BF16)
        tokens[part, :] = low
        return low

    def activate(part, column, product):
        pre = product + bias_ref[:, column]
        phi = 0.5 + 0.5 * lax.erf(pre * INV_SQRT2)
        wide[part, column] = (pre * phi).astype(BF16)
        deep[part, column] = (phi + pre * (INV_SQRT_2PI * jnp.exp(-0.5 * pre * pre))).astype(BF16)

    number = 0
    lows = [before(part) for part in parts]
    step(fifth_group, 4)
    for part, low in zip(parts, lows):
        ready = mm(low, w_in()[:, columns[0]])
        for index, column in enumerate(columns):
            upcoming = mm(low, w_in()[:, columns[index + 1]]) if index + 1 < len(columns) else None
            activate(part, column, ready)
            ready = upcoming
            for group, stage in work[number]:
                step(group, stage)
            number += 1
    saves.append(move(tokens, hidden2_out))
    save_activ = move(wide, activ_out)
    load_cot.wait()
    step((9, 10), 4)

    sums = [None] * 6
    bias_sums = [None] * len(columns)

    def accumulate(store, index, value):
        store[index] = value if store[index] is None else store[index] + value

    for part in parts:
        low2 = tokens[part, :]
        resid3 = low2.astype(F32) + mm(wide[part, :], w_out()) + vec(OUT_B)
        xhat3, inv3 = normed(resid3)
        grad = self_att[part, :].astype(F32)
        self_att[part, :] = (xhat3 * vec(GAIN + 2) + vec(SHIFT + 2)).astype(BF16)
        dresid3 = norm_back(xhat3, inv3, vec(GAIN + 2), grad)
        low3 = dresid3.astype(BF16)
        if part is parts[0]:
            save_activ.wait()
        branch3[part, :] = low3
        saves += [move(self_att.at[part], output_out.at[part]), move(branch3.at[part], branch3_out.at[part])]
        accumulate(sums, 1, col_sum(grad * xhat3))
        accumulate(sums, 3, col_sum(grad))
        accumulate(sums, 5, col_sum(low3.astype(F32)))
        dhidden2 = dresid3
        ready = mm(low3, w_out()[columns[0]], 1, 1)
        for index, column in enumerate(columns):
            upcoming = mm(low3, w_out()[columns[index + 1]], 1, 1) if index + 1 < len(columns) else None
            dpre = (ready * deep[part, column].astype(F32)).astype(BF16)
            deep[part, column] = dpre
            accumulate(bias_sums, index, col_sum(dpre.astype(F32)))
            dhidden2 = dhidden2 + mm(dpre, w_in()[:, column], 1, 1)
            ready = upcoming
        saves.append(move(deep.at[part], dpre_out.at[part]))
        xhat2, inv2 = normed(resid[part, :])
        dresid2 = norm_back(xhat2, inv2, vec(GAIN + 1), dhidden2)
        resid[part, :] = dresid2
        branch2 = dresid2.astype(BF16)
        hidden[part, :] = branch2
        cross_att[part, :] = mm(branch2, square(w_co), 1, 1).astype(BF16)
        saves += [
            move(resid.at[part], dresid2_out.at[part]),
            move(hidden.at[part], branch2_out.at[part]),
            move(cross_att.at[part], datt_out.at[part]),
        ]
        accumulate(sums, 0, col_sum(dhidden2 * xhat2))
        accumulate(sums, 2, col_sum(dhidden2))
        accumulate(sums, 4, col_sum(branch2.astype(F32)))

    sums_ref[...] = jnp.concatenate(sums + [jnp.zeros((2, D), F32)], axis=0)
    bias_sum_ref[...] = jnp.concatenate(bias_sums, axis=1)
    for plan in plans + [small_plan]:
        plan[-1]()
    for copy in saves:
        copy.wait()


def forward_call(ints, smalls, arrays):
    rows = smalls[0].shape[1]
    square = gather_shape(rows, D)
    lse = (PAIRS, 8, LONG)
    wide = (LONG, WIDE)

    def bf(*shape):
        return jax.ShapeDtypeStruct(shape, BF16)

    def f32(*shape):
        return jax.ShapeDtypeStruct(shape, F32)

    held = [bf(*square)] * 5 + [bf(*gather_shape(rows, 2 * D))]
    saved = [
        bf(LONG, 3 * D), bf(LONG, D), f32(*lse), f32(LONG, D), bf(LONG, D), bf(LONG, D), bf(LONG, 2 * D),
        bf(LONG, D), f32(*lse), bf(*wide), bf(*wide), bf(*wide),
        bf(LONG, FF), bf(LONG, D), bf(LONG, FF), bf(LONG, D), f32(LONG, D), bf(LONG, D), bf(LONG, D), bf(LONG, D),
    ]
    outs = held + saved + [f32(16, D), f32(8, D), f32(1, FF)]
    kept = held + [bf(*square), bf(*gather_shape(rows, FF)), bf(*gather_shape(4 * rows, D))]
    kept += [bf(LONG, FF)] * 2 + [bf(LONG, D)] * 2 + [f32(LONG, D)] + [bf(LONG, D)] * 2
    kept += [f32(*lse)] * 2 + [bf(*wide)] * 3 + [f32(1, FF)]
    in_vmem = pl.BlockSpec(memory_space=pltpu.VMEM)
    scratch = [pltpu.VMEM(s.shape, s.dtype) for s in kept]
    scratch += [
        pltpu.VMEM((16, 256), F32),
        pltpu.VMEM((16, 256), BF16),
        pltpu.VMEM((4, 2, 2, 16, 256), BF16),
        pltpu.SemaphoreType.DMA((2, FORWARD_CHUNKS * GATHER_COPIES)),
        pltpu.SemaphoreType.DMA((2, SMALL_COPIES)),
        pltpu.SemaphoreType.DMA((FORWARD_CHUNKS + 1,)),
        pltpu.SemaphoreType.DMA((FORWARD_LOCAL,)),
    ]
    return pl.pallas_call(
        forward_kernel,
        out_shape=outs,
        in_specs=[pl.BlockSpec(memory_space=pltpu.SMEM)] * len(ints)
        + [in_vmem] * len(smalls)
        + [any_spec()] * len(arrays),
        out_specs=[any_spec()] * (len(outs) - 3) + [in_vmem] * 3,
        scratch_shapes=scratch,
        compiler_params=params(collective_id=0, has_side_effects=True),
        cost_estimate=cost(50 * LONG * D * D + 8 * LONG * LONG * D, 90 << 20),
        name="gather_forward_ffn",
    )(*ints, *smalls, *arrays)


def ffn_grads(activ_ref, branch3_ref, hidden2_ref, dpre_ref, out_grad_ref, in_grad_ref):
    out_grad_ref[...] = mm(activ_ref[...], branch3_ref[...], 0, 0).astype(BF16)
    in_grad_ref[...] = mm(hidden2_ref[...], dpre_ref[...], 0, 0).astype(BF16)


def ffn_grads_call(activ, branch3, hidden2, dpre):
    tile = 512
    return pl.pallas_call(
        ffn_grads,
        grid=(FF // tile,),
        in_specs=[
            pl.BlockSpec((LONG, tile), lambda i: (0, i)),
            whole((LONG, D)),
            whole((LONG, D)),
            pl.BlockSpec((LONG, tile), lambda i: (0, i)),
        ],
        out_specs=[
            pl.BlockSpec((tile, D), lambda i: (i, 0)),
            pl.BlockSpec((D, tile), lambda i: (0, i)),
        ],
        out_shape=[jax.ShapeDtypeStruct((FF, D), BF16), jax.ShapeDtypeStruct((D, FF), BF16)],
        compiler_params=params(),
        cost_estimate=cost(4 * LONG * D * FF, 8 * LONG * FF),
        name="ffn_grads",
    )(activ, branch3, hidden2, dpre)


def pair_grads(count, *refs):
    out_ref = refs[2 * count]
    for index in range(count):

        @pl.when(pl.program_id(0) == index)
        def _(index=index):
            out_ref[...] = mm(refs[index][...], refs[count + index][...], 0, 0).astype(BF16)


def pair_grads_call(lefts, rights, name):
    count = len(lefts)
    return pl.pallas_call(
        partial(pair_grads, count),
        grid=(count,),
        in_specs=[whole((LONG, D))] * (2 * count),
        out_specs=pl.BlockSpec((D, D), lambda i: (0, i)),
        out_shape=jax.ShapeDtypeStruct((D, D * count), BF16),
        compiler_params=params(),
        cost_estimate=cost(2 * LONG * D * D * count, 4 * LONG * D * count),
        name=name,
    )(*lefts, *rights)


def pair_fetcher(sources, lse, slots, lse_slots, sems):
    def copies(pair, slot):
        out = []
        for index, (ref, first) in enumerate(sources):
            cols = pl.ds(pl.multiple_of(first + pair * WIDE, WIDE), WIDE)
            out.append(
                pltpu.make_async_copy(ref.at[:, cols], slots.at[slot, index], sems.at[slot, index])
            )
        count = len(sources)
        out.append(pltpu.make_async_copy(lse.at[pair], lse_slots.at[slot, 0], sems.at[slot, count]))
        return out

    return copies


def pair_scratch():
    return [
        pltpu.VMEM((2, 5, LONG, WIDE), BF16),
        pltpu.VMEM((2, 1, 8, LONG), F32),
        pltpu.SemaphoreType.DMA((2, 6)),
    ]


def back_pairs(causal, fetch, slots, lse_slots, row_side, key_side, dq, dk, dv, after):
    @pl.loop(0, PAIRS)
    def _(pair):
        slot = pair % 2

        @pl.when(pair < PAIRS - 1)
        def _():
            for copy in fetch(pair + 1, 1 - slot):
                copy.start()

        for copy in fetch(pair, slot):
            copy.wait()

        def target(member):
            ref, first = member
            return ref.at[:, pl.ds(pl.multiple_of(first + pair * WIDE, WIDE), WIDE)]

        attend_back(
            causal,
            *[slots.at[slot, i] for i in range(5)],
            lse_slots.at[slot],
            row_side,
            key_side,
            target(dq),
            target(dk),
            target(dv),
        )
        for at, work in after.items():

            @pl.when(pair == at)
            def _(work=work):
                for member in work:
                    member()


FIRST_LOCAL = 24


def back_first_kernel(*refs):
    (
        row_side, source_side, vec_ref,
        activ_hbm, branch3_hbm, hidden2_hbm, dpre_hbm,
        query_hbm, pairs_hbm, cross_att_hbm, datt_hbm, lse_hbm,
        dresid2_hbm, resid1_hbm, w_cq_hbm, w_o_hbm,
        dcq_out, dck_out, dcv_out, branch1_out, self_datt_out, dresid1_out,
        in_quarter_out, out_quarter_out, sums_ref,
        activ, dpre, branch3, hidden2, dresid, resid, w_cq, w_o,
        slots, lse_slots, pair_sems,
        local, *scatter_bufs,
    ) = refs
    used = [0]

    def move(src, dst):
        copy = pltpu.make_async_copy(src, dst, local.at[used[0]])
        used[0] += 1
        copy.start()
        return copy

    quarters = [pl.ds(i * D, D) for i in range(FF // D)]
    load_branch3 = move(branch3_hbm, branch3)
    load_activ = [move(activ_hbm.at[:, q], activ.at[:, q]) for q in quarters]
    load_hidden2 = move(hidden2_hbm, hidden2)
    load_dpre = [move(dpre_hbm.at[:, q], dpre.at[:, q]) for q in quarters]
    greet()
    fetch = pair_fetcher(
        [(query_hbm, 0), (pairs_hbm, 0), (pairs_hbm, D), (cross_att_hbm, 0), (datt_hbm, 0)],
        lse_hbm,
        slots,
        lse_slots,
        pair_sems,
    )
    for copy in fetch(0, 0):
        copy.start()
    later = [
        move(dresid2_hbm, dresid),
        move(resid1_hbm, resid),
        move(w_cq_hbm, w_cq),
        move(w_o_hbm, w_o),
    ]
    out_bufs, in_bufs = scatter_bufs[:SCATTER_REFS], scatter_bufs[SCATTER_REFS:]
    out_plan, in_plan = scatter_steps(None, out_bufs), scatter_steps(None, in_bufs)
    out_rows = out_bufs[0].shape[3]
    tile = 2 * out_rows
    load_branch3.wait()
    for q in range(FF // D):
        load_activ[q].wait()
        for part in range(D // tile):
            index = q * (D // tile) + part
            left = activ[:, index * tile : (index + 1) * tile]
            grad = mm(left, branch3[...], 0, 0).astype(BF16)
            out_bufs[0][index // 2, index % 2] = grad.reshape(2, out_rows, D)
    out_plan[0]()
    load_hidden2.wait()
    in_rows = in_bufs[0].shape[3]
    for q in range(FF // D):
        load_dpre[q].wait()
        grad = mm(hidden2[...], dpre[:, quarters[q]], 0, 0).astype(BF16)
        in_bufs[0][:, :, :, :, quarters[q]] = grad.reshape(4, 2, 2, in_rows, D)
    out_plan[1]()
    in_plan[0]()
    back_pairs(
        False,
        fetch,
        slots,
        lse_slots,
        row_side,
        source_side,
        (activ, 0),
        (activ, D),
        (activ, 2 * D),
        {
            0: [in_plan[1]],
            3: [out_plan[2]],
            5: [out_plan[3], in_plan[2]],
        },
    )
    dcq, dck, dcv, branch1 = (activ.at[:, q] for q in quarters)
    self_datt = dpre.at[:, quarters[0]]
    saves = [move(dcq, dcq_out), move(dck, dck_out), move(dcv, dcv_out)]
    for copy in later:
        copy.wait()

    def square(ref):
        return ref[...].reshape(D, ref.shape[-1])

    block = 512
    sums_ref[...] = jnp.zeros_like(sums_ref)

    @pl.loop(0, LONG // block)
    def _(i):
        part = pl.ds(pl.multiple_of(i * block, block), block)
        left = dcq[part, :]
        dhidden = dresid[part, :] + mm(left, square(w_cq), 1, 1)
        xhat, inv = normed(resid[part, :])
        dresid1 = norm_back(xhat, inv, vec_ref[GAIN : GAIN + 1], dhidden)
        dresid[part, :] = dresid1
        low = dresid1.astype(BF16)
        branch1[part, :] = low
        self_datt[part, :] = mm(low, square(w_o), 1, 1).astype(BF16)
        sums_ref[0:1] += col_sum(dhidden * xhat)
        sums_ref[1:2] += col_sum(dhidden)
        sums_ref[2:3] += col_sum(low.astype(F32))
        sums_ref[3:4] += col_sum(left.astype(F32))
        sums_ref[4:5] += col_sum(dcv[part, :].astype(F32))

    saves += [move(branch1, branch1_out), move(self_datt, self_datt_out), move(dresid, dresid1_out)]
    saves.append(move(out_bufs[6], out_quarter_out))
    in_plan[3]()
    saves.append(move(in_bufs[6], in_quarter_out))
    in_plan[-1]()
    out_plan[-1]()
    for copy in saves:
        copy.wait()


def back_first_call(vmem_arrays, hbm_arrays, rows):
    in_vmem = pl.BlockSpec(memory_space=pltpu.VMEM)
    square = gather_shape(rows, D)

    def bf(*shape):
        return jax.ShapeDtypeStruct(shape, BF16)

    def f32(*shape):
        return jax.ShapeDtypeStruct(shape, F32)

    outs = [bf(LONG, D)] * 5 + [f32(LONG, D)]
    outs += [bf(4, rows, FF // 2), bf(4, 4 * rows, D // 2), f32(8, D)]
    held = [bf(LONG, FF)] * 2 + [bf(LONG, D)] * 2 + [f32(LONG, D)] * 2
    held += [bf(*square)] * 2
    scratch = [pltpu.VMEM(h.shape, h.dtype) for h in held] + pair_scratch()
    scratch += [pltpu.SemaphoreType.DMA((FIRST_LOCAL,))]
    scratch += scatter_scratch(4 * rows, D) + scatter_scratch(rows, FF)
    return pl.pallas_call(
        back_first_kernel,
        out_shape=outs,
        in_specs=[in_vmem] * len(vmem_arrays) + [any_spec()] * len(hbm_arrays),
        out_specs=[any_spec()] * 8 + [in_vmem],
        scratch_shapes=scratch,
        compiler_params=params(collective_id=1, has_side_effects=True),
        cost_estimate=cost(26 * LONG * D * D + 10 * LONG * LONG * D, 60 << 20),
        name="backward_cross_scatter_ffn",
    )(*vmem_arrays, *hbm_arrays)


SECOND_LOCAL = 32
SECOND_SHARES = 10
CROSS_PARTS = 5
SELF_PARTS = 3


def back_second_kernel(*refs):
    (
        row_side, target_side, sums_mid, bias_sum, sums_cross,
        self_att_hbm, cross_att_hbm, hidden1_hbm, encoded_hbm,
        branch1_hbm, branch2_hbm, dcq_hbm, dck_hbm, dcv_hbm,
        mixed_hbm, datt_hbm, lse_hbm, tokens_hbm, dresid1_hbm, w_q_hbm, w_k_hbm, w_v_hbm, w_ckv_hbm,
        in_quarter_hbm, out_quarter_hbm,
        tokens_grad_out, encoded_grad_out, *rest,
    ) = refs
    shares, small_share, rest = rest[:SECOND_SHARES], rest[SECOND_SHARES], rest[SECOND_SHARES + 1 :]
    (
        lefts, rights, tokens, dresid, w_q, w_k, w_v, w_ckv, vec_sums,
        slots, lse_slots, pair_sems,
        in_quarter, in_z, in_halves, in_sems, out_quarter, out_z, out_halves, out_sems,
        local, *scatter_bufs,
    ) = rest
    used = [0]

    def move(src, dst):
        copy = pltpu.make_async_copy(src, dst, local.at[used[0]])
        used[0] += 1
        copy.start()
        return copy

    left_sources = (self_att_hbm, cross_att_hbm, hidden1_hbm, encoded_hbm)
    right_sources = (branch1_hbm, branch2_hbm, dcq_hbm, dck_hbm, dcv_hbm)
    load_ffn = [move(in_quarter_hbm, in_quarter), move(out_quarter_hbm, out_quarter)]
    load_left, load_right = [], []
    for index, source in enumerate(right_sources):
        if index < len(left_sources):
            load_left.append(move(left_sources[index], lefts.at[index]))
        load_right.append(move(source, rights.at[index]))
    greet()
    fetch = pair_fetcher(
        [(mixed_hbm, 0), (mixed_hbm, D), (mixed_hbm, 2 * D), (self_att_hbm, 0), (datt_hbm, 0)],
        lse_hbm,
        slots,
        lse_slots,
        pair_sems,
    )
    for copy in fetch(0, 0):
        copy.start()
    load_tokens = move(tokens_hbm, tokens)
    later = [
        move(dresid1_hbm, dresid),
        move(w_q_hbm, w_q),
        move(w_k_hbm, w_k),
        move(w_v_hbm, w_v),
        move(w_ckv_hbm, w_ckv),
    ]

    def bufs(index):
        return scatter_bufs[index * SCATTER_REFS : (index + 1) * SCATTER_REFS]

    plans = [scatter_steps(shares[i], bufs(i)) for i in range(CROSS_PARTS + SELF_PARTS)]
    cross_plans, self_plans = plans[:CROSS_PARTS], plans[CROSS_PARTS:]
    in_plan = scatter_tail(shares[CROSS_PARTS + SELF_PARTS], in_quarter, in_z, in_halves, in_sems)
    out_plan = scatter_tail(shares[CROSS_PARTS + SELF_PARTS + 1], out_quarter, out_z, out_halves, out_sems)
    small_bufs = scatter_bufs[(CROSS_PARTS + SELF_PARTS) * SCATTER_REFS :]
    small_plan = small_scatter_steps(small_share, small_bufs)
    for copy in load_ffn:
        copy.wait()
    in_plan[0]()
    out_plan[0]()
    rows = bufs(0)[0].shape[3]
    for index in range(CROSS_PARTS):
        if index < len(load_left):
            load_left[index].wait()
        load_right[index].wait()
        left = lefts[min(index, len(left_sources) - 1)]
        grad = mm(left, rights[index], 0, 0).astype(BF16)
        bufs(index)[0][...] = grad.reshape(4, 2, 2, rows, D)
        cross_plans[index][0]()
        if index:
            cross_plans[index - 1][1]()
    load_tokens.wait()
    vec_sums[...] = jnp.zeros_like(vec_sums)
    dq, dk, dv = rights.at[0], rights.at[1], rights.at[2]

    def self_part(part):
        def work():
            cols = pl.ds(part * 256, 256)
            target = bufs(CROSS_PARTS + part)[0]
            left = tokens[...]
            ones = jnp.ones((8, LONG), BF16)
            for index, ref in enumerate((dq, dk, dv)):
                right = ref[:, cols]
                grad = mm(left, right, 0, 0).astype(BF16)
                target[:, :, :, :, index * 256 : (index + 1) * 256] = grad.reshape(4, 2, 2, rows, 256)
                if index != 1:
                    row = SELF_B + index // 2
                    vec_sums[row : row + 1, cols] = mm(ones, right)[0:1]
            self_plans[part][0]()

        return work

    def both(members, number):
        return [cross_plans[i][number] for i in members]

    back_pairs(
        True,
        fetch,
        slots,
        lse_slots,
        row_side,
        target_side,
        (dq, 0),
        (dk, 0),
        (dv, 0),
        {
            0: both((4,), 1),
            1: [self_part(0)] + both((0, 1, 2, 3), 2),
            2: [self_plans[0][1]] + both((4,), 2) + both((0, 1), 3) + both((0, 1), 4),
            3: [self_part(1), self_plans[0][2], in_plan[1], out_plan[1], in_plan[2], out_plan[2]]
            + both((2, 3, 4), 3)
            + both((2, 3, 4), 4),
            4: [self_plans[1][1], self_plans[0][3], self_plans[0][4]] + both((0, 1), 5) + both((0, 1), 6),
            5: [self_part(2), self_plans[1][2]]
            + both((2, 3, 4), 5)
            + both((2, 3, 4), 6)
            + both((0, 1), 7)
            + [self_plans[0][5], self_plans[0][6], in_plan[3], out_plan[3]],
        },
    )

    vec_sums[SELF_B + 2 : CROSS_B + 2] = sums_cross[2:5]
    vec_sums[CROSS_B + 2 : CROSS_B + 3] = sums_mid[4:5]
    vec_sums[GAIN : GAIN + 1] = sums_cross[0:1]
    vec_sums[GAIN + 1 : GAIN + 3] = sums_mid[0:2]
    vec_sums[SHIFT : SHIFT + 1] = sums_cross[1:2]
    vec_sums[SHIFT + 1 : SHIFT + 3] = sums_mid[2:4]
    vec_sums[OUT_B : OUT_B + 1] = sums_mid[5:6]
    held = small_bufs[0]
    held[...] = jnp.zeros_like(held)
    for owner in range(16):
        tile = held.at[owner // 4, (owner // 2) % 2, owner % 2]
        tile[:, :rows] = vec_sums[:, owner * rows : (owner + 1) * rows]
        tile[IN_B : IN_B + 1, : 4 * rows] = bias_sum[:, owner * 4 * rows : (owner + 1) * 4 * rows]
    small_plan[0]()
    for copy in later:
        copy.wait()

    def square(ref):
        return ref[...].reshape(D, D)

    block = 256

    def rows_back(index):
        part = pl.ds(index * block, block)
        total = dresid[part, :] + mm(dq[part, :], square(w_q), 1, 1)
        total = total + mm(dk[part, :], square(w_k), 1, 1)
        tokens[part, :] = (total + mm(dv[part, :], square(w_v), 1, 1)).astype(BF16)

    encoded_grad = lefts.at[0]

    def encoded_back(index):
        part = pl.ds(index * block, block)
        weight = w_ckv[...].reshape(D, 2 * D)
        total = mm(rights[CROSS_PARTS - 2, part, :], weight[:, :D], 1, 1)
        total = total + mm(rights[CROSS_PARTS - 1, part, :], weight[:, D:], 1, 1)
        encoded_grad[part, :] = total.astype(BF16)

    rows_back(0)
    self_plans[2][1]()
    small_plan[1]()
    self_plans[1][3]()
    self_plans[1][4]()
    rows_back(1)
    for index in (2, 3, 4):
        cross_plans[index][7]()
    rows_back(2)
    small_plan[2]()
    self_plans[2][2]()
    self_plans[0][7]()
    rows_back(3)
    save = [move(tokens, tokens_grad_out)]
    small_plan[3]()
    self_plans[1][5]()
    self_plans[1][6]()
    self_plans[2][3]()
    self_plans[2][4]()
    encoded_back(0)
    encoded_back(1)
    encoded_back(2)
    small_plan[4]()
    self_plans[1][7]()
    self_plans[2][5]()
    self_plans[2][6]()
    encoded_back(3)
    save.append(move(encoded_grad, encoded_grad_out))
    self_plans[2][7]()
    for copy in save:
        copy.wait()


def back_second_call(vmem_arrays, hbm_arrays, rows):
    in_vmem = pl.BlockSpec(memory_space=pltpu.VMEM)
    square = gather_shape(rows, D)

    def bf(*shape):
        return jax.ShapeDtypeStruct(shape, BF16)

    def f32(*shape):
        return jax.ShapeDtypeStruct(shape, F32)

    outs = [bf(LONG, D)] * 2 + [bf(2, rows, D // 2)] * (CROSS_PARTS + SELF_PARTS)
    outs += [bf(2, rows, FF // 2), bf(2, 4 * rows, D // 2), f32(*SMALL_TILE)]
    held = [bf(4, LONG, D), bf(5, LONG, D), bf(LONG, D), f32(LONG, D)] + [bf(*square)] * 3
    held += [bf(*gather_shape(rows, 2 * D)), f32(16, D)]
    scratch = [pltpu.VMEM(h.shape, h.dtype) for h in held] + pair_scratch()
    scratch += [
        pltpu.VMEM((4, rows, FF // 2), BF16),
        pltpu.VMEM((3, rows, FF // 2), BF16),
        pltpu.VMEM((2, rows, FF // 2), BF16),
        pltpu.SemaphoreType.DMA((2, SCATTER_COPIES)),
        pltpu.VMEM((4, 4 * rows, D // 2), BF16),
        pltpu.VMEM((3, 4 * rows, D // 2), BF16),
        pltpu.VMEM((2, 4 * rows, D // 2), BF16),
        pltpu.SemaphoreType.DMA((2, SCATTER_COPIES)),
        pltpu.SemaphoreType.DMA((SECOND_LOCAL,)),
    ]
    for _ in range(CROSS_PARTS + SELF_PARTS):
        scratch += scatter_scratch(rows, D)
    scratch += small_scatter_scratch()
    return pl.pallas_call(
        back_second_kernel,
        out_shape=outs,
        in_specs=[in_vmem] * len(vmem_arrays) + [any_spec()] * len(hbm_arrays),
        out_specs=[any_spec()] * 2 + [in_vmem] * (len(outs) - 2),
        scratch_shapes=scratch,
        compiler_params=params(collective_id=2, has_side_effects=True),
        cost_estimate=cost(22 * LONG * D * D + 10 * LONG * LONG * D, 60 << 20),
        name="backward_self_scatter_rest",
    )(*vmem_arrays, *hbm_arrays)


BIG = 3


def hand_out_kernel(*refs):
    big_in, shares = refs[:BIG], list(refs[BIG : BIG + 11])
    big_out, outs = refs[BIG + 11 : 2 * BIG + 11], refs[2 * BIG + 11 : 2 * BIG + 24]
    held, sems = refs[2 * BIG + 24 :]
    small = shares.pop()
    loads = [pltpu.make_async_copy(ref, held.at[i], sems.at[i]) for i, ref in enumerate(big_in)]
    copies = [pltpu.make_async_copy(held.at[i], ref, sems.at[BIG + i]) for i, ref in enumerate(big_out)]
    for load in loads:
        load.start()
    for load, copy in zip(loads, copies):
        load.wait()
        copy.start()
    self_in, self_b, self_out, cross_q, cross_kv, cross_b, cross_out, ffn_in, in_b, ffn_out, out_b, gain, shift = outs
    plain = [(self_out, 0, 0), (cross_out, 1, 0), (cross_q, 2, 0), (cross_kv, 3, 0), (cross_kv, 4, D)]
    plain += [(ffn_in, 8, 0), (ffn_out, 9, 0)]
    for ref, index, first in plain:
        half = shares[index].shape[2]
        for h in range(2):
            ref[:, first + h * half : first + (h + 1) * half] = shares[index][h].astype(F32)
    for part in range(SELF_PARTS):
        for at in range(6):
            first = (at // 2) * D + part * 256 + (at % 2) * 128
            piece = shares[CROSS_PARTS + part][at // 3, :, (at % 3) * 128 : (at % 3 + 1) * 128]
            self_in[:, first : first + 128] = piece.astype(F32)
    rows = self_b.shape[1]
    for start, ref in ((SELF_B, self_b), (CROSS_B, cross_b), (GAIN, gain), (SHIFT, shift), (OUT_B, out_b)):
        ref[...] = small[start : start + ref.shape[0], :rows]
    in_b[...] = small[IN_B : IN_B + 1, : 4 * rows]
    for copy in copies:
        copy.wait()


def hand_out_call(arrays, rows):
    in_vmem = pl.BlockSpec(memory_space=pltpu.VMEM)

    def f32(*shape):
        return jax.ShapeDtypeStruct(shape, F32)

    outs = [jax.ShapeDtypeStruct((LONG, D), BF16)] * BIG
    outs += [f32(rows, 3 * D), f32(3, rows), f32(rows, D), f32(rows, D), f32(rows, 2 * D), f32(3, rows)]
    outs += [f32(rows, D), f32(rows, FF), f32(1, 4 * rows), f32(4 * rows, D), f32(1, rows), f32(3, rows), f32(3, rows)]
    return pl.pallas_call(
        hand_out_kernel,
        out_shape=outs,
        in_specs=[any_spec()] * BIG + [in_vmem] * (len(arrays) - BIG),
        out_specs=[any_spec()] * BIG + [in_vmem] * (len(outs) - BIG),
        scratch_shapes=[pltpu.VMEM((BIG, LONG, D), BF16), pltpu.SemaphoreType.DMA((2 * BIG,))],
        compiler_params=params(),
        name="hand_out",
    )(*arrays)


def body(
    tokens,
    encoded,
    cotangent,
    bucket,
    target_len,
    source_len,
    self_in,
    self_bias,
    self_out,
    cross_q,
    cross_kv,
    cross_bias,
    cross_out,
    ffn_in,
    ffn_in_bias,
    ffn_out,
    ffn_out_bias,
    norm_gain,
    norm_shift,
):
    rows = self_in.shape[0]
    owners = D // rows
    direct = owners == 16
    square = (D, D)
    if direct:
        smalls = [self_bias, cross_bias, norm_gain, norm_shift]
        smalls += [ffn_out_bias.reshape(1, rows), ffn_in_bias.reshape(1, 4 * rows)]
        arrays = [tokens, encoded, cotangent, self_in, self_out, cross_q, cross_kv, cross_out, ffn_in, ffn_out]
        results = forward_call([bucket, target_len, source_len], smalls, arrays)
        pieces = results[:6]
        (mixed, self_att, self_lse, resid1, hidden1, query, pairs, cross_att, cross_lse) = results[6:15]
        row_side, target_side, source_side = results[15:18]
        (activ, branch3, dpre, hidden2, dresid2, branch2, d_cross_att, output) = results[18:26]
        vec, sums_mid, bias_sum = results[26:]
        first = back_first_call(
            [row_side, source_side, vec],
            [activ, branch3, hidden2, dpre, query, pairs, cross_att, d_cross_att, cross_lse]
            + [dresid2, resid1, pieces[4], pieces[3]],
            rows,
        )
        dcq, dck, dcv, branch1, d_self_att, dresid1, in_quarter, out_half, sums_cross = first
        second = back_second_call(
            [row_side, target_side, sums_mid, bias_sum, sums_cross],
            [self_att, cross_att, hidden1, encoded, branch1, branch2, dcq, dck, dcv]
            + [mixed, d_self_att, self_lse, tokens, dresid1, pieces[0], pieces[1], pieces[2], pieces[5]]
            + [in_quarter, out_half],
            rows,
        )
        final = list(hand_out_call([output, *second], rows))
        final[11], final[13] = final[11].reshape(-1), final[13].reshape(-1)
        return tuple(final)

    else:
        everyone = partial(lax.all_gather, axis_name="fsdp", axis=0, tiled=True)
        self_w = everyone(self_in)
        weights = [self_w[:, i * D : (i + 1) * D] for i in range(3)]
        weights += [everyone(w) for w in (self_out, cross_q, cross_kv, cross_out, ffn_in, ffn_out)]
        small = [self_bias, cross_bias, norm_gain, norm_shift, ffn_out_bias, ffn_in_bias]
        small_all = everyone(jnp.concatenate([w.reshape(1, -1) for w in small], axis=1)).astype(F32)
        vec = small_all[:, : IN_B * rows].reshape(owners, IN_B, rows).transpose(1, 0, 2).reshape(IN_B, D)
        vec = jnp.pad(vec, ((0, 3), (0, 0)))
        bias = small_all[:, IN_B * rows : VEC_ROWS * rows].reshape(1, FF)
        row_side, target_side, source_side = mask_lanes(bucket[0], target_len[0], source_len[0])
        (mixed,) = row_call(
            project_in,
            512,
            [tokens],
            [(w, square, (0, 0)) for w in weights[:3]] + [(vec, (16, D), (0, 0))],
            [(3 * D, BF16)],
            [],
            "project_in",
            6 * LONG * D * D,
        )
        self_att, self_lse = attention_forward(
            (mixed, 0), (mixed, PAIRS), (mixed, 2 * PAIRS), row_side, target_side, True, "self_forward"
        )
        resid1, hidden1, query, pairs = row_call(
            between,
            512,
            [tokens, self_att, encoded],
            [(weights[3], square, (0, 0)), (weights[4], square, (0, 0)), (weights[5], (D, 2 * D), (0, 0))]
            + [(vec, (16, D), (0, 0))],
            [(D, F32), (D, BF16), (D, BF16), (2 * D, BF16)],
            [],
            "between",
            8 * LONG * D * D,
        )
        cross_att, cross_lse = attention_forward(
            (query, 0), (pairs, 0), (pairs, PAIRS), row_side, source_side, False, "cross_forward"
        )
    w_q, w_k, w_v, w_o, w_cq, w_ckv, w_co, w_fi, w_fo = weights
    vec_weight = (vec, (16, D), (0, 0))
    (output, activ, branch3, dpre, hidden2, dresid2, branch2, d_cross_att, sums_mid, bias_sum) = row_call(
        middle,
        256,
        [hidden1, cross_att, cotangent],
        [
            (w_co, square, (0, 0)),
            (w_fi, (D, FF), (0, 0)),
            (w_fo, (FF, D), (0, 0)),
            vec_weight,
            (bias, (1, FF), (0, 0)),
        ],
        [(D, BF16), (FF, BF16), (D, BF16), (FF, BF16), (D, BF16), (D, F32), (D, BF16), (D, BF16)],
        [(8, D), (1, FF)],
        "middle",
        36 * LONG * D * D,
    )
    ffn_out_grad, ffn_in_grad = ffn_grads_call(activ, branch3, hidden2, dpre)
    dcq, dck, dcv = attention_backward(
        (query, 0),
        (pairs, 0),
        (pairs, PAIRS),
        cross_att,
        d_cross_att,
        cross_lse,
        row_side,
        source_side,
        False,
        "cross_backward",
    )
    encoded_grad, dresid1, branch1, d_self_att, sums_cross = row_call(
        after_cross,
        512,
        [dcq, dck, dcv, dresid2, resid1],
        [(w_cq, square, (0, 0)), (w_ckv, (D, 2 * D), (0, 0)), (w_o, square, (0, 0)), vec_weight],
        [(D, BF16), (D, F32), (D, BF16), (D, BF16)],
        [(8, D)],
        "after_cross",
        8 * LONG * D * D,
    )
    cross_grad = pair_grads_call(
        [self_att, hidden1, encoded, encoded, cross_att],
        [branch1, dcq, dck, dcv, branch2],
        "cross_grads",
    )
    dq, dk, dv = attention_backward(
        (mixed, 0),
        (mixed, PAIRS),
        (mixed, 2 * PAIRS),
        self_att,
        d_self_att,
        self_lse,
        row_side,
        target_side,
        True,
        "self_backward",
    )
    self_grad = pair_grads_call([tokens] * 3, [dq, dk, dv], "self_grads")
    (tokens_grad,) = row_call(
        tokens_back,
        512,
        [dq, dk, dv, dresid1],
        [(w, square, (0, 0)) for w in weights[:3]],
        [(D, BF16)],
        [],
        "tokens_back",
        6 * LONG * D * D,
    )

    def share_of(grad):
        share = lax.psum_scatter(grad.astype(F32), "fsdp", scatter_dimension=0, tiled=True)
        return lax.psum(share, "dp")

    dq_sum = jnp.sum(dq.astype(F32), axis=0, keepdims=True)
    dv_sum = jnp.sum(dv.astype(F32), axis=0, keepdims=True)
    small_rows = jnp.concatenate(
        [
            dq_sum,
            dv_sum,
            sums_cross[2:5],
            sums_mid[4:5],
            sums_cross[0:1],
            sums_mid[0:2],
            sums_cross[1:2],
            sums_mid[2:4],
            sums_mid[5:6],
        ],
        axis=0,
    )
    packed = small_rows.reshape(IN_B, owners, rows).transpose(1, 0, 2).reshape(owners, IN_B * rows)
    packed = jnp.concatenate([packed, bias_sum.reshape(owners, 4 * rows)], axis=1)
    packed_share = share_of(packed).reshape(-1)
    self_share, cross_share, ffn_in_share, ffn_out_share = map(
        share_of, (self_grad, cross_grad, ffn_in_grad, ffn_out_grad)
    )

    def rows_of(first, count):
        return packed_share[first * rows : (first + count) * rows]

    return (
        output,
        tokens_grad,
        encoded_grad,
        self_share,
        rows_of(SELF_B, 3).reshape(3, rows),
        cross_share[:, :D],
        cross_share[:, D : 2 * D],
        cross_share[:, 2 * D : 4 * D],
        rows_of(CROSS_B, 3).reshape(3, rows),
        cross_share[:, 4 * D :],
        ffn_in_share,
        rows_of(IN_B, 4),
        ffn_out_share,
        rows_of(OUT_B, 1),
        rows_of(GAIN, 3).reshape(3, rows),
        rows_of(SHIFT, 3).reshape(3, rows),
    )


def solution(mesh):
    both = P(("dp", "fsdp"), None)
    rows, cols, flat = P("fsdp", None), P(None, "fsdp"), P("fsdp")
    return jax.shard_map(
        body,
        mesh=mesh,
        in_specs=(both, both, both, P(("dp", "fsdp")), both, both)
        + (rows, cols, rows, rows, rows, cols, rows, rows, flat, rows, flat, cols, cols),
        out_specs=(both, both, both)
        + (rows, cols, rows, rows, rows, cols, rows, rows, flat, rows, flat, cols, cols),
        check_vma=False,
    )
```

```python
from functools import partial

import jax
import jax.numpy as jnp
from jax import lax
from jax.experimental import pallas as pl
from jax.experimental.pallas import tpu as pltpu
from jax.sharding import PartitionSpec as P

D = 768
H = 12
HD = 64
FF = 3072
LONG = 1024
SEGS = 4
SHORT = 256
PAIRS = H // 2
WIDE = 2 * HD

EPS = 1e-05
NEG = -1e30
SCALE = HD ** (-0.5)
F32 = jnp.float32
BF16 = jnp.bfloat16
MESH_ID = pl.DeviceIdType.MESH
VMEM_LIMIT = 60 << 20

SELF_B, CROSS_B, GAIN, SHIFT, OUT_B, IN_B = 0, 3, 6, 9, 12, 13
VEC_ROWS = 17
PACK = 2048


def mm(left, right, left_dim=1, right_dim=0):
    return lax.dot_general(
        left, right, (((left_dim,), (right_dim,)), ((), ())), preferred_element_type=F32
    )


def params(**kwargs):
    return pltpu.CompilerParams(vmem_limit_bytes=VMEM_LIMIT, **kwargs)


def cost(flops, nbytes, trans=0):
    return pl.CostEstimate(flops=int(flops), bytes_accessed=int(nbytes), transcendentals=int(trans))


def any_spec():
    return pl.BlockSpec(memory_space=pl.ANY)


def whole(shape):
    return pl.BlockSpec(shape, lambda *_: (0,) * len(shape))


def normed(resid):
    centered = resid - jnp.mean(resid, axis=-1, keepdims=True)
    inv = lax.rsqrt(jnp.mean(centered * centered, axis=-1, keepdims=True) + EPS)
    return centered * inv, inv


def norm_back(xhat, inv, gain, grad):
    scaled = grad * gain
    first = jnp.mean(scaled, axis=-1, keepdims=True)
    second = jnp.mean(scaled * xhat, axis=-1, keepdims=True)
    return (scaled - first - xhat * second) * inv


def col_sum(values):
    return jnp.sum(values, axis=0, keepdims=True)


def my_place():
    dp, index = lax.axis_index("dp"), lax.axis_index("fsdp")
    return dp, index // 4, (index // 2) % 2, index % 2


def far_first(z):
    first, second = 3 - 2 * (z % 2), 1 + (z + 1) // 2
    return (first, second, 6 - first - second)


def place(dp, z, y, core):
    return {"dp": dp, "fsdp": (z * 2 + y) * 2 + core}


def neighbours():
    x, z, y, c = my_place()
    return [place(x, (z + k) % 4, y, c) for k in (1, 2, 3)] + [
        place(1 - x, z, y, c),
        place(x, z, 1 - y, c),
        place(x, z, y, 1 - c),
    ]


def greet():
    barrier = pltpu.get_barrier_semaphore()
    others = neighbours()
    for other in others:
        pl.semaphore_signal(barrier, inc=1, device_id=other, device_id_type=MESH_ID)
    pl.semaphore_wait(barrier, len(others))


def remote(src, dst, sems, index, device):
    return pltpu.make_async_remote_copy(
        src_ref=src,
        dst_ref=dst,
        send_sem=sems.at[0, index],
        recv_sem=sems.at[1, index],
        device_id=device,
        device_id_type=MESH_ID,
    )


GATHER_COPIES = 11


def gather_copies(shard, full, sems, local_sem):
    x, z, y, c = my_place()
    half = shard.shape[-1] // 2
    mine = pl.ds(pl.multiple_of(x * half, 128), half)
    other = pl.ds(pl.multiple_of((1 - x) * half, 128), half)
    to_x, to_y, to_c = place(1 - x, z, y, c), place(x, z, 1 - y, c), place(x, z, y, 1 - c)

    def same(index, where, device):
        ref = full.at[where]
        return remote(ref, ref, sems, index, device)

    own = (slice(None), y, c, slice(None), mine)
    from_x = (slice(None), y, c, slice(None), other)
    from_y = (slice(None), 1 - y, c, slice(None), mine)
    diagonal = (slice(None), 1 - y, c, slice(None), other)
    copies = [
        remote(shard.at[:, mine], full.at[z, y, c, :, mine], sems, k - 1, place(x, (z + k) % 4, y, c))
        for k in far_first(z)
    ]
    copies += [same(3, own, to_x), same(4, own, to_y)]
    copies += [
        same(5, (pl.ds(0, 2), 1 - y, c, slice(None), mine), to_x),
        same(6, (pl.ds(2, 2), y, c, slice(None), other), to_y),
    ]
    copies += [same(7, own, to_c), same(8, from_x, to_c), same(9, from_y, to_c), same(10, diagonal, to_c)]
    local = pltpu.make_async_copy(shard.at[:, mine], full.at[z, y, c, :, mine], local_sem)
    return copies, local


def gather_steps(shard, full, sems, local_sem):
    copies, local = gather_copies(shard, full, sems, local_sem)

    def first():
        local.start()
        for copy in copies[:3]:
            copy.start()

    def second():
        local.wait()
        for copy in copies[:3]:
            copy.wait_recv()
        for index in (3, 4, 7):
            copies[index].start()

    def third():
        copies[3].wait_recv()
        copies[4].wait_recv()
        for index in (5, 6, 8, 9):
            copies[index].start()

    def fourth():
        copies[5].wait_recv()
        copies[6].wait_recv()
        copies[10].start()

    def arrive():
        for index in (7, 8, 9, 10):
            copies[index].wait_recv()

    def last():
        for copy in copies:
            copy.wait_send()

    return [first, second, third, fourth, arrive, last]


SMALL_COPIES = 5


def small_gather_steps(shard, full, sems, local_sem):
    x, z, y, c = my_place()
    local = pltpu.make_async_copy(shard, full.at[z, y, c], local_sem)
    copies = [
        remote(shard, full.at[z, y, c], sems, k - 1, place(x, (z + k) % 4, y, c)) for k in far_first(z)
    ]
    copies.append(remote(full.at[:, y, c], full.at[:, y, c], sems, 3, place(x, z, 1 - y, c)))
    copies.append(remote(full.at[:, :, c], full.at[:, :, c], sems, 4, place(x, z, y, 1 - c)))

    def first():
        local.start()
        for copy in copies[:3]:
            copy.start()

    def second():
        local.wait()
        for copy in copies[:3]:
            copy.wait_recv()
        copies[3].start()

    def third():
        copies[3].wait_recv()
        copies[4].start()

    def fourth():
        copies[4].wait_recv()

    def last():
        for copy in copies:
            copy.wait_send()

    return [first, second, third, fourth, last]


def gather_shape(rows, cols):
    return (4, 2, 2, rows, cols)


SCATTER_COPIES = 9
SCATTER_REFS = 10


def scatter_scratch(rows, cols):
    half = cols // 2
    return [
        pltpu.VMEM((4, 2, 2, rows, cols), BF16),
        pltpu.VMEM((4, 2, rows, cols), BF16),
        pltpu.VMEM((2, 2, rows, half), BF16),
        pltpu.VMEM((2, rows, half), BF16),
        pltpu.VMEM((2, rows, cols), BF16),
        pltpu.VMEM((2, rows, half), BF16),
        pltpu.VMEM((4, rows, half), BF16),
        pltpu.VMEM((3, rows, half), BF16),
        pltpu.VMEM((2, rows, half), BF16),
        pltpu.SemaphoreType.DMA((2, SCATTER_COPIES)),
    ]


def add_into(dst, where, left, right):
    dst[where] = (left.astype(F32) + right.astype(F32)).astype(BF16)


def scatter_steps(share, bufs):
    grads, peer, x_one, x_two, y_one, y_two, quarter, z_in, halves, sems = bufs
    x, z, y, c = my_place()
    half = grads.shape[-1] // 2
    to_x, to_y, to_c = place(1 - x, z, y, c), place(x, z, 1 - y, c), place(x, z, y, 1 - c)
    mine = pl.ds(pl.multiple_of(x * half, 128), half)
    other = pl.ds(pl.multiple_of((1 - x) * half, 128), half)
    every = slice(None)
    low, high = pl.ds(0, 2), pl.ds(2, 2)
    swap = remote(grads.at[:, :, 1 - c], peer, sems, 0, to_c)
    x_first = remote(grads.at[low, :, c, :, other], x_one, sems, 1, to_x)
    y_first = remote(grads.at[high, 1 - y, c], y_one, sems, 2, to_y)
    x_second = remote(grads.at[high, y, c, :, other], x_two, sems, 3, to_x)
    y_second = remote(grads.at[low, 1 - y, c, :, mine], y_two, sems, 4, to_y)
    def start():
        swap.start()

    def sum_cores():
        swap.wait_recv()

        @pl.loop(0, 8)
        def _(i):
            where = (i // 2, i % 2, c)
            add_into(grads, where, grads[where], peer[i // 2, i % 2])

        x_first.start()
        y_first.start()

    def sum_first():
        x_first.wait_recv()
        y_first.wait_recv()

        @pl.loop(0, 2)
        def _(i):
            where = (i, 1 - y, c, every, mine)
            add_into(grads, where, grads[where], x_one[i, 1 - y])
            where = (2 + i, y, c, every, other)
            add_into(grads, where, grads[where], y_one[i, :, other])

        x_second.start()
        y_second.start()

        @pl.loop(0, 2)
        def _(i):
            add_into(quarter, i, grads[i, y, c, :, mine], x_one[i, y])
            add_into(quarter, 2 + i, grads[2 + i, y, c, :, mine], y_one[i, :, mine])

    def sum_second():
        x_second.wait_recv()
        y_second.wait_recv()

        @pl.loop(0, 2)
        def _(i):
            add_into(quarter, i, quarter[i], y_two[i])
            add_into(quarter, 2 + i, quarter[2 + i], x_two[i])

    def sent():
        for copy in (swap, x_first, y_first, x_second, y_second):
            copy.wait_send()

    tail = scatter_tail(share, quarter, z_in, halves, sems)
    last = tail[-1]

    def finish():
        sent()
        last()

    return [start, sum_cores, sum_first, sum_second] + tail[:-1] + [finish, sent]


def scatter_tail(share, quarter, z_in, halves, sems):
    x, z, y, c = my_place()
    z_sends = [
        remote(quarter.at[(z + k) % 4], z_in.at[k - 1], sems, 4 + k, place(x, (z + k) % 4, y, c))
        for k in far_first(z)
    ]

    def send_z():
        for copy in z_sends:
            copy.start()

    def sum_z():
        for copy in z_sends:
            copy.wait_recv()
        total = quarter[z].astype(F32)
        for k in range(3):
            total = total + z_in[k].astype(F32)
        halves[0] = total.astype(BF16)
        for copy in z_sends:
            copy.wait_send()

    return [send_z, sum_z] + scatter_last(share, halves, sems)


def scatter_last(share, halves, sems):
    x, z, y, c = my_place()
    last_swap = remote(halves.at[0], halves.at[1], sems, 8, place(1 - x, z, y, c))

    def swap_x():
        last_swap.start()

    def finish():
        last_swap.wait()
        share[x] = halves[0]
        share[1 - x] = halves[1]

    return [swap_x, finish]


SMALL_SCATTER = 6
SMALL_REFS = 9
SMALL_TILE = (16, 256)


def small_scatter_scratch():
    return [
        pltpu.VMEM((4, 2, 2) + SMALL_TILE, F32),
        pltpu.VMEM((4, 2) + SMALL_TILE, F32),
        pltpu.VMEM((4, 2) + SMALL_TILE, F32),
        pltpu.VMEM((4,) + SMALL_TILE, F32),
        pltpu.VMEM((4,) + SMALL_TILE, F32),
        pltpu.VMEM((3,) + SMALL_TILE, F32),
        pltpu.VMEM(SMALL_TILE, F32),
        pltpu.VMEM(SMALL_TILE, F32),
        pltpu.SemaphoreType.DMA((2, SMALL_SCATTER)),
    ]


def small_scatter_steps(share, bufs):
    held, pair, peer, line, from_y, z_in, mine, other, sems = bufs
    x, z, y, c = my_place()
    swap = remote(held.at[:, :, 1 - c], peer, sems, 0, place(x, z, y, 1 - c))
    to_y = remote(pair.at[:, 1 - y], from_y, sems, 1, place(x, z, 1 - y, c))
    z_sends = [
        remote(line.at[(z + k) % 4], z_in.at[k - 1], sems, 1 + k, place(x, (z + k) % 4, y, c))
        for k in far_first(z)
    ]
    to_x = remote(mine, other, sems, 5, place(1 - x, z, y, c))

    def start():
        swap.start()

    def sum_cores():
        swap.wait_recv()
        pair[...] = held[:, :, c] + peer[...]
        to_y.start()

    def sum_y():
        to_y.wait_recv()
        line[...] = pair[:, y] + from_y[...]
        for copy in z_sends:
            copy.start()

    def sum_z():
        for copy in z_sends:
            copy.wait_recv()
        mine[...] = line[z] + z_in[0] + z_in[1] + z_in[2]
        to_x.start()

    def finish():
        to_x.wait_recv()
        share[...] = mine[...] + other[...]
        for copy in [swap, to_y, to_x] + z_sends:
            copy.wait_send()

    return [start, sum_cores, sum_y, sum_z, finish]


def mask_lanes(kind, target_row, source_row):
    places = jnp.arange(LONG, dtype=jnp.int32)
    segment = jnp.where(kind == 1, 0, places // SHORT)
    offset = jnp.where(kind == 1, places, places % SHORT)
    lane = jnp.arange(WIDE, dtype=jnp.int32) % HD
    inside = segment[:, None] == lane[None, :]
    row_side = jnp.where(inside | (lane == SEGS)[None, :], 1.0, 0.0).astype(BF16)
    picker = segment[:, None] == jnp.arange(SEGS, dtype=jnp.int32)[None, :]

    def key_side(lengths):
        live = offset < jnp.sum(jnp.where(picker, lengths[None, :], 0), axis=1)
        blocked = ((lane < SEGS)[None, :] & ~inside) | ((lane == SEGS)[None, :] & ~live[:, None])
        ones = ((lane > SEGS) & (lane < SEGS + 4))[None, :]
        return jnp.where(blocked, NEG, jnp.where(ones, 1.0, 0.0)).astype(BF16)

    return row_side, key_side(target_row), key_side(source_row)


def lower(block, row_dim):
    rows = lax.broadcasted_iota(jnp.int32, (block, block), row_dim)
    cols = lax.broadcasted_iota(jnp.int32, (block, block), 1 - row_dim)
    return cols <= rows


def attend(causal, q_ref, k_ref, v_ref, row_ref, key_ref, att_ref, lse_ref):
    block, cuts = 512, 1 if causal else 2
    lane = lax.broadcasted_iota(jnp.int32, (1, WIDE), 1)
    feature = lax.broadcasted_iota(jnp.int32, (WIDE, 1), 0)
    vals_across = v_ref[...].T
    keys = [jnp.where(lane // HD == head, k_ref[...], key_ref[...]) for head in range(2)]
    vals = [jnp.where(feature // HD == head, vals_across, jnp.ones((), BF16)) for head in range(2)]
    items = [(head, index) for index in range(LONG // block) for head in range(2)]

    def reach_of(index):
        return (index + 1) * block if causal else LONG

    def score(item):
        head, index = item
        part, reach = pl.ds(index * block, block), reach_of(index)
        rows = jnp.where(lane // HD == head, q_ref[part, :], row_ref[part, :])
        scores = mm(keys[head][:reach], rows, 1, 1)
        if causal:
            edge = jnp.where(lower(block, 1), scores[reach - block :], NEG)
            scores = (
                edge
                if reach == block
                else jnp.concatenate([scores[: reach - block], edge], axis=0)
            )
        return scores, jnp.max(scores, axis=0, keepdims=True)

    def mix(item, scores, top):
        head, index = item
        step = reach_of(index) // cuts
        mixed = None
        for cut in range(cuts):
            part = slice(cut * step, (cut + 1) * step)
            term = mm(vals[head][:, part], jnp.exp(scores[part] - top).astype(BF16))
            mixed = term if mixed is None else mixed + term
        spare = HD * (1 - head)
        total = mixed[spare : spare + 1]
        return mixed[head * HD : (head + 1) * HD] / total, top + jnp.log(total)

    results = {}
    ready = score(items[0])
    for number, item in enumerate(items):
        upcoming = score(items[number + 1]) if number + 1 < len(items) else None
        results[item] = mix(item, *ready)
        ready = upcoming
    for index in range(LONG // block):
        part = pl.ds(index * block, block)
        (first, lse_first), (second, lse_second) = results[0, index], results[1, index]
        att_ref[part, :] = jnp.concatenate([first, second], axis=0).T.astype(BF16)
        lse_ref[0, 0:1, part] = lse_first
        lse_ref[0, 1:2, part] = lse_second


def pair_spec(offset):
    return pl.BlockSpec((LONG, WIDE), lambda i: (0, offset + i))


def lse_spec():
    return pl.BlockSpec((1, 8, LONG), lambda i: (i, 0, 0))


def attention_forward(query, keys, values, row_side, key_side, causal, name):
    return pl.pallas_call(
        partial(attend, causal),
        grid=(PAIRS,),
        in_specs=[pair_spec(query[1]), pair_spec(keys[1]), pair_spec(values[1])]
        + [whole((LONG, WIDE))] * 2,
        out_specs=[pair_spec(0), lse_spec()],
        out_shape=[
            jax.ShapeDtypeStruct((LONG, D), BF16),
            jax.ShapeDtypeStruct((PAIRS, 8, LONG), F32),
        ],
        compiler_params=params(),
        cost_estimate=cost(4 * LONG * LONG * D, 8 * LONG * D, H * LONG * LONG),
        name=name,
    )(query[0], keys[0], values[0], row_side, key_side)


def three_parts(value):
    high = value.astype(BF16)
    rest = value - high.astype(F32)
    middle = rest.astype(BF16)
    return high, middle, (rest - middle.astype(F32)).astype(BF16)


def attend_back(
    causal, q_ref, k_ref, v_ref, att_ref, grad_ref, lse_ref, row_ref, key_ref, dq_ref, dk_ref, dv_ref
):
    block = 256 if causal else 512
    blocks = LONG // block
    lane = lax.broadcasted_iota(jnp.int32, (1, WIDE), 1)
    product = att_ref[...].astype(F32) * grad_ref[...].astype(F32)
    q_across, grad_across = q_ref[...].T, grad_ref[...].T
    lse_down = lse_ref[0].T
    results = []
    for head in range(2):
        inside = lane // HD == head
        spare = HD * (1 - head)
        lse_parts = three_parts(-lse_down[:, head : head + 1])
        delta_parts = three_parts(
            -jnp.sum(jnp.where(inside, product, 0.0), axis=1, keepdims=True)
        )
        row_extra, grad_extra = row_ref[...], jnp.zeros((LONG, WIDE), BF16)
        for i in range(3):
            here = lane == spare + SEGS + 1 + i
            row_extra = jnp.where(here, lse_parts[i], row_extra)
            grad_extra = jnp.where(here, delta_parts[i], grad_extra)
        rows = jnp.where(inside, q_ref[...], row_extra)
        grads = jnp.where(inside, grad_ref[...], grad_extra)
        keys = jnp.where(inside, k_ref[...], key_ref[...])
        ones = (lane > spare + SEGS) & (lane < spare + SEGS + 4)
        vals = jnp.where(inside, v_ref[...], jnp.where(ones, 1.0, 0.0).astype(BF16))
        dq, dk, dv = [], [None] * blocks, [None] * blocks
        for index in range(blocks):
            part = slice(index * block, (index + 1) * block)
            reach = (index + 1) * block if causal else LONG
            scores = mm(rows[part], keys[:reach], 1, 1)
            if causal:
                edge = jnp.where(lower(block, 0), scores[:, reach - block :], NEG)
                scores = (
                    edge
                    if reach == block
                    else jnp.concatenate([scores[:, : reach - block], edge], axis=1)
                )
            probs = jnp.exp(scores)
            dscores = (probs * mm(grads[part], vals[:reach], 1, 1)).astype(BF16)
            dq.append(mm(dscores, keys[:reach]))
            dv_terms = mm(grad_across[:, part], probs.astype(BF16))
            dk_terms = mm(q_across[:, part], dscores)
            for other in range(reach // block):
                cols = slice(other * block, (other + 1) * block)
                for sums, terms in ((dk, dk_terms), (dv, dv_terms)):
                    term = terms[:, cols]
                    sums[other] = term if sums[other] is None else sums[other] + term
        results.append((dq, dk, dv))
    for index in range(blocks):
        part = pl.ds(index * block, block)
        both = jnp.where(lane < HD, results[0][0][index], results[1][0][index])
        dq_ref[part, :] = (both * SCALE).astype(BF16)
        for ref, member in ((dk_ref, 1), (dv_ref, 2)):
            both = [results[0][member][index][:HD], results[1][member][index][HD:]]
            ref[part, :] = jnp.concatenate(both, axis=0).T.astype(BF16)


def attention_backward(query, keys, values, att, grad, lse, row_side, key_side, causal, name):
    shape = jax.ShapeDtypeStruct((LONG, D), BF16)
    return pl.pallas_call(
        partial(attend_back, causal),
        grid=(PAIRS,),
        in_specs=[pair_spec(query[1]), pair_spec(keys[1]), pair_spec(values[1]), pair_spec(0), pair_spec(0)]
        + [lse_spec()]
        + [whole((LONG, WIDE))] * 2,
        out_specs=[pair_spec(0)] * 3,
        out_shape=[shape] * 3,
        compiler_params=params(),
        cost_estimate=cost(10 * LONG * LONG * D, 16 * LONG * D, H * LONG * LONG),
        name=name,
    )(query[0], keys[0], values[0], att, grad, lse, row_side, key_side)


def rows_spec(block, width):
    return pl.BlockSpec((block, width), lambda i: (i, 0))


def project_in(tokens_ref, q_w, k_w, v_w, vec_ref, out_ref):
    left = tokens_ref[...]
    out_ref[:, :D] = ((mm(left, q_w[...]) + vec_ref[SELF_B : SELF_B + 1]) * SCALE).astype(BF16)
    out_ref[:, D : 2 * D] = mm(left, k_w[...]).astype(BF16)
    out_ref[:, 2 * D :] = (mm(left, v_w[...]) + vec_ref[SELF_B + 1 : SELF_B + 2]).astype(BF16)


def between(
    tokens_ref, att_ref, encoded_ref, out_w, q_w, kv_w, vec_ref, resid_ref, hidden_ref, query_ref, pairs_ref
):
    pairs = mm(encoded_ref[...], kv_w[...])
    pairs_ref[:, :D] = pairs[:, :D].astype(BF16)
    pairs_ref[:, D:] = (pairs[:, D:] + vec_ref[CROSS_B + 1 : CROSS_B + 2]).astype(BF16)
    resid = tokens_ref[...].astype(F32) + mm(att_ref[...], out_w[...]) + vec_ref[SELF_B + 2 : SELF_B + 3]
    resid_ref[...] = resid
    xhat, _ = normed(resid)
    hidden = (xhat * vec_ref[GAIN : GAIN + 1] + vec_ref[SHIFT : SHIFT + 1]).astype(BF16)
    hidden_ref[...] = hidden
    query_ref[...] = ((mm(hidden, q_w[...]) + vec_ref[CROSS_B : CROSS_B + 1]) * SCALE).astype(BF16)


INV_SQRT2 = 0.7071067811865476
INV_SQRT_2PI = 0.3989422804014327


def middle(
    hidden1_ref,
    att_ref,
    cot_ref,
    cross_out,
    ffn_in,
    ffn_out,
    vec_ref,
    bias_ref,
    out_ref,
    activ_ref,
    branch3_ref,
    dpre_ref,
    hidden2_ref,
    dresid2_ref,
    branch2_ref,
    datt_ref,
    sums_ref,
    bias_sum_ref,
):
    def vec(row):
        return vec_ref[row : row + 1]

    resid2 = hidden1_ref[...].astype(F32) + mm(att_ref[...], cross_out[...]) + vec(CROSS_B + 2)
    xhat2, inv2 = normed(resid2)
    hidden2 = (xhat2 * vec(GAIN + 1) + vec(SHIFT + 1)).astype(BF16)
    hidden2_ref[...] = hidden2
    pre = mm(hidden2, ffn_in[...]) + bias_ref[...]
    phi = 0.5 + 0.5 * lax.erf(pre * INV_SQRT2)
    activ = (pre * phi).astype(BF16)
    slope = phi + pre * (INV_SQRT_2PI * jnp.exp(-0.5 * pre * pre))
    activ_ref[...] = activ
    resid3 = hidden2.astype(F32) + mm(activ, ffn_out[...]) + vec(OUT_B)
    xhat3, inv3 = normed(resid3)
    out_ref[...] = (xhat3 * vec(GAIN + 2) + vec(SHIFT + 2)).astype(BF16)
    cot = cot_ref[...].astype(F32)
    dresid3 = norm_back(xhat3, inv3, vec(GAIN + 2), cot)
    branch3 = dresid3.astype(BF16)
    branch3_ref[...] = branch3
    dpre = (mm(branch3, ffn_out[...], 1, 1) * slope).astype(BF16)
    dpre_ref[...] = dpre
    dhidden2 = dresid3 + mm(dpre, ffn_in[...], 1, 1)
    dresid2 = norm_back(xhat2, inv2, vec(GAIN + 1), dhidden2)
    dresid2_ref[...] = dresid2
    branch2 = dresid2.astype(BF16)
    branch2_ref[...] = branch2
    datt_ref[...] = mm(branch2, cross_out[...], 1, 1).astype(BF16)

    sums = jnp.concatenate(
        [
            col_sum(dhidden2 * xhat2),
            col_sum(cot * xhat3),
            col_sum(dhidden2),
            col_sum(cot),
            col_sum(branch2.astype(F32)),
            col_sum(branch3.astype(F32)),
            jnp.zeros((2, D), F32),
        ],
        axis=0,
    )
    bias_sum = col_sum(dpre.astype(F32))
    fresh = pl.program_id(0) == 0
    sums_ref[...] = jnp.where(fresh, sums, sums_ref[...] + sums)
    bias_sum_ref[...] = jnp.where(fresh, bias_sum, bias_sum_ref[...] + bias_sum)


def after_cross(
    dq_ref,
    dk_ref,
    dv_ref,
    dresid2_ref,
    resid1_ref,
    q_w,
    kv_w,
    out_w,
    vec_ref,
    encoded_grad_ref,
    dresid1_ref,
    branch1_ref,
    datt_ref,
    sums_ref,
):
    dq, dk, dv = dq_ref[...], dk_ref[...], dv_ref[...]
    encoded_grad_ref[...] = (mm(dk, kv_w[:, :D], 1, 1) + mm(dv, kv_w[:, D:], 1, 1)).astype(BF16)
    dhidden1 = dresid2_ref[...] + mm(dq, q_w[...], 1, 1)
    xhat, inv = normed(resid1_ref[...])
    dresid1 = norm_back(xhat, inv, vec_ref[GAIN : GAIN + 1], dhidden1)
    dresid1_ref[...] = dresid1
    branch1 = dresid1.astype(BF16)
    branch1_ref[...] = branch1
    datt_ref[...] = mm(branch1, out_w[...], 1, 1).astype(BF16)
    sums = jnp.concatenate(
        [
            col_sum(dhidden1 * xhat),
            col_sum(dhidden1),
            col_sum(branch1.astype(F32)),
            col_sum(dq.astype(F32)),
            col_sum(dv.astype(F32)),
            jnp.zeros((3, D), F32),
        ],
        axis=0,
    )
    sums_ref[...] = jnp.where(pl.program_id(0) == 0, sums, sums_ref[...] + sums)


def tokens_back(dq_ref, dk_ref, dv_ref, dresid1_ref, q_w, k_w, v_w, out_ref):
    total = dresid1_ref[...] + mm(dq_ref[...], q_w[...], 1, 1)
    total = total + mm(dk_ref[...], k_w[...], 1, 1)
    out_ref[...] = (total + mm(dv_ref[...], v_w[...], 1, 1)).astype(BF16)


def row_call(kernel, block, ins, weights, outs, sums, name, flops):
    in_specs = [rows_spec(block, a.shape[1]) for a in ins]
    for _, shape, index in weights:
        in_specs.append(pl.BlockSpec(shape, lambda i, index=index: index))
    out_specs = [rows_spec(block, width) for width, _ in outs] + [whole(s) for s in sums]
    out_shape = [jax.ShapeDtypeStruct((LONG, width), dtype) for width, dtype in outs]
    out_shape += [jax.ShapeDtypeStruct(s, F32) for s in sums]
    return pl.pallas_call(
        kernel,
        grid=(LONG // block,),
        in_specs=in_specs,
        out_specs=out_specs,
        out_shape=out_shape,
        compiler_params=params(),
        cost_estimate=cost(flops, flops / 500),
        name=name,
    )(*ins, *[w[0] for w in weights])


def write_masks(kind, target_row, source_row, row_ref, target_ref, source_ref):
    places = lax.broadcasted_iota(jnp.int32, (LONG, 1), 0)
    long = kind == 1
    segment = jnp.where(long, 0, lax.shift_right_logical(places, 8))
    offset = jnp.where(long, places, places & (SHORT - 1))
    lane = lax.broadcasted_iota(jnp.int32, (1, WIDE), 1) & (HD - 1)
    inside = segment == lane
    row_ref[...] = jnp.where(inside | (lane == SEGS), 1.0, 0.0).astype(BF16)
    ones = (lane > SEGS) & (lane < SEGS + 4)
    for ref, lengths in ((target_ref, target_row), (source_ref, source_row)):
        length = jnp.zeros((LONG, 1), jnp.int32)
        for index in range(SEGS):
            length = jnp.where(segment == index, lengths[index], length)
        dead = offset >= length
        blocked = ((lane < SEGS) & ~inside) | ((lane == SEGS) & dead)
        ref[...] = jnp.where(blocked, NEG, jnp.where(ones, 1.0, 0.0)).astype(BF16)


FORWARD_CHUNKS = 11
FORWARD_LOCAL = 64


def forward_kernel(*refs):
    (
        kind_ref, target_len, source_len,
        self_b, cross_b, gain, shift, out_b, in_b,
        tokens_hbm, encoded_hbm, cot_hbm,
        self_in, self_out, cross_q, cross_kv, cross_out, ffn_in, ffn_out,
        w_q_out, w_k_out, w_v_out, w_o_out, w_cq_out, w_ckv_out,
        mixed_out, self_att_out, self_lse_out, resid_out, hidden_out, query_out, pairs_out,
        cross_att_out, cross_lse_out, row_out, target_out, source_out,
        activ_out, branch3_out, dpre_out, hidden2_out, dresid2_out, branch2_out, datt_out, output_out,
        vec_ref, sums_ref, bias_sum_ref,
        w_q, w_k, w_v, w_o, w_cq, w_ckv, w_co, w_fi, w_fo,
        wide, deep, tokens, self_att, resid, hidden, cross_att,
        self_lse, cross_lse, row_side, target_side, source_side,
        bias_ref, pack, pack16, small_full,
        sems, small_sems, chunk_local, local,
    ) = refs
    mixed, branch3 = wide, wide.at[:, pl.ds(0, D)]
    pairs, query, encoded = deep.at[:, pl.ds(0, 2 * D)], deep.at[:, pl.ds(2 * D, D)], deep.at[:, pl.ds(3 * D, D)]
    used = [0]

    def move(src, dst):
        copy = pltpu.make_async_copy(src, dst, local.at[used[0]])
        used[0] += 1
        copy.start()
        return copy

    load_tokens, load_encoded = move(tokens_hbm, tokens), move(encoded_hbm, encoded)
    rows = self_b.shape[1]
    pack[...] = jnp.zeros_like(pack)
    for start, ref in ((SELF_B, self_b), (CROSS_B, cross_b), (GAIN, gain), (SHIFT, shift), (OUT_B, out_b)):
        pack[start : start + ref.shape[0], :rows] = ref[...].astype(F32)
    pack[IN_B : IN_B + 1, : 4 * rows] = in_b[...].astype(F32).reshape(1, 4 * rows)
    pack16[...] = pack[...].astype(BF16)

    greet()
    chunks = [
        (self_in.at[:, pl.ds(0, D)], w_q),
        (self_in.at[:, pl.ds(D, D)], w_k),
        (self_in.at[:, pl.ds(2 * D, D)], w_v),
        (self_out, w_o),
        (cross_q, w_cq),
        (cross_kv, w_ckv),
        (cross_out, w_co),
        (ffn_in.at[:, pl.ds(0, FF // 2)], w_fi.at[:, :, :, :, pl.ds(0, FF // 2)]),
        (ffn_in.at[:, pl.ds(FF // 2, FF // 2)], w_fi.at[:, :, :, :, pl.ds(FF // 2, FF // 2)]),
        (ffn_out.at[pl.ds(0, 2 * rows)], w_fo.at[:, :, :, pl.ds(0, 2 * rows)]),
        (ffn_out.at[pl.ds(2 * rows, 2 * rows)], w_fo.at[:, :, :, pl.ds(2 * rows, 2 * rows)]),
    ]
    def chunk_sems(index):
        return sems.at[:, pl.ds(index * GATHER_COPIES, GATHER_COPIES)], chunk_local.at[index]

    plans = [gather_steps(shard, full, *chunk_sems(i)) for i, (shard, full) in enumerate(chunks)]
    small_plan = small_gather_steps(pack16, small_full, small_sems, chunk_local.at[FORWARD_CHUNKS])
    first_group, second_group, third_group, fourth_group, fifth_group = (0, 1, 2), (3, 4), (5,), (6, 7), (8,)

    def step(group, number):
        for index in group:
            plans[index][number]()

    def vec(row):
        return vec_ref[row : row + 1, :]

    def square(ref):
        return ref[...].reshape(-1, ref.shape[-1])

    block = 512

    def project(weight, column, finish):
        @pl.loop(0, LONG // block)
        def _(i):
            part = pl.ds(pl.multiple_of(i * block, block), block)
            mixed[part, column * D : (column + 1) * D] = finish(mm(tokens[part, :], square(weight))).astype(BF16)

    small_plan[0]()
    step(first_group, 0)
    write_masks(
        kind_ref[0],
        [target_len[0, i] for i in range(SEGS)],
        [source_len[0, i] for i in range(SEGS)],
        row_side,
        target_side,
        source_side,
    )
    saves = [move(row_side, row_out), move(target_side, target_out), move(source_side, source_out)]
    small_plan[1]()
    step((0, 1), 1)
    step((0,), 2)
    step((2,), 1)
    step(second_group, 0)
    step(third_group, 0)
    small_plan[2]()
    step((1,), 2)
    step((0,), 3)
    small_plan[3]()
    for z in range(4):
        for y in range(2):
            for c in range(2):
                owner = (z * 2 + y) * 2 + c
                tile = small_full[z, y, c].astype(F32)
                vec_ref[:, owner * rows : (owner + 1) * rows] = tile[:, :rows]
                bias_ref[:, owner * 4 * rows : (owner + 1) * 4 * rows] = tile[IN_B : IN_B + 1, : 4 * rows]
    step((2,), 2)
    step((1,), 3)
    step((0,), 4)
    load_tokens.wait()
    project(w_q, 0, lambda value: (value + vec(SELF_B)) * SCALE)
    step((2,), 3)
    step((1,), 4)
    step(second_group, 1)
    step(fourth_group, 0)
    project(w_k, 1, lambda value: value)
    step((2,), 4)
    project(w_v, 2, lambda value: value + vec(SELF_B + 1))
    saves += [move(w_q, w_q_out), move(w_k, w_k_out), move(w_v, w_v_out)]
    save_mixed = move(mixed.at[:, pl.ds(0, 3 * D)], mixed_out)
    step(third_group, 1)
    step(fifth_group, 0)

    def ticks(index, table):
        for at, work in table.items():

            @pl.when(index == at)
            def _(work=work):
                for group, number in work:
                    step(group, number)

    @pl.loop(0, PAIRS)
    def _(pair):
        def cols(offset):
            return pl.ds(pl.multiple_of(offset + pair * WIDE, WIDE), WIDE)

        attend(
            True,
            mixed.at[:, cols(0)],
            mixed.at[:, cols(D)],
            mixed.at[:, cols(2 * D)],
            row_side,
            target_side,
            self_att.at[:, cols(0)],
            self_lse.at[pl.ds(pair, 1)],
        )
        ticks(
            pair,
            {
                3: [(second_group, 2)],
                5: [(third_group, 2), (second_group, 3), (fourth_group, 1)],
            },
        )

    save_self = move(self_att, self_att_out)
    saves.append(move(self_lse, self_lse_out))
    step((9,), 0)
    step(second_group, 4)
    saves += [move(w_o, w_o_out), move(w_cq, w_cq_out)]

    @pl.loop(0, LONG // block)
    def _(i):
        part = pl.ds(pl.multiple_of(i * block, block), block)
        total = tokens[part, :].astype(F32) + mm(self_att[part, :], square(w_o)) + vec(SELF_B + 2)
        resid[part, :] = total
        xhat, _ = normed(total)
        normal = (xhat * vec(GAIN) + vec(SHIFT)).astype(BF16)
        hidden[part, :] = normal
        query[part, :] = ((mm(normal, square(w_cq)) + vec(CROSS_B)) * SCALE).astype(BF16)

    save_later = [move(resid, resid_out), move(hidden, hidden_out), move(query, query_out)]
    step(third_group, 3)
    step(fifth_group, 1)
    step((10,), 0)
    step(third_group, 4)
    saves.append(move(w_ckv, w_ckv_out))
    load_encoded.wait()

    @pl.loop(0, LONG // block)
    def _(i):
        part = pl.ds(pl.multiple_of(i * block, block), block)
        both = mm(encoded[part, :], square(w_ckv))
        pairs[part, :D] = both[:, :D].astype(BF16)
        pairs[part, D:] = (both[:, D:] + vec(CROSS_B + 1)).astype(BF16)

    save_later.append(move(pairs, pairs_out))
    save_self.wait()
    load_cot = move(cot_hbm, self_att)

    @pl.loop(0, PAIRS)
    def _(pair):
        def cols(offset):
            return pl.ds(pl.multiple_of(offset + pair * WIDE, WIDE), WIDE)

        attend(
            False,
            query.at[:, cols(0)],
            pairs.at[:, cols(0)],
            pairs.at[:, cols(D)],
            row_side,
            source_side,
            cross_att.at[:, cols(0)],
            cross_lse.at[pl.ds(pair, 1)],
        )
        ticks(
            pair,
            {
                1: [(fourth_group, 2)],
                3: [(fifth_group, 2), ((9,), 1)],
                4: [(fourth_group, 3)],
                5: [(fifth_group, 3)],
            },
        )

    saves.append(move(cross_lse, cross_lse_out))
    save_later.append(move(cross_att, cross_att_out))
    step(fourth_group, 4)
    save_mixed.wait()
    for copy in save_later:
        copy.wait()

    width = D
    parts = [pl.ds(i * block, block) for i in range(LONG // block)]
    columns = [slice(i * width, (i + 1) * width) for i in range(FF // width)]
    w_in, w_out = (lambda: square(w_fi)), (lambda: square(w_fo))
    work = [
        [((10,), 1)], [], [((9,), 2)], [], [((9,), 3)], [((10,), 2)], [], [((10,), 3)],
    ]

    def before(part):
        total = hidden[part, :].astype(F32) + mm(cross_att[part, :], square(w_co)) + vec(CROSS_B + 2)
        resid[part, :] = total
        xhat, _ = normed(total)
        low = (xhat * vec(GAIN + 1) + vec(SHIFT + 1)).astype(BF16)
        tokens[part, :] = low
        return low

    def activate(part, column, product):
        pre = product + bias_ref[:, column]
        phi = 0.5 + 0.5 * lax.erf(pre * INV_SQRT2)
        wide[part, column] = (pre * phi).astype(BF16)
        deep[part, column] = (phi + pre * (INV_SQRT_2PI * jnp.exp(-0.5 * pre * pre))).astype(BF16)

    number = 0
    lows = [before(part) for part in parts]
    step(fifth_group, 4)
    for part, low in zip(parts, lows):
        ready = mm(low, w_in()[:, columns[0]])
        for index, column in enumerate(columns):
            upcoming = mm(low, w_in()[:, columns[index + 1]]) if index + 1 < len(columns) else None
            activate(part, column, ready)
            ready = upcoming
            for group, stage in work[number]:
                step(group, stage)
            number += 1
    saves.append(move(tokens, hidden2_out))
    save_activ = move(wide, activ_out)
    load_cot.wait()
    step((9, 10), 4)

    sums = [None] * 6
    bias_sums = [None] * len(columns)

    def accumulate(store, index, value):
        store[index] = value if store[index] is None else store[index] + value

    for part in parts:
        low2 = tokens[part, :]
        resid3 = low2.astype(F32) + mm(wide[part, :], w_out()) + vec(OUT_B)
        xhat3, inv3 = normed(resid3)
        grad = self_att[part, :].astype(F32)
        self_att[part, :] = (xhat3 * vec(GAIN + 2) + vec(SHIFT + 2)).astype(BF16)
        dresid3 = norm_back(xhat3, inv3, vec(GAIN + 2), grad)
        low3 = dresid3.astype(BF16)
        if part is parts[0]:
            save_activ.wait()
        branch3[part, :] = low3
        saves += [move(self_att.at[part], output_out.at[part]), move(branch3.at[part], branch3_out.at[part])]
        accumulate(sums, 1, col_sum(grad * xhat3))
        accumulate(sums, 3, col_sum(grad))
        accumulate(sums, 5, col_sum(low3.astype(F32)))
        dhidden2 = dresid3
        ready = mm(low3, w_out()[columns[0]], 1, 1)
        for index, column in enumerate(columns):
            upcoming = mm(low3, w_out()[columns[index + 1]], 1, 1) if index + 1 < len(columns) else None
            dpre = (ready * deep[part, column].astype(F32)).astype(BF16)
            deep[part, column] = dpre
            accumulate(bias_sums, index, col_sum(dpre.astype(F32)))
            dhidden2 = dhidden2 + mm(dpre, w_in()[:, column], 1, 1)
            ready = upcoming
        saves.append(move(deep.at[part], dpre_out.at[part]))
        xhat2, inv2 = normed(resid[part, :])
        dresid2 = norm_back(xhat2, inv2, vec(GAIN + 1), dhidden2)
        resid[part, :] = dresid2
        branch2 = dresid2.astype(BF16)
        hidden[part, :] = branch2
        cross_att[part, :] = mm(branch2, square(w_co), 1, 1).astype(BF16)
        saves += [
            move(resid.at[part], dresid2_out.at[part]),
            move(hidden.at[part], branch2_out.at[part]),
            move(cross_att.at[part], datt_out.at[part]),
        ]
        accumulate(sums, 0, col_sum(dhidden2 * xhat2))
        accumulate(sums, 2, col_sum(dhidden2))
        accumulate(sums, 4, col_sum(branch2.astype(F32)))

    sums_ref[...] = jnp.concatenate(sums + [jnp.zeros((2, D), F32)], axis=0)
    bias_sum_ref[...] = jnp.concatenate(bias_sums, axis=1)
    for plan in plans + [small_plan]:
        plan[-1]()
    for copy in saves:
        copy.wait()


def forward_call(ints, smalls, arrays):
    rows = smalls[0].shape[1]
    square = gather_shape(rows, D)
    lse = (PAIRS, 8, LONG)
    wide = (LONG, WIDE)

    def bf(*shape):
        return jax.ShapeDtypeStruct(shape, BF16)

    def f32(*shape):
        return jax.ShapeDtypeStruct(shape, F32)

    held = [bf(*square)] * 5 + [bf(*gather_shape(rows, 2 * D))]
    saved = [
        bf(LONG, 3 * D), bf(LONG, D), f32(*lse), f32(LONG, D), bf(LONG, D), bf(LONG, D), bf(LONG, 2 * D),
        bf(LONG, D), f32(*lse), bf(*wide), bf(*wide), bf(*wide),
        bf(LONG, FF), bf(LONG, D), bf(LONG, FF), bf(LONG, D), f32(LONG, D), bf(LONG, D), bf(LONG, D), bf(LONG, D),
    ]
    outs = held + saved + [f32(16, D), f32(8, D), f32(1, FF)]
    kept = held + [bf(*square), bf(*gather_shape(rows, FF)), bf(*gather_shape(4 * rows, D))]
    kept += [bf(LONG, FF)] * 2 + [bf(LONG, D)] * 2 + [f32(LONG, D)] + [bf(LONG, D)] * 2
    kept += [f32(*lse)] * 2 + [bf(*wide)] * 3 + [f32(1, FF)]
    in_vmem = pl.BlockSpec(memory_space=pltpu.VMEM)
    scratch = [pltpu.VMEM(s.shape, s.dtype) for s in kept]
    scratch += [
        pltpu.VMEM((16, 256), F32),
        pltpu.VMEM((16, 256), BF16),
        pltpu.VMEM((4, 2, 2, 16, 256), BF16),
        pltpu.SemaphoreType.DMA((2, FORWARD_CHUNKS * GATHER_COPIES)),
        pltpu.SemaphoreType.DMA((2, SMALL_COPIES)),
        pltpu.SemaphoreType.DMA((FORWARD_CHUNKS + 1,)),
        pltpu.SemaphoreType.DMA((FORWARD_LOCAL,)),
    ]
    return pl.pallas_call(
        forward_kernel,
        out_shape=outs,
        in_specs=[pl.BlockSpec(memory_space=pltpu.SMEM)] * len(ints)
        + [in_vmem] * len(smalls)
        + [any_spec()] * len(arrays),
        out_specs=[any_spec()] * (len(outs) - 3) + [in_vmem] * 3,
        scratch_shapes=scratch,
        compiler_params=params(collective_id=0, has_side_effects=True),
        cost_estimate=cost(50 * LONG * D * D + 8 * LONG * LONG * D, 90 << 20),
        name="gather_forward_ffn",
    )(*ints, *smalls, *arrays)


def ffn_grads(activ_ref, branch3_ref, hidden2_ref, dpre_ref, out_grad_ref, in_grad_ref):
    out_grad_ref[...] = mm(activ_ref[...], branch3_ref[...], 0, 0).astype(BF16)
    in_grad_ref[...] = mm(hidden2_ref[...], dpre_ref[...], 0, 0).astype(BF16)


def ffn_grads_call(activ, branch3, hidden2, dpre):
    tile = 512
    return pl.pallas_call(
        ffn_grads,
        grid=(FF // tile,),
        in_specs=[
            pl.BlockSpec((LONG, tile), lambda i: (0, i)),
            whole((LONG, D)),
            whole((LONG, D)),
            pl.BlockSpec((LONG, tile), lambda i: (0, i)),
        ],
        out_specs=[
            pl.BlockSpec((tile, D), lambda i: (i, 0)),
            pl.BlockSpec((D, tile), lambda i: (0, i)),
        ],
        out_shape=[jax.ShapeDtypeStruct((FF, D), BF16), jax.ShapeDtypeStruct((D, FF), BF16)],
        compiler_params=params(),
        cost_estimate=cost(4 * LONG * D * FF, 8 * LONG * FF),
        name="ffn_grads",
    )(activ, branch3, hidden2, dpre)


def pair_grads(count, *refs):
    out_ref = refs[2 * count]
    for index in range(count):

        @pl.when(pl.program_id(0) == index)
        def _(index=index):
            out_ref[...] = mm(refs[index][...], refs[count + index][...], 0, 0).astype(BF16)


def pair_grads_call(lefts, rights, name):
    count = len(lefts)
    return pl.pallas_call(
        partial(pair_grads, count),
        grid=(count,),
        in_specs=[whole((LONG, D))] * (2 * count),
        out_specs=pl.BlockSpec((D, D), lambda i: (0, i)),
        out_shape=jax.ShapeDtypeStruct((D, D * count), BF16),
        compiler_params=params(),
        cost_estimate=cost(2 * LONG * D * D * count, 4 * LONG * D * count),
        name=name,
    )(*lefts, *rights)


def pair_fetcher(sources, lse, slots, lse_slots, sems):
    def copies(pair, slot):
        out = []
        for index, (ref, first) in enumerate(sources):
            cols = pl.ds(pl.multiple_of(first + pair * WIDE, WIDE), WIDE)
            out.append(
                pltpu.make_async_copy(ref.at[:, cols], slots.at[slot, index], sems.at[slot, index])
            )
        count = len(sources)
        out.append(pltpu.make_async_copy(lse.at[pair], lse_slots.at[slot, 0], sems.at[slot, count]))
        return out

    return copies


def pair_scratch():
    return [
        pltpu.VMEM((2, 5, LONG, WIDE), BF16),
        pltpu.VMEM((2, 1, 8, LONG), F32),
        pltpu.SemaphoreType.DMA((2, 6)),
    ]


def back_pairs(causal, fetch, slots, lse_slots, row_side, key_side, dq, dk, dv, after):
    @pl.loop(0, PAIRS)
    def _(pair):
        slot = pair % 2

        @pl.when(pair < PAIRS - 1)
        def _():
            for copy in fetch(pair + 1, 1 - slot):
                copy.start()

        for copy in fetch(pair, slot):
            copy.wait()

        def target(member):
            ref, first = member
            return ref.at[:, pl.ds(pl.multiple_of(first + pair * WIDE, WIDE), WIDE)]

        attend_back(
            causal,
            *[slots.at[slot, i] for i in range(5)],
            lse_slots.at[slot],
            row_side,
            key_side,
            target(dq),
            target(dk),
            target(dv),
        )
        for at, work in after.items():

            @pl.when(pair == at)
            def _(work=work):
                for member in work:
                    member()


FIRST_LOCAL = 24


def back_first_kernel(*refs):
    (
        row_side, source_side, vec_ref,
        activ_hbm, branch3_hbm, hidden2_hbm, dpre_hbm,
        query_hbm, pairs_hbm, cross_att_hbm, datt_hbm, lse_hbm,
        dresid2_hbm, resid1_hbm, w_cq_hbm, w_o_hbm,
        dcq_out, dck_out, dcv_out, branch1_out, self_datt_out, dresid1_out,
        in_quarter_out, out_quarter_out, sums_ref,
        activ, dpre, branch3, hidden2, dresid, resid, w_cq, w_o,
        slots, lse_slots, pair_sems,
        local, *scatter_bufs,
    ) = refs
    used = [0]

    def move(src, dst):
        copy = pltpu.make_async_copy(src, dst, local.at[used[0]])
        used[0] += 1
        copy.start()
        return copy

    quarters = [pl.ds(i * D, D) for i in range(FF // D)]
    load_branch3 = move(branch3_hbm, branch3)
    load_activ = [move(activ_hbm.at[:, q], activ.at[:, q]) for q in quarters]
    load_hidden2 = move(hidden2_hbm, hidden2)
    load_dpre = [move(dpre_hbm.at[:, q], dpre.at[:, q]) for q in quarters]
    greet()
    fetch = pair_fetcher(
        [(query_hbm, 0), (pairs_hbm, 0), (pairs_hbm, D), (cross_att_hbm, 0), (datt_hbm, 0)],
        lse_hbm,
        slots,
        lse_slots,
        pair_sems,
    )
    for copy in fetch(0, 0):
        copy.start()
    later = [
        move(dresid2_hbm, dresid),
        move(resid1_hbm, resid),
        move(w_cq_hbm, w_cq),
        move(w_o_hbm, w_o),
    ]
    out_bufs, in_bufs = scatter_bufs[:SCATTER_REFS], scatter_bufs[SCATTER_REFS:]
    out_plan, in_plan = scatter_steps(None, out_bufs), scatter_steps(None, in_bufs)
    out_rows = out_bufs[0].shape[3]
    tile = 2 * out_rows
    load_branch3.wait()
    for q in range(FF // D):
        load_activ[q].wait()
        for part in range(D // tile):
            index = q * (D // tile) + part
            left = activ[:, index * tile : (index + 1) * tile]
            grad = mm(left, branch3[...], 0, 0).astype(BF16)
            out_bufs[0][index // 2, index % 2] = grad.reshape(2, out_rows, D)
    out_plan[0]()
    load_hidden2.wait()
    in_rows = in_bufs[0].shape[3]
    for q in range(FF // D):
        load_dpre[q].wait()
        grad = mm(hidden2[...], dpre[:, quarters[q]], 0, 0).astype(BF16)
        in_bufs[0][:, :, :, :, quarters[q]] = grad.reshape(4, 2, 2, in_rows, D)
    out_plan[1]()
    in_plan[0]()
    back_pairs(
        False,
        fetch,
        slots,
        lse_slots,
        row_side,
        source_side,
        (activ, 0),
        (activ, D),
        (activ, 2 * D),
        {
            0: [in_plan[1]],
            3: [out_plan[2]],
            5: [out_plan[3], in_plan[2]],
        },
    )
    dcq, dck, dcv, branch1 = (activ.at[:, q] for q in quarters)
    self_datt = dpre.at[:, quarters[0]]
    saves = [move(dcq, dcq_out), move(dck, dck_out), move(dcv, dcv_out)]
    for copy in later:
        copy.wait()

    def square(ref):
        return ref[...].reshape(D, ref.shape[-1])

    block = 512
    sums_ref[...] = jnp.zeros_like(sums_ref)

    @pl.loop(0, LONG // block)
    def _(i):
        part = pl.ds(pl.multiple_of(i * block, block), block)
        left = dcq[part, :]
        dhidden = dresid[part, :] + mm(left, square(w_cq), 1, 1)
        xhat, inv = normed(resid[part, :])
        dresid1 = norm_back(xhat, inv, vec_ref[GAIN : GAIN + 1], dhidden)
        dresid[part, :] = dresid1
        low = dresid1.astype(BF16)
        branch1[part, :] = low
        self_datt[part, :] = mm(low, square(w_o), 1, 1).astype(BF16)
        sums_ref[0:1] += col_sum(dhidden * xhat)
        sums_ref[1:2] += col_sum(dhidden)
        sums_ref[2:3] += col_sum(low.astype(F32))
        sums_ref[3:4] += col_sum(left.astype(F32))
        sums_ref[4:5] += col_sum(dcv[part, :].astype(F32))

    saves += [move(branch1, branch1_out), move(self_datt, self_datt_out), move(dresid, dresid1_out)]
    saves.append(move(out_bufs[6], out_quarter_out))
    in_plan[3]()
    saves.append(move(in_bufs[6], in_quarter_out))
    in_plan[-1]()
    out_plan[-1]()
    for copy in saves:
        copy.wait()


def back_first_call(vmem_arrays, hbm_arrays, rows):
    in_vmem = pl.BlockSpec(memory_space=pltpu.VMEM)
    square = gather_shape(rows, D)

    def bf(*shape):
        return jax.ShapeDtypeStruct(shape, BF16)

    def f32(*shape):
        return jax.ShapeDtypeStruct(shape, F32)

    outs = [bf(LONG, D)] * 5 + [f32(LONG, D)]
    outs += [bf(4, rows, FF // 2), bf(4, 4 * rows, D // 2), f32(8, D)]
    held = [bf(LONG, FF)] * 2 + [bf(LONG, D)] * 2 + [f32(LONG, D)] * 2
    held += [bf(*square)] * 2
    scratch = [pltpu.VMEM(h.shape, h.dtype) for h in held] + pair_scratch()
    scratch += [pltpu.SemaphoreType.DMA((FIRST_LOCAL,))]
    scratch += scatter_scratch(4 * rows, D) + scatter_scratch(rows, FF)
    return pl.pallas_call(
        back_first_kernel,
        out_shape=outs,
        in_specs=[in_vmem] * len(vmem_arrays) + [any_spec()] * len(hbm_arrays),
        out_specs=[any_spec()] * 8 + [in_vmem],
        scratch_shapes=scratch,
        compiler_params=params(collective_id=1, has_side_effects=True),
        cost_estimate=cost(26 * LONG * D * D + 10 * LONG * LONG * D, 60 << 20),
        name="backward_cross_scatter_ffn",
    )(*vmem_arrays, *hbm_arrays)


SECOND_LOCAL = 32
SECOND_SHARES = 10
CROSS_PARTS = 5
SELF_PARTS = 3


def back_second_kernel(*refs):
    (
        row_side, target_side, sums_mid, bias_sum, sums_cross,
        self_att_hbm, cross_att_hbm, hidden1_hbm, encoded_hbm,
        branch1_hbm, branch2_hbm, dcq_hbm, dck_hbm, dcv_hbm,
        mixed_hbm, datt_hbm, lse_hbm, tokens_hbm, dresid1_hbm, w_q_hbm, w_k_hbm, w_v_hbm, w_ckv_hbm,
        in_quarter_hbm, out_quarter_hbm,
        tokens_grad_out, encoded_grad_out, *rest,
    ) = refs
    shares, small_share, rest = rest[:SECOND_SHARES], rest[SECOND_SHARES], rest[SECOND_SHARES + 1 :]
    (
        lefts, rights, tokens, dresid, w_q, w_k, w_v, w_ckv, vec_sums,
        slots, lse_slots, pair_sems,
        in_quarter, in_z, in_halves, in_sems, out_quarter, out_z, out_halves, out_sems,
        local, *scatter_bufs,
    ) = rest
    used = [0]

    def move(src, dst):
        copy = pltpu.make_async_copy(src, dst, local.at[used[0]])
        used[0] += 1
        copy.start()
        return copy

    left_sources = (self_att_hbm, cross_att_hbm, hidden1_hbm, encoded_hbm)
    right_sources = (branch1_hbm, branch2_hbm, dcq_hbm, dck_hbm, dcv_hbm)
    load_ffn = [move(in_quarter_hbm, in_quarter), move(out_quarter_hbm, out_quarter)]
    load_left, load_right = [], []
    for index, source in enumerate(right_sources):
        if index < len(left_sources):
            load_left.append(move(left_sources[index], lefts.at[index]))
        load_right.append(move(source, rights.at[index]))
    greet()
    fetch = pair_fetcher(
        [(mixed_hbm, 0), (mixed_hbm, D), (mixed_hbm, 2 * D), (self_att_hbm, 0), (datt_hbm, 0)],
        lse_hbm,
        slots,
        lse_slots,
        pair_sems,
    )
    for copy in fetch(0, 0):
        copy.start()
    load_tokens = move(tokens_hbm, tokens)
    later = [
        move(dresid1_hbm, dresid),
        move(w_q_hbm, w_q),
        move(w_k_hbm, w_k),
        move(w_v_hbm, w_v),
        move(w_ckv_hbm, w_ckv),
    ]

    def bufs(index):
        return scatter_bufs[index * SCATTER_REFS : (index + 1) * SCATTER_REFS]

    plans = [scatter_steps(shares[i], bufs(i)) for i in range(CROSS_PARTS + SELF_PARTS)]
    cross_plans, self_plans = plans[:CROSS_PARTS], plans[CROSS_PARTS:]
    in_plan = scatter_tail(shares[CROSS_PARTS + SELF_PARTS], in_quarter, in_z, in_halves, in_sems)
    out_plan = scatter_tail(shares[CROSS_PARTS + SELF_PARTS + 1], out_quarter, out_z, out_halves, out_sems)
    small_bufs = scatter_bufs[(CROSS_PARTS + SELF_PARTS) * SCATTER_REFS :]
    small_plan = small_scatter_steps(small_share, small_bufs)
    for copy in load_ffn:
        copy.wait()
    in_plan[0]()
    out_plan[0]()
    rows = bufs(0)[0].shape[3]
    for index in range(CROSS_PARTS):
        if index < len(load_left):
            load_left[index].wait()
        load_right[index].wait()
        left = lefts[min(index, len(left_sources) - 1)]
        grad = mm(left, rights[index], 0, 0).astype(BF16)
        bufs(index)[0][...] = grad.reshape(4, 2, 2, rows, D)
        cross_plans[index][0]()
        if index:
            cross_plans[index - 1][1]()
    load_tokens.wait()
    vec_sums[...] = jnp.zeros_like(vec_sums)
    dq, dk, dv = rights.at[0], rights.at[1], rights.at[2]

    def self_part(part):
        def work():
            cols = pl.ds(part * 256, 256)
            target = bufs(CROSS_PARTS + part)[0]
            left = tokens[...]
            ones = jnp.ones((8, LONG), BF16)
            for index, ref in enumerate((dq, dk, dv)):
                right = ref[:, cols]
                grad = mm(left, right, 0, 0).astype(BF16)
                target[:, :, :, :, index * 256 : (index + 1) * 256] = grad.reshape(4, 2, 2, rows, 256)
                if index != 1:
                    row = SELF_B + index // 2
                    vec_sums[row : row + 1, cols] = mm(ones, right)[0:1]
            self_plans[part][0]()

        return work

    def both(members, number):
        return [cross_plans[i][number] for i in members]

    back_pairs(
        True,
        fetch,
        slots,
        lse_slots,
        row_side,
        target_side,
        (dq, 0),
        (dk, 0),
        (dv, 0),
        {
            0: both((4,), 1),
            1: [self_part(0)] + both((0, 1, 2, 3), 2),
            2: [self_plans[0][1]] + both((4,), 2) + both((0, 1), 3) + both((0, 1), 4),
            3: [self_part(1), self_plans[0][2], in_plan[1], out_plan[1], in_plan[2], out_plan[2]]
            + both((2, 3, 4), 3)
            + both((2, 3, 4), 4),
            4: [self_plans[1][1], self_plans[0][3], self_plans[0][4]] + both((0, 1), 5) + both((0, 1), 6),
            5: [self_part(2), self_plans[1][2]]
            + both((2, 3, 4), 5)
            + both((2, 3, 4), 6)
            + both((0, 1), 7)
            + [self_plans[0][5], self_plans[0][6], in_plan[3], out_plan[3]],
        },
    )

    vec_sums[SELF_B + 2 : CROSS_B + 2] = sums_cross[2:5]
    vec_sums[CROSS_B + 2 : CROSS_B + 3] = sums_mid[4:5]
    vec_sums[GAIN : GAIN + 1] = sums_cross[0:1]
    vec_sums[GAIN + 1 : GAIN + 3] = sums_mid[0:2]
    vec_sums[SHIFT : SHIFT + 1] = sums_cross[1:2]
    vec_sums[SHIFT + 1 : SHIFT + 3] = sums_mid[2:4]
    vec_sums[OUT_B : OUT_B + 1] = sums_mid[5:6]
    held = small_bufs[0]
    held[...] = jnp.zeros_like(held)
    for owner in range(16):
        tile = held.at[owner // 4, (owner // 2) % 2, owner % 2]
        tile[:, :rows] = vec_sums[:, owner * rows : (owner + 1) * rows]
        tile[IN_B : IN_B + 1, : 4 * rows] = bias_sum[:, owner * 4 * rows : (owner + 1) * 4 * rows]
    small_plan[0]()
    for copy in later:
        copy.wait()

    def square(ref):
        return ref[...].reshape(D, D)

    block = 256

    def rows_back(index):
        part = pl.ds(index * block, block)
        total = dresid[part, :] + mm(dq[part, :], square(w_q), 1, 1)
        total = total + mm(dk[part, :], square(w_k), 1, 1)
        tokens[part, :] = (total + mm(dv[part, :], square(w_v), 1, 1)).astype(BF16)

    encoded_grad = lefts.at[0]

    def encoded_back(index):
        part = pl.ds(index * block, block)
        weight = w_ckv[...].reshape(D, 2 * D)
        total = mm(rights[CROSS_PARTS - 2, part, :], weight[:, :D], 1, 1)
        total = total + mm(rights[CROSS_PARTS - 1, part, :], weight[:, D:], 1, 1)
        encoded_grad[part, :] = total.astype(BF16)

    rows_back(0)
    self_plans[2][1]()
    small_plan[1]()
    self_plans[1][3]()
    self_plans[1][4]()
    rows_back(1)
    for index in (2, 3, 4):
        cross_plans[index][7]()
    rows_back(2)
    small_plan[2]()
    self_plans[2][2]()
    self_plans[0][7]()
    rows_back(3)
    save = [move(tokens, tokens_grad_out)]
    small_plan[3]()
    self_plans[1][5]()
    self_plans[1][6]()
    self_plans[2][3]()
    self_plans[2][4]()
    encoded_back(0)
    encoded_back(1)
    encoded_back(2)
    small_plan[4]()
    self_plans[1][7]()
    self_plans[2][5]()
    self_plans[2][6]()
    encoded_back(3)
    save.append(move(encoded_grad, encoded_grad_out))
    self_plans[2][7]()
    for copy in save:
        copy.wait()


def back_second_call(vmem_arrays, hbm_arrays, rows):
    in_vmem = pl.BlockSpec(memory_space=pltpu.VMEM)
    square = gather_shape(rows, D)

    def bf(*shape):
        return jax.ShapeDtypeStruct(shape, BF16)

    def f32(*shape):
        return jax.ShapeDtypeStruct(shape, F32)

    outs = [bf(LONG, D)] * 2 + [bf(2, rows, D // 2)] * (CROSS_PARTS + SELF_PARTS)
    outs += [bf(2, rows, FF // 2), bf(2, 4 * rows, D // 2), f32(*SMALL_TILE)]
    held = [bf(4, LONG, D), bf(5, LONG, D), bf(LONG, D), f32(LONG, D)] + [bf(*square)] * 3
    held += [bf(*gather_shape(rows, 2 * D)), f32(16, D)]
    scratch = [pltpu.VMEM(h.shape, h.dtype) for h in held] + pair_scratch()
    scratch += [
        pltpu.VMEM((4, rows, FF // 2), BF16),
        pltpu.VMEM((3, rows, FF // 2), BF16),
        pltpu.VMEM((2, rows, FF // 2), BF16),
        pltpu.SemaphoreType.DMA((2, SCATTER_COPIES)),
        pltpu.VMEM((4, 4 * rows, D // 2), BF16),
        pltpu.VMEM((3, 4 * rows, D // 2), BF16),
        pltpu.VMEM((2, 4 * rows, D // 2), BF16),
        pltpu.SemaphoreType.DMA((2, SCATTER_COPIES)),
        pltpu.SemaphoreType.DMA((SECOND_LOCAL,)),
    ]
    for _ in range(CROSS_PARTS + SELF_PARTS):
        scratch += scatter_scratch(rows, D)
    scratch += small_scatter_scratch()
    return pl.pallas_call(
        back_second_kernel,
        out_shape=outs,
        in_specs=[in_vmem] * len(vmem_arrays) + [any_spec()] * len(hbm_arrays),
        out_specs=[any_spec()] * 2 + [in_vmem] * (len(outs) - 2),
        scratch_shapes=scratch,
        compiler_params=params(collective_id=2, has_side_effects=True),
        cost_estimate=cost(22 * LONG * D * D + 10 * LONG * LONG * D, 60 << 20),
        name="backward_self_scatter_rest",
    )(*vmem_arrays, *hbm_arrays)


BIG = 3


SHARES = 10


def hand_out_kernel(*refs):
    big_in, shares, small_in = refs[:BIG], refs[BIG : BIG + SHARES], refs[BIG + SHARES]
    refs = refs[BIG + SHARES + 1 :]
    big_out, outs, refs = refs[:BIG], refs[BIG : BIG + 13], refs[BIG + 13 :]
    held, small, sems, refs = refs[0], refs[1], refs[2], refs[3:]
    share_bufs, out_bufs = refs[:SHARES], refs[SHARES:]
    used = [0]

    def move(src, dst):
        copy = pltpu.make_async_copy(src, dst, sems.at[used[0]])
        used[0] += 1
        copy.start()
        return copy

    load_shares = [move(shares[i], share_bufs[i]) for i in (9, 8)]
    load_big = [move(ref, held.at[i]) for i, ref in enumerate(big_in)]
    load_shares = load_shares[::-1]
    load_rest = [move(shares[i], share_bufs[i]) for i in range(8)] + [move(small_in, small)]
    self_in, self_b, self_out, cross_q, cross_kv, cross_b, cross_out, ffn_in, in_b, ffn_out, out_b, gain, shift = outs
    self_in_buf, self_out_buf, cross_q_buf, cross_kv_buf, cross_out_buf, ffn_in_buf, ffn_out_buf = out_bufs
    saves = []

    def halves(index, buf, first):
        half = share_bufs[index].shape[2]
        for h in range(2):
            buf[:, first + h * half : first + (h + 1) * half] = share_bufs[index][h].astype(F32)

    load_shares[1].wait()
    halves(9, ffn_out_buf, 0)
    saves.append(move(ffn_out_buf, ffn_out))
    load_shares[0].wait()
    halves(8, ffn_in_buf, 0)
    saves.append(move(ffn_in_buf, ffn_in))
    for copy, src, dst in zip(load_big, range(BIG), big_out):
        copy.wait()
        saves.append(move(held.at[src], dst))
    for copy in load_rest:
        copy.wait()
    for index, buf, first in ((0, self_out_buf, 0), (1, cross_out_buf, 0), (2, cross_q_buf, 0), (3, cross_kv_buf, 0)):
        halves(index, buf, first)
    halves(4, cross_kv_buf, D)
    for part in range(SELF_PARTS):
        for at in range(6):
            first = (at // 2) * D + part * 256 + (at % 2) * 128
            piece = share_bufs[CROSS_PARTS + part][at // 3, :, (at % 3) * 128 : (at % 3 + 1) * 128]
            self_in_buf[:, first : first + 128] = piece.astype(F32)
    for buf, dst in (
        (self_in_buf, self_in),
        (self_out_buf, self_out),
        (cross_q_buf, cross_q),
        (cross_kv_buf, cross_kv),
        (cross_out_buf, cross_out),
    ):
        saves.append(move(buf, dst))
    rows = self_b.shape[1]
    for start, ref in ((SELF_B, self_b), (CROSS_B, cross_b), (GAIN, gain), (SHIFT, shift), (OUT_B, out_b)):
        ref[...] = small[start : start + ref.shape[0], :rows]
    in_b[...] = small[IN_B : IN_B + 1, : 4 * rows]
    for copy in saves:
        copy.wait()


def hand_out_call(arrays, rows):
    in_vmem = pl.BlockSpec(memory_space=pltpu.VMEM)

    def f32(*shape):
        return jax.ShapeDtypeStruct(shape, F32)

    outs = [jax.ShapeDtypeStruct((LONG, D), BF16)] * BIG
    outs += [f32(rows, 3 * D), f32(3, rows), f32(rows, D), f32(rows, D), f32(rows, 2 * D), f32(3, rows)]
    outs += [f32(rows, D), f32(rows, FF), f32(1, 4 * rows), f32(4 * rows, D), f32(1, rows), f32(3, rows), f32(3, rows)]
    large = [outs[BIG + i] for i in (0, 2, 3, 4, 6, 7, 9)]
    scratch = [pltpu.VMEM((BIG, LONG, D), BF16), pltpu.VMEM(SMALL_TILE, F32), pltpu.SemaphoreType.DMA((32,))]
    scratch += [pltpu.VMEM(a.shape, a.dtype) for a in arrays[BIG : BIG + SHARES]]
    scratch += [pltpu.VMEM(o.shape, o.dtype) for o in large]
    places = [any_spec() if i < BIG or i - BIG in (0, 2, 3, 4, 6, 7, 9) else in_vmem for i in range(len(outs))]
    return pl.pallas_call(
        hand_out_kernel,
        out_shape=outs,
        in_specs=[any_spec()] * len(arrays),
        out_specs=places,
        scratch_shapes=scratch,
        compiler_params=params(),
        name="hand_out",
    )(*arrays)


def body(
    tokens,
    encoded,
    cotangent,
    bucket,
    target_len,
    source_len,
    self_in,
    self_bias,
    self_out,
    cross_q,
    cross_kv,
    cross_bias,
    cross_out,
    ffn_in,
    ffn_in_bias,
    ffn_out,
    ffn_out_bias,
    norm_gain,
    norm_shift,
):
    rows = self_in.shape[0]
    owners = D // rows
    direct = owners == 16
    square = (D, D)
    if direct:
        smalls = [self_bias, cross_bias, norm_gain, norm_shift]
        smalls += [ffn_out_bias.reshape(1, rows), ffn_in_bias]
        arrays = [tokens, encoded, cotangent, self_in, self_out, cross_q, cross_kv, cross_out, ffn_in, ffn_out]
        results = forward_call([bucket, target_len, source_len], smalls, arrays)
        pieces = results[:6]
        (mixed, self_att, self_lse, resid1, hidden1, query, pairs, cross_att, cross_lse) = results[6:15]
        row_side, target_side, source_side = results[15:18]
        (activ, branch3, dpre, hidden2, dresid2, branch2, d_cross_att, output) = results[18:26]
        vec, sums_mid, bias_sum = results[26:]
        first = back_first_call(
            [row_side, source_side, vec],
            [activ, branch3, hidden2, dpre, query, pairs, cross_att, d_cross_att, cross_lse]
            + [dresid2, resid1, pieces[4], pieces[3]],
            rows,
        )
        dcq, dck, dcv, branch1, d_self_att, dresid1, in_quarter, out_half, sums_cross = first
        second = back_second_call(
            [row_side, target_side, sums_mid, bias_sum, sums_cross],
            [self_att, cross_att, hidden1, encoded, branch1, branch2, dcq, dck, dcv]
            + [mixed, d_self_att, self_lse, tokens, dresid1, pieces[0], pieces[1], pieces[2], pieces[5]]
            + [in_quarter, out_half],
            rows,
        )
        final = list(hand_out_call([output, *second], rows))
        final[11], final[13] = final[11].reshape(-1), final[13].reshape(-1)
        return tuple(final)

    else:
        everyone = partial(lax.all_gather, axis_name="fsdp", axis=0, tiled=True)
        self_w = everyone(self_in)
        weights = [self_w[:, i * D : (i + 1) * D] for i in range(3)]
        weights += [everyone(w) for w in (self_out, cross_q, cross_kv, cross_out, ffn_in, ffn_out)]
        small = [self_bias, cross_bias, norm_gain, norm_shift, ffn_out_bias, ffn_in_bias]
        small_all = everyone(jnp.concatenate([w.reshape(1, -1) for w in small], axis=1)).astype(F32)
        vec = small_all[:, : IN_B * rows].reshape(owners, IN_B, rows).transpose(1, 0, 2).reshape(IN_B, D)
        vec = jnp.pad(vec, ((0, 3), (0, 0)))
        bias = small_all[:, IN_B * rows : VEC_ROWS * rows].reshape(1, FF)
        row_side, target_side, source_side = mask_lanes(bucket[0], target_len[0], source_len[0])
        (mixed,) = row_call(
            project_in,
            512,
            [tokens],
            [(w, square, (0, 0)) for w in weights[:3]] + [(vec, (16, D), (0, 0))],
            [(3 * D, BF16)],
            [],
            "project_in",
            6 * LONG * D * D,
        )
        self_att, self_lse = attention_forward(
            (mixed, 0), (mixed, PAIRS), (mixed, 2 * PAIRS), row_side, target_side, True, "self_forward"
        )
        resid1, hidden1, query, pairs = row_call(
            between,
            512,
            [tokens, self_att, encoded],
            [(weights[3], square, (0, 0)), (weights[4], square, (0, 0)), (weights[5], (D, 2 * D), (0, 0))]
            + [(vec, (16, D), (0, 0))],
            [(D, F32), (D, BF16), (D, BF16), (2 * D, BF16)],
            [],
            "between",
            8 * LONG * D * D,
        )
        cross_att, cross_lse = attention_forward(
            (query, 0), (pairs, 0), (pairs, PAIRS), row_side, source_side, False, "cross_forward"
        )
    w_q, w_k, w_v, w_o, w_cq, w_ckv, w_co, w_fi, w_fo = weights
    vec_weight = (vec, (16, D), (0, 0))
    (output, activ, branch3, dpre, hidden2, dresid2, branch2, d_cross_att, sums_mid, bias_sum) = row_call(
        middle,
        256,
        [hidden1, cross_att, cotangent],
        [
            (w_co, square, (0, 0)),
            (w_fi, (D, FF), (0, 0)),
            (w_fo, (FF, D), (0, 0)),
            vec_weight,
            (bias, (1, FF), (0, 0)),
        ],
        [(D, BF16), (FF, BF16), (D, BF16), (FF, BF16), (D, BF16), (D, F32), (D, BF16), (D, BF16)],
        [(8, D), (1, FF)],
        "middle",
        36 * LONG * D * D,
    )
    ffn_out_grad, ffn_in_grad = ffn_grads_call(activ, branch3, hidden2, dpre)
    dcq, dck, dcv = attention_backward(
        (query, 0),
        (pairs, 0),
        (pairs, PAIRS),
        cross_att,
        d_cross_att,
        cross_lse,
        row_side,
        source_side,
        False,
        "cross_backward",
    )
    encoded_grad, dresid1, branch1, d_self_att, sums_cross = row_call(
        after_cross,
        512,
        [dcq, dck, dcv, dresid2, resid1],
        [(w_cq, square, (0, 0)), (w_ckv, (D, 2 * D), (0, 0)), (w_o, square, (0, 0)), vec_weight],
        [(D, BF16), (D, F32), (D, BF16), (D, BF16)],
        [(8, D)],
        "after_cross",
        8 * LONG * D * D,
    )
    cross_grad = pair_grads_call(
        [self_att, hidden1, encoded, encoded, cross_att],
        [branch1, dcq, dck, dcv, branch2],
        "cross_grads",
    )
    dq, dk, dv = attention_backward(
        (mixed, 0),
        (mixed, PAIRS),
        (mixed, 2 * PAIRS),
        self_att,
        d_self_att,
        self_lse,
        row_side,
        target_side,
        True,
        "self_backward",
    )
    self_grad = pair_grads_call([tokens] * 3, [dq, dk, dv], "self_grads")
    (tokens_grad,) = row_call(
        tokens_back,
        512,
        [dq, dk, dv, dresid1],
        [(w, square, (0, 0)) for w in weights[:3]],
        [(D, BF16)],
        [],
        "tokens_back",
        6 * LONG * D * D,
    )

    def share_of(grad):
        share = lax.psum_scatter(grad.astype(F32), "fsdp", scatter_dimension=0, tiled=True)
        return lax.psum(share, "dp")

    dq_sum = jnp.sum(dq.astype(F32), axis=0, keepdims=True)
    dv_sum = jnp.sum(dv.astype(F32), axis=0, keepdims=True)
    small_rows = jnp.concatenate(
        [
            dq_sum,
            dv_sum,
            sums_cross[2:5],
            sums_mid[4:5],
            sums_cross[0:1],
            sums_mid[0:2],
            sums_cross[1:2],
            sums_mid[2:4],
            sums_mid[5:6],
        ],
        axis=0,
    )
    packed = small_rows.reshape(IN_B, owners, rows).transpose(1, 0, 2).reshape(owners, IN_B * rows)
    packed = jnp.concatenate([packed, bias_sum.reshape(owners, 4 * rows)], axis=1)
    packed_share = share_of(packed).reshape(-1)
    self_share, cross_share, ffn_in_share, ffn_out_share = map(
        share_of, (self_grad, cross_grad, ffn_in_grad, ffn_out_grad)
    )

    def rows_of(first, count):
        return packed_share[first * rows : (first + count) * rows]

    return (
        output,
        tokens_grad,
        encoded_grad,
        self_share,
        rows_of(SELF_B, 3).reshape(3, rows),
        cross_share[:, :D],
        cross_share[:, D : 2 * D],
        cross_share[:, 2 * D : 4 * D],
        rows_of(CROSS_B, 3).reshape(3, rows),
        cross_share[:, 4 * D :],
        ffn_in_share,
        rows_of(IN_B, 4),
        ffn_out_share,
        rows_of(OUT_B, 1),
        rows_of(GAIN, 3).reshape(3, rows),
        rows_of(SHIFT, 3).reshape(3, rows),
    )


def solution(mesh):
    both = P(("dp", "fsdp"), None)
    rows, cols, flat = P("fsdp", None), P(None, "fsdp"), P("fsdp")
    return jax.shard_map(
        body,
        mesh=mesh,
        in_specs=(both, both, both, P(("dp", "fsdp")), both, both)
        + (rows, cols, rows, rows, rows, cols, rows, rows, flat, rows, flat, cols, cols),
        out_specs=(both, both, both)
        + (rows, cols, rows, rows, rows, cols, rows, rows, flat, rows, flat, cols, cols),
        check_vma=False,
    )
```
